32 devices in a mesh: section: 2 (over x), wide: 16 (over z, y, core).
Axes of the slice: x: 2, y: 2, z: 4, core: 2. Of those that a mesh axis runs over, the one named last changes fastest.
Arguments:
- tokens: bfloat16 [2, 2048, 1152], P(None, 'wide'), may hold values from -6 to 6
- cotangent: bfloat16 [2, 2048, 1152], P(None, 'wide'), may hold values from -6 to 6
- image_of_block: int32 [2, 16], replicated, may hold values from 0 to 3, never falling along the last dimension, each value on 1 to 6 neighbouring positions
- ln1_gain: bfloat16 [2, 1152], P('section', 'wide'), may hold values from 0.5 to 1.5
- ln1_bias: bfloat16 [2, 1152], P('section', 'wide'), may hold values from -1.25 to 1.25
- qkv_weight: bfloat16 [2, 1152, 3456], P('section', 'wide'), may hold values from -0.1875 to 0.1875
- qv_bias: bfloat16 [2, 2, 1152], P('section', None, 'wide'), may hold values from -1.25 to 1.25
- out_weight: bfloat16 [2, 1152, 1152], P('section', 'wide'), may hold values from -0.75 to 0.75
- out_bias: bfloat16 [2, 1152], P('section', 'wide'), may hold values from -1.25 to 1.25
- ln2_gain: bfloat16 [2, 1152], P('section', 'wide'), may hold values from 0.5 to 1.5
- ln2_bias: bfloat16 [2, 1152], P('section', 'wide'), may hold values from -1.25 to 1.25
- fc1_weight: bfloat16 [2, 1152, 4304], P('section', 'wide'), may hold values from -0.1875 to 0.1875
- fc1_bias: bfloat16 [2, 4304], P('section'), may hold values from -1.75 to 1.75
- fc2_weight: bfloat16 [2, 4304, 1152], P('section', None, 'wide'), may hold values from -0.09375 to 0.09375
- fc2_bias: bfloat16 [2, 1152], P('section', 'wide'), may hold values from -1.25 to 1.25
Outputs:
- section_outputs: bfloat16 [2, 2, 2048, 1152], P('section', None, 'wide')
- section_input_grads: float32 [2, 2, 2048, 1152], P('section', None, 'wide')
- ln1_gain_grad: float32 [2, 1152], P('section', 'wide')
- ln1_bias_grad: float32 [2, 1152], P('section', 'wide')
- qkv_weight_grad: float32 [2, 1152, 3456], P('section', 'wide')
- qv_bias_grad: float32 [2, 2, 1152], P('section', None, 'wide')
- out_weight_grad: float32 [2, 1152, 1152], P('section', 'wide')
- out_bias_grad: float32 [2, 1152], P('section', 'wide')
- ln2_gain_grad: float32 [2, 1152], P('section', 'wide')
- ln2_bias_grad: float32 [2, 1152], P('section', 'wide')
- fc1_weight_grad: float32 [2, 1152, 4304], P('section', 'wide')
- fc1_bias_grad: float32 [2, 4304], P('section')
- fc2_weight_grad: float32 [2, 4304, 1152], P('section', None, 'wide')
- fc2_bias_grad: float32 [2, 1152], P('section', 'wide')
The draws below stay inside these ranges and needn't reach their ends.
Inputs may be any that keep to these rules, and one draw needn't show every extreme that they name: `image_of_block`: in each micro-batch the image numbers never fall along the blocks and each image covers 1 to 6 consecutive blocks; some image covers exactly 6.
All inputs are finite; a program needn't handle non-finite values.
Results may differ from the reference program's by a relative error of at most 0.014.
Values may be sent and summed in bfloat16 or wider, within the bound.
A program may use at most 320 MiB of HBM per device.

```python
import math
import jax
import jax.numpy as jnp
import numpy as np
from jax import lax

D = 1152
HEADS = 16
HEAD_DIM = 72
FF = 4304
BLOCK = 128
IMG_BLOCKS = 6
MICRO = 2
NBLK = 16
NTOK = 2048
IMAGES = 4
N_SECTION = 2


def levels(key, shape, cuts, smallest, high):
    loudness, own = 1.0, jax.random.fold_in(key, 6)
    for dim, shards_of in cuts:
        draws = jnp.exp(jax.random.uniform(jax.random.fold_in(own, dim), (shards_of,), jnp.float32, smallest / len(cuts), high / len(cuts)))
        loudness = loudness * jnp.repeat(draws, shape[dim] // shards_of).reshape([-1 if axis == dim else 1 for axis in range(len(shape))])
    return loudness


def split_up(number_of, total, reach, lean):
    loads = [(1 << 20) // math.isqrt(standing ** lean) + 1 for standing in range(2, number_of + 1)]
    spare, given = total - reach - (number_of - 1), [1] * (number_of - 1)
    while spare > 0:
        free = [i for i in range(number_of - 1) if given[i] < reach]
        mass, left = sum([loads[i] for i in free]), spare
        for i in free:
            addition = min(reach - given[i], max(1, left * loads[i] // mass), spare)
            given[i] = given[i] + addition
            spare = spare - addition
    return np.array([reach] + given)


def uneven(own_key, count, total, most, skew):
    if count == 2:
        one = jax.random.randint(own_key, (), max(1, total - most), min(most, total - 1) + 1)
        return jnp.stack([one, total - one])
    sizes = jnp.asarray(split_up(count, total, most, skew), jnp.int32)
    couples = (count - 1) // 2
    source_of, taker = sizes[1:1 + 2 * couples:2], sizes[2:2 + 2 * couples:2]
    room = jnp.minimum(source_of - 1, most - taker)
    moved = jax.random.randint(jax.random.fold_in(own_key, 1), (couples,), 0, 1 << 20) % (room + 1)
    sizes = sizes.at[1:1 + 2 * couples:2].set(source_of - moved).at[2:2 + 2 * couples:2].set(taker + moved)
    return sizes[jax.random.permutation(jax.random.fold_in(own_key, 2), count)]


def noise(own_key, dims, spread, bound, pieces=(), held_as=jnp.bfloat16):
    entries = spread * jax.random.normal(own_key, dims, jnp.float32)
    if pieces:
        entries = entries * levels(own_key, dims, pieces, -0.22, 0.18)
    return jnp.clip(entries, -bound, bound).astype(held_as)


def setup_inputs(seed: int = 0) -> dict:
    keys = jax.random.split(jax.random.key(seed), 16)
    return {
        "tokens": noise(keys[0], (MICRO, NTOK, D), 1.0, 6.0, ((1, 16),)),
        "cotangent": noise(keys[1], (MICRO, NTOK, D), 1.0, 6.0, ((1, 16),)),
        "image_of_block": jax.vmap(lambda own: jnp.searchsorted(jnp.cumsum(uneven(own, IMAGES, NBLK, IMG_BLOCKS, 1)), jnp.arange(NBLK), side="right"))(jax.random.split(keys[2], MICRO)).reshape((MICRO, NBLK)).astype(jnp.int32),
        "ln1_gain": jnp.clip(1.0 + 0.1 * jax.random.normal(keys[3], (N_SECTION, D), jnp.float32), 0.5, 1.5).astype(jnp.bfloat16),
        "ln1_bias": noise(keys[4], (N_SECTION, D), 0.2, 1.25, ((0, 2), (1, 16))),
        "qkv_weight": noise(keys[5], (N_SECTION, D, 3 * D), D ** -0.5, 0.1875, ((0, 2), (1, 16))),
        "qv_bias": noise(keys[6], (N_SECTION, 2, D), 0.2, 1.25, ((0, 2), (2, 16))),
        "out_weight": noise(keys[7], (N_SECTION, D, D), (D // 16) ** -0.5, 0.75, ((0, 2), (1, 16))),
        "out_bias": noise(keys[8], (N_SECTION, D), 0.2, 1.25, ((0, 2), (1, 16))),
        "ln2_gain": jnp.clip(1.0 + 0.1 * jax.random.normal(keys[9], (N_SECTION, D), jnp.float32), 0.5, 1.5).astype(jnp.bfloat16),
        "ln2_bias": noise(keys[10], (N_SECTION, D), 0.2, 1.25, ((0, 2), (1, 16))),
        "fc1_weight": noise(keys[11], (N_SECTION, D, FF), D ** -0.5, 0.1875, ((0, 2), (1, 16))),
        "fc1_bias": noise(keys[12], (N_SECTION, FF), 0.3, 1.75, ((0, 2),)),
        "fc2_weight": noise(keys[13], (N_SECTION, FF, D), FF ** -0.5, 0.09375, ((0, 2), (2, 16))),
        "fc2_bias": noise(keys[14], (N_SECTION, D), 0.2, 1.25, ((0, 2), (1, 16))),
    }


EPSILON = 1e-06
MASKED_SCORE = -1e+30
HIGHEST = lax.Precision.HIGHEST

@jax.custom_vjp
def low(v):
    return lax.optimization_barrier(v.astype(jnp.bfloat16)).astype(jnp.float32)

@jax.custom_vjp
def low_back(v):
    return v

def low_keep(v):
    return (low(v), None)

def low_pass(kept, grad):
    return (grad,)

def back_keep(v):
    return (v, None)

def back_low(kept, grad):
    return (low(grad),)
low.defvjp(low_keep, low_pass)
low_back.defvjp(back_keep, back_low)

def rounded_both(value_in):
    return low(low_back(value_in))

def layer_norm(values_in, scale_gain, shift_bias):
    row_mean = lax.optimization_barrier(jnp.mean(values_in, axis=-1, keepdims=True))
    centred = values_in - row_mean
    row_var = lax.optimization_barrier(jnp.mean(centred * centred, axis=-1, keepdims=True))
    return centred * lax.rsqrt(row_var + EPSILON) * scale_gain + shift_bias

def matmul(left_side, right_side):
    return jnp.dot(left_side, right_side, preferred_element_type=jnp.float32, precision=HIGHEST)

def attend(queries, keys_all, values_all, token_ids):
    margin = (IMG_BLOCKS - 1) * BLOCK
    row_total = queries.shape[0]
    block_rows = min(512, row_total)
    score_scale = 1.0 / math.sqrt(HEAD_DIM)
    query_heads = queries.reshape(row_total, HEADS, HEAD_DIM)
    padded_keys = jnp.pad(keys_all, ((margin, margin), (0, 0))).reshape(row_total + 2 * margin, HEADS, HEAD_DIM)
    padded_values = jnp.pad(values_all, ((margin, margin), (0, 0))).reshape(row_total + 2 * margin, HEADS, HEAD_DIM)
    padded_ids = jnp.pad(token_ids, (margin, margin), constant_values=-1)

    def one_block(block_number):
        first_row = block_number * block_rows
        query_block = lax.dynamic_slice_in_dim(query_heads, first_row, block_rows, 0)
        key_block = lax.dynamic_slice_in_dim(padded_keys, first_row, block_rows + 2 * margin, 0)
        value_block = lax.dynamic_slice_in_dim(padded_values, first_row, block_rows + 2 * margin, 0)
        query_ids = lax.dynamic_slice_in_dim(token_ids, first_row, block_rows, 0)
        key_ids = lax.dynamic_slice_in_dim(padded_ids, first_row, block_rows + 2 * margin, 0)
        scores = low_back(jnp.einsum('qhd,khd->hqk', query_block, key_block, precision=HIGHEST) * score_scale)
        same_image = query_ids[:, None] == key_ids[None, :]
        scores = jnp.where(same_image[None], scores, MASKED_SCORE)
        shifted = scores - lax.optimization_barrier(jnp.max(scores, axis=-1, keepdims=True))
        exponent = jnp.exp(shifted)
        probs = exponent / lax.optimization_barrier(jnp.sum(exponent, axis=-1, keepdims=True))
        result = jnp.einsum('hqk,khd->qhd', low(probs), value_block, precision=HIGHEST)
        return result.reshape(block_rows, HEADS * HEAD_DIM)
    blocks = lax.map(jax.checkpoint(one_block), jnp.arange(row_total // block_rows, dtype=jnp.int32))
    return blocks.reshape(row_total, HEADS * HEAD_DIM)

def layer(values_in, parameters, token_ids):
    gain_one, bias_one, qkv_w, qv_b, out_w, out_b, gain_two, bias_two, fc1_w, fc1_b, fc2_w, fc2_b = parameters
    normed_one = low(layer_norm(values_in, gain_one, bias_one))
    mixed = matmul(normed_one, qkv_w)
    queries = rounded_both(mixed[:, :D] + qv_b[0])
    keys_all = rounded_both(mixed[:, D:2 * D])
    values_all = rounded_both(mixed[:, 2 * D:] + qv_b[1])
    attended = rounded_both(attend(queries, keys_all, values_all, token_ids))
    branch = low_back(matmul(attended, out_w) + out_b)
    residual = values_in + branch
    normed_two = low(layer_norm(residual, gain_two, bias_two))
    hidden_pre = low_back(matmul(normed_two, fc1_w) + fc1_b)
    hidden = low(jax.nn.gelu(hidden_pre, approximate=True))
    feed = low_back(matmul(hidden, fc2_w) + fc2_b)
    return residual + feed

def reference(tokens, cotangent, image_of_block, ln1_gain, ln1_bias, qkv_weight, qv_bias, out_weight, out_bias, ln2_gain, ln2_bias, fc1_weight, fc1_bias, fc2_weight, fc2_bias):
    parameters = [ln1_gain, ln1_bias, qkv_weight, qv_bias, out_weight, out_bias, ln2_gain, ln2_bias, fc1_weight, fc1_bias, fc2_weight, fc2_bias]
    parameters = [array.astype(jnp.float32) for array in parameters]
    first_layer = tuple((array[0] for array in parameters))
    second_layer = tuple((array[1] for array in parameters))
    token_ids = jnp.repeat(image_of_block, BLOCK, axis=1).astype(jnp.int32)

    def one_batch(totals, batch):
        tokens_mb, cotangent_mb, ids_mb = batch
        tokens_float = tokens_mb.astype(jnp.float32)
        probe_zero = jnp.zeros_like(tokens_float)

        def pair(start_values, probe_value, params_first, params_second):
            middle = rounded_both(layer(start_values, params_first, ids_mb))
            final = layer(middle + probe_value, params_second, ids_mb)
            return (middle, final)
        (middle, final), pullback = jax.vjp(pair, tokens_float, probe_zero, first_layer, second_layer)
        grad_tokens, grad_middle, grads_first, grads_second = pullback((jnp.zeros_like(middle), cotangent_mb.astype(jnp.float32)))
        totals = jax.tree.map(lambda old_total, new_term: old_total + new_term, totals, (grads_first, grads_second))
        return (totals, (middle.astype(jnp.bfloat16), final.astype(jnp.bfloat16), grad_tokens, grad_middle))
    zero_totals = jax.tree.map(jnp.zeros_like, (first_layer, second_layer))
    totals, (middles, finals, grad_tokens, grad_middles) = lax.scan(one_batch, zero_totals, (tokens, cotangent, token_ids))
    stacked = [jnp.stack([first_total, second_total]) for first_total, second_total in zip(totals[0], totals[1])]
    return (jnp.stack([middles, finals]), jnp.stack([grad_tokens, grad_middles]), stacked[0], stacked[1], stacked[2], stacked[3], stacked[4], stacked[5], stacked[6], stacked[7], stacked[8], stacked[9], stacked[10], stacked[11])
```

```python
import functools
import math

import jax
import jax.numpy as jnp
from jax import lax
from jax.experimental import pallas as pl
from jax.experimental.pallas import tpu as pltpu
from jax.sharding import PartitionSpec as P

D = 1152
HEADS = 16
HEAD_DIM = 72
FF = 4304
BLOCK = 128
IMG_BLOCKS = 6
EPSILON = 1e-06
MASKED_SCORE = -1e30
SCALE = 1.0 / math.sqrt(HEAD_DIM)
MESH = pl.DeviceIdType.MESH
BF = jnp.bfloat16
F32 = jnp.float32


def place():
    return lax.axis_index("section"), lax.axis_index("wide")


def gather_kernel(count, *refs):
    ins, outs = refs[:count], refs[count : 2 * count]
    local_sem, up_send, up_recv, down_send, down_recv, y_send, y_recv, c_send, c_recv = refs[2 * count :]
    sec, me = place()
    z = me // 4
    low = me % 4
    other_y = me - low + (low + 2) % 4
    other_c = me - me % 2 + (me + 1) % 2

    barrier = pltpu.get_barrier_semaphore()

    def greet(target):
        pl.semaphore_signal(barrier, inc=1, device_id=(sec, target), device_id_type=MESH)

    greet(other_y)
    greet(other_c)

    inside = (z > 0) & (z < 3)

    @pl.when(z > 0)
    def _():
        greet(me - 4)

    @pl.when(z < 3)
    def _():
        greet(me + 4)

    @pl.when(inside)
    def _():
        pl.semaphore_wait(barrier, 4)

    @pl.when(jnp.logical_not(inside))
    def _():
        pl.semaphore_wait(barrier, 3)

    def send(piece, origin, sems, slot, target, first=False):
        return pltpu.make_async_remote_copy(
            src_ref=ins[piece] if first else outs[piece].at[origin],
            dst_ref=outs[piece].at[origin],
            send_sem=sems[0].at[piece, slot],
            recv_sem=sems[1].at[piece, slot],
            device_id=(sec, target),
            device_id_type=MESH,
        )

    up, down, yy, cc = (up_send, up_recv), (down_send, down_recv), (y_send, y_recv), (c_send, c_recv)

    def mine(piece):
        return pltpu.make_async_copy(ins[piece], outs[piece].at[me], local_sem.at[piece])

    def along(piece, origin, first, go_up, go_down):
        zo = origin // 4
        if go_up:

            @pl.when(z < 3)
            def _():
                send(piece, origin, up, zo, me + 4, first).start()

        if go_down:

            @pl.when(z > 0)
            def _():
                send(piece, origin, down, zo, me - 4, first).start()

        send(piece, origin, yy, zo, other_y, first).start()
        send(piece, origin, cc, zo, other_c, first).start()

    for piece in range(count):
        mine(piece).start()
        along(piece, me, True, True, True)
    for step in range(1, 4):
        for piece in range(count):

            @pl.when(z - step >= 0)
            def _():
                origin = me - 4 * step
                send(piece, origin, up, z - step, me).wait_recv()
                along(piece, origin, False, True, False)

            @pl.when(z + step <= 3)
            def _():
                origin = me + 4 * step
                send(piece, origin, down, z + step, me).wait_recv()
                along(piece, origin, False, False, True)

    far = other_y % 4
    for step in range(4):
        zo = (z + step) % 4
        for piece in range(count):
            origin = zo * 4 + far
            send(piece, origin, yy, zo, other_y).wait_recv()
            send(piece, origin, cc, 4 + zo, other_c).start()
    for zo in range(4):
        for piece in range(count):
            send(piece, me, yy, zo, other_y).wait_send()
            for slot in (zo, 4 + zo):
                send(piece, me, cc, slot, other_c).wait_send()
                send(piece, me, cc, slot, other_c).wait_recv()

            @pl.when((zo <= z) & (z < 3))
            def _():
                send(piece, me, up, zo, me).wait_send()

            @pl.when((zo >= z) & (z > 0))
            def _():
                send(piece, me, down, zo, me).wait_send()

    for piece in range(count):
        mine(piece).wait()


def gather(arrays, cid):
    count = len(arrays)
    return pl.pallas_call(
        functools.partial(gather_kernel, count),
        out_shape=[jax.ShapeDtypeStruct((16,) + a.shape, a.dtype) for a in arrays],
        in_specs=[pl.BlockSpec(memory_space=pl.ANY)] * count,
        out_specs=[pl.BlockSpec(memory_space=pl.ANY)] * count,
        scratch_shapes=[pltpu.SemaphoreType.DMA((count,))]
        + [pltpu.SemaphoreType.DMA((count, 4))] * 6
        + [pltpu.SemaphoreType.DMA((count, 8))] * 2,
        compiler_params=pltpu.CompilerParams(collective_id=cid, has_side_effects=True),
    )(*arrays)


def exchange_kernel(x_ref, o_ref, local_sem, send_sem, recv_sem):
    count = x_ref.shape[0]
    sec, me = place()
    barrier = pltpu.get_barrier_semaphore()
    for d in range(1, count):
        pl.semaphore_signal(barrier, inc=1, device_id=(sec, (me + d) % count), device_id_type=MESH)
    pl.semaphore_wait(barrier, count - 1)
    copies = []
    half = count // 2
    order = sorted(range(1, count), key=lambda d: abs(d - half))
    for d in order:
        target = (me + d) % count
        copies.append(
            pltpu.make_async_remote_copy(
                src_ref=x_ref.at[target],
                dst_ref=o_ref.at[me],
                send_sem=send_sem.at[d],
                recv_sem=recv_sem.at[d],
                device_id=(sec, target),
                device_id_type=MESH,
            )
        )
        copies[-1].start()
    own = pltpu.make_async_copy(x_ref.at[me], o_ref.at[me], local_sem)
    own.start()
    own.wait()
    for copy in copies:
        copy.wait()


def exchange(x, cid):
    count = x.shape[0]
    return pl.pallas_call(
        exchange_kernel,
        out_shape=jax.ShapeDtypeStruct(x.shape, x.dtype),
        in_specs=[pl.BlockSpec(memory_space=pl.ANY)],
        out_specs=pl.BlockSpec(memory_space=pl.ANY),
        scratch_shapes=[
            pltpu.SemaphoreType.DMA,
            pltpu.SemaphoreType.DMA((count,)),
            pltpu.SemaphoreType.DMA((count,)),
        ],
        compiler_params=pltpu.CompilerParams(collective_id=cid, has_side_effects=True),
    )(x)


def dot(a, b):
    return jnp.dot(a, b, preferred_element_type=F32)


def window_bias(img_ref, i, start):
    own = img_ref[i]
    return [jnp.where(img_ref[start + j] == own, 0.0, MASKED_SCORE).astype(F32) for j in range(IMG_BLOCKS)]


def attn_fwd_kernel(img_ref, first_ref, qkv_ref, o_ref, lse_ref, k_all, vt_all):
    blocks = qkv_ref.shape[0]
    for j in range(blocks):
        part = qkv_ref[j].astype(F32)
        k_all[j * BLOCK : (j + 1) * BLOCK, :] = part[HEAD_DIM : 2 * HEAD_DIM].T.astype(BF)
        vt_all[:, j * BLOCK : (j + 1) * BLOCK] = part[2 * HEAD_DIM :].astype(BF)

    def one(i, carry):
        start = first_ref[i]
        base = pl.multiple_of(start * BLOCK, BLOCK)
        qt = qkv_ref[i].astype(F32)[:HEAD_DIM].astype(BF)
        s = dot(k_all[pl.ds(base, IMG_BLOCKS * BLOCK), :], qt) * SCALE
        bias = window_bias(img_ref, i, start)
        parts = [s[j * BLOCK : (j + 1) * BLOCK] + bias[j] for j in range(IMG_BLOCKS)]
        top = parts[0]
        for part in parts[1:]:
            top = jnp.maximum(top, part)
        top = jnp.max(top, axis=0, keepdims=True)
        exps = [jnp.exp(part - top) for part in parts]
        total = exps[0]
        for part in exps[1:]:
            total = total + part
        total = jnp.sum(total, axis=0, keepdims=True)
        e = jnp.concatenate([part.astype(BF) for part in exps], axis=0)
        o = dot(vt_all[:, pl.ds(base, IMG_BLOCKS * BLOCK)], e)
        o_ref[i] = (o / total).astype(BF)
        lse_ref[i] = top + jnp.log(total)
        return carry

    lax.fori_loop(0, blocks, one, 0)


def window_first(image_row):
    blocks = image_row.shape[0]
    first = jnp.argmax(image_row[None, :] == image_row[:, None], axis=1).astype(jnp.int32)
    return jnp.minimum(first, blocks - IMG_BLOCKS)


def attention_fwd(image_row, first, qkv):
    blocks = qkv.shape[0]
    return pl.pallas_call(
        attn_fwd_kernel,
        out_shape=[
            jax.ShapeDtypeStruct((blocks, HEAD_DIM, BLOCK), BF),
            jax.ShapeDtypeStruct((blocks, 1, BLOCK), F32),
        ],
        in_specs=[
            pl.BlockSpec(memory_space=pltpu.SMEM),
            pl.BlockSpec(memory_space=pltpu.SMEM),
            pl.BlockSpec(memory_space=pltpu.VMEM),
        ],
        out_specs=[pl.BlockSpec(memory_space=pltpu.VMEM)] * 2,
        scratch_shapes=[
            pltpu.VMEM((blocks * BLOCK, HEAD_DIM), BF),
            pltpu.VMEM((HEAD_DIM, blocks * BLOCK), BF),
        ],
        compiler_params=pltpu.CompilerParams(vmem_limit_bytes=32 << 20),
    )(image_row, first, qkv)


def attn_bwd_kernel(
    img_ref, first_ref, qkv_ref, lse_ref, do_ref, o_ref, k_all, kt_all, v_all, q_all, do_all, dk_all, dv_all
):
    blocks = qkv_ref.shape[0]
    for j in range(blocks):
        part = qkv_ref[j].astype(F32)
        rows = slice(j * BLOCK, (j + 1) * BLOCK)
        q_all[rows, :] = part[:HEAD_DIM].T.astype(BF)
        k_all[rows, :] = part[HEAD_DIM : 2 * HEAD_DIM].T.astype(BF)
        v_all[rows, :] = part[2 * HEAD_DIM :].T.astype(BF)
        kt_all[:, rows] = part[HEAD_DIM : 2 * HEAD_DIM].astype(BF)
        do_all[rows, :] = do_ref[j].astype(F32).T.astype(BF)
    dk_all[...] = jnp.zeros_like(dk_all)
    dv_all[...] = jnp.zeros_like(dv_all)

    def one(i, carry):
        start = first_ref[i]
        base = pl.multiple_of(start * BLOCK, BLOCK)
        here = pl.multiple_of(i * BLOCK, BLOCK)
        near = pl.ds(base, IMG_BLOCKS * BLOCK)
        qt = qkv_ref[i].astype(F32)[:HEAD_DIM].astype(BF)
        s = dot(k_all[near, :], qt) * SCALE
        lse = lse_ref[i]
        bias = window_bias(img_ref, i, start)
        probs = [jnp.exp(s[j * BLOCK : (j + 1) * BLOCK] + bias[j] - lse) for j in range(IMG_BLOCKS)]
        dp = dot(v_all[near, :], do_ref[i])
        total = probs[0] * dp[:BLOCK]
        for j in range(1, IMG_BLOCKS):
            total = total + probs[j] * dp[j * BLOCK : (j + 1) * BLOCK]
        total = jnp.sum(total, axis=0, keepdims=True)
        ds = jnp.concatenate(
            [(probs[j] * (dp[j * BLOCK : (j + 1) * BLOCK] - total)).astype(BF) for j in range(IMG_BLOCKS)], axis=0
        )
        p = jnp.concatenate([part.astype(BF) for part in probs], axis=0)
        dv_all[near, :] += dot(p, do_all[pl.ds(here, BLOCK), :])
        dk_all[near, :] += dot(ds, q_all[pl.ds(here, BLOCK), :])
        dq = dot(kt_all[:, near], ds) * SCALE
        o_ref[i, :HEAD_DIM, :] = dq.astype(BF)
        return carry

    lax.fori_loop(0, blocks, one, 0)
    for j in range(blocks):
        rows = slice(j * BLOCK, (j + 1) * BLOCK)
        kv = jnp.concatenate([(dk_all[rows, :] * SCALE).T, dv_all[rows, :].T], axis=0)
        o_ref[j, HEAD_DIM:, :] = kv.astype(BF)


def attention_bwd(image_row, first, qkv, lse, grad):
    blocks = qkv.shape[0]
    tokens = blocks * BLOCK
    return pl.pallas_call(
        attn_bwd_kernel,
        out_shape=jax.ShapeDtypeStruct((blocks, 3 * HEAD_DIM, BLOCK), BF),
        in_specs=[
            pl.BlockSpec(memory_space=pltpu.SMEM),
            pl.BlockSpec(memory_space=pltpu.SMEM),
        ]
        + [pl.BlockSpec(memory_space=pltpu.VMEM)] * 3,
        out_specs=pl.BlockSpec(memory_space=pltpu.VMEM),
        scratch_shapes=[
            pltpu.VMEM((tokens, HEAD_DIM), BF),
            pltpu.VMEM((HEAD_DIM, tokens), BF),
            pltpu.VMEM((tokens, HEAD_DIM), BF),
            pltpu.VMEM((tokens, HEAD_DIM), BF),
            pltpu.VMEM((tokens, HEAD_DIM), BF),
            pltpu.VMEM((tokens, HEAD_DIM), F32),
            pltpu.VMEM((tokens, HEAD_DIM), F32),
        ],
        compiler_params=pltpu.CompilerParams(vmem_limit_bytes=32 << 20),
    )(image_row, first, qkv, lse, grad)


def normalised(x):
    mean = jnp.mean(x, axis=-1, keepdims=True)
    centred = x - mean
    rstd = lax.rsqrt(jnp.mean(centred * centred, axis=-1, keepdims=True) + EPSILON)
    return centred * rstd, rstd


def norm_backward(grad, xhat, rstd, gain):
    g = grad * gain
    part = g - jnp.mean(g, axis=-1, keepdims=True) - xhat * jnp.mean(g * xhat, axis=-1, keepdims=True)
    return part * rstd, jnp.sum(grad * xhat, axis=0), jnp.sum(grad, axis=0)


def gelu_and_slope(v):
    c = math.sqrt(2.0 / math.pi)
    t = jnp.tanh(c * (v + 0.044715 * v * v * v))
    value = 0.5 * v * (1.0 + t)
    slope = 0.5 * (1.0 + t) + 0.5 * v * (1.0 - t * t) * c * (1.0 + 3 * 0.044715 * v * v)
    return value, slope


def by_rows(x):
    return x.T.reshape(HEADS, HEAD_DIM, x.shape[0])


def swap(x, bits):
    return lax.ppermute(x, "wide", [(i, i ^ bits) for i in range(HEADS)])


def dw_kernel(count, x_ref, *refs):
    ys, o_ref = refs[:count], refs[count]
    for t in range(count):
        term = dot(x_ref[t], ys[t][...])
        if t == 0:
            total = term
        else:
            total = total + term
    o_ref[...] = total.astype(o_ref.dtype)


def weight_grad(x, ys, tile):
    count, rows, block = x.shape
    cols = ys[0].shape[1]
    return pl.pallas_call(
        functools.partial(dw_kernel, count),
        grid=(pl.cdiv(cols, tile),),
        out_shape=jax.ShapeDtypeStruct((rows, cols), BF),
        in_specs=[pl.BlockSpec((count, rows, block), lambda j: (0, 0, 0))]
        + [pl.BlockSpec((block, tile), lambda j: (0, j))] * count,
        out_specs=pl.BlockSpec((rows, tile), lambda j: (0, j)),
        compiler_params=pltpu.CompilerParams(vmem_limit_bytes=48 << 20),
    )(x, *ys)


def on_device(
    tokens,
    cotangent,
    image_of_block,
    ln1_gain,
    ln1_bias,
    qkv_weight,
    qv_bias,
    out_weight,
    out_bias,
    ln2_gain,
    ln2_bias,
    fc1_weight,
    fc1_bias,
    fc2_weight,
    fc2_bias,
):
    sec, me = place()
    micro = tokens.shape[0]
    low = me % 4
    own_qkv = qkv_weight[0].reshape(HEAD_DIM, 3, HEADS, HEAD_DIM).transpose(0, 2, 1, 3).reshape(HEAD_DIM, 3 * D)
    small = jnp.stack(
        [ln1_gain[0], ln1_bias[0], qv_bias[0, 0], qv_bias[0, 1], out_bias[0], ln2_gain[0], ln2_bias[0], fc2_bias[0]]
    )
    small = jnp.pad(small, ((0, 8), (0, BLOCK - HEAD_DIM)))
    w_qkv, w_out, w_fc1, w_fc2t, small_all = gather(
        [own_qkv, out_weight[0], fc1_weight[0], fc2_weight[0].T, small], 1
    )
    w_qkv = w_qkv.reshape(D, 3 * D)
    w_out = w_out.reshape(D, D)
    w_fc1 = w_fc1.reshape(D, FF)
    w_fc2t = w_fc2t.reshape(D, FF)
    vectors = small_all[:, :8, :HEAD_DIM].astype(F32)
    gain1, bias1, _, _, b_out, gain2, bias2, b_fc2 = [vectors[:, i].reshape(D) for i in range(8)]
    b_qkv = jnp.stack([vectors[:, 2], jnp.zeros_like(vectors[:, 2]), vectors[:, 3]], axis=1).reshape(3 * D, 1)
    b_fc1 = fc1_bias[0].astype(F32)

    firsts = [window_first(image_of_block[m]) for m in range(micro)]

    def slot_of(batch):
        return jnp.clip(batch, 0, micro - 1)

    saved = []
    incoming = jnp.zeros_like(tokens[0])
    for tick in range(micro + 1):
        slot = slot_of(tick - sec)
        image_row = lax.dynamic_index_in_dim(image_of_block, slot, 0, keepdims=False)
        first = window_first(image_row)
        x = jnp.where(sec == 0, tokens[min(tick, micro - 1)], incoming).astype(F32)
        xhat1, rstd1 = normalised(x)
        n1 = (xhat1 * gain1 + bias1).astype(BF)
        qkv = jnp.einsum("ck,tc->kt", w_qkv, n1, preferred_element_type=F32) + b_qkv
        qkv = exchange(qkv.astype(BF).reshape(HEADS, 3 * HEAD_DIM, BLOCK), 2)
        att, lse = attention_fwd(image_row, first, qkv)
        att = exchange(att, 3)
        residual = x + jnp.einsum("ct,cd->td", att.reshape(D, BLOCK), w_out, preferred_element_type=F32) + b_out
        xhat2, rstd2 = normalised(residual)
        n2 = (xhat2 * gain2 + bias2).astype(BF)
        hidden_pre = jnp.einsum("td,df->tf", n2, w_fc1, preferred_element_type=F32) + b_fc1
        value, _ = gelu_and_slope(hidden_pre)
        hidden = value.astype(BF)
        out = residual + jnp.einsum("tf,df->td", hidden, w_fc2t, preferred_element_type=F32) + b_fc2
        out_low = out.astype(BF)
        saved.append((x, qkv, lse, att, residual, n2, hidden_pre, hidden, n1, out_low, image_row, first))
        if tick < micro:
            incoming = lax.ppermute(out_low, "section", [(0, 1)])
    outputs = jnp.stack([jnp.where(sec == 0, saved[m][9], saved[m + 1][9]) for m in range(micro)])

    incoming_grad = jnp.zeros(tokens.shape[1:], BF)
    input_grads = []
    x_terms, y_terms, small_total, fc1_bias_total = [], [], 0.0, 0.0
    for tick in range(micro + 1):
        live = jnp.where(sec == 1, tick < micro, tick >= 1).astype(F32)
        late, early = min(tick + 1, micro), max(tick - 1, 0)
        if tick == 0:
            early = late
        if tick == micro:
            late = early
        if late == early:
            kept = saved[late]
        else:
            kept = tuple(jnp.where(sec == 1, a, b) for a, b in zip(saved[late], saved[early]))
        x, qkv, lse, att, residual, n2, hidden_pre, hidden, n1, _, image_row, first = kept
        grad = jnp.where(sec == 1, cotangent[min(tick, micro - 1)], incoming_grad).astype(F32) * live
        fc_grad = grad.astype(BF)
        hidden_grad = jnp.einsum("td,df->tf", fc_grad, w_fc2t, preferred_element_type=F32)
        _, slope = gelu_and_slope(hidden_pre)
        pre_grad = (hidden_grad * slope).astype(BF)
        n2_grad = jnp.einsum("tf,df->td", pre_grad, w_fc1, preferred_element_type=F32)
        xhat2, rstd2 = normalised(residual)
        part, g_gain2, g_bias2 = norm_backward(n2_grad, xhat2, rstd2, gain2)
        residual_grad = grad + part
        branch = residual_grad.astype(BF)
        att_grad = jnp.einsum("td,cd->ct", branch, w_out, preferred_element_type=F32).astype(BF)
        att_grad = exchange(att_grad.reshape(HEADS, HEAD_DIM, BLOCK), 3)
        dqkv = attention_bwd(image_row, first, qkv, lse, att_grad)
        dqkv = exchange(dqkv, 2)
        dqkv_rows = dqkv.reshape(3 * D, BLOCK)
        n1_grad = jnp.einsum("kt,ck->tc", dqkv_rows, w_qkv, preferred_element_type=F32)
        xhat1, rstd1 = normalised(x)
        part, g_gain1, g_bias1 = norm_backward(n1_grad, xhat1, rstd1, gain1)
        input_grad = residual_grad + part
        input_grads.append(input_grad)
        if tick < micro:
            incoming_grad = lax.ppermute(input_grad.astype(BF), "section", [(1, 0)])
        sums = jnp.sum(dqkv.astype(F32), axis=2)
        small_total = small_total + jnp.stack(
            [
                g_gain1,
                g_bias1,
                sums[:, :HEAD_DIM].reshape(D),
                sums[:, 2 * HEAD_DIM :].reshape(D),
                jnp.sum(branch.astype(F32), axis=0),
                g_gain2,
                g_bias2,
                jnp.sum(fc_grad.astype(F32), axis=0),
            ]
        )
        fc1_bias_total = fc1_bias_total + jnp.sum(pre_grad.astype(F32), axis=0)
        xs = jnp.stack([by_rows(n1), att, by_rows(n2), by_rows(fc_grad)]).reshape(4, 4, 4, HEAD_DIM, BLOCK)
        x_of = [lax.dynamic_index_in_dim(xs, low ^ k, 2, keepdims=False) for k in range(4)]
        x_all = [x_of[0]] + [swap(x_of[k], k) for k in range(1, 4)]
        y_own = (dqkv_rows.T, branch, pre_grad, hidden)
        y_two = tuple(swap(y, 2) for y in y_own)
        y_one = tuple(swap(y, 1) for y in y_own)
        y_three = tuple(swap(y, 1) for y in y_two)
        x_terms += x_all
        y_terms += [y_own, y_one, y_two, y_three]
    input_grads = jnp.stack([jnp.where(sec == 0, input_grads[m + 1], input_grads[m]) for m in range(micro)])

    def owned(index, tile):
        x = jnp.stack([x[index] for x in x_terms]).reshape(len(x_terms), 4 * HEAD_DIM, BLOCK)
        total = weight_grad(x, [y[index] for y in y_terms], tile)
        total = total.reshape(4, HEAD_DIM, total.shape[1])
        z = me // 4
        result = lax.dynamic_index_in_dim(total, z, 0, keepdims=False).astype(F32)
        for k in range(1, 4):
            part = lax.dynamic_index_in_dim(total, z ^ k, 0, keepdims=False)
            result = result + swap(part, 4 * k).astype(F32)
        return result

    g_fc2t = owned(3, 512)
    g_fc1 = owned(2, 512)
    g_out = owned(1, 384)
    g_qkv = owned(0, 384)
    g_qkv = g_qkv.reshape(HEAD_DIM, HEADS, 3, HEAD_DIM).transpose(0, 2, 1, 3).reshape(HEAD_DIM, 3 * D)
    packed = jnp.concatenate([small_total.reshape(8 * D), fc1_bias_total])
    packed = lax.psum(packed, "wide")
    g_small = lax.dynamic_slice_in_dim(packed[: 8 * D].reshape(8, HEADS, HEAD_DIM), me, 1, 1)[:, 0]
    g_fc1_bias = packed[8 * D :]
    return (
        outputs[None],
        input_grads[None],
        g_small[0][None],
        g_small[1][None],
        g_qkv[None],
        g_small[2:4][None],
        g_out[None],
        g_small[4][None],
        g_small[5][None],
        g_small[6][None],
        g_fc1[None],
        g_fc1_bias[None],
        g_fc2t.T[None],
        g_small[7][None],
    )


BLK_DEV = 1
REACH = 5


def shifted(value, axis, steps):
    count = lax.axis_size(axis)
    initial, last = (max(0, -steps), min(count, count - steps))
    return lax.ppermute(value, axis, [(source, source + steps) for source in range(initial, last)])


def layer_norm(values_in, scale_gain, shift_bias):
    row_mean = jnp.mean(values_in, axis=-1, keepdims=True)
    centred = values_in - row_mean
    row_var = jnp.mean(centred * centred, axis=-1, keepdims=True)
    return centred * lax.rsqrt(row_var + EPSILON) * scale_gain + shift_bias


def gelu_tanh(pre_value):
    return jax.nn.gelu(pre_value, approximate=True)


def heads_of(values_in):
    return values_in.reshape(values_in.shape[0], HEADS, HEAD_DIM)


def image_mask(image_of_block, batch_slot, wide_rank):
    padding = REACH * BLK_DEV
    padded = jnp.pad(image_of_block, ((0, 0), (padding, padding)), constant_values=-1)
    image_row = lax.dynamic_index_in_dim(padded, batch_slot, 0, keepdims=False)
    key_blocks = lax.dynamic_slice_in_dim(image_row, wide_rank * BLK_DEV, (2 * REACH + 1) * BLK_DEV)
    query_blocks = lax.dynamic_slice_in_dim(image_row, wide_rank * BLK_DEV + padding, BLK_DEV)
    return jnp.repeat(query_blocks, BLOCK)[:, None] == jnp.repeat(key_blocks, BLOCK)[None, :]


def keep_slot(buffer_all, new_value, batch_slot, is_live):
    previous = lax.dynamic_index_in_dim(buffer_all, batch_slot, 0, keepdims=False)
    chosen = jnp.where(is_live, new_value, previous)
    return lax.dynamic_update_index_in_dim(buffer_all, chosen, batch_slot, 0)


def near_keys(key_own, value_own, backward_pass):
    key_parts = []
    value_parts = []
    for offset in range(-REACH, REACH + 1):
        if offset == 0:
            received = (key_own, value_own)
        elif backward_pass:
            received = shifted((key_own, value_own), "wide", -offset)
        else:
            received = shifted((key_own, value_own), "wide", -offset)
        key_parts.append(received[0])
        value_parts.append(received[1])
    return (jnp.concatenate(key_parts, axis=0), jnp.concatenate(value_parts, axis=0))


def return_key_grads(key_terms, value_terms):
    row_count = key_terms.shape[0] // (2 * REACH + 1)
    key_total = key_terms[REACH * row_count : (REACH + 1) * row_count]
    value_total = value_terms[REACH * row_count : (REACH + 1) * row_count]
    for position, offset in enumerate(range(-REACH, REACH + 1)):
        if offset != 0:
            piece_pair = (
                key_terms[position * row_count : (position + 1) * row_count],
                value_terms[position * row_count : (position + 1) * row_count],
            )
            received = shifted((piece_pair[0], piece_pair[1]), "wide", offset)
            key_total = key_total + received[0]
            value_total = value_total + received[1]
    return (key_total, value_total)


def project_qkv(layer_in, weights):
    layer_float = layer_in.astype(jnp.float32)
    normed_one = layer_norm(
        layer_float, weights[0].astype(jnp.float32), weights[1].astype(jnp.float32)
    ).astype(jnp.bfloat16)
    mixed = jnp.dot(normed_one, weights[2], preferred_element_type=jnp.float32)
    queries = (mixed[:, :D] + weights[3][0].astype(jnp.float32)).astype(jnp.bfloat16)
    key_own = mixed[:, D : 2 * D].astype(jnp.bfloat16)
    value_own = (mixed[:, 2 * D :] + weights[3][1].astype(jnp.float32)).astype(jnp.bfloat16)
    return (layer_float, normed_one, queries, key_own, value_own)


def attention_probs(queries, keys_near, same_image):
    score_scale = 1.0 / math.sqrt(HEAD_DIM)
    scores = (
        jnp.einsum(
            "qhd,khd->hqk",
            heads_of(queries),
            heads_of(keys_near),
            preferred_element_type=jnp.float32,
        )
        * score_scale
    )
    scores = jnp.where(same_image[None], scores, MASKED_SCORE)
    row_max = jnp.max(scores, axis=-1, keepdims=True)
    exponent = jnp.exp(scores - row_max)
    return exponent / jnp.sum(exponent, axis=-1, keepdims=True)


def finish_layer(layer_float, queries, keys_near, values_near, same_image, weights, hidden_bias):
    probs = attention_probs(queries, keys_near, same_image)
    probs_low = probs.astype(jnp.bfloat16)
    attended = jnp.einsum(
        "hqk,khd->qhd", probs_low, heads_of(values_near), preferred_element_type=jnp.float32
    )
    attended = attended.reshape(queries.shape[0], D).astype(jnp.bfloat16)
    residual = (
        layer_float
        + jnp.dot(attended, weights[4], preferred_element_type=jnp.float32)
        + weights[5].astype(jnp.float32)
    )
    normed_two = layer_norm(
        residual, weights[6].astype(jnp.float32), weights[7].astype(jnp.float32)
    ).astype(jnp.bfloat16)
    hidden_pre = jnp.dot(
        normed_two, weights[8], preferred_element_type=jnp.float32
    ) + hidden_bias.astype(jnp.float32)
    hidden = gelu_tanh(hidden_pre).astype(jnp.bfloat16)
    output = (
        residual
        + jnp.dot(hidden, weights[9], preferred_element_type=jnp.float32)
        + weights[10].astype(jnp.float32)
    )
    return (probs, probs_low, attended, residual, normed_two, hidden_pre, hidden, output)


def layer_backward(
    layer_float,
    normed_one,
    queries,
    keys_near,
    values_near,
    same_image,
    weights,
    hidden_bias,
    grad_out,
):
    score_scale = 1.0 / math.sqrt(HEAD_DIM)
    probs, probs_low, attended, residual, normed_two, hidden_pre, hidden, output = finish_layer(
        layer_float, queries, keys_near, values_near, same_image, weights, hidden_bias
    )
    feed_grad = grad_out.astype(jnp.bfloat16)
    grad_fc2_weight = jnp.einsum("tf,td->fd", hidden, feed_grad, preferred_element_type=jnp.float32)
    grad_fc2_bias = jnp.sum(feed_grad.astype(jnp.float32), axis=0)
    hidden_grad = jnp.einsum("td,fd->tf", feed_grad, weights[9], preferred_element_type=jnp.float32)
    primal_gelu, gelu_pull = jax.vjp(gelu_tanh, hidden_pre)
    pre_grad = gelu_pull(hidden_grad)[0].astype(jnp.bfloat16)
    grad_fc1_bias = jnp.sum(pre_grad.astype(jnp.float32), axis=0)
    grad_fc1_weight = jnp.einsum(
        "td,tf->df", normed_two, pre_grad, preferred_element_type=jnp.float32
    )
    normed_two_grad = jnp.einsum(
        "tf,df->td", pre_grad, weights[8], preferred_element_type=jnp.float32
    )
    primal_two, norm_two_pull = jax.vjp(
        layer_norm, residual, weights[6].astype(jnp.float32), weights[7].astype(jnp.float32)
    )
    residual_part, grad_ln2_gain, grad_ln2_bias = norm_two_pull(normed_two_grad)
    residual_grad = grad_out + residual_part
    branch_grad = residual_grad.astype(jnp.bfloat16)
    grad_out_bias = jnp.sum(branch_grad.astype(jnp.float32), axis=0)
    grad_out_weight = jnp.einsum(
        "tc,td->cd", attended, branch_grad, preferred_element_type=jnp.float32
    )
    attended_grad = jnp.einsum(
        "td,cd->tc", branch_grad, weights[4], preferred_element_type=jnp.float32
    ).astype(jnp.bfloat16)
    attended_heads = heads_of(attended_grad)
    probs_grad = jnp.einsum(
        "qhd,khd->hqk", attended_heads, heads_of(values_near), preferred_element_type=jnp.float32
    )
    value_terms = jnp.einsum(
        "hqk,qhd->khd", probs_low, attended_heads, preferred_element_type=jnp.float32
    )
    score_grad = (
        probs * (probs_grad - jnp.sum(probs * probs_grad, axis=-1, keepdims=True))
    ).astype(jnp.bfloat16)
    query_grad = (
        jnp.einsum(
            "hqk,khd->qhd", score_grad, heads_of(keys_near), preferred_element_type=jnp.float32
        )
        * score_scale
    )
    query_grad = query_grad.reshape(queries.shape[0], D).astype(jnp.bfloat16)
    key_terms = (
        jnp.einsum(
            "hqk,qhd->khd", score_grad, heads_of(queries), preferred_element_type=jnp.float32
        )
        * score_scale
    )
    key_total, value_total = return_key_grads(key_terms.reshape(-1, D), value_terms.reshape(-1, D))
    key_grad = key_total.astype(jnp.bfloat16)
    value_grad = value_total.astype(jnp.bfloat16)
    grad_qv_bias = jnp.stack(
        [
            jnp.sum(query_grad.astype(jnp.float32), axis=0),
            jnp.sum(value_grad.astype(jnp.float32), axis=0),
        ]
    )
    mixed_grad = jnp.concatenate([query_grad, key_grad, value_grad], axis=1)
    grad_qkv_weight = jnp.einsum(
        "tc,tk->ck", normed_one, mixed_grad, preferred_element_type=jnp.float32
    )
    normed_one_grad = jnp.einsum(
        "tk,ck->tc", mixed_grad, weights[2], preferred_element_type=jnp.float32
    )
    primal_one, norm_one_pull = jax.vjp(
        layer_norm, layer_float, weights[0].astype(jnp.float32), weights[1].astype(jnp.float32)
    )
    input_part, grad_ln1_gain, grad_ln1_bias = norm_one_pull(normed_one_grad)
    input_grad = residual_grad + input_part
    grad_terms = (
        grad_ln1_gain,
        grad_ln1_bias,
        grad_qkv_weight,
        grad_qv_bias,
        grad_out_weight,
        grad_out_bias,
        grad_ln2_gain,
        grad_ln2_bias,
        grad_fc1_weight,
        grad_fc2_weight,
        grad_fc2_bias,
    )
    return (input_grad, grad_terms, grad_fc1_bias)


def on_device_near(
    tokens,
    cotangent,
    image_of_block,
    ln1_gain,
    ln1_bias,
    qkv_weight,
    qv_bias,
    out_weight,
    out_bias,
    ln2_gain,
    ln2_bias,
    fc1_weight,
    fc1_bias,
    fc2_weight,
    fc2_bias,
):
    section_rank = lax.axis_index("section")
    wide_rank = lax.axis_index("wide")
    micro_count = tokens.shape[0]
    weights = (
        lax.all_gather(ln1_gain[0], "wide", axis=0, tiled=True),
        lax.all_gather(ln1_bias[0], "wide", axis=0, tiled=True),
        lax.all_gather(qkv_weight[0], "wide", axis=0, tiled=True),
        lax.all_gather(qv_bias[0], "wide", axis=1, tiled=True),
        lax.all_gather(out_weight[0], "wide", axis=0, tiled=True),
        lax.all_gather(out_bias[0], "wide", axis=0, tiled=True),
        lax.all_gather(ln2_gain[0], "wide", axis=0, tiled=True),
        lax.all_gather(ln2_bias[0], "wide", axis=0, tiled=True),
        lax.all_gather(fc1_weight[0], "wide", axis=0, tiled=True),
        lax.all_gather(fc2_weight[0], "wide", axis=1, tiled=True),
        lax.all_gather(fc2_bias[0], "wide", axis=0, tiled=True),
    )
    hidden_bias = fc1_bias[0]
    inputs_kept = jnp.zeros_like(tokens)
    outputs_kept = jnp.zeros_like(tokens)
    incoming = jnp.zeros_like(tokens[0])
    for tick_number in range(micro_count + 1):
        batch_index = tick_number - section_rank
        is_live = (batch_index >= 0) & (batch_index < micro_count)
        batch_slot = jnp.clip(batch_index, 0, micro_count - 1)
        own_tokens = tokens[min(tick_number, micro_count - 1)]
        layer_in = jnp.where(section_rank == 0, own_tokens, incoming)
        same_image = image_mask(image_of_block, batch_slot, wide_rank)
        layer_float, normed_one, queries, key_own, value_own = project_qkv(layer_in, weights)
        keys_near, values_near = near_keys(key_own, value_own, False)
        output = finish_layer(
            layer_float, queries, keys_near, values_near, same_image, weights, hidden_bias
        )[-1]
        output_low = output.astype(jnp.bfloat16)
        inputs_kept = keep_slot(inputs_kept, layer_in, batch_slot, is_live)
        outputs_kept = keep_slot(outputs_kept, output_low, batch_slot, is_live)
        if tick_number < micro_count:
            incoming = shifted(output_low, "section", 1)
    weights_back = (
        lax.all_gather(ln1_gain[0], "wide", axis=0, tiled=True),
        lax.all_gather(ln1_bias[0], "wide", axis=0, tiled=True),
        lax.all_gather(qkv_weight[0], "wide", axis=0, tiled=True),
        lax.all_gather(qv_bias[0], "wide", axis=1, tiled=True),
        lax.all_gather(out_weight[0], "wide", axis=0, tiled=True),
        lax.all_gather(out_bias[0], "wide", axis=0, tiled=True),
        lax.all_gather(ln2_gain[0], "wide", axis=0, tiled=True),
        lax.all_gather(ln2_bias[0], "wide", axis=0, tiled=True),
        lax.all_gather(fc1_weight[0], "wide", axis=0, tiled=True),
        lax.all_gather(fc2_weight[0], "wide", axis=1, tiled=True),
        lax.all_gather(fc2_bias[0], "wide", axis=0, tiled=True),
    )
    grad_totals = tuple((jnp.zeros(array.shape, jnp.float32) for array in weights_back))
    hidden_bias_total = jnp.zeros(hidden_bias.shape, jnp.float32)
    input_grads = jnp.zeros(tokens.shape, jnp.float32)
    incoming_grad = jnp.zeros(tokens.shape[1:], jnp.bfloat16)
    for tick_number in range(micro_count + 1):
        batch_index = tick_number - 1 + section_rank
        is_live = (batch_index >= 0) & (batch_index < micro_count)
        batch_slot = jnp.clip(batch_index, 0, micro_count - 1)
        from_cotangent = cotangent[min(tick_number, micro_count - 1)].astype(jnp.float32)
        grad_out = jnp.where(
            section_rank == 1, from_cotangent, incoming_grad.astype(jnp.float32)
        ) * is_live.astype(jnp.float32)
        layer_in = lax.dynamic_index_in_dim(inputs_kept, batch_slot, 0, keepdims=False)
        same_image = image_mask(image_of_block, batch_slot, wide_rank)
        layer_float, normed_one, queries, key_own, value_own = project_qkv(layer_in, weights_back)
        keys_near, values_near = near_keys(key_own, value_own, True)
        input_grad, grad_terms, hidden_bias_term = layer_backward(
            layer_float,
            normed_one,
            queries,
            keys_near,
            values_near,
            same_image,
            weights_back,
            hidden_bias,
            grad_out,
        )
        grad_totals = tuple(
            (old_total + new_term for old_total, new_term in zip(grad_totals, grad_terms))
        )
        hidden_bias_total = hidden_bias_total + hidden_bias_term
        input_grads = keep_slot(input_grads, input_grad, batch_slot, is_live)
        if tick_number < micro_count:
            incoming_grad = shifted(input_grad.astype(jnp.bfloat16), "section", -1)
    (
        grad_ln1_gain,
        grad_ln1_bias,
        grad_qkv_weight,
        grad_qv_bias,
        grad_out_weight,
        grad_out_bias,
        grad_ln2_gain,
        grad_ln2_bias,
        grad_fc1_weight,
        grad_fc2_weight,
        grad_fc2_bias,
    ) = grad_totals
    row_sums = (
        lax.psum_scatter(grad_ln1_gain, "wide", scatter_dimension=0, tiled=True),
        lax.psum_scatter(grad_ln1_bias, "wide", scatter_dimension=0, tiled=True),
        lax.psum_scatter(grad_qkv_weight, "wide", scatter_dimension=0, tiled=True),
        lax.psum_scatter(grad_out_weight, "wide", scatter_dimension=0, tiled=True),
        lax.psum_scatter(grad_out_bias, "wide", scatter_dimension=0, tiled=True),
        lax.psum_scatter(grad_ln2_gain, "wide", scatter_dimension=0, tiled=True),
        lax.psum_scatter(grad_ln2_bias, "wide", scatter_dimension=0, tiled=True),
        lax.psum_scatter(grad_fc1_weight, "wide", scatter_dimension=0, tiled=True),
        lax.psum_scatter(grad_fc2_bias, "wide", scatter_dimension=0, tiled=True),
    )
    column_sums = (
        lax.psum_scatter(grad_qv_bias, "wide", scatter_dimension=1, tiled=True),
        lax.psum_scatter(grad_fc2_weight, "wide", scatter_dimension=1, tiled=True),
    )
    hidden_bias_sum = lax.psum(hidden_bias_total, "wide")
    return (
        outputs_kept[None],
        input_grads[None],
        row_sums[0][None],
        row_sums[1][None],
        row_sums[2][None],
        column_sums[0][None],
        row_sums[3][None],
        row_sums[4][None],
        row_sums[5][None],
        row_sums[6][None],
        row_sums[7][None],
        hidden_bias_sum[None],
        column_sums[1][None],
        row_sums[8][None],
    )


def specs():
    ins = (
        P(None, "wide", None),
        P(None, "wide", None),
        P(),
        P("section", "wide"),
        P("section", "wide"),
        P("section", "wide", None),
        P("section", None, "wide"),
        P("section", "wide", None),
        P("section", "wide"),
        P("section", "wide"),
        P("section", "wide"),
        P("section", "wide", None),
        P("section", None),
        P("section", None, "wide"),
        P("section", "wide"),
    )
    outs = (
        P("section", None, "wide", None),
        P("section", None, "wide", None),
        P("section", "wide"),
        P("section", "wide"),
        P("section", "wide", None),
        P("section", None, "wide"),
        P("section", "wide", None),
        P("section", "wide"),
        P("section", "wide"),
        P("section", "wide"),
        P("section", "wide", None),
        P("section", None),
        P("section", None, "wide"),
        P("section", "wide"),
    )
    return ins, outs


def solution(mesh):
    ins, outs = specs()
    body = on_device if mesh.shape["wide"] == HEADS else on_device_near
    return jax.shard_map(body, mesh=mesh, in_specs=ins, out_specs=outs, check_vma=False)
```

```python
import functools
import math

import jax
import jax.numpy as jnp
from jax import lax
from jax.experimental import pallas as pl
from jax.experimental.pallas import tpu as pltpu
from jax.sharding import PartitionSpec as P

D = 1152
HEADS = 16
HEAD_DIM = 72
FF = 4304
FFP = -(-FF // 256) * 256
SPLIT = 9 * 256
BLOCK = 128
IMG_BLOCKS = 6
EPSILON = 1e-06
MASKED_SCORE = -1e30
SCALE = 1.0 / math.sqrt(HEAD_DIM)
MESH = pl.DeviceIdType.MESH
BF = jnp.bfloat16
F32 = jnp.float32


def place():
    return lax.axis_index("section"), lax.axis_index("wide")


def gather_kernel(count, *refs):
    ins, outs = refs[:count], refs[count : 2 * count]
    local_sem, up_send, up_recv, down_send, down_recv, y_send, y_recv, c_send, c_recv = refs[2 * count :]
    sec, me = place()
    z = me // 4
    low = me % 4
    other_y = me - low + (low + 2) % 4
    other_c = me - me % 2 + (me + 1) % 2

    barrier = pltpu.get_barrier_semaphore()

    def greet(target):
        pl.semaphore_signal(barrier, inc=1, device_id=(sec, target), device_id_type=MESH)

    greet(other_y)
    greet(other_c)

    inside = (z > 0) & (z < 3)

    @pl.when(z > 0)
    def _():
        greet(me - 4)

    @pl.when(z < 3)
    def _():
        greet(me + 4)

    @pl.when(inside)
    def _():
        pl.semaphore_wait(barrier, 4)

    @pl.when(jnp.logical_not(inside))
    def _():
        pl.semaphore_wait(barrier, 3)

    def send(piece, origin, sems, slot, target, first=False):
        return pltpu.make_async_remote_copy(
            src_ref=ins[piece] if first else outs[piece].at[origin],
            dst_ref=outs[piece].at[origin],
            send_sem=sems[0].at[piece, slot],
            recv_sem=sems[1].at[piece, slot],
            device_id=(sec, target),
            device_id_type=MESH,
        )

    up, down, yy, cc = (up_send, up_recv), (down_send, down_recv), (y_send, y_recv), (c_send, c_recv)

    def mine(piece):
        return pltpu.make_async_copy(ins[piece], outs[piece].at[me], local_sem.at[piece])

    def along(piece, origin, first, go_up, go_down):
        zo = origin // 4
        if go_up:

            @pl.when(z < 3)
            def _():
                send(piece, origin, up, zo, me + 4, first).start()

        if go_down:

            @pl.when(z > 0)
            def _():
                send(piece, origin, down, zo, me - 4, first).start()

        send(piece, origin, yy, zo, other_y, first).start()
        send(piece, origin, cc, zo, other_c, first).start()

    for piece in range(count):
        mine(piece).start()
        along(piece, me, True, True, True)
    for step in range(1, 4):
        for piece in range(count):

            @pl.when(z - step >= 0)
            def _():
                origin = me - 4 * step
                send(piece, origin, up, z - step, me).wait_recv()
                along(piece, origin, False, True, False)

            @pl.when(z + step <= 3)
            def _():
                origin = me + 4 * step
                send(piece, origin, down, z + step, me).wait_recv()
                along(piece, origin, False, False, True)

    far = other_y % 4
    for step in range(4):
        zo = (z + step) % 4
        for piece in range(count):
            origin = zo * 4 + far
            send(piece, origin, yy, zo, other_y).wait_recv()
            send(piece, origin, cc, 4 + zo, other_c).start()
    for zo in range(4):
        for piece in range(count):
            send(piece, me, yy, zo, other_y).wait_send()
            for slot in (zo, 4 + zo):
                send(piece, me, cc, slot, other_c).wait_send()
                send(piece, me, cc, slot, other_c).wait_recv()

            @pl.when((zo <= z) & (z < 3))
            def _():
                send(piece, me, up, zo, me).wait_send()

            @pl.when((zo >= z) & (z > 0))
            def _():
                send(piece, me, down, zo, me).wait_send()

    for piece in range(count):
        mine(piece).wait()


def gather(arrays, cid):
    count = len(arrays)
    return pl.pallas_call(
        functools.partial(gather_kernel, count),
        out_shape=[jax.ShapeDtypeStruct((16,) + a.shape, a.dtype) for a in arrays],
        in_specs=[pl.BlockSpec(memory_space=pl.ANY)] * count,
        out_specs=[pl.BlockSpec(memory_space=pl.ANY)] * count,
        scratch_shapes=[pltpu.SemaphoreType.DMA((count,))]
        + [pltpu.SemaphoreType.DMA((count, 4))] * 6
        + [pltpu.SemaphoreType.DMA((count, 8))] * 2,
        compiler_params=pltpu.CompilerParams(collective_id=cid, has_side_effects=True),
    )(*arrays)


def flip(low, k):
    return [low, low + 1 - 2 * (low % 2), (low + 2) % 4, 3 - low][k]


def greet_all(count, sec, me):
    barrier = pltpu.get_barrier_semaphore()
    for d in range(1, count):
        pl.semaphore_signal(barrier, inc=1, device_id=(sec, (me + d) % count), device_id_type=MESH)
    pl.semaphore_wait(barrier, count - 1)


class Whole:
    def __init__(self, zero, one, cols=None):
        self.sources, self.cols = (zero, one), cols

    def shape(self):
        rows, cols = self.sources[0].shape
        return (4, rows, cols if self.cols is None else self.cols[1] - self.cols[0])

    def source(self, ref, low, k):
        return ref if self.cols is None else ref.at[:, self.cols[0] : self.cols[1]]

    forwarded = True


class Rows:
    def __init__(self, zero, one):
        self.sources = (zero, one)

    def shape(self):
        return self.sources[0].shape

    def source(self, ref, low, k):
        return ref.at[flip(low, k)]

    forwarded = False


class PlaneCopies:
    def __init__(self, item, zero_ref, one_ref, slot, local_sem, send_sem, recv_sem):
        self.item, self.refs, self.slot = item, (zero_ref, one_ref), slot
        self.local_sem, self.send_sem, self.recv_sem = local_sem, send_sem, recv_sem
        self.sec, self.me = place()
        self.low = self.me % 4

    def remote(self, src, k, to):
        return pltpu.make_async_remote_copy(
            src_ref=src,
            dst_ref=self.slot(k),
            send_sem=self.send_sem.at[k],
            recv_sem=self.recv_sem.at[k],
            device_id=(self.sec, self.me - self.low + flip(self.low, to)),
            device_id_type=MESH,
        )

    def local(self, ref):
        return pltpu.make_async_copy(self.item.source(ref, self.low, 0), self.slot(0), self.local_sem)

    def start(self):
        def go(ref):
            self.local(ref).start()
            for k in (2, 1) if self.item.forwarded else (2, 3, 1):
                self.remote(self.item.source(ref, self.low, k), k, k).start()

        @pl.when(self.sec == 0)
        def _():
            go(self.refs[0])

        @pl.when(self.sec == 1)
        def _():
            go(self.refs[1])

    def forward(self):
        if self.item.forwarded:
            self.remote(self.slot(2), 2, 2).wait_recv()
            self.remote(self.slot(2), 3, 1).start()

    def finish(self):
        self.local(self.refs[0]).wait()
        for k in (1, 2, 3):
            self.remote(self.slot(k), k, k).wait_send()
            if k != 2 or not self.item.forwarded:
                self.remote(self.slot(k), k, k).wait_recv()


def exchange_kernel(items, x_ref, *refs):
    n = len(items)
    sources, o_ref, outs = refs[: 2 * n], refs[2 * n], refs[2 * n + 1 : 3 * n + 1]
    local_sem, send_sem, recv_sem = refs[3 * n + 1 : 3 * n + 4]
    count = x_ref.shape[0]
    sec, me = place()
    greet_all(count, sec, me)
    copies = []
    half = count // 2
    order = sorted(range(1, count), key=lambda d: abs(d - half))
    for d in order:
        target = (me + d) % count
        copies.append(
            pltpu.make_async_remote_copy(
                src_ref=x_ref.at[target],
                dst_ref=o_ref.at[me],
                send_sem=send_sem.at[d],
                recv_sem=recv_sem.at[d],
                device_id=(sec, target),
                device_id_type=MESH,
            )
        )
        copies[-1].start()
    own = pltpu.make_async_copy(x_ref.at[me], o_ref.at[me], local_sem)
    own.start()
    behind = []
    for i, item in enumerate(items):
        sems = refs[3 * n + 4 + 3 * i : 3 * n + 7 + 3 * i]
        behind.append(
            PlaneCopies(item, sources[2 * i], sources[2 * i + 1], lambda k, i=i: outs[i].at[k], *sems)
        )
        behind[-1].start()
    own.wait()
    for one in behind:
        one.forward()
    for copy in copies:
        copy.wait()
    for one in behind:
        one.finish()


def exchange(x, cid, items=()):
    count = x.shape[0]
    sources = [source for item in items for source in item.sources]
    anywhere = pl.BlockSpec(memory_space=pl.ANY)
    out = pl.pallas_call(
        functools.partial(exchange_kernel, list(items)),
        out_shape=[jax.ShapeDtypeStruct(x.shape, x.dtype)]
        + [jax.ShapeDtypeStruct(item.shape(), item.sources[0].dtype) for item in items],
        in_specs=[anywhere] * (1 + len(sources)),
        out_specs=[anywhere] * (1 + len(items)),
        scratch_shapes=[
            pltpu.SemaphoreType.DMA,
            pltpu.SemaphoreType.DMA((count,)),
            pltpu.SemaphoreType.DMA((count,)),
        ]
        + [pltpu.SemaphoreType.DMA, pltpu.SemaphoreType.DMA((4,)), pltpu.SemaphoreType.DMA((4,))] * len(items),
        compiler_params=pltpu.CompilerParams(collective_id=cid, has_side_effects=True),
    )(x, *sources)
    return out if items else out[0]


def dot(a, b):
    return jnp.dot(a, b, preferred_element_type=F32)


def window_bias(img_ref, i, start):
    own = img_ref[i]
    return [jnp.where(img_ref[start + j] == own, 0.0, MASKED_SCORE).astype(F32) for j in range(IMG_BLOCKS)]


def attn_fwd_kernel(img_ref, first_ref, qkv_ref, o_ref, lse_ref, k_all, vt_all):
    blocks = qkv_ref.shape[0]
    for j in range(blocks):
        part = qkv_ref[j].astype(F32)
        k_all[j * BLOCK : (j + 1) * BLOCK, :] = part[HEAD_DIM : 2 * HEAD_DIM].T.astype(BF)
        vt_all[:, j * BLOCK : (j + 1) * BLOCK] = part[2 * HEAD_DIM :].astype(BF)

    def one(i, carry):
        start = first_ref[i]
        base = pl.multiple_of(start * BLOCK, BLOCK)
        qt = qkv_ref[i].astype(F32)[:HEAD_DIM].astype(BF)
        s = dot(k_all[pl.ds(base, IMG_BLOCKS * BLOCK), :], qt) * SCALE
        bias = window_bias(img_ref, i, start)
        parts = [s[j * BLOCK : (j + 1) * BLOCK] + bias[j] for j in range(IMG_BLOCKS)]
        top = parts[0]
        for part in parts[1:]:
            top = jnp.maximum(top, part)
        top = jnp.max(top, axis=0, keepdims=True)
        exps = [jnp.exp(part - top) for part in parts]
        total = exps[0]
        for part in exps[1:]:
            total = total + part
        total = jnp.sum(total, axis=0, keepdims=True)
        e = jnp.concatenate([part.astype(BF) for part in exps], axis=0)
        o = dot(vt_all[:, pl.ds(base, IMG_BLOCKS * BLOCK)], e)
        o_ref[i] = (o / total).astype(BF)
        lse_ref[i] = top + jnp.log(total)
        return carry

    lax.fori_loop(0, blocks, one, 0)


def window_first(image_row):
    blocks = image_row.shape[0]
    first = jnp.argmax(image_row[None, :] == image_row[:, None], axis=1).astype(jnp.int32)
    return jnp.minimum(first, blocks - IMG_BLOCKS)


def attention_fwd(image_row, first, qkv):
    blocks = qkv.shape[0]
    return pl.pallas_call(
        attn_fwd_kernel,
        out_shape=[
            jax.ShapeDtypeStruct((blocks, HEAD_DIM, BLOCK), BF),
            jax.ShapeDtypeStruct((blocks, 1, BLOCK), F32),
        ],
        in_specs=[
            pl.BlockSpec(memory_space=pltpu.SMEM),
            pl.BlockSpec(memory_space=pltpu.SMEM),
            pl.BlockSpec(memory_space=pltpu.VMEM),
        ],
        out_specs=[pl.BlockSpec(memory_space=pltpu.VMEM)] * 2,
        scratch_shapes=[
            pltpu.VMEM((blocks * BLOCK, HEAD_DIM), BF),
            pltpu.VMEM((HEAD_DIM, blocks * BLOCK), BF),
        ],
        compiler_params=pltpu.CompilerParams(vmem_limit_bytes=32 << 20),
    )(image_row, first, qkv)


def attn_bwd_kernel(
    img_ref, first_ref, qkv_ref, lse_ref, do_ref, o_ref, k_all, kt_all, v_all, q_all, do_all, dk_all, dv_all
):
    blocks = qkv_ref.shape[0]
    for j in range(blocks):
        part = qkv_ref[j].astype(F32)
        rows = slice(j * BLOCK, (j + 1) * BLOCK)
        q_all[rows, :] = part[:HEAD_DIM].T.astype(BF)
        k_all[rows, :] = part[HEAD_DIM : 2 * HEAD_DIM].T.astype(BF)
        v_all[rows, :] = part[2 * HEAD_DIM :].T.astype(BF)
        kt_all[:, rows] = part[HEAD_DIM : 2 * HEAD_DIM].astype(BF)
        do_all[rows, :] = do_ref[j].astype(F32).T.astype(BF)
    dk_all[...] = jnp.zeros_like(dk_all)
    dv_all[...] = jnp.zeros_like(dv_all)

    def one(i, carry):
        start = first_ref[i]
        base = pl.multiple_of(start * BLOCK, BLOCK)
        here = pl.multiple_of(i * BLOCK, BLOCK)
        near = pl.ds(base, IMG_BLOCKS * BLOCK)
        qt = qkv_ref[i].astype(F32)[:HEAD_DIM].astype(BF)
        s = dot(k_all[near, :], qt) * SCALE
        lse = lse_ref[i]
        bias = window_bias(img_ref, i, start)
        probs = [jnp.exp(s[j * BLOCK : (j + 1) * BLOCK] + bias[j] - lse) for j in range(IMG_BLOCKS)]
        dp = dot(v_all[near, :], do_ref[i])
        total = probs[0] * dp[:BLOCK]
        for j in range(1, IMG_BLOCKS):
            total = total + probs[j] * dp[j * BLOCK : (j + 1) * BLOCK]
        total = jnp.sum(total, axis=0, keepdims=True)
        ds = jnp.concatenate(
            [(probs[j] * (dp[j * BLOCK : (j + 1) * BLOCK] - total)).astype(BF) for j in range(IMG_BLOCKS)], axis=0
        )
        p = jnp.concatenate([part.astype(BF) for part in probs], axis=0)
        dv_all[near, :] += dot(p, do_all[pl.ds(here, BLOCK), :])
        dk_all[near, :] += dot(ds, q_all[pl.ds(here, BLOCK), :])
        dq = dot(kt_all[:, near], ds) * SCALE
        o_ref[i, :HEAD_DIM, :] = dq.astype(BF)
        return carry

    lax.fori_loop(0, blocks, one, 0)
    for j in range(blocks):
        rows = slice(j * BLOCK, (j + 1) * BLOCK)
        kv = jnp.concatenate([(dk_all[rows, :] * SCALE).T, dv_all[rows, :].T], axis=0)
        o_ref[j, HEAD_DIM:, :] = kv.astype(BF)


def attention_bwd(image_row, first, qkv, lse, grad):
    blocks = qkv.shape[0]
    tokens = blocks * BLOCK
    return pl.pallas_call(
        attn_bwd_kernel,
        out_shape=jax.ShapeDtypeStruct((blocks, 3 * HEAD_DIM, BLOCK), BF),
        in_specs=[
            pl.BlockSpec(memory_space=pltpu.SMEM),
            pl.BlockSpec(memory_space=pltpu.SMEM),
        ]
        + [pl.BlockSpec(memory_space=pltpu.VMEM)] * 3,
        out_specs=pl.BlockSpec(memory_space=pltpu.VMEM),
        scratch_shapes=[
            pltpu.VMEM((tokens, HEAD_DIM), BF),
            pltpu.VMEM((HEAD_DIM, tokens), BF),
            pltpu.VMEM((tokens, HEAD_DIM), BF),
            pltpu.VMEM((tokens, HEAD_DIM), BF),
            pltpu.VMEM((tokens, HEAD_DIM), BF),
            pltpu.VMEM((tokens, HEAD_DIM), F32),
            pltpu.VMEM((tokens, HEAD_DIM), F32),
        ],
        compiler_params=pltpu.CompilerParams(vmem_limit_bytes=32 << 20),
    )(image_row, first, qkv, lse, grad)


def normalised(x):
    mean = jnp.mean(x, axis=-1, keepdims=True)
    centred = x - mean
    rstd = lax.rsqrt(jnp.mean(centred * centred, axis=-1, keepdims=True) + EPSILON)
    return centred * rstd, rstd


def norm_backward(grad, xhat, rstd, gain):
    g = grad * gain
    part = g - jnp.mean(g, axis=-1, keepdims=True) - xhat * jnp.mean(g * xhat, axis=-1, keepdims=True)
    return part * rstd, jnp.sum(grad * xhat, axis=0), jnp.sum(grad, axis=0)


def gelu_and_slope(v):
    c = math.sqrt(2.0 / math.pi)
    t = jnp.tanh(c * (v + 0.044715 * v * v * v))
    value = 0.5 * v * (1.0 + t)
    slope = 0.5 * (1.0 + t) + 0.5 * v * (1.0 - t * t) * c * (1.0 + 3 * 0.044715 * v * v)
    return value, slope


def by_rows(x):
    return x.T.reshape(HEADS, HEAD_DIM, x.shape[0])


def pad_ff(x):
    return jnp.pad(x, ((0, 0),) * (x.ndim - 1) + ((0, FFP - FF),))


def owners(x):
    return x.reshape(4, 4, HEAD_DIM, BLOCK).swapaxes(0, 1)


TENSORS = ("fc2", "fc1", "out", "qkv")


def final_kernel(tiles, early, late, *refs):
    refs = list(refs)

    def take(n):
        part = refs[:n]
        del refs[:n]
        return part

    small_ref = take(1)[0]
    x_refs = {name: take(2) for name in TENSORS}
    early_refs = take(len(early))
    late_refs = take(2 * len(late))
    small_out = take(1)[0]
    out_refs = dict(zip(TENSORS, take(4)))
    y_bufs = dict(zip(TENSORS, take(4)))
    x_buf = take(1)[0]
    g_bufs, one_bufs, two_bufs = [dict(zip(TENSORS, take(4))) for _ in range(3)]
    small_got = take(1)[0]
    early_sem, small_send, small_recv = take(3)
    sems = {name: take(4) for name in TENSORS}
    late_sems = [take(3) for _ in late]

    sec, me = place()
    z, low = me // 4, me % 4
    pair = z + 1 - 2 * (z % 2)
    count = small_ref.shape[0]
    greet_all(count, sec, me)

    loads = []
    for i, (name, batch, cols) in enumerate(early):
        dst = y_bufs[name].at[4 * batch : 4 * batch + 4]
        if cols is not None:
            dst = dst.at[:, :, cols[0] : cols[1]]
        loads.append((name, pltpu.make_async_copy(early_refs[i], dst, early_sem.at[i])))
        loads[-1][1].start()
    behind = []
    for i, (name, batch, item) in enumerate(late):

        def slot(k, name=name, batch=batch, item=item):
            ref = y_bufs[name].at[4 * batch + k]
            return ref if item.cols is None else ref.at[:, item.cols[0] : item.cols[1]]

        behind.append((name, PlaneCopies(item, late_refs[2 * i], late_refs[2 * i + 1], slot, *late_sems[i])))
        behind[-1][1].start()
    smalls = []
    for d in range(1, count):
        target = (me + d) % count
        smalls.append(
            pltpu.make_async_remote_copy(
                src_ref=small_ref.at[target],
                dst_ref=small_got.at[d],
                send_sem=small_send.at[d],
                recv_sem=small_recv.at[d],
                device_id=(sec, target),
                device_id_type=MESH,
            )
        )
        smalls[-1].start()

    def first(name, i):
        send, recv = sems[name][0], sems[name][1]
        return pltpu.make_async_remote_copy(
            src_ref=g_bufs[name].at[i, 2:4],
            dst_ref=one_bufs[name].at[i],
            send_sem=send.at[i],
            recv_sem=recv.at[i],
            device_id=(sec, pair * 4 + low),
            device_id_type=MESH,
        )

    def second(name, i):
        send, recv = sems[name][2], sems[name][3]
        return pltpu.make_async_remote_copy(
            src_ref=g_bufs[name].at[i, 1],
            dst_ref=two_bufs[name].at[i],
            send_sem=send.at[i],
            recv_sem=recv.at[i],
            device_id=(sec, (3 - z) * 4 + low),
            device_id_type=MESH,
        )

    def ready(name):
        for other, one in behind:
            if other == name:
                one.forward()
        for other, load in loads:
            if other == name:
                load.wait()
        for other, one in behind:
            if other == name:
                one.finish()
        rows = []
        for owner in (z, 3 - z, pair, 3 - pair):
            rows.append(
                jnp.concatenate(
                    [x_refs[name][batch][k, owner].astype(F32) for batch in range(2) for k in range(4)], axis=1
                )
            )
        x_buf[...] = jnp.concatenate(rows, axis=0).astype(BF)

    def columns(name, i):
        width = tiles[name][1]
        return pl.ds(pl.multiple_of(i * width, 128), width)

    def compute(name, i):
        width = tiles[name][1]
        buf = y_bufs[name]
        if name == "qkv":
            rows = pl.ds(pl.multiple_of(i * width, 128), width)
            y = jnp.concatenate([buf[part, rows, :] for part in range(8)], axis=1)
            total = lax.dot_general(x_buf[...], y, (((1,), (1,)), ((), ())), preferred_element_type=F32)
        else:
            y = jnp.concatenate([buf[part, :, columns(name, i)] for part in range(8)], axis=0)
            total = dot(x_buf[...], y)
        g_bufs[name][i] = total.reshape(4, HEAD_DIM, width).astype(BF)
        first(name, i).start()

    def middle(name, i):
        first(name, i).wait_recv()
        out_refs[name][:, columns(name, i)] = g_bufs[name][i, 0].astype(F32) + one_bufs[name][i, 0].astype(F32)
        g_bufs[name][i, 1] = (g_bufs[name][i, 1].astype(F32) + one_bufs[name][i, 1].astype(F32)).astype(BF)
        second(name, i).start()

    def finish(name, i):
        second(name, i).wait_recv()
        out_refs[name][:, columns(name, i)] += two_bufs[name][i].astype(F32)
        first(name, i).wait_send()
        second(name, i).wait_send()

    def loop(name, *steps):
        def body(i, carry):
            for step, which in steps:
                step(which, i)
            return carry

        lax.fori_loop(0, tiles[name][0], body, 0)

    ready("fc2")
    loop("fc2", (compute, "fc2"))
    ready("fc1")
    loop("fc1", (compute, "fc1"), (middle, "fc2"))
    ready("out")
    loop("out", (compute, "out"))
    loop("fc1", (middle, "fc1"), (finish, "fc2"))
    ready("qkv")
    loop("qkv", (compute, "qkv"))
    loop("out", (middle, "out"))
    loop("fc1", (finish, "fc1"))
    loop("qkv", (middle, "qkv"))
    loop("out", (finish, "out"))
    for copy in smalls:
        copy.wait()
    total = small_ref[me]
    for d in range(1, count):
        total = total + small_got[d]
    small_out[...] = total
    loop("qkv", (finish, "qkv"))


def final(small, xs, early, late, cid):
    count = small.shape[0]
    tokens = xs["qkv"][0].shape[-1]
    widths = {"fc2": FFP, "fc1": FFP, "out": D, "qkv": 3 * D}
    tiles = {name: (w // (256 if name[0] == "f" else 384), 256 if name[0] == "f" else 384) for name, w in widths.items()}
    anywhere, vmem = pl.BlockSpec(memory_space=pl.ANY), pl.BlockSpec(memory_space=pltpu.VMEM)
    args = [small] + [x for name in TENSORS for x in xs[name]]
    n_vmem = len(args)
    args += [e[3] for e in early] + [source for _, _, item in late for source in item.sources]
    dma = pltpu.SemaphoreType.DMA
    scratch = []
    for name in TENSORS:
        shape = (8, widths[name], tokens) if name == "qkv" else (8, tokens, widths[name])
        scratch.append(pltpu.VMEM(shape, BF))
    scratch.append(pltpu.VMEM((4 * HEAD_DIM, 8 * tokens), BF))
    for lead in ((4,), (2,), ()):
        for name in TENSORS:
            scratch.append(pltpu.VMEM((tiles[name][0],) + lead + (HEAD_DIM, tiles[name][1]), BF))
    scratch.append(pltpu.VMEM(small.shape, F32))
    scratch += [dma((len(early),)), dma((count,)), dma((count,))]
    for name in TENSORS:
        scratch += [dma((tiles[name][0],))] * 4
    scratch += [dma, dma((4,)), dma((4,))] * len(late)
    out = pl.pallas_call(
        functools.partial(final_kernel, tiles, [e[:3] for e in early], late),
        out_shape=[jax.ShapeDtypeStruct(small.shape[1:], F32)]
        + [jax.ShapeDtypeStruct((HEAD_DIM, widths[name]), F32) for name in TENSORS],
        in_specs=[vmem] * n_vmem + [anywhere] * (len(args) - n_vmem),
        out_specs=[vmem] * 5,
        scratch_shapes=scratch,
        compiler_params=pltpu.CompilerParams(
            collective_id=cid, has_side_effects=True, vmem_limit_bytes=60 << 20
        ),
    )(*args)
    return out[0], dict(zip(TENSORS, out[1:]))


def on_device(
    tokens,
    cotangent,
    image_of_block,
    ln1_gain,
    ln1_bias,
    qkv_weight,
    qv_bias,
    out_weight,
    out_bias,
    ln2_gain,
    ln2_bias,
    fc1_weight,
    fc1_bias,
    fc2_weight,
    fc2_bias,
):
    sec, me = place()
    own_qkv = qkv_weight[0].reshape(HEAD_DIM, 3, HEADS, HEAD_DIM).transpose(0, 2, 1, 3).reshape(HEAD_DIM, 3 * D)
    small = jnp.stack(
        [ln1_gain[0], ln1_bias[0], qv_bias[0, 0], qv_bias[0, 1], out_bias[0], ln2_gain[0], ln2_bias[0], fc2_bias[0]]
    )
    small = jnp.pad(small, ((0, 8), (0, BLOCK - HEAD_DIM)))
    w_qkv, w_out, w_fc1, w_fc2t, small_all = gather(
        [own_qkv, out_weight[0], pad_ff(fc1_weight[0]), pad_ff(fc2_weight[0].T), small], 1
    )
    w_qkv = w_qkv.reshape(D, 3 * D)
    w_out = w_out.reshape(D, D)
    w_fc1 = w_fc1.reshape(D, FFP)
    w_fc2t = w_fc2t.reshape(D, FFP)
    vectors = small_all[:, :8, :HEAD_DIM].astype(F32)
    gain1, bias1, _, _, b_out, gain2, bias2, b_fc2 = [vectors[:, i].reshape(D) for i in range(8)]
    b_qkv = jnp.stack([vectors[:, 2], jnp.zeros_like(vectors[:, 2]), vectors[:, 3]], axis=1).reshape(3 * D, 1)
    b_fc1 = pad_ff(fc1_bias[0]).astype(F32)

    def choose(at_zero, at_one):
        return jax.tree.map(lambda a, b: jnp.where(sec == 0, a, b), at_zero, at_one)

    saved = []
    incoming = jnp.zeros_like(tokens[0])
    sent = {}
    for tick in range(3):
        slot = jnp.clip(tick - sec, 0, 1)
        image_row = lax.dynamic_index_in_dim(image_of_block, slot, 0, keepdims=False)
        first = window_first(image_row)
        x = jnp.where(sec == 0, tokens[min(tick, 1)], incoming).astype(F32)
        xhat1, _ = normalised(x)
        n1 = (xhat1 * gain1 + bias1).astype(BF)
        qkv = jnp.einsum("ck,tc->kt", w_qkv, n1, preferred_element_type=F32) + b_qkv
        qkv = qkv.astype(BF).reshape(HEADS, 3 * HEAD_DIM, BLOCK)
        if tick < 2:
            qkv = exchange(qkv, 2)
            att, lse = attention_fwd(image_row, first, qkv)
            att = exchange(att, 3)
        else:
            old = [saved[0], saved[1]]
            qkv, sent["h0a"] = exchange(qkv, 4, [Whole(old[0]["hidden"], old[1]["hidden"], (0, SPLIT))])
            att, lse = attention_fwd(image_row, first, qkv)
            att, sent["n1_0"], sent["att_0"], sent["n2_0"] = exchange(
                att, 5, [Rows(old[0][name], old[1][name]) for name in ("n1", "att_rows", "n2")]
            )
        residual = x + jnp.einsum("ct,cd->td", att.reshape(D, BLOCK), w_out, preferred_element_type=F32) + b_out
        xhat2, _ = normalised(residual)
        n2 = (xhat2 * gain2 + bias2).astype(BF)
        hidden_pre = jnp.einsum("td,df->tf", n2, w_fc1, preferred_element_type=F32) + b_fc1
        value, _ = gelu_and_slope(hidden_pre)
        hidden = value.astype(BF)
        out = residual + jnp.einsum("tf,df->td", hidden, w_fc2t, preferred_element_type=F32) + b_fc2
        out_low = out.astype(BF)
        saved.append(
            dict(
                x=x, qkv=qkv, lse=lse, residual=residual, hidden_pre=hidden_pre, hidden=hidden, low=out_low,
                att_rows=owners(att), n1=owners(by_rows(n1)), n2=owners(by_rows(n2)), image=image_row, first=first,
            )
        )
        if tick < 2:
            incoming = lax.ppermute(out_low, "section", [(0, 1)])
    outputs = jnp.stack([choose(saved[m]["low"], saved[m + 1]["low"]) for m in range(2)])

    incoming_grad = jnp.zeros(tokens.shape[1:], BF)
    input_grads, done, back = [], [], []
    needed = ("x", "qkv", "lse", "residual", "hidden_pre", "image", "first")
    for tick in range(3):
        if tick == 1:
            k = choose({name: saved[0][name] for name in needed}, {name: saved[2][name] for name in needed})
        else:
            k = saved[1]
        grad = jnp.where(sec == 1, cotangent[min(tick, 1)], incoming_grad).astype(F32)
        fc_grad = grad.astype(BF)
        hidden_grad = jnp.einsum("td,df->tf", fc_grad, w_fc2t, preferred_element_type=F32)
        _, slope = gelu_and_slope(k["hidden_pre"])
        pre_grad = (hidden_grad * slope).astype(BF)
        n2_grad = jnp.einsum("tf,df->td", pre_grad, w_fc1, preferred_element_type=F32)
        xhat2, rstd2 = normalised(k["residual"])
        part, g_gain2, g_bias2 = norm_backward(n2_grad, xhat2, rstd2, gain2)
        residual_grad = grad + part
        branch = residual_grad.astype(BF)
        att_grad = jnp.einsum("td,cd->ct", branch, w_out, preferred_element_type=F32).astype(BF)
        att_grad = att_grad.reshape(HEADS, HEAD_DIM, BLOCK)
        back.append(dict(fc=owners(by_rows(fc_grad)), pre=pre_grad, branch=branch))
        if tick == 0:
            att_grad, sent["h0b"] = exchange(att_grad, 6, [Whole(saved[0]["hidden"], saved[1]["hidden"], (SPLIT, FFP))])
        elif tick == 1:
            att_grad, sent["n1_1"], sent["att_1"], sent["n2_1"] = exchange(
                att_grad, 8, [Rows(saved[1][name], saved[2][name]) for name in ("n1", "att_rows", "n2")]
            )
        else:
            att_grad, sent["fc_0"], sent["fc_1"] = exchange(
                att_grad, 10, [Rows(back[1]["fc"], back[0]["fc"]), Rows(back[2]["fc"], back[1]["fc"])]
            )
        dqkv = attention_bwd(k["image"], k["first"], k["qkv"], k["lse"], att_grad)
        if tick == 0:
            dqkv, sent["h1a"] = exchange(dqkv, 7, [Whole(saved[1]["hidden"], saved[2]["hidden"], (0, SPLIT))])
        elif tick == 1:
            dqkv, sent["h1b"] = exchange(dqkv, 9, [Whole(saved[1]["hidden"], saved[2]["hidden"], (SPLIT, FFP))])
        else:
            dqkv, sent["pre_0a"] = exchange(dqkv, 11, [Whole(back[1]["pre"], back[0]["pre"], (0, SPLIT))])
        back[-1]["dqkv"] = dqkv.reshape(3 * D, BLOCK)
        n1_grad = jnp.einsum("kt,ck->tc", back[-1]["dqkv"], w_qkv, preferred_element_type=F32)
        xhat1, rstd1 = normalised(k["x"])
        part, g_gain1, g_bias1 = norm_backward(n1_grad, xhat1, rstd1, gain1)
        input_grad = residual_grad + part
        input_grads.append(input_grad)
        sums = jnp.sum(dqkv.astype(F32), axis=2)
        done.append(
            [
                g_gain1,
                g_bias1,
                sums[:, :HEAD_DIM].reshape(D),
                sums[:, 2 * HEAD_DIM :].reshape(D),
                jnp.sum(branch.astype(F32), axis=0),
                g_gain2,
                g_bias2,
                jnp.sum(fc_grad.astype(F32), axis=0),
                jnp.sum(pre_grad.astype(F32), axis=0),
            ]
        )
        if tick < 2:
            incoming_grad = lax.ppermute(input_grad.astype(BF), "section", [(1, 0)])
    input_grads = jnp.stack([choose(input_grads[m + 1], input_grads[m]) for m in range(2)])

    sums = [choose(done[1][i] + done[2][i], done[0][i] + done[1][i]) for i in range(9)]
    by_owner = jnp.stack(sums[:8]).reshape(8, HEADS, HEAD_DIM).transpose(1, 0, 2)
    by_owner = jnp.pad(by_owner, ((0, 0), (0, 0), (0, BLOCK - HEAD_DIM)))
    lines = FFP // BLOCK
    to_all = jnp.broadcast_to(sums[8].reshape(1, lines, BLOCK), (HEADS, lines, BLOCK))
    to_all = jnp.pad(to_all, ((0, 0), (0, 40 - lines), (0, 0)))
    xs = {
        "fc2": [sent["fc_0"], sent["fc_1"]],
        "fc1": [sent["n2_0"], sent["n2_1"]],
        "out": [sent["att_0"], sent["att_1"]],
        "qkv": [sent["n1_0"], sent["n1_1"]],
    }
    early = [
        ("fc2", 0, (0, SPLIT), sent["h0a"]),
        ("fc2", 0, (SPLIT, FFP), sent["h0b"]),
        ("fc2", 1, (0, SPLIT), sent["h1a"]),
        ("fc2", 1, (SPLIT, FFP), sent["h1b"]),
        ("fc1", 0, (0, SPLIT), sent["pre_0a"]),
    ]
    late = [
        ("fc1", 0, Whole(back[1]["pre"], back[0]["pre"], (SPLIT, FFP))),
        ("fc1", 1, Whole(back[2]["pre"], back[1]["pre"])),
        ("out", 0, Whole(back[1]["branch"], back[0]["branch"])),
        ("out", 1, Whole(back[2]["branch"], back[1]["branch"])),
        ("qkv", 0, Whole(back[1]["dqkv"], back[0]["dqkv"])),
        ("qkv", 1, Whole(back[2]["dqkv"], back[1]["dqkv"])),
    ]
    packed, grads = final(jnp.concatenate([by_owner, to_all], axis=1), xs, early, late, 12)
    g_small = packed[:8, :HEAD_DIM]
    g_fc1_bias = packed[8 : 8 + lines].reshape(FFP)[:FF]
    g_qkv = grads["qkv"].reshape(HEAD_DIM, HEADS, 3, HEAD_DIM).transpose(0, 2, 1, 3).reshape(HEAD_DIM, 3 * D)
    return (
        outputs[None],
        input_grads[None],
        g_small[0][None],
        g_small[1][None],
        g_qkv[None],
        g_small[2:4][None],
        grads["out"][None],
        g_small[4][None],
        g_small[5][None],
        g_small[6][None],
        grads["fc1"][:, :FF][None],
        g_fc1_bias[None],
        grads["fc2"].T[:FF][None],
        g_small[7][None],
    )


BLK_DEV = 1
REACH = 5


def shifted(value, axis, steps):
    count = lax.axis_size(axis)
    initial, last = (max(0, -steps), min(count, count - steps))
    return lax.ppermute(value, axis, [(source, source + steps) for source in range(initial, last)])


def layer_norm(values_in, scale_gain, shift_bias):
    row_mean = jnp.mean(values_in, axis=-1, keepdims=True)
    centred = values_in - row_mean
    row_var = jnp.mean(centred * centred, axis=-1, keepdims=True)
    return centred * lax.rsqrt(row_var + EPSILON) * scale_gain + shift_bias


def gelu_tanh(pre_value):
    return jax.nn.gelu(pre_value, approximate=True)


def heads_of(values_in):
    return values_in.reshape(values_in.shape[0], HEADS, HEAD_DIM)


def image_mask(image_of_block, batch_slot, wide_rank):
    padding = REACH * BLK_DEV
    padded = jnp.pad(image_of_block, ((0, 0), (padding, padding)), constant_values=-1)
    image_row = lax.dynamic_index_in_dim(padded, batch_slot, 0, keepdims=False)
    key_blocks = lax.dynamic_slice_in_dim(image_row, wide_rank * BLK_DEV, (2 * REACH + 1) * BLK_DEV)
    query_blocks = lax.dynamic_slice_in_dim(image_row, wide_rank * BLK_DEV + padding, BLK_DEV)
    return jnp.repeat(query_blocks, BLOCK)[:, None] == jnp.repeat(key_blocks, BLOCK)[None, :]


def keep_slot(buffer_all, new_value, batch_slot, is_live):
    previous = lax.dynamic_index_in_dim(buffer_all, batch_slot, 0, keepdims=False)
    chosen = jnp.where(is_live, new_value, previous)
    return lax.dynamic_update_index_in_dim(buffer_all, chosen, batch_slot, 0)


def near_keys(key_own, value_own, backward_pass):
    key_parts = []
    value_parts = []
    for offset in range(-REACH, REACH + 1):
        if offset == 0:
            received = (key_own, value_own)
        elif backward_pass:
            received = shifted((key_own, value_own), "wide", -offset)
        else:
            received = shifted((key_own, value_own), "wide", -offset)
        key_parts.append(received[0])
        value_parts.append(received[1])
    return (jnp.concatenate(key_parts, axis=0), jnp.concatenate(value_parts, axis=0))


def return_key_grads(key_terms, value_terms):
    row_count = key_terms.shape[0] // (2 * REACH + 1)
    key_total = key_terms[REACH * row_count : (REACH + 1) * row_count]
    value_total = value_terms[REACH * row_count : (REACH + 1) * row_count]
    for position, offset in enumerate(range(-REACH, REACH + 1)):
        if offset != 0:
            piece_pair = (
                key_terms[position * row_count : (position + 1) * row_count],
                value_terms[position * row_count : (position + 1) * row_count],
            )
            received = shifted((piece_pair[0], piece_pair[1]), "wide", offset)
            key_total = key_total + received[0]
            value_total = value_total + received[1]
    return (key_total, value_total)


def project_qkv(layer_in, weights):
    layer_float = layer_in.astype(jnp.float32)
    normed_one = layer_norm(
        layer_float, weights[0].astype(jnp.float32), weights[1].astype(jnp.float32)
    ).astype(jnp.bfloat16)
    mixed = jnp.dot(normed_one, weights[2], preferred_element_type=jnp.float32)
    queries = (mixed[:, :D] + weights[3][0].astype(jnp.float32)).astype(jnp.bfloat16)
    key_own = mixed[:, D : 2 * D].astype(jnp.bfloat16)
    value_own = (mixed[:, 2 * D :] + weights[3][1].astype(jnp.float32)).astype(jnp.bfloat16)
    return (layer_float, normed_one, queries, key_own, value_own)


def attention_probs(queries, keys_near, same_image):
    score_scale = 1.0 / math.sqrt(HEAD_DIM)
    scores = (
        jnp.einsum(
            "qhd,khd->hqk",
            heads_of(queries),
            heads_of(keys_near),
            preferred_element_type=jnp.float32,
        )
        * score_scale
    )
    scores = jnp.where(same_image[None], scores, MASKED_SCORE)
    row_max = jnp.max(scores, axis=-1, keepdims=True)
    exponent = jnp.exp(scores - row_max)
    return exponent / jnp.sum(exponent, axis=-1, keepdims=True)


def finish_layer(layer_float, queries, keys_near, values_near, same_image, weights, hidden_bias):
    probs = attention_probs(queries, keys_near, same_image)
    probs_low = probs.astype(jnp.bfloat16)
    attended = jnp.einsum(
        "hqk,khd->qhd", probs_low, heads_of(values_near), preferred_element_type=jnp.float32
    )
    attended = attended.reshape(queries.shape[0], D).astype(jnp.bfloat16)
    residual = (
        layer_float
        + jnp.dot(attended, weights[4], preferred_element_type=jnp.float32)
        + weights[5].astype(jnp.float32)
    )
    normed_two = layer_norm(
        residual, weights[6].astype(jnp.float32), weights[7].astype(jnp.float32)
    ).astype(jnp.bfloat16)
    hidden_pre = jnp.dot(
        normed_two, weights[8], preferred_element_type=jnp.float32
    ) + hidden_bias.astype(jnp.float32)
    hidden = gelu_tanh(hidden_pre).astype(jnp.bfloat16)
    output = (
        residual
        + jnp.dot(hidden, weights[9], preferred_element_type=jnp.float32)
        + weights[10].astype(jnp.float32)
    )
    return (probs, probs_low, attended, residual, normed_two, hidden_pre, hidden, output)


def layer_backward(
    layer_float,
    normed_one,
    queries,
    keys_near,
    values_near,
    same_image,
    weights,
    hidden_bias,
    grad_out,
):
    score_scale = 1.0 / math.sqrt(HEAD_DIM)
    probs, probs_low, attended, residual, normed_two, hidden_pre, hidden, output = finish_layer(
        layer_float, queries, keys_near, values_near, same_image, weights, hidden_bias
    )
    feed_grad = grad_out.astype(jnp.bfloat16)
    grad_fc2_weight = jnp.einsum("tf,td->fd", hidden, feed_grad, preferred_element_type=jnp.float32)
    grad_fc2_bias = jnp.sum(feed_grad.astype(jnp.float32), axis=0)
    hidden_grad = jnp.einsum("td,fd->tf", feed_grad, weights[9], preferred_element_type=jnp.float32)
    primal_gelu, gelu_pull = jax.vjp(gelu_tanh, hidden_pre)
    pre_grad = gelu_pull(hidden_grad)[0].astype(jnp.bfloat16)
    grad_fc1_bias = jnp.sum(pre_grad.astype(jnp.float32), axis=0)
    grad_fc1_weight = jnp.einsum(
        "td,tf->df", normed_two, pre_grad, preferred_element_type=jnp.float32
    )
    normed_two_grad = jnp.einsum(
        "tf,df->td", pre_grad, weights[8], preferred_element_type=jnp.float32
    )
    primal_two, norm_two_pull = jax.vjp(
        layer_norm, residual, weights[6].astype(jnp.float32), weights[7].astype(jnp.float32)
    )
    residual_part, grad_ln2_gain, grad_ln2_bias = norm_two_pull(normed_two_grad)
    residual_grad = grad_out + residual_part
    branch_grad = residual_grad.astype(jnp.bfloat16)
    grad_out_bias = jnp.sum(branch_grad.astype(jnp.float32), axis=0)
    grad_out_weight = jnp.einsum(
        "tc,td->cd", attended, branch_grad, preferred_element_type=jnp.float32
    )
    attended_grad = jnp.einsum(
        "td,cd->tc", branch_grad, weights[4], preferred_element_type=jnp.float32
    ).astype(jnp.bfloat16)
    attended_heads = heads_of(attended_grad)
    probs_grad = jnp.einsum(
        "qhd,khd->hqk", attended_heads, heads_of(values_near), preferred_element_type=jnp.float32
    )
    value_terms = jnp.einsum(
        "hqk,qhd->khd", probs_low, attended_heads, preferred_element_type=jnp.float32
    )
    score_grad = (
        probs * (probs_grad - jnp.sum(probs * probs_grad, axis=-1, keepdims=True))
    ).astype(jnp.bfloat16)
    query_grad = (
        jnp.einsum(
            "hqk,khd->qhd", score_grad, heads_of(keys_near), preferred_element_type=jnp.float32
        )
        * score_scale
    )
    query_grad = query_grad.reshape(queries.shape[0], D).astype(jnp.bfloat16)
    key_terms = (
        jnp.einsum(
            "hqk,qhd->khd", score_grad, heads_of(queries), preferred_element_type=jnp.float32
        )
        * score_scale
    )
    key_total, value_total = return_key_grads(key_terms.reshape(-1, D), value_terms.reshape(-1, D))
    key_grad = key_total.astype(jnp.bfloat16)
    value_grad = value_total.astype(jnp.bfloat16)
    grad_qv_bias = jnp.stack(
        [
            jnp.sum(query_grad.astype(jnp.float32), axis=0),
            jnp.sum(value_grad.astype(jnp.float32), axis=0),
        ]
    )
    mixed_grad = jnp.concatenate([query_grad, key_grad, value_grad], axis=1)
    grad_qkv_weight = jnp.einsum(
        "tc,tk->ck", normed_one, mixed_grad, preferred_element_type=jnp.float32
    )
    normed_one_grad = jnp.einsum(
        "tk,ck->tc", mixed_grad, weights[2], preferred_element_type=jnp.float32
    )
    primal_one, norm_one_pull = jax.vjp(
        layer_norm, layer_float, weights[0].astype(jnp.float32), weights[1].astype(jnp.float32)
    )
    input_part, grad_ln1_gain, grad_ln1_bias = norm_one_pull(normed_one_grad)
    input_grad = residual_grad + input_part
    grad_terms = (
        grad_ln1_gain,
        grad_ln1_bias,
        grad_qkv_weight,
        grad_qv_bias,
        grad_out_weight,
        grad_out_bias,
        grad_ln2_gain,
        grad_ln2_bias,
        grad_fc1_weight,
        grad_fc2_weight,
        grad_fc2_bias,
    )
    return (input_grad, grad_terms, grad_fc1_bias)


def on_device_near(
    tokens,
    cotangent,
    image_of_block,
    ln1_gain,
    ln1_bias,
    qkv_weight,
    qv_bias,
    out_weight,
    out_bias,
    ln2_gain,
    ln2_bias,
    fc1_weight,
    fc1_bias,
    fc2_weight,
    fc2_bias,
):
    section_rank = lax.axis_index("section")
    wide_rank = lax.axis_index("wide")
    micro_count = tokens.shape[0]
    weights = (
        lax.all_gather(ln1_gain[0], "wide", axis=0, tiled=True),
        lax.all_gather(ln1_bias[0], "wide", axis=0, tiled=True),
        lax.all_gather(qkv_weight[0], "wide", axis=0, tiled=True),
        lax.all_gather(qv_bias[0], "wide", axis=1, tiled=True),
        lax.all_gather(out_weight[0], "wide", axis=0, tiled=True),
        lax.all_gather(out_bias[0], "wide", axis=0, tiled=True),
        lax.all_gather(ln2_gain[0], "wide", axis=0, tiled=True),
        lax.all_gather(ln2_bias[0], "wide", axis=0, tiled=True),
        lax.all_gather(fc1_weight[0], "wide", axis=0, tiled=True),
        lax.all_gather(fc2_weight[0], "wide", axis=1, tiled=True),
        lax.all_gather(fc2_bias[0], "wide", axis=0, tiled=True),
    )
    hidden_bias = fc1_bias[0]
    inputs_kept = jnp.zeros_like(tokens)
    outputs_kept = jnp.zeros_like(tokens)
    incoming = jnp.zeros_like(tokens[0])
    for tick_number in range(micro_count + 1):
        batch_index = tick_number - section_rank
        is_live = (batch_index >= 0) & (batch_index < micro_count)
        batch_slot = jnp.clip(batch_index, 0, micro_count - 1)
        own_tokens = tokens[min(tick_number, micro_count - 1)]
        layer_in = jnp.where(section_rank == 0, own_tokens, incoming)
        same_image = image_mask(image_of_block, batch_slot, wide_rank)
        layer_float, normed_one, queries, key_own, value_own = project_qkv(layer_in, weights)
        keys_near, values_near = near_keys(key_own, value_own, False)
        output = finish_layer(
            layer_float, queries, keys_near, values_near, same_image, weights, hidden_bias
        )[-1]
        output_low = output.astype(jnp.bfloat16)
        inputs_kept = keep_slot(inputs_kept, layer_in, batch_slot, is_live)
        outputs_kept = keep_slot(outputs_kept, output_low, batch_slot, is_live)
        if tick_number < micro_count:
            incoming = shifted(output_low, "section", 1)
    weights_back = (
        lax.all_gather(ln1_gain[0], "wide", axis=0, tiled=True),
        lax.all_gather(ln1_bias[0], "wide", axis=0, tiled=True),
        lax.all_gather(qkv_weight[0], "wide", axis=0, tiled=True),
        lax.all_gather(qv_bias[0], "wide", axis=1, tiled=True),
        lax.all_gather(out_weight[0], "wide", axis=0, tiled=True),
        lax.all_gather(out_bias[0], "wide", axis=0, tiled=True),
        lax.all_gather(ln2_gain[0], "wide", axis=0, tiled=True),
        lax.all_gather(ln2_bias[0], "wide", axis=0, tiled=True),
        lax.all_gather(fc1_weight[0], "wide", axis=0, tiled=True),
        lax.all_gather(fc2_weight[0], "wide", axis=1, tiled=True),
        lax.all_gather(fc2_bias[0], "wide", axis=0, tiled=True),
    )
    grad_totals = tuple((jnp.zeros(array.shape, jnp.float32) for array in weights_back))
    hidden_bias_total = jnp.zeros(hidden_bias.shape, jnp.float32)
    input_grads = jnp.zeros(tokens.shape, jnp.float32)
    incoming_grad = jnp.zeros(tokens.shape[1:], jnp.bfloat16)
    for tick_number in range(micro_count + 1):
        batch_index = tick_number - 1 + section_rank
        is_live = (batch_index >= 0) & (batch_index < micro_count)
        batch_slot = jnp.clip(batch_index, 0, micro_count - 1)
        from_cotangent = cotangent[min(tick_number, micro_count - 1)].astype(jnp.float32)
        grad_out = jnp.where(
            section_rank == 1, from_cotangent, incoming_grad.astype(jnp.float32)
        ) * is_live.astype(jnp.float32)
        layer_in = lax.dynamic_index_in_dim(inputs_kept, batch_slot, 0, keepdims=False)
        same_image = image_mask(image_of_block, batch_slot, wide_rank)
        layer_float, normed_one, queries, key_own, value_own = project_qkv(layer_in, weights_back)
        keys_near, values_near = near_keys(key_own, value_own, True)
        input_grad, grad_terms, hidden_bias_term = layer_backward(
            layer_float,
            normed_one,
            queries,
            keys_near,
            values_near,
            same_image,
            weights_back,
            hidden_bias,
            grad_out,
        )
        grad_totals = tuple(
            (old_total + new_term for old_total, new_term in zip(grad_totals, grad_terms))
        )
        hidden_bias_total = hidden_bias_total + hidden_bias_term
        input_grads = keep_slot(input_grads, input_grad, batch_slot, is_live)
        if tick_number < micro_count:
            incoming_grad = shifted(input_grad.astype(jnp.bfloat16), "section", -1)
    (
        grad_ln1_gain,
        grad_ln1_bias,
        grad_qkv_weight,
        grad_qv_bias,
        grad_out_weight,
        grad_out_bias,
        grad_ln2_gain,
        grad_ln2_bias,
        grad_fc1_weight,
        grad_fc2_weight,
        grad_fc2_bias,
    ) = grad_totals
    row_sums = (
        lax.psum_scatter(grad_ln1_gain, "wide", scatter_dimension=0, tiled=True),
        lax.psum_scatter(grad_ln1_bias, "wide", scatter_dimension=0, tiled=True),
        lax.psum_scatter(grad_qkv_weight, "wide", scatter_dimension=0, tiled=True),
        lax.psum_scatter(grad_out_weight, "wide", scatter_dimension=0, tiled=True),
        lax.psum_scatter(grad_out_bias, "wide", scatter_dimension=0, tiled=True),
        lax.psum_scatter(grad_ln2_gain, "wide", scatter_dimension=0, tiled=True),
        lax.psum_scatter(grad_ln2_bias, "wide", scatter_dimension=0, tiled=True),
        lax.psum_scatter(grad_fc1_weight, "wide", scatter_dimension=0, tiled=True),
        lax.psum_scatter(grad_fc2_bias, "wide", scatter_dimension=0, tiled=True),
    )
    column_sums = (
        lax.psum_scatter(grad_qv_bias, "wide", scatter_dimension=1, tiled=True),
        lax.psum_scatter(grad_fc2_weight, "wide", scatter_dimension=1, tiled=True),
    )
    hidden_bias_sum = lax.psum(hidden_bias_total, "wide")
    return (
        outputs_kept[None],
        input_grads[None],
        row_sums[0][None],
        row_sums[1][None],
        row_sums[2][None],
        column_sums[0][None],
        row_sums[3][None],
        row_sums[4][None],
        row_sums[5][None],
        row_sums[6][None],
        row_sums[7][None],
        hidden_bias_sum[None],
        column_sums[1][None],
        row_sums[8][None],
    )


def specs():
    ins = (
        P(None, "wide", None),
        P(None, "wide", None),
        P(),
        P("section", "wide"),
        P("section", "wide"),
        P("section", "wide", None),
        P("section", None, "wide"),
        P("section", "wide", None),
        P("section", "wide"),
        P("section", "wide"),
        P("section", "wide"),
        P("section", "wide", None),
        P("section", None),
        P("section", None, "wide"),
        P("section", "wide"),
    )
    outs = (
        P("section", None, "wide", None),
        P("section", None, "wide", None),
        P("section", "wide"),
        P("section", "wide"),
        P("section", "wide", None),
        P("section", None, "wide"),
        P("section", "wide", None),
        P("section", "wide"),
        P("section", "wide"),
        P("section", "wide"),
        P("section", "wide", None),
        P("section", None),
        P("section", None, "wide"),
        P("section", "wide"),
    )
    return ins, outs


def solution(mesh):
    ins, outs = specs()
    body = on_device if mesh.shape["wide"] == HEADS else on_device_near
    return jax.shard_map(body, mesh=mesh, in_specs=ins, out_specs=outs, check_vma=False)
```

```python
import functools
import math

import jax
import jax.numpy as jnp
from jax import lax
from jax.experimental import pallas as pl
from jax.experimental.pallas import tpu as pltpu
from jax.sharding import PartitionSpec as P

D = 1152
HEADS = 16
HEAD_DIM = 72
FF = 4304
FFP = -(-FF // 256) * 256
SPLIT = 9 * 256
BLOCK = 128
IMG_BLOCKS = 6
EPSILON = 1e-06
MASKED_SCORE = -1e30
SCALE = 1.0 / math.sqrt(HEAD_DIM)
MESH = pl.DeviceIdType.MESH
BF = jnp.bfloat16
F32 = jnp.float32


def place():
    return lax.axis_index("section"), lax.axis_index("wide")


class Gather:
    def __init__(self, ins, outs, sems):
        self.ins, self.outs, self.count = ins, outs, len(ins)
        self.local_sem = sems[0]
        self.up, self.down, self.yy, self.cc = [(sems[1 + 2 * i], sems[2 + 2 * i]) for i in range(4)]
        self.sec, self.me = place()
        self.z, self.low = self.me // 4, self.me % 4
        self.other_y = self.me - self.low + flip(self.low, 2)
        self.other_c = self.me - self.low + flip(self.low, 1)

    @staticmethod
    def semaphores(count):
        dma = pltpu.SemaphoreType.DMA
        return [dma((count,))] + [dma((count, 4))] * 6 + [dma((count, 8))] * 2

    def send(self, piece, origin, sems, slot, target, first=False):
        return pltpu.make_async_remote_copy(
            src_ref=self.ins[piece] if first else self.outs[piece].at[origin],
            dst_ref=self.outs[piece].at[origin],
            send_sem=sems[0].at[piece, slot],
            recv_sem=sems[1].at[piece, slot],
            device_id=(self.sec, target),
            device_id_type=MESH,
        )

    def mine(self, piece):
        return pltpu.make_async_copy(self.ins[piece], self.outs[piece].at[self.me], self.local_sem.at[piece])

    def along(self, piece, origin, first, go_up, go_down):
        zo = origin // 4
        if go_up:

            @pl.when(self.z < 3)
            def _():
                self.send(piece, origin, self.up, zo, self.me + 4, first).start()

        if go_down:

            @pl.when(self.z > 0)
            def _():
                self.send(piece, origin, self.down, zo, self.me - 4, first).start()

        self.send(piece, origin, self.yy, zo, self.other_y, first).start()
        self.send(piece, origin, self.cc, zo, self.other_c, first).start()

    def start(self):
        for piece in range(self.count):
            self.mine(piece).start()
            self.along(piece, self.me, True, True, True)

    def step(self, step):
        for piece in range(self.count):

            @pl.when(self.z - step >= 0)
            def _():
                origin = self.me - 4 * step
                self.send(piece, origin, self.up, self.z - step, self.me).wait_recv()
                self.along(piece, origin, False, True, False)

            @pl.when(self.z + step <= 3)
            def _():
                origin = self.me + 4 * step
                self.send(piece, origin, self.down, self.z + step, self.me).wait_recv()
                self.along(piece, origin, False, False, True)

    def across(self):
        far = self.other_y % 4
        for step in range(4):
            zo = (self.z + step) % 4
            for piece in range(self.count):
                origin = zo * 4 + far
                self.send(piece, origin, self.yy, zo, self.other_y).wait_recv()
                self.send(piece, origin, self.cc, 4 + zo, self.other_c).start()

    def finish(self):
        for zo in range(4):
            for piece in range(self.count):
                self.send(piece, self.me, self.yy, zo, self.other_y).wait_send()
                for slot in (zo, 4 + zo):
                    self.send(piece, self.me, self.cc, slot, self.other_c).wait_send()
                    self.send(piece, self.me, self.cc, slot, self.other_c).wait_recv()

                @pl.when((zo <= self.z) & (self.z < 3))
                def _():
                    self.send(piece, self.me, self.up, zo, self.me).wait_send()

                @pl.when((zo >= self.z) & (self.z > 0))
                def _():
                    self.send(piece, self.me, self.down, zo, self.me).wait_send()

        for piece in range(self.count):
            self.mine(piece).wait()


def gather_kernel(count, *refs):
    sec, me = place()
    greet_all(16, sec, me)
    work = Gather(refs[:count], refs[count : 2 * count], refs[2 * count :])
    work.start()
    for step in range(1, 4):
        work.step(step)
    work.across()
    work.finish()


def gather(arrays, cid):
    count = len(arrays)
    return pl.pallas_call(
        functools.partial(gather_kernel, count),
        out_shape=[jax.ShapeDtypeStruct((16,) + a.shape, a.dtype) for a in arrays],
        in_specs=[pl.BlockSpec(memory_space=pl.ANY)] * count,
        out_specs=[pl.BlockSpec(memory_space=pl.ANY)] * count,
        scratch_shapes=Gather.semaphores(count),
        compiler_params=pltpu.CompilerParams(collective_id=cid, has_side_effects=True),
    )(*arrays)


def flip(low, k):
    return [low, low + 1 - 2 * (low % 2), (low + 2) % 4, 3 - low][k]


def greet_all(count, sec, me):
    barrier = pltpu.get_barrier_semaphore()
    for d in range(1, count):
        pl.semaphore_signal(barrier, inc=1, device_id=(sec, (me + d) % count), device_id_type=MESH)
    pl.semaphore_wait(barrier, count - 1)


class Whole:
    def __init__(self, zero, one, cols=None):
        self.sources, self.cols = (zero, one), cols

    def shape(self):
        rows, cols = self.sources[0].shape
        return (4, rows, cols if self.cols is None else self.cols[1] - self.cols[0])

    def source(self, ref, low, k):
        return ref if self.cols is None else ref.at[:, self.cols[0] : self.cols[1]]

    forwarded = True


class Rows:
    def __init__(self, zero, one):
        self.sources = (zero, one)

    def shape(self):
        return self.sources[0].shape

    def source(self, ref, low, k):
        return ref.at[flip(low, k)]

    forwarded = False


class PlaneCopies:
    def __init__(self, item, zero_ref, one_ref, slot, local_sem, send_sem, recv_sem):
        self.item, self.refs, self.slot = item, (zero_ref, one_ref), slot
        self.local_sem, self.send_sem, self.recv_sem = local_sem, send_sem, recv_sem
        self.sec, self.me = place()
        self.low = self.me % 4

    def remote(self, src, k, to):
        return pltpu.make_async_remote_copy(
            src_ref=src,
            dst_ref=self.slot(k),
            send_sem=self.send_sem.at[k],
            recv_sem=self.recv_sem.at[k],
            device_id=(self.sec, self.me - self.low + flip(self.low, to)),
            device_id_type=MESH,
        )

    def local(self, ref):
        return pltpu.make_async_copy(self.item.source(ref, self.low, 0), self.slot(0), self.local_sem)

    def start(self):
        def go(ref):
            self.local(ref).start()
            for k in (2, 1) if self.item.forwarded else (2, 3, 1):
                self.remote(self.item.source(ref, self.low, k), k, k).start()

        @pl.when(self.sec == 0)
        def _():
            go(self.refs[0])

        @pl.when(self.sec == 1)
        def _():
            go(self.refs[1])

    def forward(self):
        if self.item.forwarded:
            self.remote(self.slot(2), 2, 2).wait_recv()
            self.remote(self.slot(2), 3, 1).start()

    def finish(self):
        self.local(self.refs[0]).wait()
        for k in (1, 2, 3):
            self.remote(self.slot(k), k, k).wait_send()
            if k != 2 or not self.item.forwarded:
                self.remote(self.slot(k), k, k).wait_recv()


def dot(a, b):
    return jnp.dot(a, b, preferred_element_type=F32)


def window(image_row):
    blocks = image_row.shape[0]
    first = jnp.argmax(image_row[None, :] == image_row[:, None], axis=1).astype(jnp.int32)
    first = jnp.minimum(first, blocks - IMG_BLOCKS)
    near = image_row[first[:, None] + jnp.arange(IMG_BLOCKS)[None, :]]
    bias = jnp.where(near == image_row[:, None], 0.0, MASKED_SCORE).astype(F32)
    return first, jnp.broadcast_to(bias[:, :, None], (blocks, IMG_BLOCKS, BLOCK))


def near_rows(ref, start):
    return jnp.concatenate([ref[start + j] for j in range(IMG_BLOCKS)], axis=0)


def near_columns(ref, start):
    return jnp.concatenate([ref[start + j] for j in range(IMG_BLOCKS)], axis=1)


def attend_kernel(items, pieces, first_ref, bias_ref, x_ref, *refs):
    refs = list(refs)

    def take(n):
        part = refs[:n]
        del refs[:n]
        return part

    n = len(items)
    sources, shards = take(2 * n), take(pieces)
    qkv_ref, lse_ref, att_ref = take(3)
    outs, whole = take(n), take(pieces)
    k_all, vt_all, o_buf, local_sem, send_sem, recv_sem, att_send, att_recv = take(8)
    blocks = x_ref.shape[0]
    sec, me = place()
    greet_all(blocks, sec, me)

    def incoming(d):
        target = (me + d) % blocks
        return pltpu.make_async_remote_copy(
            src_ref=x_ref.at[target],
            dst_ref=qkv_ref.at[me],
            send_sem=send_sem.at[d],
            recv_sem=recv_sem.at[d],
            device_id=(sec, target),
            device_id_type=MESH,
        )

    def outgoing(d):
        target = (me + d) % blocks
        return pltpu.make_async_remote_copy(
            src_ref=o_buf.at[d],
            dst_ref=att_ref.at[me],
            send_sem=att_send.at[d],
            recv_sem=att_recv.at[d],
            device_id=(sec, target),
            device_id_type=MESH,
        )

    for d in sorted(range(1, blocks), key=lambda d: abs(d - blocks // 2)):
        incoming(d).start()
    own = pltpu.make_async_copy(x_ref.at[me], qkv_ref.at[me], local_sem)
    own.start()
    behind_sems = [take(3) for _ in items]
    work = None
    if pieces:
        work = Gather(shards, whole, take(9))
        work.start()
    own.wait()
    for d in range(1, blocks):
        incoming(d).wait()
    if work:
        work.step(1)
    behind = []
    for i, item in enumerate(items):
        slot = lambda k, i=i: outs[i].at[k]
        behind.append(PlaneCopies(item, sources[2 * i], sources[2 * i + 1], slot, *behind_sems[i]))
        behind[-1].start()

    def arrange(j, carry):
        part = qkv_ref[j].astype(F32)
        k_all[j] = part[HEAD_DIM : 2 * HEAD_DIM].T.astype(BF)
        vt_all[j] = part[2 * HEAD_DIM :].astype(BF)
        return carry

    lax.fori_loop(0, blocks, arrange, 0)

    def one_block(d, carry):
        i = (me + d) % blocks
        start = first_ref[i]
        qt = qkv_ref[i].astype(F32)[:HEAD_DIM].astype(BF)
        s = dot(near_rows(k_all, start), qt) * SCALE
        bias = bias_ref[i]
        parts = [s[j * BLOCK : (j + 1) * BLOCK] + bias[j : j + 1] for j in range(IMG_BLOCKS)]
        top = parts[0]
        for part in parts[1:]:
            top = jnp.maximum(top, part)
        top = jnp.max(top, axis=0, keepdims=True)
        exps = [jnp.exp(part - top) for part in parts]
        total = exps[0]
        for part in exps[1:]:
            total = total + part
        total = jnp.sum(total, axis=0, keepdims=True)
        e = jnp.concatenate([part.astype(BF) for part in exps], axis=0)
        o = dot(near_columns(vt_all, start), e)
        o_buf[d] = (o / total).astype(BF)
        lse_ref[i] = top + jnp.log(total)

        @pl.when(d > 0)
        def _():
            outgoing(d).start()

        return carry

    lax.fori_loop(0, blocks, one_block, 0)
    att_ref[me] = o_buf[0]
    if work:
        work.step(2)
    for one in behind:
        one.forward()
    for d in range(1, blocks):
        outgoing(d).wait()
    if work:
        work.step(3)
        work.across()
        work.finish()
    for one in behind:
        one.finish()


def attend(qkv, near, cid, items=(), shards=()):
    blocks = qkv.shape[0]
    n = len(items)
    sources = [source for item in items for source in item.sources]
    anywhere, vmem, smem = [pl.BlockSpec(memory_space=m) for m in (pl.ANY, pltpu.VMEM, pltpu.SMEM)]
    dma = pltpu.SemaphoreType.DMA
    scratch = [
        pltpu.VMEM((blocks, BLOCK, HEAD_DIM), BF),
        pltpu.VMEM((blocks, HEAD_DIM, BLOCK), BF),
        pltpu.VMEM((blocks, HEAD_DIM, BLOCK), BF),
        dma,
    ] + [dma((blocks,))] * 4
    scratch += [dma, dma((4,)), dma((4,))] * n
    if shards:
        scratch += Gather.semaphores(len(shards))
    out = pl.pallas_call(
        functools.partial(attend_kernel, list(items), len(shards)),
        out_shape=[
            jax.ShapeDtypeStruct(qkv.shape, BF),
            jax.ShapeDtypeStruct((blocks, 1, BLOCK), F32),
            jax.ShapeDtypeStruct((blocks, HEAD_DIM, BLOCK), BF),
        ]
        + [jax.ShapeDtypeStruct(item.shape(), BF) for item in items]
        + [jax.ShapeDtypeStruct((blocks,) + shard.shape, BF) for shard in shards],
        in_specs=[smem, vmem] + [anywhere] * (1 + len(sources) + len(shards)),
        out_specs=[vmem] * 3 + [anywhere] * (n + len(shards)),
        scratch_shapes=scratch,
        compiler_params=pltpu.CompilerParams(collective_id=cid, has_side_effects=True, vmem_limit_bytes=32 << 20),
    )(*near, qkv, *sources, *shards)
    return out[0], out[1], out[2], out[3 : 3 + n], out[3 + n :]


def attend_back_kernel(items, first_ref, bias_ref, qkv_ref, lse_ref, x_ref, *refs):
    refs = list(refs)

    def take(n):
        part = refs[:n]
        del refs[:n]
        return part

    n = len(items)
    sources = take(2 * n)
    dq_ref, dkv_ref = take(2)
    outs = take(n)
    do_ref, k_all, kt_all, v_all, q_all, do_all, p_all, s_all, dq_buf, dkv_buf = take(10)
    local_sem, send_sem, recv_sem, q_send, q_recv, kv_send, kv_recv = take(7)
    blocks = x_ref.shape[0]
    sec, me = place()
    greet_all(blocks, sec, me)

    def remote(src, dst, send, recv, d):
        return pltpu.make_async_remote_copy(
            src_ref=src,
            dst_ref=dst,
            send_sem=send.at[d],
            recv_sem=recv.at[d],
            device_id=(sec, (me + d) % blocks),
            device_id_type=MESH,
        )

    def incoming(d):
        return remote(x_ref.at[(me + d) % blocks], do_ref.at[me], send_sem, recv_sem, d)

    def send_q(d):
        return remote(dq_buf.at[d], dq_ref.at[me], q_send, q_recv, d)

    def send_kv(d):
        return remote(dkv_buf.at[d], dkv_ref.at[me], kv_send, kv_recv, d)

    for d in sorted(range(1, blocks), key=lambda d: abs(d - blocks // 2)):
        incoming(d).start()
    own = pltpu.make_async_copy(x_ref.at[me], do_ref.at[me], local_sem)
    own.start()

    def arrange(j, carry):
        part = qkv_ref[j].astype(F32)
        q_all[j] = part[:HEAD_DIM].T.astype(BF)
        k_all[j] = part[HEAD_DIM : 2 * HEAD_DIM].T.astype(BF)
        v_all[j] = part[2 * HEAD_DIM :].T.astype(BF)
        kt_all[j] = part[HEAD_DIM : 2 * HEAD_DIM].astype(BF)
        return carry

    lax.fori_loop(0, blocks, arrange, 0)
    own.wait()
    for d in range(1, blocks):
        incoming(d).wait()
    behind = []
    for i, item in enumerate(items):
        behind.append(
            PlaneCopies(item, sources[2 * i], sources[2 * i + 1], lambda k, i=i: outs[i].at[k], *take(3))
        )
        behind[-1].start()

    def arrange_grad(j, carry):
        do_all[j] = do_ref[j].astype(F32).T.astype(BF)
        return carry

    lax.fori_loop(0, blocks, arrange_grad, 0)

    def by_query(d, carry):
        i = (me + d) % blocks
        start = first_ref[i]
        qt = qkv_ref[i].astype(F32)[:HEAD_DIM].astype(BF)
        s = dot(near_rows(k_all, start), qt) * SCALE
        shift = bias_ref[i] - lse_ref[i]
        probs = [jnp.exp(s[j * BLOCK : (j + 1) * BLOCK] + shift[j : j + 1]) for j in range(IMG_BLOCKS)]
        dp = dot(near_rows(v_all, start), do_ref[i])
        total = probs[0] * dp[:BLOCK]
        for j in range(1, IMG_BLOCKS):
            total = total + probs[j] * dp[j * BLOCK : (j + 1) * BLOCK]
        total = jnp.sum(total, axis=0, keepdims=True)
        ds = jnp.concatenate(
            [(probs[j] * (dp[j * BLOCK : (j + 1) * BLOCK] - total)).astype(BF) for j in range(IMG_BLOCKS)], axis=0
        )
        for j in range(IMG_BLOCKS):
            p_all[i, j] = probs[j].astype(BF)
            s_all[i, j] = ds[j * BLOCK : (j + 1) * BLOCK]
        dq_buf[d] = (dot(near_columns(kt_all, start), ds) * SCALE).astype(BF)

        @pl.when(d > 0)
        def _():
            send_q(d).start()

        return carry

    lax.fori_loop(0, blocks, by_query, 0)
    for one in behind:
        one.forward()

    def by_key(d, carry):
        j = (me + d) % blocks
        start = first_ref[j]
        place_in = jnp.clip(j - start, 0, IMG_BLOCKS - 1)
        same = (bias_ref[j] == 0.0).astype(F32).astype(BF)
        p, ds = [], []
        for m in range(IMG_BLOCKS):
            p.append(p_all[start + m, place_in] * same[m : m + 1])
            ds.append(s_all[start + m, place_in] * same[m : m + 1])
        dv = dot(jnp.concatenate(p, axis=1), near_rows(do_all, start))
        dk = dot(jnp.concatenate(ds, axis=1), near_rows(q_all, start)) * SCALE
        dkv_buf[d] = jnp.concatenate([dk.T, dv.T], axis=0).astype(BF)

        @pl.when(d > 0)
        def _():
            send_kv(d).start()

        return carry

    lax.fori_loop(0, blocks, by_key, 0)
    dq_ref[me] = dq_buf[0]
    dkv_ref[me] = dkv_buf[0]
    for d in range(1, blocks):
        send_q(d).wait()
        send_kv(d).wait()
    for one in behind:
        one.finish()


def attend_back(att_grad, near, qkv, lse, cid, items=()):
    blocks = qkv.shape[0]
    n = len(items)
    sources = [source for item in items for source in item.sources]
    anywhere, vmem, smem = [pl.BlockSpec(memory_space=m) for m in (pl.ANY, pltpu.VMEM, pltpu.SMEM)]
    dma = pltpu.SemaphoreType.DMA
    scratch = [
        pltpu.VMEM((blocks, HEAD_DIM, BLOCK), BF),
        pltpu.VMEM((blocks, BLOCK, HEAD_DIM), BF),
        pltpu.VMEM((blocks, HEAD_DIM, BLOCK), BF),
        pltpu.VMEM((blocks, BLOCK, HEAD_DIM), BF),
        pltpu.VMEM((blocks, BLOCK, HEAD_DIM), BF),
        pltpu.VMEM((blocks, BLOCK, HEAD_DIM), BF),
        pltpu.VMEM((blocks, IMG_BLOCKS, BLOCK, BLOCK), BF),
        pltpu.VMEM((blocks, IMG_BLOCKS, BLOCK, BLOCK), BF),
        pltpu.VMEM((blocks, HEAD_DIM, BLOCK), BF),
        pltpu.VMEM((blocks, 2 * HEAD_DIM, BLOCK), BF),
        dma,
    ] + [dma((blocks,))] * 6
    scratch += [dma, dma((4,)), dma((4,))] * n
    out = pl.pallas_call(
        functools.partial(attend_back_kernel, list(items)),
        out_shape=[
            jax.ShapeDtypeStruct((blocks, HEAD_DIM, BLOCK), BF),
            jax.ShapeDtypeStruct((blocks, 2 * HEAD_DIM, BLOCK), BF),
        ]
        + [jax.ShapeDtypeStruct(item.shape(), BF) for item in items],
        in_specs=[smem, vmem, vmem, vmem] + [anywhere] * (1 + len(sources)),
        out_specs=[vmem] * 2 + [anywhere] * n,
        scratch_shapes=scratch,
        compiler_params=pltpu.CompilerParams(collective_id=cid, has_side_effects=True, vmem_limit_bytes=40 << 20),
    )(*near, qkv, lse, att_grad, *sources)
    return jnp.concatenate(out[:2], axis=1), out[2:]


def normalised(x):
    mean = jnp.mean(x, axis=-1, keepdims=True)
    centred = x - mean
    rstd = lax.rsqrt(jnp.mean(centred * centred, axis=-1, keepdims=True) + EPSILON)
    return centred * rstd, rstd


def norm_backward(grad, xhat, rstd, gain):
    g = grad * gain
    part = g - jnp.mean(g, axis=-1, keepdims=True) - xhat * jnp.mean(g * xhat, axis=-1, keepdims=True)
    return part * rstd, jnp.sum(grad * xhat, axis=0), jnp.sum(grad, axis=0)


def gelu_and_slope(v):
    c = math.sqrt(2.0 / math.pi)
    t = jnp.tanh(c * (v + 0.044715 * v * v * v))
    value = 0.5 * v * (1.0 + t)
    slope = 0.5 * (1.0 + t) + 0.5 * v * (1.0 - t * t) * c * (1.0 + 3 * 0.044715 * v * v)
    return value, slope


def by_rows(x):
    return x.T.reshape(HEADS, HEAD_DIM, x.shape[0])


def pad_ff(x):
    return jnp.pad(x, ((0, 0),) * (x.ndim - 1) + ((0, FFP - FF),))


def owners(x):
    return x.reshape(4, 4, HEAD_DIM, BLOCK).swapaxes(0, 1)


TENSORS = ("fc2", "fc1", "out", "qkv")


def final_kernel(tiles, early, late, *refs):
    refs = list(refs)

    def take(n):
        part = refs[:n]
        del refs[:n]
        return part

    small_ref = take(1)[0]
    x_refs = {name: take(2) for name in TENSORS}
    early_refs = take(len(early))
    late_refs = take(2 * len(late))
    small_out = take(1)[0]
    out_refs = dict(zip(TENSORS, take(4)))
    y_bufs = dict(zip(TENSORS, take(4)))
    x_buf = take(1)[0]
    g_bufs, one_bufs, two_bufs = [dict(zip(TENSORS, take(4))) for _ in range(3)]
    small_got = take(1)[0]
    early_sem, small_send, small_recv = take(3)
    sems = {name: take(4) for name in TENSORS}
    late_sems = [take(3) for _ in late]

    sec, me = place()
    z, low = me // 4, me % 4
    pair = z + 1 - 2 * (z % 2)
    count = small_ref.shape[0]
    greet_all(count, sec, me)

    loads = []
    for i, (name, batch, cols) in enumerate(early):
        dst = y_bufs[name].at[4 * batch : 4 * batch + 4]
        if cols is not None:
            dst = dst.at[:, :, cols[0] : cols[1]]
        loads.append((name, pltpu.make_async_copy(early_refs[i], dst, early_sem.at[i])))
        loads[-1][1].start()
    behind = []
    for i, (name, batch, item) in enumerate(late):

        def slot(k, name=name, batch=batch, item=item):
            ref = y_bufs[name].at[4 * batch + k]
            return ref if item.cols is None else ref.at[:, item.cols[0] : item.cols[1]]

        behind.append((name, PlaneCopies(item, late_refs[2 * i], late_refs[2 * i + 1], slot, *late_sems[i])))
        behind[-1][1].start()
    smalls = []
    for d in range(1, count):
        target = (me + d) % count
        smalls.append(
            pltpu.make_async_remote_copy(
                src_ref=small_ref.at[target],
                dst_ref=small_got.at[d],
                send_sem=small_send.at[d],
                recv_sem=small_recv.at[d],
                device_id=(sec, target),
                device_id_type=MESH,
            )
        )
        smalls[-1].start()

    def first(name, i):
        send, recv = sems[name][0], sems[name][1]
        return pltpu.make_async_remote_copy(
            src_ref=g_bufs[name].at[i, 2:4],
            dst_ref=one_bufs[name].at[i],
            send_sem=send.at[i],
            recv_sem=recv.at[i],
            device_id=(sec, pair * 4 + low),
            device_id_type=MESH,
        )

    def second(name, i):
        send, recv = sems[name][2], sems[name][3]
        return pltpu.make_async_remote_copy(
            src_ref=g_bufs[name].at[i, 1],
            dst_ref=two_bufs[name].at[i],
            send_sem=send.at[i],
            recv_sem=recv.at[i],
            device_id=(sec, (3 - z) * 4 + low),
            device_id_type=MESH,
        )

    def ready(name):
        for other, one in behind:
            if other == name:
                one.forward()
        for other, load in loads:
            if other == name:
                load.wait()
        for other, one in behind:
            if other == name:
                one.finish()
        rows = []
        for owner in (z, 3 - z, pair, 3 - pair):
            rows.append(
                jnp.concatenate(
                    [x_refs[name][batch][k, owner].astype(F32) for batch in range(2) for k in range(4)], axis=1
                )
            )
        x_buf[...] = jnp.concatenate(rows, axis=0).astype(BF)

    def columns(name, i):
        width = tiles[name][1]
        return pl.ds(pl.multiple_of(i * width, 128), width)

    def compute(name, i):
        width = tiles[name][1]
        buf = y_bufs[name]
        if name == "qkv":
            rows = pl.ds(pl.multiple_of(i * width, 128), width)
            y = jnp.concatenate([buf[part, rows, :] for part in range(8)], axis=1)
            total = lax.dot_general(x_buf[...], y, (((1,), (1,)), ((), ())), preferred_element_type=F32)
        else:
            y = jnp.concatenate([buf[part, :, columns(name, i)] for part in range(8)], axis=0)
            total = dot(x_buf[...], y)
        g_bufs[name][i] = total.reshape(4, HEAD_DIM, width).astype(BF)
        first(name, i).start()

    def middle(name, i):
        first(name, i).wait_recv()
        out_refs[name][:, columns(name, i)] = g_bufs[name][i, 0].astype(F32) + one_bufs[name][i, 0].astype(F32)
        g_bufs[name][i, 1] = (g_bufs[name][i, 1].astype(F32) + one_bufs[name][i, 1].astype(F32)).astype(BF)
        second(name, i).start()

    def finish(name, i):
        second(name, i).wait_recv()
        out_refs[name][:, columns(name, i)] += two_bufs[name][i].astype(F32)
        first(name, i).wait_send()
        second(name, i).wait_send()

    def loop(name, *steps):
        def body(i, carry):
            for step, which in steps:
                step(which, i)
            return carry

        lax.fori_loop(0, tiles[name][0], body, 0)

    ready("fc2")
    loop("fc2", (compute, "fc2"))
    ready("fc1")
    loop("fc1", (compute, "fc1"), (middle, "fc2"))
    ready("out")
    loop("out", (compute, "out"))
    loop("fc1", (middle, "fc1"), (finish, "fc2"))
    ready("qkv")
    loop("qkv", (compute, "qkv"))
    loop("out", (middle, "out"))
    loop("fc1", (finish, "fc1"))
    loop("qkv", (middle, "qkv"))
    loop("out", (finish, "out"))
    for copy in smalls:
        copy.wait()
    total = small_ref[me]
    for d in range(1, count):
        total = total + small_got[d]
    small_out[...] = total
    loop("qkv", (finish, "qkv"))


def final(small, xs, early, late, cid):
    count = small.shape[0]
    tokens = xs["qkv"][0].shape[-1]
    widths = {"fc2": FFP, "fc1": FFP, "out": D, "qkv": 3 * D}
    tiles = {name: (w // (256 if name[0] == "f" else 384), 256 if name[0] == "f" else 384) for name, w in widths.items()}
    anywhere, vmem = pl.BlockSpec(memory_space=pl.ANY), pl.BlockSpec(memory_space=pltpu.VMEM)
    args = [small] + [x for name in TENSORS for x in xs[name]]
    n_vmem = len(args)
    args += [e[3] for e in early] + [source for _, _, item in late for source in item.sources]
    dma = pltpu.SemaphoreType.DMA
    scratch = []
    for name in TENSORS:
        shape = (8, widths[name], tokens) if name == "qkv" else (8, tokens, widths[name])
        scratch.append(pltpu.VMEM(shape, BF))
    scratch.append(pltpu.VMEM((4 * HEAD_DIM, 8 * tokens), BF))
    for lead in ((4,), (2,), ()):
        for name in TENSORS:
            scratch.append(pltpu.VMEM((tiles[name][0],) + lead + (HEAD_DIM, tiles[name][1]), BF))
    scratch.append(pltpu.VMEM(small.shape, F32))
    scratch += [dma((len(early),)), dma((count,)), dma((count,))]
    for name in TENSORS:
        scratch += [dma((tiles[name][0],))] * 4
    scratch += [dma, dma((4,)), dma((4,))] * len(late)
    out = pl.pallas_call(
        functools.partial(final_kernel, tiles, [e[:3] for e in early], late),
        out_shape=[jax.ShapeDtypeStruct(small.shape[1:], F32)]
        + [jax.ShapeDtypeStruct((HEAD_DIM, widths[name]), F32) for name in TENSORS],
        in_specs=[vmem] * n_vmem + [anywhere] * (len(args) - n_vmem),
        out_specs=[vmem] * 5,
        scratch_shapes=scratch,
        compiler_params=pltpu.CompilerParams(
            collective_id=cid, has_side_effects=True, vmem_limit_bytes=60 << 20
        ),
    )(*args)
    return out[0], dict(zip(TENSORS, out[1:]))


def on_device(
    tokens,
    cotangent,
    image_of_block,
    ln1_gain,
    ln1_bias,
    qkv_weight,
    qv_bias,
    out_weight,
    out_bias,
    ln2_gain,
    ln2_bias,
    fc1_weight,
    fc1_bias,
    fc2_weight,
    fc2_bias,
):
    sec, me = place()
    own_qkv = qkv_weight[0].reshape(HEAD_DIM, 3, HEADS, HEAD_DIM).transpose(0, 2, 1, 3).reshape(HEAD_DIM, 3 * D)
    small = jnp.stack(
        [ln1_gain[0], ln1_bias[0], qv_bias[0, 0], qv_bias[0, 1], out_bias[0], ln2_gain[0], ln2_bias[0], fc2_bias[0]]
    )
    small = jnp.pad(small, ((0, 8), (0, BLOCK - HEAD_DIM)))
    w_qkv, w_out, small_all = gather([own_qkv, out_weight[0], small], 1)
    ff_shards = [pad_ff(fc1_weight[0]), pad_ff(fc2_weight[0].T)]
    w_qkv = w_qkv.reshape(D, 3 * D)
    w_out = w_out.reshape(D, D)
    vectors = small_all[:, :8, :HEAD_DIM].astype(F32)
    gain1, bias1, _, _, b_out, gain2, bias2, b_fc2 = [vectors[:, i].reshape(D) for i in range(8)]
    b_qkv = jnp.stack([vectors[:, 2], jnp.zeros_like(vectors[:, 2]), vectors[:, 3]], axis=1).reshape(3 * D, 1)
    b_fc1 = pad_ff(fc1_bias[0]).astype(F32)

    def choose(at_zero, at_one):
        return jax.tree.map(lambda a, b: jnp.where(sec == 0, a, b), at_zero, at_one)

    saved = []
    incoming = jnp.zeros_like(tokens[0])
    sent = {}
    for tick in range(3):
        slot = jnp.clip(tick - sec, 0, 1)
        image_row = lax.dynamic_index_in_dim(image_of_block, slot, 0, keepdims=False)
        near = window(image_row)
        x = jnp.where(sec == 0, tokens[min(tick, 1)], incoming).astype(F32)
        xhat1, _ = normalised(x)
        n1 = (xhat1 * gain1 + bias1).astype(BF)
        qkv = jnp.einsum("ck,tc->kt", w_qkv, n1, preferred_element_type=F32) + b_qkv
        qkv = qkv.astype(BF).reshape(HEADS, 3 * HEAD_DIM, BLOCK)
        if tick == 0:
            qkv, lse, att, _, whole = attend(qkv, near, 2, shards=ff_shards)
            w_fc1, w_fc2t = [w.reshape(D, FFP) for w in whole]
        elif tick == 1:
            qkv, lse, att, _, _ = attend(qkv, near, 3)
        else:
            old = saved
            items = [Rows(old[0][name], old[1][name]) for name in ("n1", "att_rows", "n2")]
            items.append(Whole(old[0]["hidden"], old[1]["hidden"], (0, SPLIT)))
            qkv, lse, att, got, _ = attend(qkv, near, 4, items)
            sent["n1_0"], sent["att_0"], sent["n2_0"], sent["h0a"] = got
        residual = x + jnp.einsum("ct,cd->td", att.reshape(D, BLOCK), w_out, preferred_element_type=F32) + b_out
        xhat2, _ = normalised(residual)
        n2 = (xhat2 * gain2 + bias2).astype(BF)
        hidden_pre = jnp.einsum("td,df->tf", n2, w_fc1, preferred_element_type=F32) + b_fc1
        value, _ = gelu_and_slope(hidden_pre)
        hidden = value.astype(BF)
        out = residual + jnp.einsum("tf,df->td", hidden, w_fc2t, preferred_element_type=F32) + b_fc2
        out_low = out.astype(BF)
        saved.append(
            dict(
                x=x, qkv=qkv, lse=lse, residual=residual, hidden_pre=hidden_pre, hidden=hidden, low=out_low,
                att_rows=owners(att), n1=owners(by_rows(n1)), n2=owners(by_rows(n2)), near=near,
            )
        )
        if tick < 2:
            incoming = lax.ppermute(out_low, "section", [(0, 1)])
    outputs = jnp.stack([choose(saved[m]["low"], saved[m + 1]["low"]) for m in range(2)])

    incoming_grad = jnp.zeros(tokens.shape[1:], BF)
    input_grads, done, back = [], [], []
    needed = ("x", "qkv", "lse", "residual", "hidden_pre", "near")
    for tick in range(3):
        if tick == 1:
            k = choose({name: saved[0][name] for name in needed}, {name: saved[2][name] for name in needed})
        else:
            k = saved[1]
        grad = jnp.where(sec == 1, cotangent[min(tick, 1)], incoming_grad).astype(F32)
        fc_grad = grad.astype(BF)
        hidden_grad = jnp.einsum("td,df->tf", fc_grad, w_fc2t, preferred_element_type=F32)
        _, slope = gelu_and_slope(k["hidden_pre"])
        pre_grad = (hidden_grad * slope).astype(BF)
        n2_grad = jnp.einsum("tf,df->td", pre_grad, w_fc1, preferred_element_type=F32)
        xhat2, rstd2 = normalised(k["residual"])
        part, g_gain2, g_bias2 = norm_backward(n2_grad, xhat2, rstd2, gain2)
        residual_grad = grad + part
        branch = residual_grad.astype(BF)
        att_grad = jnp.einsum("td,cd->ct", branch, w_out, preferred_element_type=F32).astype(BF)
        att_grad = att_grad.reshape(HEADS, HEAD_DIM, BLOCK)
        back.append(dict(fc=owners(by_rows(fc_grad)), pre=pre_grad, branch=branch))
        if tick == 0:
            items = [
                Whole(saved[0]["hidden"], saved[1]["hidden"], (SPLIT, FFP)),
                Whole(saved[1]["hidden"], saved[2]["hidden"], (0, SPLIT)),
            ]
            names = ["h0b", "h1a"]
        elif tick == 1:
            items = [Rows(saved[1][name], saved[2][name]) for name in ("n1", "att_rows", "n2")]
            items.append(Whole(saved[1]["hidden"], saved[2]["hidden"], (SPLIT, FFP)))
            names = ["n1_1", "att_1", "n2_1", "h1b"]
        else:
            items = [Rows(back[1]["fc"], back[0]["fc"]), Rows(back[2]["fc"], back[1]["fc"])]
            items.append(Whole(back[1]["pre"], back[0]["pre"], (0, SPLIT)))
            names = ["fc_0", "fc_1", "pre_0a"]
        dqkv, got = attend_back(att_grad, k["near"], k["qkv"], k["lse"], 5 + tick, items)
        sent.update(zip(names, got))
        back[-1]["dqkv"] = dqkv.reshape(3 * D, BLOCK)
        n1_grad = jnp.einsum("kt,ck->tc", back[-1]["dqkv"], w_qkv, preferred_element_type=F32)
        xhat1, rstd1 = normalised(k["x"])
        part, g_gain1, g_bias1 = norm_backward(n1_grad, xhat1, rstd1, gain1)
        input_grad = residual_grad + part
        input_grads.append(input_grad)
        sums = jnp.sum(dqkv.astype(F32), axis=2)
        done.append(
            [
                g_gain1,
                g_bias1,
                sums[:, :HEAD_DIM].reshape(D),
                sums[:, 2 * HEAD_DIM :].reshape(D),
                jnp.sum(branch.astype(F32), axis=0),
                g_gain2,
                g_bias2,
                jnp.sum(fc_grad.astype(F32), axis=0),
                jnp.sum(pre_grad.astype(F32), axis=0),
            ]
        )
        if tick < 2:
            incoming_grad = lax.ppermute(input_grad.astype(BF), "section", [(1, 0)])
    input_grads = jnp.stack([choose(input_grads[m + 1], input_grads[m]) for m in range(2)])

    sums = [choose(done[1][i] + done[2][i], done[0][i] + done[1][i]) for i in range(9)]
    by_owner = jnp.stack(sums[:8]).reshape(8, HEADS, HEAD_DIM).transpose(1, 0, 2)
    by_owner = jnp.pad(by_owner, ((0, 0), (0, 0), (0, BLOCK - HEAD_DIM)))
    lines = FFP // BLOCK
    to_all = jnp.broadcast_to(sums[8].reshape(1, lines, BLOCK), (HEADS, lines, BLOCK))
    to_all = jnp.pad(to_all, ((0, 0), (0, 40 - lines), (0, 0)))
    xs = {
        "fc2": [sent["fc_0"], sent["fc_1"]],
        "fc1": [sent["n2_0"], sent["n2_1"]],
        "out": [sent["att_0"], sent["att_1"]],
        "qkv": [sent["n1_0"], sent["n1_1"]],
    }
    early = [
        ("fc2", 0, (0, SPLIT), sent["h0a"]),
        ("fc2", 0, (SPLIT, FFP), sent["h0b"]),
        ("fc2", 1, (0, SPLIT), sent["h1a"]),
        ("fc2", 1, (SPLIT, FFP), sent["h1b"]),
        ("fc1", 0, (0, SPLIT), sent["pre_0a"]),
    ]
    late = [
        ("fc1", 0, Whole(back[1]["pre"], back[0]["pre"], (SPLIT, FFP))),
        ("fc1", 1, Whole(back[2]["pre"], back[1]["pre"])),
        ("out", 0, Whole(back[1]["branch"], back[0]["branch"])),
        ("out", 1, Whole(back[2]["branch"], back[1]["branch"])),
        ("qkv", 0, Whole(back[1]["dqkv"], back[0]["dqkv"])),
        ("qkv", 1, Whole(back[2]["dqkv"], back[1]["dqkv"])),
    ]
    packed, grads = final(jnp.concatenate([by_owner, to_all], axis=1), xs, early, late, 12)
    g_small = packed[:8, :HEAD_DIM]
    g_fc1_bias = packed[8 : 8 + lines].reshape(FFP)[:FF]
    g_qkv = grads["qkv"].reshape(HEAD_DIM, HEADS, 3, HEAD_DIM).transpose(0, 2, 1, 3).reshape(HEAD_DIM, 3 * D)
    return (
        outputs[None],
        input_grads[None],
        g_small[0][None],
        g_small[1][None],
        g_qkv[None],
        g_small[2:4][None],
        grads["out"][None],
        g_small[4][None],
        g_small[5][None],
        g_small[6][None],
        grads["fc1"][:, :FF][None],
        g_fc1_bias[None],
        grads["fc2"].T[:FF][None],
        g_small[7][None],
    )


BLK_DEV = 1
REACH = 5


def shifted(value, axis, steps):
    count = lax.axis_size(axis)
    initial, last = (max(0, -steps), min(count, count - steps))
    return lax.ppermute(value, axis, [(source, source + steps) for source in range(initial, last)])


def layer_norm(values_in, scale_gain, shift_bias):
    row_mean = jnp.mean(values_in, axis=-1, keepdims=True)
    centred = values_in - row_mean
    row_var = jnp.mean(centred * centred, axis=-1, keepdims=True)
    return centred * lax.rsqrt(row_var + EPSILON) * scale_gain + shift_bias


def gelu_tanh(pre_value):
    return jax.nn.gelu(pre_value, approximate=True)


def heads_of(values_in):
    return values_in.reshape(values_in.shape[0], HEADS, HEAD_DIM)


def image_mask(image_of_block, batch_slot, wide_rank):
    padding = REACH * BLK_DEV
    padded = jnp.pad(image_of_block, ((0, 0), (padding, padding)), constant_values=-1)
    image_row = lax.dynamic_index_in_dim(padded, batch_slot, 0, keepdims=False)
    key_blocks = lax.dynamic_slice_in_dim(image_row, wide_rank * BLK_DEV, (2 * REACH + 1) * BLK_DEV)
    query_blocks = lax.dynamic_slice_in_dim(image_row, wide_rank * BLK_DEV + padding, BLK_DEV)
    return jnp.repeat(query_blocks, BLOCK)[:, None] == jnp.repeat(key_blocks, BLOCK)[None, :]


def keep_slot(buffer_all, new_value, batch_slot, is_live):
    previous = lax.dynamic_index_in_dim(buffer_all, batch_slot, 0, keepdims=False)
    chosen = jnp.where(is_live, new_value, previous)
    return lax.dynamic_update_index_in_dim(buffer_all, chosen, batch_slot, 0)


def near_keys(key_own, value_own, backward_pass):
    key_parts = []
    value_parts = []
    for offset in range(-REACH, REACH + 1):
        if offset == 0:
            received = (key_own, value_own)
        elif backward_pass:
            received = shifted((key_own, value_own), "wide", -offset)
        else:
            received = shifted((key_own, value_own), "wide", -offset)
        key_parts.append(received[0])
        value_parts.append(received[1])
    return (jnp.concatenate(key_parts, axis=0), jnp.concatenate(value_parts, axis=0))


def return_key_grads(key_terms, value_terms):
    row_count = key_terms.shape[0] // (2 * REACH + 1)
    key_total = key_terms[REACH * row_count : (REACH + 1) * row_count]
    value_total = value_terms[REACH * row_count : (REACH + 1) * row_count]
    for position, offset in enumerate(range(-REACH, REACH + 1)):
        if offset != 0:
            piece_pair = (
                key_terms[position * row_count : (position + 1) * row_count],
                value_terms[position * row_count : (position + 1) * row_count],
            )
            received = shifted((piece_pair[0], piece_pair[1]), "wide", offset)
            key_total = key_total + received[0]
            value_total = value_total + received[1]
    return (key_total, value_total)


def project_qkv(layer_in, weights):
    layer_float = layer_in.astype(jnp.float32)
    normed_one = layer_norm(
        layer_float, weights[0].astype(jnp.float32), weights[1].astype(jnp.float32)
    ).astype(jnp.bfloat16)
    mixed = jnp.dot(normed_one, weights[2], preferred_element_type=jnp.float32)
    queries = (mixed[:, :D] + weights[3][0].astype(jnp.float32)).astype(jnp.bfloat16)
    key_own = mixed[:, D : 2 * D].astype(jnp.bfloat16)
    value_own = (mixed[:, 2 * D :] + weights[3][1].astype(jnp.float32)).astype(jnp.bfloat16)
    return (layer_float, normed_one, queries, key_own, value_own)


def attention_probs(queries, keys_near, same_image):
    score_scale = 1.0 / math.sqrt(HEAD_DIM)
    scores = (
        jnp.einsum(
            "qhd,khd->hqk",
            heads_of(queries),
            heads_of(keys_near),
            preferred_element_type=jnp.float32,
        )
        * score_scale
    )
    scores = jnp.where(same_image[None], scores, MASKED_SCORE)
    row_max = jnp.max(scores, axis=-1, keepdims=True)
    exponent = jnp.exp(scores - row_max)
    return exponent / jnp.sum(exponent, axis=-1, keepdims=True)


def finish_layer(layer_float, queries, keys_near, values_near, same_image, weights, hidden_bias):
    probs = attention_probs(queries, keys_near, same_image)
    probs_low = probs.astype(jnp.bfloat16)
    attended = jnp.einsum(
        "hqk,khd->qhd", probs_low, heads_of(values_near), preferred_element_type=jnp.float32
    )
    attended = attended.reshape(queries.shape[0], D).astype(jnp.bfloat16)
    residual = (
        layer_float
        + jnp.dot(attended, weights[4], preferred_element_type=jnp.float32)
        + weights[5].astype(jnp.float32)
    )
    normed_two = layer_norm(
        residual, weights[6].astype(jnp.float32), weights[7].astype(jnp.float32)
    ).astype(jnp.bfloat16)
    hidden_pre = jnp.dot(
        normed_two, weights[8], preferred_element_type=jnp.float32
    ) + hidden_bias.astype(jnp.float32)
    hidden = gelu_tanh(hidden_pre).astype(jnp.bfloat16)
    output = (
        residual
        + jnp.dot(hidden, weights[9], preferred_element_type=jnp.float32)
        + weights[10].astype(jnp.float32)
    )
    return (probs, probs_low, attended, residual, normed_two, hidden_pre, hidden, output)


def layer_backward(
    layer_float,
    normed_one,
    queries,
    keys_near,
    values_near,
    same_image,
    weights,
    hidden_bias,
    grad_out,
):
    score_scale = 1.0 / math.sqrt(HEAD_DIM)
    probs, probs_low, attended, residual, normed_two, hidden_pre, hidden, output = finish_layer(
        layer_float, queries, keys_near, values_near, same_image, weights, hidden_bias
    )
    feed_grad = grad_out.astype(jnp.bfloat16)
    grad_fc2_weight = jnp.einsum("tf,td->fd", hidden, feed_grad, preferred_element_type=jnp.float32)
    grad_fc2_bias = jnp.sum(feed_grad.astype(jnp.float32), axis=0)
    hidden_grad = jnp.einsum("td,fd->tf", feed_grad, weights[9], preferred_element_type=jnp.float32)
    primal_gelu, gelu_pull = jax.vjp(gelu_tanh, hidden_pre)
    pre_grad = gelu_pull(hidden_grad)[0].astype(jnp.bfloat16)
    grad_fc1_bias = jnp.sum(pre_grad.astype(jnp.float32), axis=0)
    grad_fc1_weight = jnp.einsum(
        "td,tf->df", normed_two, pre_grad, preferred_element_type=jnp.float32
    )
    normed_two_grad = jnp.einsum(
        "tf,df->td", pre_grad, weights[8], preferred_element_type=jnp.float32
    )
    primal_two, norm_two_pull = jax.vjp(
        layer_norm, residual, weights[6].astype(jnp.float32), weights[7].astype(jnp.float32)
    )
    residual_part, grad_ln2_gain, grad_ln2_bias = norm_two_pull(normed_two_grad)
    residual_grad = grad_out + residual_part
    branch_grad = residual_grad.astype(jnp.bfloat16)
    grad_out_bias = jnp.sum(branch_grad.astype(jnp.float32), axis=0)
    grad_out_weight = jnp.einsum(
        "tc,td->cd", attended, branch_grad, preferred_element_type=jnp.float32
    )
    attended_grad = jnp.einsum(
        "td,cd->tc", branch_grad, weights[4], preferred_element_type=jnp.float32
    ).astype(jnp.bfloat16)
    attended_heads = heads_of(attended_grad)
    probs_grad = jnp.einsum(
        "qhd,khd->hqk", attended_heads, heads_of(values_near), preferred_element_type=jnp.float32
    )
    value_terms = jnp.einsum(
        "hqk,qhd->khd", probs_low, attended_heads, preferred_element_type=jnp.float32
    )
    score_grad = (
        probs * (probs_grad - jnp.sum(probs * probs_grad, axis=-1, keepdims=True))
    ).astype(jnp.bfloat16)
    query_grad = (
        jnp.einsum(
            "hqk,khd->qhd", score_grad, heads_of(keys_near), preferred_element_type=jnp.float32
        )
        * score_scale
    )
    query_grad = query_grad.reshape(queries.shape[0], D).astype(jnp.bfloat16)
    key_terms = (
        jnp.einsum(
            "hqk,qhd->khd", score_grad, heads_of(queries), preferred_element_type=jnp.float32
        )
        * score_scale
    )
    key_total, value_total = return_key_grads(key_terms.reshape(-1, D), value_terms.reshape(-1, D))
    key_grad = key_total.astype(jnp.bfloat16)
    value_grad = value_total.astype(jnp.bfloat16)
    grad_qv_bias = jnp.stack(
        [
            jnp.sum(query_grad.astype(jnp.float32), axis=0),
            jnp.sum(value_grad.astype(jnp.float32), axis=0),
        ]
    )
    mixed_grad = jnp.concatenate([query_grad, key_grad, value_grad], axis=1)
    grad_qkv_weight = jnp.einsum(
        "tc,tk->ck", normed_one, mixed_grad, preferred_element_type=jnp.float32
    )
    normed_one_grad = jnp.einsum(
        "tk,ck->tc", mixed_grad, weights[2], preferred_element_type=jnp.float32
    )
    primal_one, norm_one_pull = jax.vjp(
        layer_norm, layer_float, weights[0].astype(jnp.float32), weights[1].astype(jnp.float32)
    )
    input_part, grad_ln1_gain, grad_ln1_bias = norm_one_pull(normed_one_grad)
    input_grad = residual_grad + input_part
    grad_terms = (
        grad_ln1_gain,
        grad_ln1_bias,
        grad_qkv_weight,
        grad_qv_bias,
        grad_out_weight,
        grad_out_bias,
        grad_ln2_gain,
        grad_ln2_bias,
        grad_fc1_weight,
        grad_fc2_weight,
        grad_fc2_bias,
    )
    return (input_grad, grad_terms, grad_fc1_bias)


def on_device_near(
    tokens,
    cotangent,
    image_of_block,
    ln1_gain,
    ln1_bias,
    qkv_weight,
    qv_bias,
    out_weight,
    out_bias,
    ln2_gain,
    ln2_bias,
    fc1_weight,
    fc1_bias,
    fc2_weight,
    fc2_bias,
):
    section_rank = lax.axis_index("section")
    wide_rank = lax.axis_index("wide")
    micro_count = tokens.shape[0]
    weights = (
        lax.all_gather(ln1_gain[0], "wide", axis=0, tiled=True),
        lax.all_gather(ln1_bias[0], "wide", axis=0, tiled=True),
        lax.all_gather(qkv_weight[0], "wide", axis=0, tiled=True),
        lax.all_gather(qv_bias[0], "wide", axis=1, tiled=True),
        lax.all_gather(out_weight[0], "wide", axis=0, tiled=True),
        lax.all_gather(out_bias[0], "wide", axis=0, tiled=True),
        lax.all_gather(ln2_gain[0], "wide", axis=0, tiled=True),
        lax.all_gather(ln2_bias[0], "wide", axis=0, tiled=True),
        lax.all_gather(fc1_weight[0], "wide", axis=0, tiled=True),
        lax.all_gather(fc2_weight[0], "wide", axis=1, tiled=True),
        lax.all_gather(fc2_bias[0], "wide", axis=0, tiled=True),
    )
    hidden_bias = fc1_bias[0]
    inputs_kept = jnp.zeros_like(tokens)
    outputs_kept = jnp.zeros_like(tokens)
    incoming = jnp.zeros_like(tokens[0])
    for tick_number in range(micro_count + 1):
        batch_index = tick_number - section_rank
        is_live = (batch_index >= 0) & (batch_index < micro_count)
        batch_slot = jnp.clip(batch_index, 0, micro_count - 1)
        own_tokens = tokens[min(tick_number, micro_count - 1)]
        layer_in = jnp.where(section_rank == 0, own_tokens, incoming)
        same_image = image_mask(image_of_block, batch_slot, wide_rank)
        layer_float, normed_one, queries, key_own, value_own = project_qkv(layer_in, weights)
        keys_near, values_near = near_keys(key_own, value_own, False)
        output = finish_layer(
            layer_float, queries, keys_near, values_near, same_image, weights, hidden_bias
        )[-1]
        output_low = output.astype(jnp.bfloat16)
        inputs_kept = keep_slot(inputs_kept, layer_in, batch_slot, is_live)
        outputs_kept = keep_slot(outputs_kept, output_low, batch_slot, is_live)
        if tick_number < micro_count:
            incoming = shifted(output_low, "section", 1)
    weights_back = (
        lax.all_gather(ln1_gain[0], "wide", axis=0, tiled=True),
        lax.all_gather(ln1_bias[0], "wide", axis=0, tiled=True),
        lax.all_gather(qkv_weight[0], "wide", axis=0, tiled=True),
        lax.all_gather(qv_bias[0], "wide", axis=1, tiled=True),
        lax.all_gather(out_weight[0], "wide", axis=0, tiled=True),
        lax.all_gather(out_bias[0], "wide", axis=0, tiled=True),
        lax.all_gather(ln2_gain[0], "wide", axis=0, tiled=True),
        lax.all_gather(ln2_bias[0], "wide", axis=0, tiled=True),
        lax.all_gather(fc1_weight[0], "wide", axis=0, tiled=True),
        lax.all_gather(fc2_weight[0], "wide", axis=1, tiled=True),
        lax.all_gather(fc2_bias[0], "wide", axis=0, tiled=True),
    )
    grad_totals = tuple((jnp.zeros(array.shape, jnp.float32) for array in weights_back))
    hidden_bias_total = jnp.zeros(hidden_bias.shape, jnp.float32)
    input_grads = jnp.zeros(tokens.shape, jnp.float32)
    incoming_grad = jnp.zeros(tokens.shape[1:], jnp.bfloat16)
    for tick_number in range(micro_count + 1):
        batch_index = tick_number - 1 + section_rank
        is_live = (batch_index >= 0) & (batch_index < micro_count)
        batch_slot = jnp.clip(batch_index, 0, micro_count - 1)
        from_cotangent = cotangent[min(tick_number, micro_count - 1)].astype(jnp.float32)
        grad_out = jnp.where(
            section_rank == 1, from_cotangent, incoming_grad.astype(jnp.float32)
        ) * is_live.astype(jnp.float32)
        layer_in = lax.dynamic_index_in_dim(inputs_kept, batch_slot, 0, keepdims=False)
        same_image = image_mask(image_of_block, batch_slot, wide_rank)
        layer_float, normed_one, queries, key_own, value_own = project_qkv(layer_in, weights_back)
        keys_near, values_near = near_keys(key_own, value_own, True)
        input_grad, grad_terms, hidden_bias_term = layer_backward(
            layer_float,
            normed_one,
            queries,
            keys_near,
            values_near,
            same_image,
            weights_back,
            hidden_bias,
            grad_out,
        )
        grad_totals = tuple(
            (old_total + new_term for old_total, new_term in zip(grad_totals, grad_terms))
        )
        hidden_bias_total = hidden_bias_total + hidden_bias_term
        input_grads = keep_slot(input_grads, input_grad, batch_slot, is_live)
        if tick_number < micro_count:
            incoming_grad = shifted(input_grad.astype(jnp.bfloat16), "section", -1)
    (
        grad_ln1_gain,
        grad_ln1_bias,
        grad_qkv_weight,
        grad_qv_bias,
        grad_out_weight,
        grad_out_bias,
        grad_ln2_gain,
        grad_ln2_bias,
        grad_fc1_weight,
        grad_fc2_weight,
        grad_fc2_bias,
    ) = grad_totals
    row_sums = (
        lax.psum_scatter(grad_ln1_gain, "wide", scatter_dimension=0, tiled=True),
        lax.psum_scatter(grad_ln1_bias, "wide", scatter_dimension=0, tiled=True),
        lax.psum_scatter(grad_qkv_weight, "wide", scatter_dimension=0, tiled=True),
        lax.psum_scatter(grad_out_weight, "wide", scatter_dimension=0, tiled=True),
        lax.psum_scatter(grad_out_bias, "wide", scatter_dimension=0, tiled=True),
        lax.psum_scatter(grad_ln2_gain, "wide", scatter_dimension=0, tiled=True),
        lax.psum_scatter(grad_ln2_bias, "wide", scatter_dimension=0, tiled=True),
        lax.psum_scatter(grad_fc1_weight, "wide", scatter_dimension=0, tiled=True),
        lax.psum_scatter(grad_fc2_bias, "wide", scatter_dimension=0, tiled=True),
    )
    column_sums = (
        lax.psum_scatter(grad_qv_bias, "wide", scatter_dimension=1, tiled=True),
        lax.psum_scatter(grad_fc2_weight, "wide", scatter_dimension=1, tiled=True),
    )
    hidden_bias_sum = lax.psum(hidden_bias_total, "wide")
    return (
        outputs_kept[None],
        input_grads[None],
        row_sums[0][None],
        row_sums[1][None],
        row_sums[2][None],
        column_sums[0][None],
        row_sums[3][None],
        row_sums[4][None],
        row_sums[5][None],
        row_sums[6][None],
        row_sums[7][None],
        hidden_bias_sum[None],
        column_sums[1][None],
        row_sums[8][None],
    )


def specs():
    ins = (
        P(None, "wide", None),
        P(None, "wide", None),
        P(),
        P("section", "wide"),
        P("section", "wide"),
        P("section", "wide", None),
        P("section", None, "wide"),
        P("section", "wide", None),
        P("section", "wide"),
        P("section", "wide"),
        P("section", "wide"),
        P("section", "wide", None),
        P("section", None),
        P("section", None, "wide"),
        P("section", "wide"),
    )
    outs = (
        P("section", None, "wide", None),
        P("section", None, "wide", None),
        P("section", "wide"),
        P("section", "wide"),
        P("section", "wide", None),
        P("section", None, "wide"),
        P("section", "wide", None),
        P("section", "wide"),
        P("section", "wide"),
        P("section", "wide"),
        P("section", "wide", None),
        P("section", None),
        P("section", None, "wide"),
        P("section", "wide"),
    )
    return ins, outs


def solution(mesh):
    ins, outs = specs()
    body = on_device if mesh.shape["wide"] == HEADS else on_device_near
    return jax.shard_map(body, mesh=mesh, in_specs=ins, out_specs=outs, check_vma=False)
```

```python
import functools
import math

import jax
import jax.numpy as jnp
from jax import lax
from jax.experimental import pallas as pl
from jax.experimental.pallas import tpu as pltpu
from jax.sharding import PartitionSpec as P

D = 1152
HEADS = 16
HEAD_DIM = 72
FF = 4304
FFP = -(-FF // 256) * 256
SPLIT = 9 * 256
BLOCK = 128
IMG_BLOCKS = 6
EPSILON = 1e-06
MASKED_SCORE = -1e30
SCALE = 1.0 / math.sqrt(HEAD_DIM)
MESH = pl.DeviceIdType.MESH
BF = jnp.bfloat16
F32 = jnp.float32


def place():
    return lax.axis_index("section"), lax.axis_index("wide")


class Gather:
    def __init__(self, ins, outs, sems):
        self.ins, self.outs, self.count = ins, outs, len(ins)
        self.local_sem = sems[0]
        self.up, self.down, self.yy, self.cc = [(sems[1 + 2 * i], sems[2 + 2 * i]) for i in range(4)]
        self.sec, self.me = place()
        self.z, self.low = self.me // 4, self.me % 4
        self.other_y = self.me - self.low + flip(self.low, 2)
        self.other_c = self.me - self.low + flip(self.low, 1)

    @staticmethod
    def semaphores(count):
        dma = pltpu.SemaphoreType.DMA
        return [dma((count,))] + [dma((count, 4))] * 6 + [dma((count, 8))] * 2

    def send(self, piece, origin, sems, slot, target, first=False):
        return pltpu.make_async_remote_copy(
            src_ref=self.ins[piece] if first else self.outs[piece].at[origin],
            dst_ref=self.outs[piece].at[origin],
            send_sem=sems[0].at[piece, slot],
            recv_sem=sems[1].at[piece, slot],
            device_id=(self.sec, target),
            device_id_type=MESH,
        )

    def mine(self, piece):
        return pltpu.make_async_copy(self.ins[piece], self.outs[piece].at[self.me], self.local_sem.at[piece])

    def along(self, piece, origin, first, go_up, go_down):
        zo = origin // 4
        if go_up:

            @pl.when(self.z < 3)
            def _():
                self.send(piece, origin, self.up, zo, self.me + 4, first).start()

        if go_down:

            @pl.when(self.z > 0)
            def _():
                self.send(piece, origin, self.down, zo, self.me - 4, first).start()

        self.send(piece, origin, self.yy, zo, self.other_y, first).start()
        self.send(piece, origin, self.cc, zo, self.other_c, first).start()

    def start(self):
        for piece in range(self.count):
            self.mine(piece).start()
            self.along(piece, self.me, True, True, True)

    def step(self, step):
        for piece in range(self.count):

            @pl.when(self.z - step >= 0)
            def _():
                origin = self.me - 4 * step
                self.send(piece, origin, self.up, self.z - step, self.me).wait_recv()
                self.along(piece, origin, False, True, False)

            @pl.when(self.z + step <= 3)
            def _():
                origin = self.me + 4 * step
                self.send(piece, origin, self.down, self.z + step, self.me).wait_recv()
                self.along(piece, origin, False, False, True)

    def across(self):
        far = self.other_y % 4
        for step in range(4):
            zo = (self.z + step) % 4
            for piece in range(self.count):
                origin = zo * 4 + far
                self.send(piece, origin, self.yy, zo, self.other_y).wait_recv()
                self.send(piece, origin, self.cc, 4 + zo, self.other_c).start()

    def finish(self):
        for zo in range(4):
            for piece in range(self.count):
                self.send(piece, self.me, self.yy, zo, self.other_y).wait_send()
                for slot in (zo, 4 + zo):
                    self.send(piece, self.me, self.cc, slot, self.other_c).wait_send()
                    self.send(piece, self.me, self.cc, slot, self.other_c).wait_recv()

                @pl.when((zo <= self.z) & (self.z < 3))
                def _():
                    self.send(piece, self.me, self.up, zo, self.me).wait_send()

                @pl.when((zo >= self.z) & (self.z > 0))
                def _():
                    self.send(piece, self.me, self.down, zo, self.me).wait_send()

        for piece in range(self.count):
            self.mine(piece).wait()


def gather_kernel(count, *refs):
    sec, me = place()
    greet_all(16, sec, me)
    work = Gather(refs[:count], refs[count : 2 * count], refs[2 * count :])
    work.start()
    for step in range(1, 4):
        work.step(step)
    work.across()
    work.finish()


def gather(arrays, cid):
    count = len(arrays)
    return pl.pallas_call(
        functools.partial(gather_kernel, count),
        out_shape=[jax.ShapeDtypeStruct((16,) + a.shape, a.dtype) for a in arrays],
        in_specs=[pl.BlockSpec(memory_space=pl.ANY)] * count,
        out_specs=[pl.BlockSpec(memory_space=pl.ANY)] * count,
        scratch_shapes=Gather.semaphores(count),
        compiler_params=pltpu.CompilerParams(collective_id=cid, has_side_effects=True),
    )(*arrays)


def flip(low, k):
    return [low, low + 1 - 2 * (low % 2), (low + 2) % 4, 3 - low][k]


def greet_all(count, sec, me):
    barrier = pltpu.get_barrier_semaphore()
    for d in range(1, count):
        pl.semaphore_signal(barrier, inc=1, device_id=(sec, (me + d) % count), device_id_type=MESH)
    pl.semaphore_wait(barrier, count - 1)


class Whole:
    def __init__(self, zero, one, cols=None):
        self.sources, self.cols = (zero, one), cols

    def shape(self):
        rows, cols = self.sources[0].shape
        return (4, rows, cols if self.cols is None else self.cols[1] - self.cols[0])

    def source(self, ref, low, k):
        return ref if self.cols is None else ref.at[:, self.cols[0] : self.cols[1]]

    forwarded = True


class Rows:
    def __init__(self, zero, one):
        self.sources = (zero, one)

    def shape(self):
        return self.sources[0].shape

    def source(self, ref, low, k):
        return ref.at[flip(low, k)]

    forwarded = False


class PlaneCopies:
    def __init__(self, item, zero_ref, one_ref, slot, local_sem, send_sem, recv_sem):
        self.item, self.refs, self.slot = item, (zero_ref, one_ref), slot
        self.local_sem, self.send_sem, self.recv_sem = local_sem, send_sem, recv_sem
        self.sec, self.me = place()
        self.low = self.me % 4

    def remote(self, src, k, to):
        return pltpu.make_async_remote_copy(
            src_ref=src,
            dst_ref=self.slot(k),
            send_sem=self.send_sem.at[k],
            recv_sem=self.recv_sem.at[k],
            device_id=(self.sec, self.me - self.low + flip(self.low, to)),
            device_id_type=MESH,
        )

    def local(self, ref):
        return pltpu.make_async_copy(self.item.source(ref, self.low, 0), self.slot(0), self.local_sem)

    def start(self):
        def go(ref):
            self.local(ref).start()
            for k in (2, 1) if self.item.forwarded else (2, 3, 1):
                self.remote(self.item.source(ref, self.low, k), k, k).start()

        @pl.when(self.sec == 0)
        def _():
            go(self.refs[0])

        @pl.when(self.sec == 1)
        def _():
            go(self.refs[1])

    def forward(self):
        if self.item.forwarded:
            self.remote(self.slot(2), 2, 2).wait_recv()
            self.remote(self.slot(2), 3, 1).start()

    def finish(self):
        self.local(self.refs[0]).wait()
        for k in (1, 2, 3):
            self.remote(self.slot(k), k, k).wait_send()
            if k != 2 or not self.item.forwarded:
                self.remote(self.slot(k), k, k).wait_recv()


def dot(a, b):
    return jnp.dot(a, b, preferred_element_type=F32)


def window(image_of_block):
    micro, blocks = image_of_block.shape
    own, other = image_of_block[:, :, None], image_of_block[:, None, :]
    begin = jnp.sum((other < own).astype(jnp.int32), axis=2)
    end = jnp.sum((other <= own).astype(jnp.int32), axis=2)
    first = jnp.minimum(begin, blocks - IMG_BLOCKS)
    shape = (micro, blocks, IMG_BLOCKS, BLOCK)
    at = first[:, :, None, None] + lax.broadcasted_iota(jnp.int32, shape, 2)
    same = (at >= begin[:, :, None, None]) & (at < end[:, :, None, None])
    return first, jnp.where(same, 0.0, MASKED_SCORE).astype(F32)


def near_rows(ref, start):
    return jnp.concatenate([ref[start + j] for j in range(IMG_BLOCKS)], axis=0)


def near_columns(ref, start):
    return jnp.concatenate([ref[start + j] for j in range(IMG_BLOCKS)], axis=1)


def fetch(pairs, buffers, sems, sec):
    for which in range(2):

        @pl.when(sec == which)
        def _():
            for i, buffer in enumerate(buffers):
                pltpu.make_async_copy(pairs[2 * i + which], buffer, sems.at[i]).start()


def fetched(pairs, buffers, sems):
    for i, buffer in enumerate(buffers):
        pltpu.make_async_copy(pairs[2 * i], buffer, sems.at[i]).wait()


class ToAll:
    def __init__(self, block, dst, send, recv, sec, me, count):
        self.block, self.dst, self.send, self.recv = block, dst, send, recv
        self.sec, self.me, self.count = sec, me, count

    def copy(self, d):
        return pltpu.make_async_remote_copy(
            src_ref=self.block(d),
            dst_ref=self.dst.at[self.me],
            send_sem=self.send.at[d],
            recv_sem=self.recv.at[d],
            device_id=(self.sec, (self.me + d) % self.count),
            device_id_type=MESH,
        )

    def start(self):
        for d in sorted(range(1, self.count), key=lambda d: abs(d - self.count // 2)):
            self.copy(d).start()

    def start_one(self, d):
        @pl.when(d > 0)
        def _():
            self.copy(d).start()

    def wait(self):
        for d in range(1, self.count):
            self.copy(d).wait()


class Forward:
    def __init__(self, tick, near, x_ref, outs, scratch):
        self.first_ref, self.bias_ref = near
        self.x_ref = x_ref
        self.qkv_ref, self.lse_ref, self.att_ref = outs
        self.k_all, self.vt_all, self.o_buf, self.local_sem, *sems = scratch
        self.count = x_ref.shape[0]
        sec, self.me = place()
        self.slot = jnp.minimum(jnp.maximum(tick - sec, 0), 1)
        rest = (sec, self.me, self.count)
        self.arrive = ToAll(lambda d: x_ref.at[(self.me + d) % self.count], self.qkv_ref, *sems[:2], *rest)
        self.leave = ToAll(lambda d: self.o_buf.at[d], self.att_ref, *sems[2:], *rest)

    @staticmethod
    def scratch(blocks):
        dma = pltpu.SemaphoreType.DMA
        return [
            pltpu.VMEM((blocks, BLOCK, HEAD_DIM), BF),
            pltpu.VMEM((blocks, HEAD_DIM, BLOCK), BF),
            pltpu.VMEM((blocks, HEAD_DIM, BLOCK), BF),
            dma,
        ] + [dma((blocks,))] * 4

    def own(self):
        return pltpu.make_async_copy(self.x_ref.at[self.me], self.qkv_ref.at[self.me], self.local_sem)

    def start(self):
        self.arrive.start()
        self.own().start()

    def wait_in(self):
        self.own().wait()
        self.arrive.wait()

    def compute(self):
        def arrange(j, carry):
            part = self.qkv_ref[j].astype(F32)
            self.k_all[j] = part[HEAD_DIM : 2 * HEAD_DIM].T.astype(BF)
            self.vt_all[j] = part[2 * HEAD_DIM :].astype(BF)
            return carry

        lax.fori_loop(0, self.count, arrange, 0)

        def one_block(d, carry):
            i = (self.me + d) % self.count
            start = self.first_ref[self.slot, i]
            qt = self.qkv_ref[i].astype(F32)[:HEAD_DIM].astype(BF)
            s = dot(near_rows(self.k_all, start), qt) * SCALE
            bias = self.bias_ref[self.slot, i]
            parts = [s[j * BLOCK : (j + 1) * BLOCK] + bias[j : j + 1] for j in range(IMG_BLOCKS)]
            top = parts[0]
            for part in parts[1:]:
                top = jnp.maximum(top, part)
            top = jnp.max(top, axis=0, keepdims=True)
            exps = [jnp.exp(part - top) for part in parts]
            total = exps[0]
            for part in exps[1:]:
                total = total + part
            total = jnp.sum(total, axis=0, keepdims=True)
            e = jnp.concatenate([part.astype(BF) for part in exps], axis=0)
            o = dot(near_columns(self.vt_all, start), e)
            self.o_buf[d] = (o / total).astype(BF)
            self.lse_ref[i] = top + jnp.log(total)
            self.leave.start_one(d)
            return carry

        lax.fori_loop(0, self.count, one_block, 0)
        self.att_ref[self.me] = self.o_buf[0]

    def wait_out(self):
        self.leave.wait()


class Backward:
    def __init__(self, tick, near, kept, x_ref, outs, scratch):
        self.first_ref, self.bias_ref = near
        self.kept, self.x_ref = kept, x_ref
        self.dq_ref, self.dkv_ref = outs
        self.qkv_ref, self.lse_ref, self.do_ref = scratch[:3]
        self.k_all, self.kt_all, self.v_all, self.q_all, self.do_all, self.p_all, self.s_all = scratch[3:10]
        self.dq_buf, self.dkv_buf, self.kept_sem, self.local_sem = scratch[10:14]
        sems = scratch[14:]
        self.count = x_ref.shape[0]
        self.sec, self.me = place()
        self.slot = jnp.minimum(jnp.maximum(tick - 1 + self.sec, 0), 1)
        rest = (self.sec, self.me, self.count)
        self.arrive = ToAll(lambda d: x_ref.at[(self.me + d) % self.count], self.do_ref, *sems[:2], *rest)
        self.leave_q = ToAll(lambda d: self.dq_buf.at[d], self.dq_ref, *sems[2:4], *rest)
        self.leave_kv = ToAll(lambda d: self.dkv_buf.at[d], self.dkv_ref, *sems[4:], *rest)

    @staticmethod
    def scratch(blocks):
        dma = pltpu.SemaphoreType.DMA
        return [
            pltpu.VMEM((blocks, 3 * HEAD_DIM, BLOCK), BF),
            pltpu.VMEM((blocks, 1, BLOCK), F32),
            pltpu.VMEM((blocks, HEAD_DIM, BLOCK), BF),
            pltpu.VMEM((blocks, BLOCK, HEAD_DIM), BF),
            pltpu.VMEM((blocks, HEAD_DIM, BLOCK), BF),
            pltpu.VMEM((blocks, BLOCK, HEAD_DIM), BF),
            pltpu.VMEM((blocks, BLOCK, HEAD_DIM), BF),
            pltpu.VMEM((blocks, BLOCK, HEAD_DIM), BF),
            pltpu.VMEM((blocks, IMG_BLOCKS, BLOCK, BLOCK), BF),
            pltpu.VMEM((blocks, IMG_BLOCKS, BLOCK, BLOCK), BF),
            pltpu.VMEM((blocks, HEAD_DIM, BLOCK), BF),
            pltpu.VMEM((blocks, 2 * HEAD_DIM, BLOCK), BF),
            dma((2,)),
            dma,
        ] + [dma((blocks,))] * 6

    def own(self):
        return pltpu.make_async_copy(self.x_ref.at[self.me], self.do_ref.at[self.me], self.local_sem)

    def start(self):
        self.arrive.start()
        self.own().start()
        fetch(self.kept, (self.qkv_ref, self.lse_ref), self.kept_sem, self.sec)

    def arrange(self):
        fetched(self.kept, (self.qkv_ref, self.lse_ref), self.kept_sem)

        def one(j, carry):
            part = self.qkv_ref[j].astype(F32)
            self.q_all[j] = part[:HEAD_DIM].T.astype(BF)
            self.k_all[j] = part[HEAD_DIM : 2 * HEAD_DIM].T.astype(BF)
            self.v_all[j] = part[2 * HEAD_DIM :].T.astype(BF)
            self.kt_all[j] = part[HEAD_DIM : 2 * HEAD_DIM].astype(BF)
            return carry

        lax.fori_loop(0, self.count, one, 0)

    def wait_in(self):
        self.own().wait()
        self.arrive.wait()

    def by_query(self):
        def turn(j, carry):
            self.do_all[j] = self.do_ref[j].astype(F32).T.astype(BF)
            return carry

        lax.fori_loop(0, self.count, turn, 0)

        def one(d, carry):
            i = (self.me + d) % self.count
            start = self.first_ref[self.slot, i]
            qt = self.qkv_ref[i].astype(F32)[:HEAD_DIM].astype(BF)
            s = dot(near_rows(self.k_all, start), qt) * SCALE
            shift = self.bias_ref[self.slot, i] - self.lse_ref[i]
            probs = [jnp.exp(s[j * BLOCK : (j + 1) * BLOCK] + shift[j : j + 1]) for j in range(IMG_BLOCKS)]
            dp = dot(near_rows(self.v_all, start), self.do_ref[i])
            total = probs[0] * dp[:BLOCK]
            for j in range(1, IMG_BLOCKS):
                total = total + probs[j] * dp[j * BLOCK : (j + 1) * BLOCK]
            total = jnp.sum(total, axis=0, keepdims=True)
            ds = jnp.concatenate(
                [(probs[j] * (dp[j * BLOCK : (j + 1) * BLOCK] - total)).astype(BF) for j in range(IMG_BLOCKS)], axis=0
            )
            for j in range(IMG_BLOCKS):
                self.p_all[i, j] = probs[j].astype(BF)
                self.s_all[i, j] = ds[j * BLOCK : (j + 1) * BLOCK]
            self.dq_buf[d] = (dot(near_columns(self.kt_all, start), ds) * SCALE).astype(BF)
            self.leave_q.start_one(d)
            return carry

        lax.fori_loop(0, self.count, one, 0)
        self.dq_ref[self.me] = self.dq_buf[0]

    def by_key(self):
        def one(d, carry):
            j = (self.me + d) % self.count
            start = self.first_ref[self.slot, j]
            place_in = jnp.clip(j - start, 0, IMG_BLOCKS - 1)
            same = (self.bias_ref[self.slot, j] == 0.0).astype(F32).astype(BF)
            p, ds = [], []
            for m in range(IMG_BLOCKS):
                p.append(self.p_all[start + m, place_in] * same[m : m + 1])
                ds.append(self.s_all[start + m, place_in] * same[m : m + 1])
            dv = dot(jnp.concatenate(p, axis=1), near_rows(self.do_all, start))
            dk = dot(jnp.concatenate(ds, axis=1), near_rows(self.q_all, start)) * SCALE
            self.dkv_buf[d] = jnp.concatenate([dk.T, dv.T], axis=0).astype(BF)
            self.leave_kv.start_one(d)
            return carry

        lax.fori_loop(0, self.count, one, 0)
        self.dkv_ref[self.me] = self.dkv_buf[0]

    def wait_out(self):
        self.leave_q.wait()
        self.leave_kv.wait()


def attention_kernel(ahead, behind, items, pieces, *refs):
    refs = list(refs)

    def take(n):
        part = refs[:n]
        del refs[:n]
        return part

    n = len(items)
    near = take(2)
    x_ref = take(1) if ahead is not None else None
    kept, g_ref = (take(4), take(1)) if behind is not None else (None, None)
    sources, shards = take(2 * n), take(pieces)
    ahead_out = take(3) if ahead is not None else None
    behind_out = take(2) if behind is not None else None
    outs, whole = take(n), take(pieces)
    f = b = work = None
    blocks = (x_ref or g_ref)[0].shape[0]
    sec, me = place()
    if ahead is not None:
        f = Forward(ahead, near, x_ref[0], ahead_out, take(len(Forward.scratch(blocks))))
    if behind is not None:
        b = Backward(behind, near, kept, g_ref[0], behind_out, take(len(Backward.scratch(blocks))))
    copies = []
    for i, item in enumerate(items):
        into = lambda k, i=i: outs[i].at[k]
        copies.append(PlaneCopies(item, sources[2 * i], sources[2 * i + 1], into, *take(3)))
    if pieces:
        work = Gather(shards, whole, take(9))
    greet_all(blocks, sec, me)

    if b:
        b.start()
        b.arrange()
        b.wait_in()
    if f:
        f.start()
    if work:
        work.start()
    if f and not b:
        f.wait_in()
    if work:
        work.step(1)
    if not (f and b):
        for copy in copies:
            copy.start()
    if b:
        b.by_query()
        b.by_key()
    if f and b:
        f.wait_in()
        for copy in copies:
            copy.start()
    if f:
        f.compute()
    if work:
        work.step(2)
    for copy in copies:
        copy.forward()
    if f:
        f.wait_out()
    if b:
        b.wait_out()
    if work:
        work.step(3)
        work.across()
        work.finish()
    for copy in copies:
        copy.finish()


def attention(near, cid, ahead=None, behind=None, items=(), shards=()):
    first_in = ahead[1] if ahead else behind[1]
    blocks = first_in.shape[0]
    n = len(items)
    sources = [source for item in items for source in item.sources]
    anywhere, vmem, smem = [pl.BlockSpec(memory_space=m) for m in (pl.ANY, pltpu.VMEM, pltpu.SMEM)]
    dma = pltpu.SemaphoreType.DMA
    args, scratch, shapes = [], [], []
    if ahead:
        args.append(ahead[1])
        scratch += Forward.scratch(blocks)
        shapes += [
            jax.ShapeDtypeStruct((blocks, 3 * HEAD_DIM, BLOCK), BF),
            jax.ShapeDtypeStruct((blocks, 1, BLOCK), F32),
            jax.ShapeDtypeStruct((blocks, HEAD_DIM, BLOCK), BF),
        ]
    if behind:
        args += [*behind[2], behind[1]]
        scratch += Backward.scratch(blocks)
        shapes += [
            jax.ShapeDtypeStruct((blocks, HEAD_DIM, BLOCK), BF),
            jax.ShapeDtypeStruct((blocks, 2 * HEAD_DIM, BLOCK), BF),
        ]
    args += sources + list(shards)
    scratch += [dma, dma((4,)), dma((4,))] * n
    if shards:
        scratch += Gather.semaphores(len(shards))
    in_vmem = len(shapes)
    shapes += [jax.ShapeDtypeStruct(item.shape(), BF) for item in items]
    shapes += [jax.ShapeDtypeStruct((blocks,) + shard.shape, BF) for shard in shards]
    out = pl.pallas_call(
        functools.partial(
            attention_kernel, ahead and ahead[0], behind and behind[0], list(items), len(shards)
        ),
        out_shape=shapes,
        in_specs=[smem, vmem] + [anywhere] * len(args),
        out_specs=[vmem] * in_vmem + [anywhere] * (n + len(shards)),
        scratch_shapes=scratch,
        compiler_params=pltpu.CompilerParams(collective_id=cid, has_side_effects=True, vmem_limit_bytes=60 << 20),
    )(*near, *args)
    out = list(out)
    three, out = (out[:3], out[3:]) if ahead else (None, out)
    two, out = (out[:2], out[2:]) if behind else (None, out)
    return three, two, out[:n], out[n:]


def slices(width, step=1024):
    return [(at, min(at + step, width)) for at in range(0, width, step)]


class Stream:
    def __init__(self, pairs, sems):
        self.copies = {}
        for i, (name, ref, buf, cols) in enumerate(pairs):
            src, dst = ref.at[:, cols[0] : cols[1]], buf.at[:, cols[0] : cols[1]]
            self.copies[name, cols[0]] = pltpu.make_async_copy(src, dst, sems.at[i])

    def start(self):
        for copy in self.copies.values():
            copy.start()

    def wait(self, name, at):
        self.copies[name, at].wait()


def normalised(x):
    mean = jnp.mean(x, axis=-1, keepdims=True)
    centred = x - mean
    rstd = lax.rsqrt(jnp.mean(centred * centred, axis=-1, keepdims=True) + EPSILON)
    return centred * rstd, rstd


def norm_backward(grad, xhat, rstd, gain):
    g = grad * gain
    part = g - jnp.mean(g, axis=-1, keepdims=True) - xhat * jnp.mean(g * xhat, axis=-1, keepdims=True)
    return part * rstd, jnp.sum(grad * xhat, axis=0, keepdims=True), jnp.sum(grad, axis=0, keepdims=True)


def gelu_tanh(v):
    c = math.sqrt(2.0 / math.pi)
    return 0.5 * v * (1.0 + jnp.tanh(c * (v + 0.044715 * (v * v * v))))


def gelu_slope(v):
    c = math.sqrt(2.0 / math.pi)
    square = v * v
    t = jnp.tanh(c * (v + 0.044715 * (square * v)))
    return 0.5 * (1.0 + t) + 0.5 * v * (1.0 - t * t) * (c * (1.0 + 3 * 0.044715 * square))


def nt(a, b):
    return lax.dot_general(a, b, (((1,), (1,)), ((), ())), preferred_element_type=F32)


def put_owners(ref, x):
    turned = x.T
    for w in range(HEADS):
        ref[w % 4, w // 4] = turned[w * HEAD_DIM : (w + 1) * HEAD_DIM].astype(BF)


GAIN1, BIAS1, OUT_BIAS, GAIN2, BIAS2, FC2_BIAS = range(6)


def row(vec_ref, i):
    return vec_ref[i : i + 1, :]


def pick(sec, zero_ref, one_ref):
    return jnp.where(sec == 0, zero_ref[...].astype(F32), one_ref[...].astype(F32))


def qkv_kernel(tok_ref, inc_ref, vec_ref, bias_ref, w_ref, qkv_ref, n1_ref, w_buf, t_buf, sems):
    sec, _ = place()
    stream = Stream([("w", w_ref, w_buf, cols) for cols in slices(3 * D, 384)], sems)
    stream.start()
    xhat, _ = normalised(pick(sec, tok_ref, inc_ref))
    n1 = xhat * row(vec_ref, GAIN1) + row(vec_ref, BIAS1)
    low = n1.astype(BF)
    for at, end in slices(3 * D, 384):
        stream.wait("w", at)
        t_buf[at:end, :] = (dot(low, w_buf[:, at:end]) + bias_ref[:, at:end]).T
    for h in range(HEADS):
        qkv_ref[h] = t_buf[h * 3 * HEAD_DIM : (h + 1) * 3 * HEAD_DIM, :].astype(BF)
    put_owners(n1_ref, low.astype(F32))


def qkv_forward(tok, inc, vec, bias, w):
    tokens = tok.shape[0]
    anywhere, vmem = pl.BlockSpec(memory_space=pl.ANY), pl.BlockSpec(memory_space=pltpu.VMEM)
    return pl.pallas_call(
        qkv_kernel,
        out_shape=[
            jax.ShapeDtypeStruct((HEADS, 3 * HEAD_DIM, tokens), BF),
            jax.ShapeDtypeStruct((4, 4, HEAD_DIM, tokens), BF),
        ],
        in_specs=[vmem] * 4 + [anywhere],
        out_specs=[vmem] * 2,
        scratch_shapes=[
            pltpu.VMEM((D, 3 * D), BF),
            pltpu.VMEM((3 * D, tokens), F32),
            pltpu.SemaphoreType.DMA((len(slices(3 * D, 384)),)),
        ],
        compiler_params=pltpu.CompilerParams(vmem_limit_bytes=60 << 20),
    )(tok, inc, vec, bias, w)


def greet_section(sec, me):
    barrier = pltpu.get_barrier_semaphore()
    pl.semaphore_signal(barrier, inc=1, device_id=(1 - sec, me), device_id_type=MESH)
    pl.semaphore_wait(barrier, 1)


def to_section(src, dst, send_sem, recv_sem, sec, me):
    return pltpu.make_async_remote_copy(
        src_ref=src, dst_ref=dst, send_sem=send_sem, recv_sem=recv_sem, device_id=(1 - sec, me), device_id_type=MESH
    )


def feed_kernel(shift, *refs):
    tok_ref, inc_ref, att_ref, vec_ref, bias_ref, out_w, fc1_w, fc2_w = refs[:8]
    res_ref, pre_ref, hidden_ref, n2_ref, att_rows_ref, low_ref = refs[8:14]
    refs = refs[14:]
    if shift:
        next_ref, refs = refs[0], refs[1:]
    out_buf, fc1_buf, fc2_buf, t_buf, sems = refs[:5]
    sec, me = place()
    pairs = [("out", out_w, out_buf, (0, D))]
    pairs += [("fc1", fc1_w, fc1_buf, cols) for cols in slices(FFP)]
    pairs += [("fc2", fc2_w, fc2_buf, cols) for cols in slices(FFP)]
    stream = Stream(pairs, sems)
    stream.start()
    if shift:
        greet_section(sec, me)
    att = jnp.concatenate([att_ref[h].astype(F32) for h in range(HEADS)], axis=0).T.astype(BF)
    for w in range(HEADS):
        att_rows_ref[w % 4, w // 4] = att_ref[w]
    stream.wait("out", 0)
    residual = pick(sec, tok_ref, inc_ref) + dot(att, out_buf[...]) + row(vec_ref, OUT_BIAS)
    res_ref[...] = residual
    xhat, _ = normalised(residual)
    n2 = (xhat * row(vec_ref, GAIN2) + row(vec_ref, BIAS2)).astype(BF)
    total = None
    for at, end in slices(FFP):
        stream.wait("fc1", at)
        pre = dot(n2, fc1_buf[:, at:end]) + bias_ref[:, at:end]
        pre_ref[:, at:end] = pre
        hidden = gelu_tanh(pre)
        hidden_ref[:, at:end] = hidden.astype(BF)
        t_buf[at:end, :] = hidden.T.astype(BF)
    for at, end in slices(FFP):
        stream.wait("fc2", at)
    total = dot(fc2_buf[...], t_buf[...])
    low_ref[...] = (residual + total.T + row(vec_ref, FC2_BIAS)).astype(BF)
    if shift:
        copy = to_section(low_ref, next_ref, refs[5], refs[6], sec, me)
        copy.start()
    put_owners(n2_ref, n2.astype(F32))
    if shift:
        copy.wait()


def feed_forward(tok, inc, att, vec, bias, out_w, fc1_w, fc2_w, cid):
    tokens = tok.shape[0]
    shift = cid is not None
    anywhere, vmem = pl.BlockSpec(memory_space=pl.ANY), pl.BlockSpec(memory_space=pltpu.VMEM)
    dma = pltpu.SemaphoreType.DMA
    params = dict(collective_id=cid, has_side_effects=True) if shift else {}
    rows = jax.ShapeDtypeStruct((4, 4, HEAD_DIM, tokens), BF)
    low = jax.ShapeDtypeStruct((tokens, D), BF)
    return pl.pallas_call(
        functools.partial(feed_kernel, shift),
        out_shape=[
            jax.ShapeDtypeStruct((tokens, D), F32),
            jax.ShapeDtypeStruct((tokens, FFP), F32),
            jax.ShapeDtypeStruct((tokens, FFP), BF),
            rows,
            rows,
            low,
        ]
        + [low] * shift,
        in_specs=[vmem] * 5 + [anywhere] * 3,
        out_specs=[vmem] * (6 + shift),
        scratch_shapes=[
            pltpu.VMEM((D, D), BF),
            pltpu.VMEM((D, FFP), BF),
            pltpu.VMEM((D, FFP), BF),
            pltpu.VMEM((FFP, tokens), BF),
            dma((1 + 2 * len(slices(FFP)),)),
        ]
        + [dma, dma] * shift,
        compiler_params=pltpu.CompilerParams(vmem_limit_bytes=60 << 20, **params),
    )(tok, inc, att, vec, bias, out_w, fc1_w, fc2_w)


def feed_back_kernel(cot_ref, inc_ref, vec_ref, *refs):
    kept, refs = refs[:4], refs[4:]
    out_w, fc1_w, fc2_w = refs[:3]
    rg_ref, ag_ref, fc_ref, pg_ref, branch_ref, sum_ref, fsum_ref = refs[3:10]
    pre_buf, res_buf, out_buf, fc1_buf, fc2_buf, t_buf, kept_sem, sems = refs[10:]
    sec, _ = place()
    pairs = []
    pairs += [("fc2", fc2_w, fc2_buf, cols) for cols in slices(FFP)]
    pairs += [("fc1", fc1_w, fc1_buf, cols) for cols in slices(FFP)]
    pairs.append(("out", out_w, out_buf, (0, D)))
    stream = Stream(pairs, sems)
    fetch(kept, (pre_buf, res_buf), kept_sem, sec)
    stream.start()
    grad = jnp.where(sec == 0, inc_ref[...].astype(F32), cot_ref[...].astype(F32))
    fc_grad = grad.astype(BF)
    put_owners(fc_ref, grad)
    fetched(kept, (pre_buf, res_buf), kept_sem)
    total = None
    for at, end in slices(FFP):
        slope = gelu_slope(pre_buf[:, at:end])
        stream.wait("fc2", at)
        pre_wide = dot(fc_grad, fc2_buf[:, at:end]) * slope
        pre_grad = pre_wide.astype(BF)
        pg_ref[:, at:end] = pre_grad
        fsum_ref[:, at:end] = jnp.sum(pre_grad.astype(F32), axis=0, keepdims=True)
        t_buf[at:end, :] = pre_wide.T.astype(BF)
    for at, end in slices(FFP):
        stream.wait("fc1", at)
    total = dot(fc1_buf[...], t_buf[...])
    xhat, rstd = normalised(res_buf[...])
    part, gain_sum, bias_sum = norm_backward(total.T, xhat, rstd, row(vec_ref, GAIN2))
    residual_grad = grad + part
    rg_ref[...] = residual_grad
    branch = residual_grad.astype(BF)
    branch_ref[...] = branch
    stream.wait("out", 0)
    att_grad = dot(out_buf[...], residual_grad.T.astype(BF))
    for h in range(HEADS):
        ag_ref[h] = att_grad[h * HEAD_DIM : (h + 1) * HEAD_DIM].astype(BF)
    sum_ref[0:1, :] = jnp.sum(branch.astype(F32), axis=0, keepdims=True)
    sum_ref[1:2, :] = gain_sum
    sum_ref[2:3, :] = bias_sum
    sum_ref[3:4, :] = jnp.sum(fc_grad.astype(F32), axis=0, keepdims=True)


def feed_backward(cot, inc, vec, kept, out_w, fc1_w, fc2_w):
    tokens = cot.shape[0]
    anywhere, vmem = pl.BlockSpec(memory_space=pl.ANY), pl.BlockSpec(memory_space=pltpu.VMEM)
    dma = pltpu.SemaphoreType.DMA
    return pl.pallas_call(
        feed_back_kernel,
        out_shape=[
            jax.ShapeDtypeStruct((tokens, D), F32),
            jax.ShapeDtypeStruct((HEADS, HEAD_DIM, tokens), BF),
            jax.ShapeDtypeStruct((4, 4, HEAD_DIM, tokens), BF),
            jax.ShapeDtypeStruct((tokens, FFP), BF),
            jax.ShapeDtypeStruct((tokens, D), BF),
            jax.ShapeDtypeStruct((4, D), F32),
            jax.ShapeDtypeStruct((1, FFP), F32),
        ],
        in_specs=[vmem] * 3 + [anywhere] * 7,
        out_specs=[vmem] * 7,
        scratch_shapes=[
            pltpu.VMEM((tokens, FFP), F32),
            pltpu.VMEM((tokens, D), F32),
            pltpu.VMEM((D, D), BF),
            pltpu.VMEM((D, FFP), BF),
            pltpu.VMEM((D, FFP), BF),
            pltpu.VMEM((FFP, tokens), BF),
            dma((2,)),
            dma((1 + 2 * len(slices(FFP)),)),
        ],
        compiler_params=pltpu.CompilerParams(vmem_limit_bytes=60 << 20),
    )(cot, inc, vec, *kept, out_w, fc1_w, fc2_w)


def qkv_back_kernel(shift, *refs):
    tok_ref, inc_ref, vec_ref, rg_ref, dq_ref, dkv_ref, w_ref = refs[:7]
    grad_ref, dqkv_ref, sum_ref, qsum_ref = refs[7:11]
    refs = refs[11:]
    if shift:
        next_ref, refs = refs[0], refs[1:]
    w_buf, sems = refs[:2]
    sec, me = place()
    stream = Stream([("w", w_ref, w_buf, cols) for cols in slices(3 * D, 384)], sems)
    stream.start()
    if shift:
        greet_section(sec, me)
    rows = []
    for h in range(HEADS):
        rows += [dq_ref[h].astype(F32), dkv_ref[h].astype(F32)]
    dqkv = jnp.concatenate(rows, axis=0).astype(BF)
    dqkv_ref[...] = dqkv
    qsum_ref[...] = nt(jnp.ones((8, dqkv.shape[1]), BF), dqkv)
    total = None
    for at, end in slices(3 * D, 384):
        stream.wait("w", at)
        part = dot(w_buf[:, at:end], dqkv[at:end])
        total = part if total is None else total + part
    xhat, rstd = normalised(pick(sec, tok_ref, inc_ref))
    part, gain_sum, bias_sum = norm_backward(total.T, xhat, rstd, row(vec_ref, GAIN1))
    grad = rg_ref[...] + part
    grad_ref[...] = grad
    if shift:
        low_buf = refs[2]
        low_buf[...] = grad.astype(BF)
        copy = to_section(low_buf, next_ref, refs[3], refs[4], sec, me)
        copy.start()
    sum_ref[0:1, :] = gain_sum
    sum_ref[1:2, :] = bias_sum
    if shift:
        copy.wait()


def qkv_backward(tok, inc, vec, residual_grad, dq, dkv, w, cid):
    tokens = tok.shape[0]
    shift = cid is not None
    anywhere, vmem = pl.BlockSpec(memory_space=pl.ANY), pl.BlockSpec(memory_space=pltpu.VMEM)
    dma = pltpu.SemaphoreType.DMA
    params = dict(collective_id=cid, has_side_effects=True) if shift else {}
    return pl.pallas_call(
        functools.partial(qkv_back_kernel, shift),
        out_shape=[
            jax.ShapeDtypeStruct((tokens, D), F32),
            jax.ShapeDtypeStruct((3 * D, tokens), BF),
            jax.ShapeDtypeStruct((2, D), F32),
            jax.ShapeDtypeStruct((8, 3 * D), F32),
        ]
        + [jax.ShapeDtypeStruct((tokens, D), BF)] * shift,
        in_specs=[vmem] * 6 + [anywhere],
        out_specs=[vmem] * (4 + shift),
        scratch_shapes=[pltpu.VMEM((D, 3 * D), BF), dma((len(slices(3 * D, 384)),))]
        + [pltpu.VMEM((tokens, D), BF), dma, dma] * shift,
        compiler_params=pltpu.CompilerParams(vmem_limit_bytes=60 << 20, **params),
    )(tok, inc, vec, residual_grad, dq, dkv, w)


def pad_ff(x):
    return jnp.pad(x, ((0, 0),) * (x.ndim - 1) + ((0, FFP - FF),))


TENSORS = ("fc2", "fc1", "out", "qkv")


def final_kernel(tiles, early, late, *refs):
    refs = list(refs)

    def take(n):
        part = refs[:n]
        del refs[:n]
        return part

    small_ref = take(1)[0]
    x_refs = {name: take(2) for name in TENSORS}
    early_refs = take(len(early))
    late_refs = take(2 * len(late))
    small_out = take(1)[0]
    out_refs = dict(zip(TENSORS, take(4)))
    y_bufs = dict(zip(TENSORS, take(4)))
    x_buf = take(1)[0]
    g_bufs, one_bufs, two_bufs = [dict(zip(TENSORS, take(4))) for _ in range(3)]
    small_got = take(1)[0]
    early_sem, small_send, small_recv = take(3)
    sems = {name: take(4) for name in TENSORS}
    late_sems = [take(3) for _ in late]

    sec, me = place()
    z, low = me // 4, me % 4
    pair = z + 1 - 2 * (z % 2)
    count = small_ref.shape[0]
    greet_all(count, sec, me)

    loads = []
    for i, (name, batch, cols) in enumerate(early):
        dst = y_bufs[name].at[4 * batch : 4 * batch + 4]
        if cols is not None:
            dst = dst.at[:, :, cols[0] : cols[1]]
        loads.append((name, pltpu.make_async_copy(early_refs[i], dst, early_sem.at[i])))
        loads[-1][1].start()
    behind = []
    for i, (name, batch, item) in enumerate(late):

        def slot(k, name=name, batch=batch, item=item):
            ref = y_bufs[name].at[4 * batch + k]
            return ref if item.cols is None else ref.at[:, item.cols[0] : item.cols[1]]

        behind.append((name, PlaneCopies(item, late_refs[2 * i], late_refs[2 * i + 1], slot, *late_sems[i])))
        behind[-1][1].start()
    smalls = []
    for d in range(1, count):
        target = (me + d) % count
        smalls.append(
            pltpu.make_async_remote_copy(
                src_ref=small_ref.at[target],
                dst_ref=small_got.at[d],
                send_sem=small_send.at[d],
                recv_sem=small_recv.at[d],
                device_id=(sec, target),
                device_id_type=MESH,
            )
        )
        smalls[-1].start()

    def first(name, i):
        send, recv = sems[name][0], sems[name][1]
        return pltpu.make_async_remote_copy(
            src_ref=g_bufs[name].at[i, 2:4],
            dst_ref=one_bufs[name].at[i],
            send_sem=send.at[i],
            recv_sem=recv.at[i],
            device_id=(sec, pair * 4 + low),
            device_id_type=MESH,
        )

    def second(name, i):
        send, recv = sems[name][2], sems[name][3]
        return pltpu.make_async_remote_copy(
            src_ref=g_bufs[name].at[i, 1],
            dst_ref=two_bufs[name].at[i],
            send_sem=send.at[i],
            recv_sem=recv.at[i],
            device_id=(sec, (3 - z) * 4 + low),
            device_id_type=MESH,
        )

    def ready(name):
        for other, one in behind:
            if other == name:
                one.forward()
        for other, load in loads:
            if other == name:
                load.wait()
        for other, one in behind:
            if other == name:
                one.finish()
        rows = []
        for owner in (z, 3 - z, pair, 3 - pair):
            rows.append(
                jnp.concatenate(
                    [x_refs[name][batch][k, owner].astype(F32) for batch in range(2) for k in range(4)], axis=1
                )
            )
        x_buf[...] = jnp.concatenate(rows, axis=0).astype(BF)

    def columns(name, i):
        width = tiles[name][1]
        return pl.ds(pl.multiple_of(i * width, 128), width)

    def compute(name, i):
        width = tiles[name][1]
        buf = y_bufs[name]
        if name == "qkv":
            rows = pl.ds(pl.multiple_of(i * width, 128), width)
            y = jnp.concatenate([buf[part, rows, :] for part in range(8)], axis=1)
            total = lax.dot_general(x_buf[...], y, (((1,), (1,)), ((), ())), preferred_element_type=F32)
        else:
            y = jnp.concatenate([buf[part, :, columns(name, i)] for part in range(8)], axis=0)
            total = dot(x_buf[...], y)
        g_bufs[name][i] = total.reshape(4, HEAD_DIM, width).astype(BF)
        first(name, i).start()

    def middle(name, i):
        first(name, i).wait_recv()
        out_refs[name][:, columns(name, i)] = g_bufs[name][i, 0].astype(F32) + one_bufs[name][i, 0].astype(F32)
        g_bufs[name][i, 1] = (g_bufs[name][i, 1].astype(F32) + one_bufs[name][i, 1].astype(F32)).astype(BF)
        second(name, i).start()

    def finish(name, i):
        second(name, i).wait_recv()
        out_refs[name][:, columns(name, i)] += two_bufs[name][i].astype(F32)
        first(name, i).wait_send()
        second(name, i).wait_send()

    def loop(name, *steps):
        def body(i, carry):
            for step, which in steps:
                step(which, i)
            return carry

        lax.fori_loop(0, tiles[name][0], body, 0)

    ready("fc2")
    loop("fc2", (compute, "fc2"))
    ready("fc1")
    loop("fc1", (compute, "fc1"), (middle, "fc2"))
    ready("out")
    loop("out", (compute, "out"))
    loop("fc1", (middle, "fc1"), (finish, "fc2"))
    ready("qkv")
    loop("qkv", (compute, "qkv"))
    loop("out", (middle, "out"))
    loop("fc1", (finish, "fc1"))
    loop("qkv", (middle, "qkv"))
    loop("out", (finish, "out"))
    for copy in smalls:
        copy.wait()
    total = small_ref[me]
    for d in range(1, count):
        total = total + small_got[d]
    small_out[...] = total
    loop("qkv", (finish, "qkv"))


def final(small, xs, early, late, cid):
    count = small.shape[0]
    tokens = xs["qkv"][0].shape[-1]
    widths = {"fc2": FFP, "fc1": FFP, "out": D, "qkv": 3 * D}
    tiles = {name: (w // (256 if name[0] == "f" else 384), 256 if name[0] == "f" else 384) for name, w in widths.items()}
    anywhere, vmem = pl.BlockSpec(memory_space=pl.ANY), pl.BlockSpec(memory_space=pltpu.VMEM)
    args = [small] + [x for name in TENSORS for x in xs[name]]
    n_vmem = len(args)
    args += [e[3] for e in early] + [source for _, _, item in late for source in item.sources]
    dma = pltpu.SemaphoreType.DMA
    scratch = []
    for name in TENSORS:
        shape = (8, widths[name], tokens) if name == "qkv" else (8, tokens, widths[name])
        scratch.append(pltpu.VMEM(shape, BF))
    scratch.append(pltpu.VMEM((4 * HEAD_DIM, 8 * tokens), BF))
    for lead in ((4,), (2,), ()):
        for name in TENSORS:
            scratch.append(pltpu.VMEM((tiles[name][0],) + lead + (HEAD_DIM, tiles[name][1]), BF))
    scratch.append(pltpu.VMEM(small.shape, F32))
    scratch += [dma((len(early),)), dma((count,)), dma((count,))]
    for name in TENSORS:
        scratch += [dma((tiles[name][0],))] * 4
    scratch += [dma, dma((4,)), dma((4,))] * len(late)
    out = pl.pallas_call(
        functools.partial(final_kernel, tiles, [e[:3] for e in early], late),
        out_shape=[jax.ShapeDtypeStruct(small.shape[1:], F32)]
        + [jax.ShapeDtypeStruct((HEAD_DIM, widths[name]), F32) for name in TENSORS],
        in_specs=[vmem] * n_vmem + [anywhere] * (len(args) - n_vmem),
        out_specs=[vmem] * 5,
        scratch_shapes=scratch,
        compiler_params=pltpu.CompilerParams(
            collective_id=cid, has_side_effects=True, vmem_limit_bytes=60 << 20
        ),
    )(*args)
    return out[0], dict(zip(TENSORS, out[1:]))


def on_device(
    tokens,
    cotangent,
    image_of_block,
    ln1_gain,
    ln1_bias,
    qkv_weight,
    qv_bias,
    out_weight,
    out_bias,
    ln2_gain,
    ln2_bias,
    fc1_weight,
    fc1_bias,
    fc2_weight,
    fc2_bias,
):
    sec, me = place()
    own_qkv = qkv_weight[0].reshape(HEAD_DIM, 3, HEADS, HEAD_DIM).transpose(0, 2, 1, 3).reshape(HEAD_DIM, 3 * D)
    small = jnp.stack(
        [ln1_gain[0], ln1_bias[0], qv_bias[0, 0], qv_bias[0, 1], out_bias[0], ln2_gain[0], ln2_bias[0], fc2_bias[0]]
    )
    small = jnp.pad(small, ((0, 8), (0, BLOCK - HEAD_DIM)))
    w_qkv, w_out, small_all = gather([own_qkv, out_weight[0], small], 1)
    ff_shards = [pad_ff(fc1_weight[0]), pad_ff(fc2_weight[0].T)]
    w_qkv = w_qkv.reshape(D, 3 * D)
    w_out = w_out.reshape(D, D)
    vectors = small_all[:, :8, :HEAD_DIM].astype(F32)
    vec = jnp.stack([vectors[:, i].reshape(D) for i in (0, 1, 4, 5, 6, 7)])
    b_qkv = jnp.stack([vectors[:, 2], jnp.zeros_like(vectors[:, 2]), vectors[:, 3]], axis=1).reshape(1, 3 * D)
    b_fc1 = pad_ff(fc1_bias[0]).astype(F32).reshape(1, FFP)
    near = window(image_of_block)

    def choose(at_zero, at_one):
        return jnp.where(sec == 0, at_zero, at_one)

    saved, sent, back, done, input_grads = [], {}, [], [], []
    incoming = [tokens[0]]

    def token_inputs(tick):
        return tokens[min(tick, 1)], incoming[tick]

    def feed(tick, qkv, lse, att, n1, cid):
        fed = feed_forward(*token_inputs(tick), att, vec, b_fc1, w_out, w_fc1, w_fc2t, cid)
        saved.append(
            dict(qkv=qkv, lse=lse, n1=n1, residual=fed[0], pre=fed[1], hidden=fed[2], n2=fed[3], att=fed[4], low=fed[5])
        )
        return fed

    def kept(tick, *names):
        return [saved[at][name] for name in names for at in ((1, 1), (0, 2), (1, 1))[tick]]

    def feed_back(tick, incoming_grad):
        residual_grad, att_grad, fc, pre, branch, four, fsum = feed_backward(
            cotangent[min(tick, 1)], incoming_grad, vec, kept(tick, "pre", "residual"), w_out, w_fc1, w_fc2t
        )
        back.append(dict(fc=fc, pre=pre, branch=branch))
        return residual_grad, att_grad, [*four, fsum]

    def qkv_back(tick, residual_grad, dq, dkv, sums, cid):
        inputs = (tokens[max(tick - 1, 0)], incoming[min(tick + 1, 2)])
        input_grad, dqkv, two, qsum, *rest = qkv_backward(*inputs, vec, residual_grad, dq, dkv, w_qkv, cid)
        back[tick]["dqkv"] = dqkv
        input_grads.append(input_grad)
        qsum = qsum[0].reshape(HEADS, 3, HEAD_DIM)
        done.append([two[0], two[1], qsum[:, 0].reshape(D), qsum[:, 2].reshape(D), *sums])
        return rest[0] if rest else input_grad.astype(BF)

    qkv, n1 = qkv_forward(*token_inputs(0), vec, b_qkv, w_qkv)
    three, _, _, whole = attention(near, 2, ahead=(0, qkv), shards=ff_shards)
    w_fc1, w_fc2t = [w.reshape(D, FFP) for w in whole]
    incoming.append(feed(0, *three, n1, 8)[6])

    qkv, n1 = qkv_forward(*token_inputs(1), vec, b_qkv, w_qkv)
    three, _, _, _ = attention(near, 3, ahead=(1, qkv))
    incoming.append(lax.ppermute(feed(1, *three, n1, None)[5], "section", [(0, 1)]))

    residual_grad, att_grad, sums = feed_back(0, tokens[0])
    qkv, n1 = qkv_forward(*token_inputs(2), vec, b_qkv, w_qkv)
    items = [Rows(saved[0][name], saved[1][name]) for name in ("n1", "att", "n2")]
    items.append(Whole(saved[0]["hidden"], saved[1]["hidden"]))
    three, two, got, _ = attention(
        near, 4, ahead=(2, qkv), behind=(0, att_grad, kept(0, "qkv", "lse")), items=items
    )
    sent["n1_0"], sent["att_0"], sent["n2_0"], sent["h0"] = got
    low = qkv_back(0, residual_grad, *two, sums, None)
    incoming_grad = lax.ppermute(low, "section", [(1, 0)])
    feed(2, *three, n1, None)
    outputs = jnp.stack([choose(saved[m]["low"], saved[m + 1]["low"]) for m in range(2)])

    residual_grad, att_grad, sums = feed_back(1, incoming_grad)
    items = [Rows(saved[1][name], saved[2][name]) for name in ("n1", "att", "n2")]
    items.append(Whole(saved[1]["hidden"], saved[2]["hidden"], (0, SPLIT)))
    _, two, got, _ = attention(near, 5, behind=(1, att_grad, kept(1, "qkv", "lse")), items=items)
    sent["n1_1"], sent["att_1"], sent["n2_1"], sent["h1a"] = got
    incoming_grad = qkv_back(1, residual_grad, *two, sums, 9)

    residual_grad, att_grad, sums = feed_back(2, incoming_grad)
    items = [Rows(back[1]["fc"], back[0]["fc"]), Rows(back[2]["fc"], back[1]["fc"])]
    items.append(Whole(saved[1]["hidden"], saved[2]["hidden"], (SPLIT, FFP)))
    _, two, got, _ = attention(near, 6, behind=(2, att_grad, kept(2, "qkv", "lse")), items=items)
    sent["fc_0"], sent["fc_1"], sent["h1b"] = got
    qkv_back(2, residual_grad, *two, sums, None)
    input_grads = jnp.stack([choose(input_grads[m + 1], input_grads[m]) for m in range(2)])

    sums = [choose(done[1][i] + done[2][i], done[0][i] + done[1][i]) for i in range(9)]
    by_owner = jnp.stack(sums[:8]).reshape(8, HEADS, HEAD_DIM).transpose(1, 0, 2)
    by_owner = jnp.pad(by_owner, ((0, 0), (0, 0), (0, BLOCK - HEAD_DIM)))
    lines = FFP // BLOCK
    to_all = jnp.broadcast_to(sums[8].reshape(1, lines, BLOCK), (HEADS, lines, BLOCK))
    to_all = jnp.pad(to_all, ((0, 0), (0, 40 - lines), (0, 0)))
    xs = {
        "fc2": [sent["fc_0"], sent["fc_1"]],
        "fc1": [sent["n2_0"], sent["n2_1"]],
        "out": [sent["att_0"], sent["att_1"]],
        "qkv": [sent["n1_0"], sent["n1_1"]],
    }
    early = [
        ("fc2", 0, None, sent["h0"]),
        ("fc2", 1, (0, SPLIT), sent["h1a"]),
        ("fc2", 1, (SPLIT, FFP), sent["h1b"]),
    ]
    late = [
        ("fc1", 0, Whole(back[1]["pre"], back[0]["pre"])),
        ("fc1", 1, Whole(back[2]["pre"], back[1]["pre"])),
        ("out", 0, Whole(back[1]["branch"], back[0]["branch"])),
        ("out", 1, Whole(back[2]["branch"], back[1]["branch"])),
        ("qkv", 0, Whole(back[1]["dqkv"], back[0]["dqkv"])),
        ("qkv", 1, Whole(back[2]["dqkv"], back[1]["dqkv"])),
    ]
    packed, grads = final(jnp.concatenate([by_owner, to_all], axis=1), xs, early, late, 10)
    g_small = packed[:8, :HEAD_DIM]
    g_fc1_bias = packed[8 : 8 + lines].reshape(FFP)[:FF]
    g_qkv = grads["qkv"].reshape(HEAD_DIM, HEADS, 3, HEAD_DIM).transpose(0, 2, 1, 3).reshape(HEAD_DIM, 3 * D)
    return (
        outputs[None],
        input_grads[None],
        g_small[0][None],
        g_small[1][None],
        g_qkv[None],
        g_small[2:4][None],
        grads["out"][None],
        g_small[4][None],
        g_small[5][None],
        g_small[6][None],
        grads["fc1"][:, :FF][None],
        g_fc1_bias[None],
        grads["fc2"].T[:FF][None],
        g_small[7][None],
    )


BLK_DEV = 1
REACH = 5


def shifted(value, axis, steps):
    count = lax.axis_size(axis)
    initial, last = (max(0, -steps), min(count, count - steps))
    return lax.ppermute(value, axis, [(source, source + steps) for source in range(initial, last)])


def layer_norm(values_in, scale_gain, shift_bias):
    row_mean = jnp.mean(values_in, axis=-1, keepdims=True)
    centred = values_in - row_mean
    row_var = jnp.mean(centred * centred, axis=-1, keepdims=True)
    return centred * lax.rsqrt(row_var + EPSILON) * scale_gain + shift_bias


def gelu_tanh(pre_value):
    return jax.nn.gelu(pre_value, approximate=True)


def heads_of(values_in):
    return values_in.reshape(values_in.shape[0], HEADS, HEAD_DIM)


def image_mask(image_of_block, batch_slot, wide_rank):
    padding = REACH * BLK_DEV
    padded = jnp.pad(image_of_block, ((0, 0), (padding, padding)), constant_values=-1)
    image_row = lax.dynamic_index_in_dim(padded, batch_slot, 0, keepdims=False)
    key_blocks = lax.dynamic_slice_in_dim(image_row, wide_rank * BLK_DEV, (2 * REACH + 1) * BLK_DEV)
    query_blocks = lax.dynamic_slice_in_dim(image_row, wide_rank * BLK_DEV + padding, BLK_DEV)
    return jnp.repeat(query_blocks, BLOCK)[:, None] == jnp.repeat(key_blocks, BLOCK)[None, :]


def keep_slot(buffer_all, new_value, batch_slot, is_live):
    previous = lax.dynamic_index_in_dim(buffer_all, batch_slot, 0, keepdims=False)
    chosen = jnp.where(is_live, new_value, previous)
    return lax.dynamic_update_index_in_dim(buffer_all, chosen, batch_slot, 0)


def near_keys(key_own, value_own, backward_pass):
    key_parts = []
    value_parts = []
    for offset in range(-REACH, REACH + 1):
        if offset == 0:
            received = (key_own, value_own)
        elif backward_pass:
            received = shifted((key_own, value_own), "wide", -offset)
        else:
            received = shifted((key_own, value_own), "wide", -offset)
        key_parts.append(received[0])
        value_parts.append(received[1])
    return (jnp.concatenate(key_parts, axis=0), jnp.concatenate(value_parts, axis=0))


def return_key_grads(key_terms, value_terms):
    row_count = key_terms.shape[0] // (2 * REACH + 1)
    key_total = key_terms[REACH * row_count : (REACH + 1) * row_count]
    value_total = value_terms[REACH * row_count : (REACH + 1) * row_count]
    for position, offset in enumerate(range(-REACH, REACH + 1)):
        if offset != 0:
            piece_pair = (
                key_terms[position * row_count : (position + 1) * row_count],
                value_terms[position * row_count : (position + 1) * row_count],
            )
            received = shifted((piece_pair[0], piece_pair[1]), "wide", offset)
            key_total = key_total + received[0]
            value_total = value_total + received[1]
    return (key_total, value_total)


def project_qkv(layer_in, weights):
    layer_float = layer_in.astype(jnp.float32)
    normed_one = layer_norm(
        layer_float, weights[0].astype(jnp.float32), weights[1].astype(jnp.float32)
    ).astype(jnp.bfloat16)
    mixed = jnp.dot(normed_one, weights[2], preferred_element_type=jnp.float32)
    queries = (mixed[:, :D] + weights[3][0].astype(jnp.float32)).astype(jnp.bfloat16)
    key_own = mixed[:, D : 2 * D].astype(jnp.bfloat16)
    value_own = (mixed[:, 2 * D :] + weights[3][1].astype(jnp.float32)).astype(jnp.bfloat16)
    return (layer_float, normed_one, queries, key_own, value_own)


def attention_probs(queries, keys_near, same_image):
    score_scale = 1.0 / math.sqrt(HEAD_DIM)
    scores = (
        jnp.einsum(
            "qhd,khd->hqk",
            heads_of(queries),
            heads_of(keys_near),
            preferred_element_type=jnp.float32,
        )
        * score_scale
    )
    scores = jnp.where(same_image[None], scores, MASKED_SCORE)
    row_max = jnp.max(scores, axis=-1, keepdims=True)
    exponent = jnp.exp(scores - row_max)
    return exponent / jnp.sum(exponent, axis=-1, keepdims=True)


def finish_layer(layer_float, queries, keys_near, values_near, same_image, weights, hidden_bias):
    probs = attention_probs(queries, keys_near, same_image)
    probs_low = probs.astype(jnp.bfloat16)
    attended = jnp.einsum(
        "hqk,khd->qhd", probs_low, heads_of(values_near), preferred_element_type=jnp.float32
    )
    attended = attended.reshape(queries.shape[0], D).astype(jnp.bfloat16)
    residual = (
        layer_float
        + jnp.dot(attended, weights[4], preferred_element_type=jnp.float32)
        + weights[5].astype(jnp.float32)
    )
    normed_two = layer_norm(
        residual, weights[6].astype(jnp.float32), weights[7].astype(jnp.float32)
    ).astype(jnp.bfloat16)
    hidden_pre = jnp.dot(
        normed_two, weights[8], preferred_element_type=jnp.float32
    ) + hidden_bias.astype(jnp.float32)
    hidden = gelu_tanh(hidden_pre).astype(jnp.bfloat16)
    output = (
        residual
        + jnp.dot(hidden, weights[9], preferred_element_type=jnp.float32)
        + weights[10].astype(jnp.float32)
    )
    return (probs, probs_low, attended, residual, normed_two, hidden_pre, hidden, output)


def layer_backward(
    layer_float,
    normed_one,
    queries,
    keys_near,
    values_near,
    same_image,
    weights,
    hidden_bias,
    grad_out,
):
    score_scale = 1.0 / math.sqrt(HEAD_DIM)
    probs, probs_low, attended, residual, normed_two, hidden_pre, hidden, output = finish_layer(
        layer_float, queries, keys_near, values_near, same_image, weights, hidden_bias
    )
    feed_grad = grad_out.astype(jnp.bfloat16)
    grad_fc2_weight = jnp.einsum("tf,td->fd", hidden, feed_grad, preferred_element_type=jnp.float32)
    grad_fc2_bias = jnp.sum(feed_grad.astype(jnp.float32), axis=0)
    hidden_grad = jnp.einsum("td,fd->tf", feed_grad, weights[9], preferred_element_type=jnp.float32)
    primal_gelu, gelu_pull = jax.vjp(gelu_tanh, hidden_pre)
    pre_grad = gelu_pull(hidden_grad)[0].astype(jnp.bfloat16)
    grad_fc1_bias = jnp.sum(pre_grad.astype(jnp.float32), axis=0)
    grad_fc1_weight = jnp.einsum(
        "td,tf->df", normed_two, pre_grad, preferred_element_type=jnp.float32
    )
    normed_two_grad = jnp.einsum(
        "tf,df->td", pre_grad, weights[8], preferred_element_type=jnp.float32
    )
    primal_two, norm_two_pull = jax.vjp(
        layer_norm, residual, weights[6].astype(jnp.float32), weights[7].astype(jnp.float32)
    )
    residual_part, grad_ln2_gain, grad_ln2_bias = norm_two_pull(normed_two_grad)
    residual_grad = grad_out + residual_part
    branch_grad = residual_grad.astype(jnp.bfloat16)
    grad_out_bias = jnp.sum(branch_grad.astype(jnp.float32), axis=0)
    grad_out_weight = jnp.einsum(
        "tc,td->cd", attended, branch_grad, preferred_element_type=jnp.float32
    )
    attended_grad = jnp.einsum(
        "td,cd->tc", branch_grad, weights[4], preferred_element_type=jnp.float32
    ).astype(jnp.bfloat16)
    attended_heads = heads_of(attended_grad)
    probs_grad = jnp.einsum(
        "qhd,khd->hqk", attended_heads, heads_of(values_near), preferred_element_type=jnp.float32
    )
    value_terms = jnp.einsum(
        "hqk,qhd->khd", probs_low, attended_heads, preferred_element_type=jnp.float32
    )
    score_grad = (
        probs * (probs_grad - jnp.sum(probs * probs_grad, axis=-1, keepdims=True))
    ).astype(jnp.bfloat16)
    query_grad = (
        jnp.einsum(
            "hqk,khd->qhd", score_grad, heads_of(keys_near), preferred_element_type=jnp.float32
        )
        * score_scale
    )
    query_grad = query_grad.reshape(queries.shape[0], D).astype(jnp.bfloat16)
    key_terms = (
        jnp.einsum(
            "hqk,qhd->khd", score_grad, heads_of(queries), preferred_element_type=jnp.float32
        )
        * score_scale
    )
    key_total, value_total = return_key_grads(key_terms.reshape(-1, D), value_terms.reshape(-1, D))
    key_grad = key_total.astype(jnp.bfloat16)
    value_grad = value_total.astype(jnp.bfloat16)
    grad_qv_bias = jnp.stack(
        [
            jnp.sum(query_grad.astype(jnp.float32), axis=0),
            jnp.sum(value_grad.astype(jnp.float32), axis=0),
        ]
    )
    mixed_grad = jnp.concatenate([query_grad, key_grad, value_grad], axis=1)
    grad_qkv_weight = jnp.einsum(
        "tc,tk->ck", normed_one, mixed_grad, preferred_element_type=jnp.float32
    )
    normed_one_grad = jnp.einsum(
        "tk,ck->tc", mixed_grad, weights[2], preferred_element_type=jnp.float32
    )
    primal_one, norm_one_pull = jax.vjp(
        layer_norm, layer_float, weights[0].astype(jnp.float32), weights[1].astype(jnp.float32)
    )
    input_part, grad_ln1_gain, grad_ln1_bias = norm_one_pull(normed_one_grad)
    input_grad = residual_grad + input_part
    grad_terms = (
        grad_ln1_gain,
        grad_ln1_bias,
        grad_qkv_weight,
        grad_qv_bias,
        grad_out_weight,
        grad_out_bias,
        grad_ln2_gain,
        grad_ln2_bias,
        grad_fc1_weight,
        grad_fc2_weight,
        grad_fc2_bias,
    )
    return (input_grad, grad_terms, grad_fc1_bias)


def on_device_near(
    tokens,
    cotangent,
    image_of_block,
    ln1_gain,
    ln1_bias,
    qkv_weight,
    qv_bias,
    out_weight,
    out_bias,
    ln2_gain,
    ln2_bias,
    fc1_weight,
    fc1_bias,
    fc2_weight,
    fc2_bias,
):
    section_rank = lax.axis_index("section")
    wide_rank = lax.axis_index("wide")
    micro_count = tokens.shape[0]
    weights = (
        lax.all_gather(ln1_gain[0], "wide", axis=0, tiled=True),
        lax.all_gather(ln1_bias[0], "wide", axis=0, tiled=True),
        lax.all_gather(qkv_weight[0], "wide", axis=0, tiled=True),
        lax.all_gather(qv_bias[0], "wide", axis=1, tiled=True),
        lax.all_gather(out_weight[0], "wide", axis=0, tiled=True),
        lax.all_gather(out_bias[0], "wide", axis=0, tiled=True),
        lax.all_gather(ln2_gain[0], "wide", axis=0, tiled=True),
        lax.all_gather(ln2_bias[0], "wide", axis=0, tiled=True),
        lax.all_gather(fc1_weight[0], "wide", axis=0, tiled=True),
        lax.all_gather(fc2_weight[0], "wide", axis=1, tiled=True),
        lax.all_gather(fc2_bias[0], "wide", axis=0, tiled=True),
    )
    hidden_bias = fc1_bias[0]
    inputs_kept = jnp.zeros_like(tokens)
    outputs_kept = jnp.zeros_like(tokens)
    incoming = jnp.zeros_like(tokens[0])
    for tick_number in range(micro_count + 1):
        batch_index = tick_number - section_rank
        is_live = (batch_index >= 0) & (batch_index < micro_count)
        batch_slot = jnp.clip(batch_index, 0, micro_count - 1)
        own_tokens = tokens[min(tick_number, micro_count - 1)]
        layer_in = jnp.where(section_rank == 0, own_tokens, incoming)
        same_image = image_mask(image_of_block, batch_slot, wide_rank)
        layer_float, normed_one, queries, key_own, value_own = project_qkv(layer_in, weights)
        keys_near, values_near = near_keys(key_own, value_own, False)
        output = finish_layer(
            layer_float, queries, keys_near, values_near, same_image, weights, hidden_bias
        )[-1]
        output_low = output.astype(jnp.bfloat16)
        inputs_kept = keep_slot(inputs_kept, layer_in, batch_slot, is_live)
        outputs_kept = keep_slot(outputs_kept, output_low, batch_slot, is_live)
        if tick_number < micro_count:
            incoming = shifted(output_low, "section", 1)
    weights_back = (
        lax.all_gather(ln1_gain[0], "wide", axis=0, tiled=True),
        lax.all_gather(ln1_bias[0], "wide", axis=0, tiled=True),
        lax.all_gather(qkv_weight[0], "wide", axis=0, tiled=True),
        lax.all_gather(qv_bias[0], "wide", axis=1, tiled=True),
        lax.all_gather(out_weight[0], "wide", axis=0, tiled=True),
        lax.all_gather(out_bias[0], "wide", axis=0, tiled=True),
        lax.all_gather(ln2_gain[0], "wide", axis=0, tiled=True),
        lax.all_gather(ln2_bias[0], "wide", axis=0, tiled=True),
        lax.all_gather(fc1_weight[0], "wide", axis=0, tiled=True),
        lax.all_gather(fc2_weight[0], "wide", axis=1, tiled=True),
        lax.all_gather(fc2_bias[0], "wide", axis=0, tiled=True),
    )
    grad_totals = tuple((jnp.zeros(array.shape, jnp.float32) for array in weights_back))
    hidden_bias_total = jnp.zeros(hidden_bias.shape, jnp.float32)
    input_grads = jnp.zeros(tokens.shape, jnp.float32)
    incoming_grad = jnp.zeros(tokens.shape[1:], jnp.bfloat16)
    for tick_number in range(micro_count + 1):
        batch_index = tick_number - 1 + section_rank
        is_live = (batch_index >= 0) & (batch_index < micro_count)
        batch_slot = jnp.clip(batch_index, 0, micro_count - 1)
        from_cotangent = cotangent[min(tick_number, micro_count - 1)].astype(jnp.float32)
        grad_out = jnp.where(
            section_rank == 1, from_cotangent, incoming_grad.astype(jnp.float32)
        ) * is_live.astype(jnp.float32)
        layer_in = lax.dynamic_index_in_dim(inputs_kept, batch_slot, 0, keepdims=False)
        same_image = image_mask(image_of_block, batch_slot, wide_rank)
        layer_float, normed_one, queries, key_own, value_own = project_qkv(layer_in, weights_back)
        keys_near, values_near = near_keys(key_own, value_own, True)
        input_grad, grad_terms, hidden_bias_term = layer_backward(
            layer_float,
            normed_one,
            queries,
            keys_near,
            values_near,
            same_image,
            weights_back,
            hidden_bias,
            grad_out,
        )
        grad_totals = tuple(
            (old_total + new_term for old_total, new_term in zip(grad_totals, grad_terms))
        )
        hidden_bias_total = hidden_bias_total + hidden_bias_term
        input_grads = keep_slot(input_grads, input_grad, batch_slot, is_live)
        if tick_number < micro_count:
            incoming_grad = shifted(input_grad.astype(jnp.bfloat16), "section", -1)
    (
        grad_ln1_gain,
        grad_ln1_bias,
        grad_qkv_weight,
        grad_qv_bias,
        grad_out_weight,
        grad_out_bias,
        grad_ln2_gain,
        grad_ln2_bias,
        grad_fc1_weight,
        grad_fc2_weight,
        grad_fc2_bias,
    ) = grad_totals
    row_sums = (
        lax.psum_scatter(grad_ln1_gain, "wide", scatter_dimension=0, tiled=True),
        lax.psum_scatter(grad_ln1_bias, "wide", scatter_dimension=0, tiled=True),
        lax.psum_scatter(grad_qkv_weight, "wide", scatter_dimension=0, tiled=True),
        lax.psum_scatter(grad_out_weight, "wide", scatter_dimension=0, tiled=True),
        lax.psum_scatter(grad_out_bias, "wide", scatter_dimension=0, tiled=True),
        lax.psum_scatter(grad_ln2_gain, "wide", scatter_dimension=0, tiled=True),
        lax.psum_scatter(grad_ln2_bias, "wide", scatter_dimension=0, tiled=True),
        lax.psum_scatter(grad_fc1_weight, "wide", scatter_dimension=0, tiled=True),
        lax.psum_scatter(grad_fc2_bias, "wide", scatter_dimension=0, tiled=True),
    )
    column_sums = (
        lax.psum_scatter(grad_qv_bias, "wide", scatter_dimension=1, tiled=True),
        lax.psum_scatter(grad_fc2_weight, "wide", scatter_dimension=1, tiled=True),
    )
    hidden_bias_sum = lax.psum(hidden_bias_total, "wide")
    return (
        outputs_kept[None],
        input_grads[None],
        row_sums[0][None],
        row_sums[1][None],
        row_sums[2][None],
        column_sums[0][None],
        row_sums[3][None],
        row_sums[4][None],
        row_sums[5][None],
        row_sums[6][None],
        row_sums[7][None],
        hidden_bias_sum[None],
        column_sums[1][None],
        row_sums[8][None],
    )


def specs():
    ins = (
        P(None, "wide", None),
        P(None, "wide", None),
        P(),
        P("section", "wide"),
        P("section", "wide"),
        P("section", "wide", None),
        P("section", None, "wide"),
        P("section", "wide", None),
        P("section", "wide"),
        P("section", "wide"),
        P("section", "wide"),
        P("section", "wide", None),
        P("section", None),
        P("section", None, "wide"),
        P("section", "wide"),
    )
    outs = (
        P("section", None, "wide", None),
        P("section", None, "wide", None),
        P("section", "wide"),
        P("section", "wide"),
        P("section", "wide", None),
        P("section", None, "wide"),
        P("section", "wide", None),
        P("section", "wide"),
        P("section", "wide"),
        P("section", "wide"),
        P("section", "wide", None),
        P("section", None),
        P("section", None, "wide"),
        P("section", "wide"),
    )
    return ins, outs


def solution(mesh):
    ins, outs = specs()
    body = on_device if mesh.shape["wide"] == HEADS else on_device_near
    return jax.shard_map(body, mesh=mesh, in_specs=ins, out_specs=outs, check_vma=False)
```

```python
import functools
import math

import jax
import jax.numpy as jnp
from jax import lax
from jax.experimental import pallas as pl
from jax.experimental.pallas import tpu as pltpu
from jax.sharding import PartitionSpec as P

D = 1152
HEADS = 16
HEAD_DIM = 72
FF = 4304
FFP = -(-FF // 256) * 256
SPLIT = 9 * 256
BLOCK = 128
IMG_BLOCKS = 6
EPSILON = 1e-06
MASKED_SCORE = -1e30
SCALE = 1.0 / math.sqrt(HEAD_DIM)
MESH = pl.DeviceIdType.MESH
BF = jnp.bfloat16
F32 = jnp.float32


def place():
    return lax.axis_index("section"), lax.axis_index("wide")


class Gather:
    def __init__(self, pieces, ins, outs, sems):
        self.pieces, self.ins, self.outs, self.count = pieces, ins, outs, len(pieces)
        self.local_sem = sems[0]
        self.up, self.down, self.yy, self.cc = [(sems[1 + 2 * i], sems[2 + 2 * i]) for i in range(4)]
        self.sec, self.me = place()
        self.z, self.low = self.me // 4, self.me % 4
        self.other_y = self.me - self.low + flip(self.low, 2)
        self.other_c = self.me - self.low + flip(self.low, 1)

    @staticmethod
    def semaphores(pieces, arrays):
        dma = pltpu.SemaphoreType.DMA
        return [dma((arrays,))] + [dma((pieces, 4))] * 6 + [dma((pieces, 8))] * 2

    def part(self, piece, origin=None):
        array, at, end = self.pieces[piece]
        return self.ins[array].at[:, at:end] if origin is None else self.outs[array].at[origin, :, at:end]

    def send(self, piece, origin, sems, slot, target, first=False):
        return pltpu.make_async_remote_copy(
            src_ref=self.part(piece) if first else self.part(piece, origin),
            dst_ref=self.part(piece, origin),
            send_sem=sems[0].at[piece, slot],
            recv_sem=sems[1].at[piece, slot],
            device_id=(self.sec, target),
            device_id_type=MESH,
        )

    def mine(self, array):
        return pltpu.make_async_copy(self.ins[array], self.outs[array].at[self.me], self.local_sem.at[array])

    def along(self, piece, origin, first, go_up, go_down):
        zo = origin // 4
        if go_up:

            @pl.when(self.z < 3)
            def _():
                self.send(piece, origin, self.up, zo, self.me + 4, first).start()

        if go_down:

            @pl.when(self.z > 0)
            def _():
                self.send(piece, origin, self.down, zo, self.me - 4, first).start()

        self.send(piece, origin, self.yy, zo, self.other_y, first).start()
        self.send(piece, origin, self.cc, zo, self.other_c, first).start()

    def step(self, piece, step):
        @pl.when(self.z - step >= 0)
        def _():
            origin = self.me - 4 * step
            self.send(piece, origin, self.up, self.z - step, self.me).wait_recv()
            self.along(piece, origin, False, True, False)

        @pl.when(self.z + step <= 3)
        def _():
            origin = self.me + 4 * step
            self.send(piece, origin, self.down, self.z + step, self.me).wait_recv()
            self.along(piece, origin, False, False, True)

    def slots(self, first, last):
        for k in range(first, last):
            if k == 0:
                for array in range(len(self.ins)):
                    self.mine(array).start()
            if k < self.count:
                self.along(k, self.me, True, True, True)
            for step in range(1, 4):
                if 0 <= k - step < self.count:
                    self.step(k - step, step)

    def across(self, pieces):
        far = self.other_y % 4
        for piece in pieces:
            for step in range(4):
                zo = (self.z + step) % 4
                origin = zo * 4 + far
                self.send(piece, origin, self.yy, zo, self.other_y).wait_recv()
                self.send(piece, origin, self.cc, 4 + zo, self.other_c).start()

    def arrived(self, pieces):
        for piece in pieces:
            for slot in range(8):
                self.send(piece, self.me, self.cc, slot, self.other_c).wait_recv()

    def finish(self):
        for zo in range(4):
            for piece in range(self.count):
                self.send(piece, self.me, self.yy, zo, self.other_y).wait_send()
                for slot in (zo, 4 + zo):
                    self.send(piece, self.me, self.cc, slot, self.other_c).wait_send()

                @pl.when((zo <= self.z) & (self.z < 3))
                def _():
                    self.send(piece, self.me, self.up, zo, self.me).wait_send()

                @pl.when((zo >= self.z) & (self.z > 0))
                def _():
                    self.send(piece, self.me, self.down, zo, self.me).wait_send()


def flip(low, k):
    return [low, low + 1 - 2 * (low % 2), (low + 2) % 4, 3 - low][k]


def greet_all(count, sec, me):
    barrier = pltpu.get_barrier_semaphore()
    for d in range(1, count):
        pl.semaphore_signal(barrier, inc=1, device_id=(sec, (me + d) % count), device_id_type=MESH)
    pl.semaphore_wait(barrier, count - 1)


class Whole:
    def __init__(self, zero, one, cols=None):
        self.sources, self.cols = (zero, one), cols

    def shape(self):
        rows, cols = self.sources[0].shape
        return (4, rows, cols if self.cols is None else self.cols[1] - self.cols[0])

    def source(self, ref, low, k):
        return ref if self.cols is None else ref.at[:, self.cols[0] : self.cols[1]]

    forwarded = True


class Rows:
    def __init__(self, zero, one):
        self.sources = (zero, one)

    def shape(self):
        return self.sources[0].shape

    def source(self, ref, low, k):
        return ref.at[flip(low, k)]

    forwarded = False


class PlaneCopies:
    def __init__(self, item, zero_ref, one_ref, slot, local_sem, send_sem, recv_sem):
        self.item, self.refs, self.slot = item, (zero_ref, one_ref), slot
        self.local_sem, self.send_sem, self.recv_sem = local_sem, send_sem, recv_sem
        self.sec, self.me = place()
        self.low = self.me % 4

    def remote(self, src, k, to):
        return pltpu.make_async_remote_copy(
            src_ref=src,
            dst_ref=self.slot(k),
            send_sem=self.send_sem.at[k],
            recv_sem=self.recv_sem.at[k],
            device_id=(self.sec, self.me - self.low + flip(self.low, to)),
            device_id_type=MESH,
        )

    def local(self, ref):
        return pltpu.make_async_copy(self.item.source(ref, self.low, 0), self.slot(0), self.local_sem)

    def start(self):
        def go(ref):
            self.local(ref).start()
            for k in (2, 1) if self.item.forwarded else (2, 3, 1):
                self.remote(self.item.source(ref, self.low, k), k, k).start()

        @pl.when(self.sec == 0)
        def _():
            go(self.refs[0])

        @pl.when(self.sec == 1)
        def _():
            go(self.refs[1])

    def forward(self):
        if self.item.forwarded:
            self.remote(self.slot(2), 2, 2).wait_recv()
            self.remote(self.slot(2), 3, 1).start()

    def finish(self):
        self.local(self.refs[0]).wait()
        for k in (1, 2, 3):
            self.remote(self.slot(k), k, k).wait_send()
            if k != 2 or not self.item.forwarded:
                self.remote(self.slot(k), k, k).wait_recv()


def dot(a, b):
    return jnp.dot(a, b, preferred_element_type=F32)


def window(image_of_block):
    micro, blocks = image_of_block.shape
    own, other = image_of_block[:, :, None], image_of_block[:, None, :]
    begin = jnp.sum((other < own).astype(jnp.int32), axis=2)
    end = jnp.sum((other <= own).astype(jnp.int32), axis=2)
    first = jnp.minimum(begin, blocks - IMG_BLOCKS)
    shape = (micro, blocks, IMG_BLOCKS, BLOCK)
    at = first[:, :, None, None] + lax.broadcasted_iota(jnp.int32, shape, 2)
    same = (at >= begin[:, :, None, None]) & (at < end[:, :, None, None])
    return first, jnp.where(same, 0.0, MASKED_SCORE).astype(F32)


def near_rows(ref, start):
    return jnp.concatenate([ref[start + j] for j in range(IMG_BLOCKS)], axis=0)


def near_columns(ref, start):
    return jnp.concatenate([ref[start + j] for j in range(IMG_BLOCKS)], axis=1)


def fetch(pairs, buffers, sems, sec):
    for which in range(2):

        @pl.when(sec == which)
        def _():
            for i, buffer in enumerate(buffers):
                pltpu.make_async_copy(pairs[2 * i + which], buffer, sems.at[i]).start()


def fetched(pairs, buffers, sems):
    for i, buffer in enumerate(buffers):
        pltpu.make_async_copy(pairs[2 * i], buffer, sems.at[i]).wait()


class ToAll:
    def __init__(self, block, dst, send, recv, sec, me, count):
        self.block, self.dst, self.send, self.recv = block, dst, send, recv
        self.sec, self.me, self.count = sec, me, count

    def copy(self, d):
        return pltpu.make_async_remote_copy(
            src_ref=self.block(d),
            dst_ref=self.dst.at[self.me],
            send_sem=self.send.at[d],
            recv_sem=self.recv.at[d],
            device_id=(self.sec, (self.me + d) % self.count),
            device_id_type=MESH,
        )

    def start(self):
        for d in sorted(range(1, self.count), key=lambda d: abs(d - self.count // 2)):
            self.copy(d).start()

    def start_one(self, d):
        @pl.when(d > 0)
        def _():
            self.copy(d).start()

    def wait(self):
        for d in range(1, self.count):
            self.copy(d).wait()


class Forward:
    def __init__(self, tick, near, x_ref, outs, scratch):
        self.first_ref, self.bias_ref = near
        self.x_ref = x_ref
        self.qkv_ref, self.lse_ref, self.att_ref = outs
        self.k_all, self.vt_all, self.o_buf, self.local_sem, *sems = scratch
        self.count = x_ref.shape[0]
        sec, self.me = place()
        self.slot = jnp.minimum(jnp.maximum(tick - sec, 0), 1)
        rest = (sec, self.me, self.count)
        self.arrive = ToAll(lambda d: x_ref.at[(self.me + d) % self.count], self.qkv_ref, *sems[:2], *rest)
        self.leave = ToAll(lambda d: self.o_buf.at[d], self.att_ref, *sems[2:], *rest)

    @staticmethod
    def scratch(blocks):
        dma = pltpu.SemaphoreType.DMA
        return [
            pltpu.VMEM((blocks, BLOCK, HEAD_DIM), BF),
            pltpu.VMEM((blocks, HEAD_DIM, BLOCK), BF),
            pltpu.VMEM((blocks, HEAD_DIM, BLOCK), BF),
            dma,
        ] + [dma((blocks,))] * 4

    @staticmethod
    def shapes(blocks):
        return [
            jax.ShapeDtypeStruct((blocks, 3 * HEAD_DIM, BLOCK), BF),
            jax.ShapeDtypeStruct((blocks, 1, BLOCK), F32),
            jax.ShapeDtypeStruct((blocks, HEAD_DIM, BLOCK), BF),
        ]

    def own(self):
        return pltpu.make_async_copy(self.x_ref.at[self.me], self.qkv_ref.at[self.me], self.local_sem)

    def start(self):
        self.arrive.start()
        self.own().start()

    def wait_in(self):
        self.own().wait()
        self.arrive.wait()

    def compute(self):
        def arrange(j, carry):
            part = self.qkv_ref[j].astype(F32)
            self.k_all[j] = part[HEAD_DIM : 2 * HEAD_DIM].T.astype(BF)
            self.vt_all[j] = part[2 * HEAD_DIM :].astype(BF)
            return carry

        lax.fori_loop(0, self.count, arrange, 0)

        def one_block(d, carry):
            i = (self.me + d) % self.count
            start = self.first_ref[self.slot, i]
            qt = self.qkv_ref[i].astype(F32)[:HEAD_DIM].astype(BF)
            s = dot(near_rows(self.k_all, start), qt) * SCALE
            bias = self.bias_ref[self.slot, i]
            parts = [s[j * BLOCK : (j + 1) * BLOCK] + bias[j : j + 1] for j in range(IMG_BLOCKS)]
            top = parts[0]
            for part in parts[1:]:
                top = jnp.maximum(top, part)
            top = jnp.max(top, axis=0, keepdims=True)
            exps = [jnp.exp(part - top) for part in parts]
            total = exps[0]
            for part in exps[1:]:
                total = total + part
            total = jnp.sum(total, axis=0, keepdims=True)
            e = jnp.concatenate([part.astype(BF) for part in exps], axis=0)
            o = dot(near_columns(self.vt_all, start), e)
            self.o_buf[d] = (o / total).astype(BF)
            self.lse_ref[i] = top + jnp.log(total)
            self.leave.start_one(d)
            return carry

        lax.fori_loop(0, self.count, one_block, 0)
        self.att_ref[self.me] = self.o_buf[0]

    def wait_out(self):
        self.leave.wait()


class Backward:
    def __init__(self, tick, near, kept, x_ref, outs, scratch):
        self.first_ref, self.bias_ref = near
        self.kept, self.x_ref = kept, x_ref
        self.dq_ref, self.dkv_ref = outs
        self.qkv_ref, self.lse_ref, self.do_ref = scratch[:3]
        self.k_all, self.kt_all, self.v_all, self.q_all, self.do_all, self.p_all, self.s_all = scratch[3:10]
        self.dq_buf, self.dkv_buf, self.kept_sem, self.local_sem = scratch[10:14]
        sems = scratch[14:]
        self.count = x_ref.shape[0]
        self.sec, self.me = place()
        self.slot = jnp.minimum(jnp.maximum(tick - 1 + self.sec, 0), 1)
        rest = (self.sec, self.me, self.count)
        self.arrive = ToAll(lambda d: x_ref.at[(self.me + d) % self.count], self.do_ref, *sems[:2], *rest)
        self.leave_q = ToAll(lambda d: self.dq_buf.at[d], self.dq_ref, *sems[2:4], *rest)
        self.leave_kv = ToAll(lambda d: self.dkv_buf.at[d], self.dkv_ref, *sems[4:], *rest)

    @staticmethod
    def scratch(blocks):
        dma = pltpu.SemaphoreType.DMA
        return [
            pltpu.VMEM((blocks, 3 * HEAD_DIM, BLOCK), BF),
            pltpu.VMEM((blocks, 1, BLOCK), F32),
            pltpu.VMEM((blocks, HEAD_DIM, BLOCK), BF),
            pltpu.VMEM((blocks, BLOCK, HEAD_DIM), BF),
            pltpu.VMEM((blocks, HEAD_DIM, BLOCK), BF),
            pltpu.VMEM((blocks, BLOCK, HEAD_DIM), BF),
            pltpu.VMEM((blocks, BLOCK, HEAD_DIM), BF),
            pltpu.VMEM((blocks, BLOCK, HEAD_DIM), BF),
            pltpu.VMEM((blocks, IMG_BLOCKS, BLOCK, BLOCK), BF),
            pltpu.VMEM((blocks, IMG_BLOCKS, BLOCK, BLOCK), BF),
            pltpu.VMEM((blocks, HEAD_DIM, BLOCK), BF),
            pltpu.VMEM((blocks, 2 * HEAD_DIM, BLOCK), BF),
            dma((2,)),
            dma,
        ] + [dma((blocks,))] * 6

    def own(self):
        return pltpu.make_async_copy(self.x_ref.at[self.me], self.do_ref.at[self.me], self.local_sem)

    def start(self):
        self.arrive.start()
        self.own().start()
        fetch(self.kept, (self.qkv_ref, self.lse_ref), self.kept_sem, self.sec)

    def arrange(self):
        fetched(self.kept, (self.qkv_ref, self.lse_ref), self.kept_sem)

        def one(j, carry):
            part = self.qkv_ref[j].astype(F32)
            self.q_all[j] = part[:HEAD_DIM].T.astype(BF)
            self.k_all[j] = part[HEAD_DIM : 2 * HEAD_DIM].T.astype(BF)
            self.v_all[j] = part[2 * HEAD_DIM :].T.astype(BF)
            self.kt_all[j] = part[HEAD_DIM : 2 * HEAD_DIM].astype(BF)
            return carry

        lax.fori_loop(0, self.count, one, 0)

    def wait_in(self):
        self.own().wait()
        self.arrive.wait()

    def by_query(self):
        def turn(j, carry):
            self.do_all[j] = self.do_ref[j].astype(F32).T.astype(BF)
            return carry

        lax.fori_loop(0, self.count, turn, 0)

        def one(d, carry):
            i = (self.me + d) % self.count
            start = self.first_ref[self.slot, i]
            qt = self.qkv_ref[i].astype(F32)[:HEAD_DIM].astype(BF)
            s = dot(near_rows(self.k_all, start), qt) * SCALE
            shift = self.bias_ref[self.slot, i] - self.lse_ref[i]
            probs = [jnp.exp(s[j * BLOCK : (j + 1) * BLOCK] + shift[j : j + 1]) for j in range(IMG_BLOCKS)]
            dp = dot(near_rows(self.v_all, start), self.do_ref[i])
            total = probs[0] * dp[:BLOCK]
            for j in range(1, IMG_BLOCKS):
                total = total + probs[j] * dp[j * BLOCK : (j + 1) * BLOCK]
            total = jnp.sum(total, axis=0, keepdims=True)
            ds = jnp.concatenate(
                [(probs[j] * (dp[j * BLOCK : (j + 1) * BLOCK] - total)).astype(BF) for j in range(IMG_BLOCKS)], axis=0
            )
            for j in range(IMG_BLOCKS):
                self.p_all[i, j] = probs[j].astype(BF)
                self.s_all[i, j] = ds[j * BLOCK : (j + 1) * BLOCK]
            self.dq_buf[d] = (dot(near_columns(self.kt_all, start), ds) * SCALE).astype(BF)
            self.leave_q.start_one(d)
            return carry

        lax.fori_loop(0, self.count, one, 0)
        self.dq_ref[self.me] = self.dq_buf[0]

    def by_key(self):
        def one(d, carry):
            j = (self.me + d) % self.count
            start = self.first_ref[self.slot, j]
            place_in = jnp.clip(j - start, 0, IMG_BLOCKS - 1)
            same = (self.bias_ref[self.slot, j] == 0.0).astype(F32).astype(BF)
            p, ds = [], []
            for m in range(IMG_BLOCKS):
                p.append(self.p_all[start + m, place_in] * same[m : m + 1])
                ds.append(self.s_all[start + m, place_in] * same[m : m + 1])
            dv = dot(jnp.concatenate(p, axis=1), near_rows(self.do_all, start))
            dk = dot(jnp.concatenate(ds, axis=1), near_rows(self.q_all, start)) * SCALE
            self.dkv_buf[d] = jnp.concatenate([dk.T, dv.T], axis=0).astype(BF)
            self.leave_kv.start_one(d)
            return carry

        lax.fori_loop(0, self.count, one, 0)
        self.dkv_ref[self.me] = self.dkv_buf[0]

    def wait_out(self):
        self.leave_q.wait()
        self.leave_kv.wait()


def attention_kernel(ahead, behind, items, *refs):
    refs = list(refs)

    def take(n):
        part = refs[:n]
        del refs[:n]
        return part

    n = len(items)
    near = take(2)
    x_ref = take(1) if ahead is not None else None
    kept, g_ref = (take(4), take(1)) if behind is not None else (None, None)
    sources = take(2 * n)
    ahead_out = take(3) if ahead is not None else None
    behind_out = take(2) if behind is not None else None
    outs = take(n)
    f = b = None
    blocks = (x_ref or g_ref)[0].shape[0]
    sec, me = place()
    if ahead is not None:
        f = Forward(ahead, near, x_ref[0], ahead_out, take(len(Forward.scratch(blocks))))
    if behind is not None:
        b = Backward(behind, near, kept, g_ref[0], behind_out, take(len(Backward.scratch(blocks))))
    copies = []
    for i, item in enumerate(items):
        into = lambda k, i=i: outs[i].at[k]
        copies.append(PlaneCopies(item, sources[2 * i], sources[2 * i + 1], into, *take(3)))
    greet_all(blocks, sec, me)

    if b:
        b.start()
        b.arrange()
        b.wait_in()
    if f:
        f.start()
    if f and not b:
        f.wait_in()
    for copy in copies:
        copy.start()
    if b:
        b.by_query()
        b.by_key()
    if f and b:
        f.wait_in()
    if f:
        f.compute()
    for copy in copies:
        copy.forward()
    if f:
        f.wait_out()
    if b:
        b.wait_out()
    for copy in copies:
        copy.finish()


def attention(near, cid, ahead=None, behind=None, items=()):
    first_in = ahead[1] if ahead else behind[1]
    blocks = first_in.shape[0]
    n = len(items)
    sources = [source for item in items for source in item.sources]
    anywhere, vmem, smem = [pl.BlockSpec(memory_space=m) for m in (pl.ANY, pltpu.VMEM, pltpu.SMEM)]
    dma = pltpu.SemaphoreType.DMA
    args, scratch, shapes = [], [], []
    if ahead:
        args.append(ahead[1])
        scratch += Forward.scratch(blocks)
        shapes += Forward.shapes(blocks)
    if behind:
        args += [*behind[2], behind[1]]
        scratch += Backward.scratch(blocks)
        shapes += [
            jax.ShapeDtypeStruct((blocks, HEAD_DIM, BLOCK), BF),
            jax.ShapeDtypeStruct((blocks, 2 * HEAD_DIM, BLOCK), BF),
        ]
    args += sources
    scratch += [dma, dma((4,)), dma((4,))] * n
    in_vmem = len(shapes)
    shapes += [jax.ShapeDtypeStruct(item.shape(), BF) for item in items]
    out = pl.pallas_call(
        functools.partial(attention_kernel, ahead and ahead[0], behind and behind[0], list(items)),
        out_shape=shapes,
        in_specs=[smem, vmem] + [anywhere] * len(args),
        out_specs=[vmem] * in_vmem + [anywhere] * n,
        scratch_shapes=scratch,
        compiler_params=pltpu.CompilerParams(collective_id=cid, has_side_effects=True, vmem_limit_bytes=60 << 20),
    )(*near, *args)
    out = list(out)
    three, out = (out[:3], out[3:]) if ahead else (None, out)
    two, out = (out[:2], out[2:]) if behind else (None, out)
    return three, two, out


def slices(width, step=1024):
    return [(at, min(at + step, width)) for at in range(0, width, step)]


class Stream:
    def __init__(self, pairs, sems):
        self.copies = {}
        for i, (name, ref, buf, cols) in enumerate(pairs):
            src, dst = ref.at[:, cols[0] : cols[1]], buf.at[:, cols[0] : cols[1]]
            self.copies[name, cols[0]] = pltpu.make_async_copy(src, dst, sems.at[i])

    def start(self):
        for copy in self.copies.values():
            copy.start()

    def wait(self, name, at):
        self.copies[name, at].wait()


def normalised(x):
    mean = jnp.mean(x, axis=-1, keepdims=True)
    centred = x - mean
    rstd = lax.rsqrt(jnp.mean(centred * centred, axis=-1, keepdims=True) + EPSILON)
    return centred * rstd, rstd


def norm_backward(grad, xhat, rstd, gain):
    g = grad * gain
    part = g - jnp.mean(g, axis=-1, keepdims=True) - xhat * jnp.mean(g * xhat, axis=-1, keepdims=True)
    return part * rstd, jnp.sum(grad * xhat, axis=0, keepdims=True), jnp.sum(grad, axis=0, keepdims=True)


def greet_plane(sec, me):
    barrier = pltpu.get_barrier_semaphore()
    low = me % 4
    for k in range(1, 4):
        pl.semaphore_signal(barrier, inc=1, device_id=(sec, me - low + flip(low, k)), device_id_type=MESH)
    pl.semaphore_wait(barrier, 3)


class Load:
    def __init__(self, items):
        self.items = list(items)
        self.sources = [source for item in items for source in item.sources]
        self.shapes = [jax.ShapeDtypeStruct(item.shape(), BF) for item in items]
        dma = pltpu.SemaphoreType.DMA
        self.scratch = [dma, dma((4,)), dma((4,))] * len(self.items)

    def begin(self, sources, outs, sems):
        copies = []
        if self.items:
            greet_plane(*place())
        for i, item in enumerate(self.items):
            into = lambda k, i=i: outs[i].at[k]
            copies.append(PlaneCopies(item, sources[2 * i], sources[2 * i + 1], into, *sems[3 * i : 3 * i + 3]))
            copies[-1].start()
        return copies


def gelu_tanh(v):
    c = math.sqrt(2.0 / math.pi)
    return 0.5 * v * (1.0 + jnp.tanh(c * (v + 0.044715 * (v * v * v))))


def gelu_slope(v):
    c = math.sqrt(2.0 / math.pi)
    square = v * v
    t = jnp.tanh(c * (v + 0.044715 * (square * v)))
    return 0.5 * (1.0 + t) + 0.5 * v * (1.0 - t * t) * (c * (1.0 + 3 * 0.044715 * square))


def nt(a, b):
    return lax.dot_general(a, b, (((1,), (1,)), ((), ())), preferred_element_type=F32)


def put_owners(ref, x):
    turned = x.T
    for w in range(HEADS):
        ref[w % 4, w // 4] = turned[w * HEAD_DIM : (w + 1) * HEAD_DIM].astype(BF)


GAIN1, BIAS1, OUT_BIAS, GAIN2, BIAS2, FC2_BIAS = 0, 1, 4, 5, 6, 7


def row(vec_ref, i):
    return vec_ref[i : i + 1, :]


def pick(sec, zero_ref, one_ref):
    return jnp.where(sec == 0, zero_ref[...].astype(F32), one_ref[...].astype(F32))


def qkv_kernel(tok_ref, inc_ref, vec_ref, bias_ref, w_ref, qkv_ref, n1_ref, w_buf, t_buf, sems):
    sec, _ = place()
    stream = Stream([("w", w_ref, w_buf, cols) for cols in slices(3 * D, 384)], sems)
    stream.start()
    xhat, _ = normalised(pick(sec, tok_ref, inc_ref))
    n1 = xhat * row(vec_ref, GAIN1) + row(vec_ref, BIAS1)
    low = n1.astype(BF)
    for at, end in slices(3 * D, 384):
        stream.wait("w", at)
        t_buf[at:end, :] = (dot(low, w_buf[:, at:end]) + bias_ref[:, at:end]).T
    for h in range(HEADS):
        parts = [t_buf[p * D + h * HEAD_DIM : p * D + (h + 1) * HEAD_DIM, :] for p in range(3)]
        qkv_ref[h] = jnp.concatenate(parts, axis=0).astype(BF)
    put_owners(n1_ref, low.astype(F32))


def qkv_forward(tok, inc, vec, bias, w):
    tokens = tok.shape[0]
    anywhere, vmem = pl.BlockSpec(memory_space=pl.ANY), pl.BlockSpec(memory_space=pltpu.VMEM)
    return pl.pallas_call(
        qkv_kernel,
        out_shape=[
            jax.ShapeDtypeStruct((HEADS, 3 * HEAD_DIM, tokens), BF),
            jax.ShapeDtypeStruct((4, 4, HEAD_DIM, tokens), BF),
        ],
        in_specs=[vmem] * 4 + [anywhere],
        out_specs=[vmem] * 2,
        scratch_shapes=[
            pltpu.VMEM((D, 3 * D), BF),
            pltpu.VMEM((3 * D, tokens), F32),
            pltpu.SemaphoreType.DMA((len(slices(3 * D, 384)),)),
        ],
        compiler_params=pltpu.CompilerParams(vmem_limit_bytes=60 << 20),
    )(tok, inc, vec, bias, w)


def first_kernel(first_ref, bias_ref, tok_ref, *refs):
    refs = list(refs)

    def take(n):
        part = refs[:n]
        del refs[:n]
        return part

    shards = take(5)
    ahead_out = take(3)
    n1_ref, small_all, w_qkv = take(3)
    whole = take(3)
    w_buf, t_buf, x_buf, w_sem = take(4)
    f = Forward(0, (first_ref, bias_ref), x_buf, ahead_out, take(len(Forward.scratch(HEADS))))
    work = Gather(first_pieces(shards), shards, (w_buf, small_all, *whole), take(9))
    soon, later = [list(range(SOON)), list(range(SOON, work.count))]
    sec, me = place()
    greet_all(HEADS, sec, me)
    work.slots(0, 1)
    xhat, _ = normalised(tok_ref[...].astype(F32))
    xhat = xhat.T
    work.slots(1, SOON + 3)
    for array in range(len(shards)):
        work.mine(array).wait()
    work.across(soon)
    work.arrived(soon)
    keep = pltpu.make_async_copy(w_buf, w_qkv, w_sem)
    keep.start()
    work.slots(SOON + 3, SOON + 4)
    small = jnp.concatenate([small_all[w].astype(F32) for w in range(HEADS)], axis=0)
    n1 = (xhat * small[:, 0:1] + small[:, 1:2]).astype(BF).astype(F32)
    for w in range(HEADS):
        n1_ref[w % 4, w // 4] = n1[w * HEAD_DIM : (w + 1) * HEAD_DIM].astype(BF)
    low = n1.T.astype(BF)

    def columns(i, carry):
        here = pl.ds(pl.multiple_of(i * 384, 384), 384)
        w = jnp.concatenate([w_buf[shard, :, here].astype(F32) for shard in range(HEADS)], axis=0)
        t_buf[here, :] = dot(low, w.astype(BF)).T
        return carry

    lax.fori_loop(0, 3 * D // 384, columns, 0)
    for h in range(HEADS):
        rows = slice(h * HEAD_DIM, (h + 1) * HEAD_DIM)
        parts = [t_buf[p * D + h * HEAD_DIM : p * D + (h + 1) * HEAD_DIM, :] for p in range(3)]
        parts = [parts[0] + small[rows, 2:3], parts[1], parts[2] + small[rows, 3:4]]
        x_buf[h] = jnp.concatenate(parts, axis=0).astype(BF)
    f.start()
    work.slots(SOON + 4, SOON + 5)
    f.wait_in()
    work.slots(SOON + 5, SOON + 7)
    f.compute()
    work.slots(SOON + 7, work.count + 3)
    f.wait_out()
    work.across(later)
    work.arrived(later)
    work.finish()
    keep.wait()


SOON = 4


def first_pieces(shards):
    pieces = [(1, 0, BLOCK)]
    for array in (0, 2, 3, 4):
        pieces += [(array, at, end) for at, end in slices(shards[array].shape[1], D)]
    return pieces


def first_tick(near, tok, shards, cid):
    tokens = tok.shape[0]
    anywhere, vmem, smem = [pl.BlockSpec(memory_space=m) for m in (pl.ANY, pltpu.VMEM, pltpu.SMEM)]
    whole = [jax.ShapeDtypeStruct((HEADS,) + shard.shape, BF) for shard in shards]
    return pl.pallas_call(
        first_kernel,
        out_shape=Forward.shapes(HEADS)
        + [jax.ShapeDtypeStruct((4, 4, HEAD_DIM, tokens), BF), whole[1], whole[0]]
        + whole[2:],
        in_specs=[smem, vmem, vmem] + [anywhere] * 5,
        out_specs=[vmem] * 5 + [anywhere] * 4,
        scratch_shapes=[
            pltpu.VMEM((HEADS,) + shards[0].shape, BF),
            pltpu.VMEM((3 * D, tokens), F32),
            pltpu.VMEM((HEADS, 3 * HEAD_DIM, tokens), BF),
            pltpu.SemaphoreType.DMA,
        ]
        + Forward.scratch(HEADS)
        + Gather.semaphores(len(first_pieces(shards)), len(shards)),
        compiler_params=pltpu.CompilerParams(collective_id=cid, has_side_effects=True, vmem_limit_bytes=60 << 20),
    )(*near, tok, *shards)


def greet_section(sec, me):
    barrier = pltpu.get_barrier_semaphore()
    pl.semaphore_signal(barrier, inc=1, device_id=(1 - sec, me), device_id_type=MESH)
    pl.semaphore_wait(barrier, 1)


def to_section(src, dst, send_sem, recv_sem, sec, me):
    return pltpu.make_async_remote_copy(
        src_ref=src, dst_ref=dst, send_sem=send_sem, recv_sem=recv_sem, device_id=(1 - sec, me), device_id_type=MESH
    )


def feed_kernel(shift, load, *refs):
    n = len(load.items)
    tok_ref, inc_ref, att_ref, vec_ref, bias_ref, out_w, fc1_w, fc2_w = refs[:8]
    sources, refs = refs[8 : 8 + 2 * n], refs[8 + 2 * n :]
    res_ref, pre_ref, hidden_ref, n2_ref, att_rows_ref, low_ref = refs[:6]
    refs = refs[6:]
    if shift:
        next_ref, refs = refs[0], refs[1:]
    outs, refs = refs[:n], refs[n:]
    refs, load_sems = refs[: len(refs) - 3 * n], refs[len(refs) - 3 * n :]
    out_buf, fc1_buf, fc2_buf, t_buf, sems = refs[:5]
    sec, me = place()
    pairs = [("out", out_w, out_buf, (0, D))]
    pairs += [("fc1", fc1_w, fc1_buf, cols) for cols in slices(FFP)]
    pairs += [("fc2", fc2_w, fc2_buf, cols) for cols in slices(FFP)]
    stream = Stream(pairs, sems)
    stream.start()
    if shift:
        greet_section(sec, me)
    taken = load.begin(sources, outs, load_sems)
    att = jnp.concatenate([att_ref[h].astype(F32) for h in range(HEADS)], axis=0).T.astype(BF)
    for w in range(HEADS):
        att_rows_ref[w % 4, w // 4] = att_ref[w]
    stream.wait("out", 0)
    residual = pick(sec, tok_ref, inc_ref) + dot(att, out_buf[...]) + row(vec_ref, OUT_BIAS)
    res_ref[...] = residual
    xhat, _ = normalised(residual)
    n2 = (xhat * row(vec_ref, GAIN2) + row(vec_ref, BIAS2)).astype(BF)
    total = None
    for at, end in slices(FFP):
        stream.wait("fc1", at)
        pre = dot(n2, fc1_buf[:, at:end]) + bias_ref[:, at:end]
        pre_ref[:, at:end] = pre
        hidden = gelu_tanh(pre)
        hidden_ref[:, at:end] = hidden.astype(BF)
        t_buf[at:end, :] = hidden.T.astype(BF)
    for at, end in slices(FFP):
        stream.wait("fc2", at)
    total = dot(fc2_buf[...], t_buf[...])
    low_ref[...] = (residual + total.T + row(vec_ref, FC2_BIAS)).astype(BF)
    if shift:
        copy = to_section(low_ref, next_ref, refs[5], refs[6], sec, me)
        copy.start()
    for one in taken:
        one.forward()
    put_owners(n2_ref, n2.astype(F32))
    if shift:
        copy.wait()
    for one in taken:
        one.finish()


def feed_forward(tok, inc, att, vec, bias, out_w, fc1_w, fc2_w, cid, shift, items=()):
    tokens = tok.shape[0]
    load = Load(items)
    anywhere, vmem = pl.BlockSpec(memory_space=pl.ANY), pl.BlockSpec(memory_space=pltpu.VMEM)
    dma = pltpu.SemaphoreType.DMA
    params = {} if cid is None else dict(collective_id=cid, has_side_effects=True)
    rows = jax.ShapeDtypeStruct((4, 4, HEAD_DIM, tokens), BF)
    low = jax.ShapeDtypeStruct((tokens, D), BF)
    return pl.pallas_call(
        functools.partial(feed_kernel, shift, load),
        out_shape=[
            jax.ShapeDtypeStruct((tokens, D), F32),
            jax.ShapeDtypeStruct((tokens, FFP), F32),
            jax.ShapeDtypeStruct((tokens, FFP), BF),
            rows,
            rows,
            low,
        ]
        + [low] * shift
        + load.shapes,
        in_specs=[vmem] * 5 + [anywhere] * (3 + len(load.sources)),
        out_specs=[vmem] * (6 + shift) + [anywhere] * len(load.shapes),
        scratch_shapes=[
            pltpu.VMEM((D, D), BF),
            pltpu.VMEM((D, FFP), BF),
            pltpu.VMEM((D, FFP), BF),
            pltpu.VMEM((FFP, tokens), BF),
            dma((1 + 2 * len(slices(FFP)),)),
        ]
        + [dma, dma] * shift
        + load.scratch,
        compiler_params=pltpu.CompilerParams(vmem_limit_bytes=60 << 20, **params),
    )(tok, inc, att, vec, bias, out_w, fc1_w, fc2_w, *load.sources)


def feed_back_kernel(load, cot_ref, inc_ref, vec_ref, *refs):
    n = len(load.items)
    kept, refs = refs[:4], refs[4:]
    out_w, fc1_w, fc2_w = refs[:3]
    sources, refs = refs[3 : 3 + 2 * n], refs[3 + 2 * n :]
    rg_ref, ag_ref, fc_ref, pg_ref, branch_ref, sum_ref, fsum_ref = refs[:7]
    outs, refs = refs[7 : 7 + n], refs[7 + n :]
    pre_buf, res_buf, out_buf, fc1_buf, fc2_buf, t_buf, kept_sem, sems = refs[:8]
    sec, _ = place()
    pairs = []
    pairs += [("fc2", fc2_w, fc2_buf, cols) for cols in slices(FFP)]
    pairs += [("fc1", fc1_w, fc1_buf, cols) for cols in slices(FFP)]
    pairs.append(("out", out_w, out_buf, (0, D)))
    stream = Stream(pairs, sems)
    fetch(kept, (pre_buf, res_buf), kept_sem, sec)
    stream.start()
    taken = load.begin(sources, outs, refs[8:])
    grad = jnp.where(sec == 0, inc_ref[...].astype(F32), cot_ref[...].astype(F32))
    fc_grad = grad.astype(BF)
    put_owners(fc_ref, grad)
    fetched(kept, (pre_buf, res_buf), kept_sem)
    total = None
    for at, end in slices(FFP):
        slope = gelu_slope(pre_buf[:, at:end])
        stream.wait("fc2", at)
        pre_wide = dot(fc_grad, fc2_buf[:, at:end]) * slope
        pre_grad = pre_wide.astype(BF)
        pg_ref[:, at:end] = pre_grad
        fsum_ref[:, at:end] = jnp.sum(pre_grad.astype(F32), axis=0, keepdims=True)
        t_buf[at:end, :] = pre_wide.T.astype(BF)
    for at, end in slices(FFP):
        stream.wait("fc1", at)
    total = dot(fc1_buf[...], t_buf[...])
    xhat, rstd = normalised(res_buf[...])
    part, gain_sum, bias_sum = norm_backward(total.T, xhat, rstd, row(vec_ref, GAIN2))
    residual_grad = grad + part
    rg_ref[...] = residual_grad
    branch = residual_grad.astype(BF)
    branch_ref[...] = branch
    for one in taken:
        one.forward()
    stream.wait("out", 0)
    att_grad = dot(out_buf[...], residual_grad.T.astype(BF))
    for h in range(HEADS):
        ag_ref[h] = att_grad[h * HEAD_DIM : (h + 1) * HEAD_DIM].astype(BF)
    sum_ref[0:1, :] = jnp.sum(branch.astype(F32), axis=0, keepdims=True)
    sum_ref[1:2, :] = gain_sum
    sum_ref[2:3, :] = bias_sum
    sum_ref[3:4, :] = jnp.sum(fc_grad.astype(F32), axis=0, keepdims=True)
    for one in taken:
        one.finish()


def feed_backward(cot, inc, vec, kept, out_w, fc1_w, fc2_w, cid, items=()):
    tokens = cot.shape[0]
    load = Load(items)
    params = {} if cid is None else dict(collective_id=cid, has_side_effects=True)
    anywhere, vmem = pl.BlockSpec(memory_space=pl.ANY), pl.BlockSpec(memory_space=pltpu.VMEM)
    dma = pltpu.SemaphoreType.DMA
    return pl.pallas_call(
        functools.partial(feed_back_kernel, load),
        out_shape=[
            jax.ShapeDtypeStruct((tokens, D), F32),
            jax.ShapeDtypeStruct((HEADS, HEAD_DIM, tokens), BF),
            jax.ShapeDtypeStruct((4, 4, HEAD_DIM, tokens), BF),
            jax.ShapeDtypeStruct((tokens, FFP), BF),
            jax.ShapeDtypeStruct((tokens, D), BF),
            jax.ShapeDtypeStruct((4, D), F32),
            jax.ShapeDtypeStruct((1, FFP), F32),
        ]
        + load.shapes,
        in_specs=[vmem] * 3 + [anywhere] * (7 + len(load.sources)),
        out_specs=[vmem] * 7 + [anywhere] * len(load.shapes),
        scratch_shapes=[
            pltpu.VMEM((tokens, FFP), F32),
            pltpu.VMEM((tokens, D), F32),
            pltpu.VMEM((D, D), BF),
            pltpu.VMEM((D, FFP), BF),
            pltpu.VMEM((D, FFP), BF),
            pltpu.VMEM((FFP, tokens), BF),
            dma((2,)),
            dma((1 + 2 * len(slices(FFP)),)),
        ]
        + load.scratch,
        compiler_params=pltpu.CompilerParams(vmem_limit_bytes=60 << 20, **params),
    )(cot, inc, vec, *kept, out_w, fc1_w, fc2_w, *load.sources)


def qkv_back_kernel(shift, load, *refs):
    n = len(load.items)
    tok_ref, inc_ref, vec_ref, rg_ref, dq_ref, dkv_ref, w_ref = refs[:7]
    sources, refs = refs[7 : 7 + 2 * n], refs[7 + 2 * n :]
    grad_ref, dqkv_ref, sum_ref, qsum_ref = refs[:4]
    refs = refs[4:]
    if shift:
        next_ref, refs = refs[0], refs[1:]
    outs, refs = refs[:n], refs[n:]
    refs, load_sems = refs[: len(refs) - 3 * n], refs[len(refs) - 3 * n :]
    w_buf, sems = refs[:2]
    sec, me = place()
    stream = Stream([("w", w_ref, w_buf, cols) for cols in slices(3 * D, 384)], sems)
    stream.start()
    if shift:
        greet_section(sec, me)
    taken = load.begin(sources, outs, load_sems)
    kv = [dkv_ref[h].astype(F32) for h in range(HEADS)]
    rows = [dq_ref[h].astype(F32) for h in range(HEADS)]
    rows += [part[:HEAD_DIM] for part in kv] + [part[HEAD_DIM:] for part in kv]
    dqkv = jnp.concatenate(rows, axis=0).astype(BF)
    dqkv_ref[...] = dqkv
    qsum_ref[...] = nt(jnp.ones((8, dqkv.shape[1]), BF), dqkv)
    total = None
    for at, end in slices(3 * D, 384):
        stream.wait("w", at)
        part = dot(w_buf[:, at:end], dqkv[at:end])
        total = part if total is None else total + part
    xhat, rstd = normalised(pick(sec, tok_ref, inc_ref))
    part, gain_sum, bias_sum = norm_backward(total.T, xhat, rstd, row(vec_ref, GAIN1))
    grad = rg_ref[...] + part
    grad_ref[...] = grad
    if shift:
        low_buf = refs[2]
        low_buf[...] = grad.astype(BF)
        copy = to_section(low_buf, next_ref, refs[3], refs[4], sec, me)
        copy.start()
    sum_ref[0:1, :] = gain_sum
    sum_ref[1:2, :] = bias_sum
    if shift:
        copy.wait()
    for one in taken:
        one.forward()
    for one in taken:
        one.finish()


def qkv_backward(tok, inc, vec, residual_grad, dq, dkv, w, cid, shift, items=()):
    tokens = tok.shape[0]
    load = Load(items)
    anywhere, vmem = pl.BlockSpec(memory_space=pl.ANY), pl.BlockSpec(memory_space=pltpu.VMEM)
    dma = pltpu.SemaphoreType.DMA
    params = {} if cid is None else dict(collective_id=cid, has_side_effects=True)
    return pl.pallas_call(
        functools.partial(qkv_back_kernel, shift, load),
        out_shape=[
            jax.ShapeDtypeStruct((tokens, D), F32),
            jax.ShapeDtypeStruct((3 * D, tokens), BF),
            jax.ShapeDtypeStruct((2, D), F32),
            jax.ShapeDtypeStruct((8, 3 * D), F32),
        ]
        + [jax.ShapeDtypeStruct((tokens, D), BF)] * shift
        + load.shapes,
        in_specs=[vmem] * 6 + [anywhere] * (1 + len(load.sources)),
        out_specs=[vmem] * (4 + shift) + [anywhere] * len(load.shapes),
        scratch_shapes=[pltpu.VMEM((D, 3 * D), BF), dma((len(slices(3 * D, 384)),))]
        + [pltpu.VMEM((tokens, D), BF), dma, dma] * shift
        + load.scratch,
        compiler_params=pltpu.CompilerParams(vmem_limit_bytes=60 << 20, **params),
    )(tok, inc, vec, residual_grad, dq, dkv, w, *load.sources)


def pad_ff(x):
    return jnp.pad(x, ((0, 0),) * (x.ndim - 1) + ((0, FFP - FF),))


TENSORS = ("fc2", "fc1", "out", "qkv")


def final_kernel(tiles, early, late, *refs):
    refs = list(refs)

    def take(n):
        part = refs[:n]
        del refs[:n]
        return part

    small_ref = take(1)[0]
    x_refs = {name: take(2) for name in TENSORS}
    early_refs = take(len(early))
    late_refs = take(2 * len(late))
    small_out = take(1)[0]
    out_refs = dict(zip(TENSORS, take(4)))
    y_bufs = dict(zip(TENSORS, take(4)))
    x_buf = take(1)[0]
    g_bufs, one_bufs, two_bufs = [dict(zip(TENSORS, take(4))) for _ in range(3)]
    small_got = take(1)[0]
    early_sem, small_send, small_recv = take(3)
    sems = {name: take(4) for name in TENSORS}
    late_sems = [take(3) for _ in late]

    sec, me = place()
    z, low = me // 4, me % 4
    pair = z + 1 - 2 * (z % 2)
    count = small_ref.shape[0]
    greet_all(count, sec, me)

    def begin(name):
        for other, one in behind:
            if other == name:
                one.start()

    loads = []
    for i, (name, batch, cols) in enumerate(early):
        dst = y_bufs[name].at[4 * batch : 4 * batch + 4]
        if cols is not None:
            dst = dst.at[:, :, cols[0] : cols[1]]
        loads.append((name, pltpu.make_async_copy(early_refs[i], dst, early_sem.at[i])))
        loads[-1][1].start()
    behind = []
    for i, (name, batch, item) in enumerate(late):

        def slot(k, name=name, batch=batch, item=item):
            ref = y_bufs[name].at[4 * batch + k]
            return ref if item.cols is None else ref.at[:, item.cols[0] : item.cols[1]]

        behind.append((name, PlaneCopies(item, late_refs[2 * i], late_refs[2 * i + 1], slot, *late_sems[i])))
    begin("fc1")
    smalls = []
    for d in range(1, count):
        target = (me + d) % count
        smalls.append(
            pltpu.make_async_remote_copy(
                src_ref=small_ref.at[target],
                dst_ref=small_got.at[d],
                send_sem=small_send.at[d],
                recv_sem=small_recv.at[d],
                device_id=(sec, target),
                device_id_type=MESH,
            )
        )
        smalls[-1].start()

    def first(name, i):
        send, recv = sems[name][0], sems[name][1]
        return pltpu.make_async_remote_copy(
            src_ref=g_bufs[name].at[i, 2:4],
            dst_ref=one_bufs[name].at[i],
            send_sem=send.at[i],
            recv_sem=recv.at[i],
            device_id=(sec, pair * 4 + low),
            device_id_type=MESH,
        )

    def second(name, i):
        send, recv = sems[name][2], sems[name][3]
        return pltpu.make_async_remote_copy(
            src_ref=g_bufs[name].at[i, 1],
            dst_ref=two_bufs[name].at[i],
            send_sem=send.at[i],
            recv_sem=recv.at[i],
            device_id=(sec, (3 - z) * 4 + low),
            device_id_type=MESH,
        )

    def ready(name):
        for other, one in behind:
            if other == name:
                one.forward()
        if name in ("fc1", "qkv"):
            begin({"fc1": "qkv", "qkv": "out"}[name])
        for other, load in loads:
            if other == name:
                load.wait()
        for other, one in behind:
            if other == name:
                one.finish()
        rows = []
        for owner in (z, 3 - z, pair, 3 - pair):
            rows.append(
                jnp.concatenate(
                    [x_refs[name][batch][k, owner].astype(F32) for batch in range(2) for k in range(4)], axis=1
                )
            )
        x_buf[...] = jnp.concatenate(rows, axis=0).astype(BF)

    def columns(name, i):
        width = tiles[name][1]
        return pl.ds(pl.multiple_of(i * width, 128), width)

    def compute(name, i):
        width = tiles[name][1]
        buf = y_bufs[name]
        if name == "qkv":
            rows = pl.ds(pl.multiple_of(i * width, 128), width)
            y = jnp.concatenate([buf[part, rows, :] for part in range(8)], axis=1)
            total = lax.dot_general(x_buf[...], y, (((1,), (1,)), ((), ())), preferred_element_type=F32)
        else:
            y = jnp.concatenate([buf[part, :, columns(name, i)] for part in range(8)], axis=0)
            total = dot(x_buf[...], y)
        g_bufs[name][i] = total.reshape(4, HEAD_DIM, width).astype(BF)
        first(name, i).start()

    def middle(name, i):
        first(name, i).wait_recv()
        out_refs[name][:, columns(name, i)] = g_bufs[name][i, 0].astype(F32) + one_bufs[name][i, 0].astype(F32)
        g_bufs[name][i, 1] = (g_bufs[name][i, 1].astype(F32) + one_bufs[name][i, 1].astype(F32)).astype(BF)
        second(name, i).start()

    def finish(name, i):
        second(name, i).wait_recv()
        out_refs[name][:, columns(name, i)] += two_bufs[name][i].astype(F32)
        first(name, i).wait_send()
        second(name, i).wait_send()

    def loop(name, *steps):
        def body(i, carry):
            for step, which in steps:
                step(which, i)
            return carry

        lax.fori_loop(0, tiles[name][0], body, 0)

    ready("fc2")
    loop("fc2", (compute, "fc2"))
    ready("fc1")
    loop("fc1", (compute, "fc1"), (middle, "fc2"))
    loop("fc1", (middle, "fc1"), (finish, "fc2"))
    ready("qkv")
    loop("qkv", (compute, "qkv"))
    ready("out")
    loop("out", (compute, "out"))
    loop("fc1", (finish, "fc1"))
    loop("qkv", (middle, "qkv"))
    loop("out", (middle, "out"))
    for copy in smalls:
        copy.wait()
    total = small_ref[me]
    for d in range(1, count):
        total = total + small_got[d]
    small_out[...] = total
    loop("qkv", (finish, "qkv"))
    loop("out", (finish, "out"))


def final(small, xs, early, late, cid):
    count = small.shape[0]
    tokens = xs["qkv"][0].shape[-1]
    widths = {"fc2": FFP, "fc1": FFP, "out": D, "qkv": 3 * D}
    tiles = {name: (w // (256 if name[0] == "f" else 384), 256 if name[0] == "f" else 384) for name, w in widths.items()}
    anywhere, vmem = pl.BlockSpec(memory_space=pl.ANY), pl.BlockSpec(memory_space=pltpu.VMEM)
    args = [small] + [x for name in TENSORS for x in xs[name]]
    n_vmem = len(args)
    args += [e[3] for e in early] + [source for _, _, item in late for source in item.sources]
    dma = pltpu.SemaphoreType.DMA
    scratch = []
    for name in TENSORS:
        shape = (8, widths[name], tokens) if name == "qkv" else (8, tokens, widths[name])
        scratch.append(pltpu.VMEM(shape, BF))
    scratch.append(pltpu.VMEM((4 * HEAD_DIM, 8 * tokens), BF))
    for lead in ((4,), (2,), ()):
        for name in TENSORS:
            scratch.append(pltpu.VMEM((tiles[name][0],) + lead + (HEAD_DIM, tiles[name][1]), BF))
    scratch.append(pltpu.VMEM(small.shape, F32))
    scratch += [dma((len(early),)), dma((count,)), dma((count,))]
    for name in TENSORS:
        scratch += [dma((tiles[name][0],))] * 4
    scratch += [dma, dma((4,)), dma((4,))] * len(late)
    out = pl.pallas_call(
        functools.partial(final_kernel, tiles, [e[:3] for e in early], late),
        out_shape=[jax.ShapeDtypeStruct(small.shape[1:], F32)]
        + [jax.ShapeDtypeStruct((HEAD_DIM, widths[name]), F32) for name in TENSORS],
        in_specs=[vmem] * n_vmem + [anywhere] * (len(args) - n_vmem),
        out_specs=[vmem] * 5,
        scratch_shapes=scratch,
        compiler_params=pltpu.CompilerParams(
            collective_id=cid, has_side_effects=True, vmem_limit_bytes=60 << 20
        ),
    )(*args)
    return out[0], dict(zip(TENSORS, out[1:]))


def on_device(
    tokens,
    cotangent,
    image_of_block,
    ln1_gain,
    ln1_bias,
    qkv_weight,
    qv_bias,
    out_weight,
    out_bias,
    ln2_gain,
    ln2_bias,
    fc1_weight,
    fc1_bias,
    fc2_weight,
    fc2_bias,
):
    sec, me = place()
    small = jnp.stack(
        [ln1_gain[0], ln1_bias[0], qv_bias[0, 0], qv_bias[0, 1], out_bias[0], ln2_gain[0], ln2_bias[0], fc2_bias[0]],
        axis=1,
    )
    small = jnp.pad(small, ((0, 0), (0, BLOCK - 8)))
    near = window(image_of_block)
    shards = [qkv_weight[0], small, out_weight[0], pad_ff(fc1_weight[0]), pad_ff(fc2_weight[0].T)]
    *three, n1, small_all, w_qkv, w_out, w_fc1, w_fc2t = first_tick(near, tokens[0], shards, 2)
    w_qkv = w_qkv.reshape(D, 3 * D)
    w_out = w_out.reshape(D, D)
    w_fc1 = w_fc1.reshape(D, FFP)
    w_fc2t = w_fc2t.reshape(D, FFP)
    vec = small_all.reshape(D, BLOCK)[:, :8].T.astype(F32)
    b_qkv = jnp.concatenate([vec[2:3], jnp.zeros((1, D), F32), vec[3:4]], axis=1)
    b_fc1 = pad_ff(fc1_bias[0]).astype(F32).reshape(1, FFP)

    def choose(at_zero, at_one):
        return jnp.where(sec == 0, at_zero, at_one)

    saved, sent, back, done, input_grads = [], {}, [], [], []
    incoming = [tokens[0]]

    def token_inputs(tick):
        return tokens[min(tick, 1)], incoming[tick]

    def feed(tick, qkv, lse, att, n1, cid, shift, items=()):
        fed = feed_forward(*token_inputs(tick), att, vec, b_fc1, w_out, w_fc1, w_fc2t, cid, shift, items)
        saved.append(
            dict(qkv=qkv, lse=lse, n1=n1, residual=fed[0], pre=fed[1], hidden=fed[2], n2=fed[3], att=fed[4], low=fed[5])
        )
        return fed

    def kept(tick, *names):
        return [saved[at][name] for name in names for at in ((1, 1), (0, 2), (1, 1))[tick]]

    def feed_back(tick, incoming_grad, cid=None, items=()):
        residual_grad, att_grad, fc, pre, branch, four, fsum, *got = feed_backward(
            cotangent[min(tick, 1)], incoming_grad, vec, kept(tick, "pre", "residual"), w_out, w_fc1, w_fc2t, cid, items
        )
        back.append(dict(fc=fc, pre=pre, branch=branch))
        return residual_grad, att_grad, [*four, fsum], got

    def qkv_back(tick, residual_grad, dq, dkv, sums, cid, shift, items=()):
        inputs = (tokens[max(tick - 1, 0)], incoming[min(tick + 1, 2)])
        input_grad, dqkv, two, qsum, *rest = qkv_backward(
            *inputs, vec, residual_grad, dq, dkv, w_qkv, cid, shift, items
        )
        back[tick]["dqkv"] = dqkv
        input_grads.append(input_grad)
        done.append([two[0], two[1], qsum[0, :D], qsum[0, 2 * D :], *sums])
        return rest

    incoming.append(feed(0, *three, n1, 8, True)[6])

    qkv, n1 = qkv_forward(*token_inputs(1), vec, b_qkv, w_qkv)
    three, _, _ = attention(near, 3, ahead=(1, qkv))
    incoming.append(lax.ppermute(feed(1, *three, n1, None, False)[5], "section", [(0, 1)]))

    def first_batch(name, cols=None):
        return Whole(saved[0][name], saved[1][name], cols)

    def second_batch(name, cols=None):
        return Whole(saved[1][name], saved[2][name], cols)

    residual_grad, att_grad, sums, _ = feed_back(0, tokens[0])
    qkv, n1 = qkv_forward(*token_inputs(2), vec, b_qkv, w_qkv)
    items = [Rows(saved[0][name], saved[1][name]) for name in ("n1", "att", "n2")]
    items.append(first_batch("hidden", (0, SPLIT)))
    three, two, got = attention(near, 4, ahead=(2, qkv), behind=(0, att_grad, kept(0, "qkv", "lse")), items=items)
    sent["n1_0"], sent["att_0"], sent["n2_0"], sent["h0a"] = got
    qkv_back(0, residual_grad, *two, sums, None, False)
    incoming_grad = lax.ppermute(input_grads[0].astype(BF), "section", [(1, 0)])
    sent["h0b"] = feed(2, *three, n1, 11, False, [first_batch("hidden", (SPLIT, FFP))])[6]
    outputs = jnp.stack([choose(saved[m]["low"], saved[m + 1]["low"]) for m in range(2)])

    residual_grad, att_grad, sums, got = feed_back(1, incoming_grad, 12, [second_batch("hidden", (0, SPLIT))])
    sent["h1a"] = got[0]
    items = [Rows(saved[1][name], saved[2][name]) for name in ("n1", "att", "n2")]
    items.append(second_batch("hidden", (SPLIT, FFP)))
    _, two, got = attention(near, 5, behind=(1, att_grad, kept(1, "qkv", "lse")), items=items)
    sent["n1_1"], sent["att_1"], sent["n2_1"], sent["h1b"] = got
    incoming_grad = qkv_back(1, residual_grad, *two, sums, 9, True)[0]

    residual_grad, att_grad, sums, got = feed_back(
        2, incoming_grad, 13, [Whole(back[1]["pre"], back[0]["pre"], (0, SPLIT))]
    )
    sent["pre_0a"] = got[0]
    items = [Rows(back[1]["fc"], back[0]["fc"]), Rows(back[2]["fc"], back[1]["fc"])]
    items.append(Whole(back[1]["pre"], back[0]["pre"], (SPLIT, FFP)))
    _, two, got = attention(near, 6, behind=(2, att_grad, kept(2, "qkv", "lse")), items=items)
    sent["fc_0"], sent["fc_1"], sent["pre_0b"] = got
    sent["branch_0"] = qkv_back(
        2, residual_grad, *two, sums, 14, False, [Whole(back[1]["branch"], back[0]["branch"])]
    )[0]
    input_grads = jnp.stack([choose(input_grads[m + 1], input_grads[m]) for m in range(2)])

    sums = [choose(done[1][i] + done[2][i], done[0][i] + done[1][i]) for i in range(9)]
    by_owner = jnp.stack(sums[:8]).reshape(8, HEADS, HEAD_DIM).transpose(1, 0, 2)
    by_owner = jnp.pad(by_owner, ((0, 0), (0, 0), (0, BLOCK - HEAD_DIM)))
    lines = FFP // BLOCK
    to_all = jnp.broadcast_to(sums[8].reshape(1, lines, BLOCK), (HEADS, lines, BLOCK))
    to_all = jnp.pad(to_all, ((0, 0), (0, 40 - lines), (0, 0)))
    xs = {
        "fc2": [sent["fc_0"], sent["fc_1"]],
        "fc1": [sent["n2_0"], sent["n2_1"]],
        "out": [sent["att_0"], sent["att_1"]],
        "qkv": [sent["n1_0"], sent["n1_1"]],
    }
    early = [
        ("fc2", 0, (0, SPLIT), sent["h0a"]),
        ("fc2", 0, (SPLIT, FFP), sent["h0b"]),
        ("fc2", 1, (0, SPLIT), sent["h1a"]),
        ("fc2", 1, (SPLIT, FFP), sent["h1b"]),
        ("fc1", 0, (0, SPLIT), sent["pre_0a"]),
        ("fc1", 0, (SPLIT, FFP), sent["pre_0b"]),
        ("out", 0, None, sent["branch_0"]),
    ]
    late = [
        ("fc1", 1, Whole(back[2]["pre"], back[1]["pre"])),
        ("qkv", 0, Whole(back[1]["dqkv"], back[0]["dqkv"])),
        ("qkv", 1, Whole(back[2]["dqkv"], back[1]["dqkv"])),
        ("out", 1, Whole(back[2]["branch"], back[1]["branch"])),
    ]
    packed, grads = final(jnp.concatenate([by_owner, to_all], axis=1), xs, early, late, 10)
    g_small = packed[:8, :HEAD_DIM]
    g_fc1_bias = packed[8 : 8 + lines].reshape(FFP)[:FF]
    return (
        outputs[None],
        input_grads[None],
        g_small[0][None],
        g_small[1][None],
        grads["qkv"][None],
        g_small[2:4][None],
        grads["out"][None],
        g_small[4][None],
        g_small[5][None],
        g_small[6][None],
        grads["fc1"][:, :FF][None],
        g_fc1_bias[None],
        grads["fc2"].T[:FF][None],
        g_small[7][None],
    )


BLK_DEV = 1
REACH = 5


def shifted(value, axis, steps):
    count = lax.axis_size(axis)
    initial, last = (max(0, -steps), min(count, count - steps))
    return lax.ppermute(value, axis, [(source, source + steps) for source in range(initial, last)])


def layer_norm(values_in, scale_gain, shift_bias):
    row_mean = jnp.mean(values_in, axis=-1, keepdims=True)
    centred = values_in - row_mean
    row_var = jnp.mean(centred * centred, axis=-1, keepdims=True)
    return centred * lax.rsqrt(row_var + EPSILON) * scale_gain + shift_bias


def gelu_tanh(pre_value):
    return jax.nn.gelu(pre_value, approximate=True)


def heads_of(values_in):
    return values_in.reshape(values_in.shape[0], HEADS, HEAD_DIM)


def image_mask(image_of_block, batch_slot, wide_rank):
    padding = REACH * BLK_DEV
    padded = jnp.pad(image_of_block, ((0, 0), (padding, padding)), constant_values=-1)
    image_row = lax.dynamic_index_in_dim(padded, batch_slot, 0, keepdims=False)
    key_blocks = lax.dynamic_slice_in_dim(image_row, wide_rank * BLK_DEV, (2 * REACH + 1) * BLK_DEV)
    query_blocks = lax.dynamic_slice_in_dim(image_row, wide_rank * BLK_DEV + padding, BLK_DEV)
    return jnp.repeat(query_blocks, BLOCK)[:, None] == jnp.repeat(key_blocks, BLOCK)[None, :]


def keep_slot(buffer_all, new_value, batch_slot, is_live):
    previous = lax.dynamic_index_in_dim(buffer_all, batch_slot, 0, keepdims=False)
    chosen = jnp.where(is_live, new_value, previous)
    return lax.dynamic_update_index_in_dim(buffer_all, chosen, batch_slot, 0)


def near_keys(key_own, value_own, backward_pass):
    key_parts = []
    value_parts = []
    for offset in range(-REACH, REACH + 1):
        if offset == 0:
            received = (key_own, value_own)
        elif backward_pass:
            received = shifted((key_own, value_own), "wide", -offset)
        else:
            received = shifted((key_own, value_own), "wide", -offset)
        key_parts.append(received[0])
        value_parts.append(received[1])
    return (jnp.concatenate(key_parts, axis=0), jnp.concatenate(value_parts, axis=0))


def return_key_grads(key_terms, value_terms):
    row_count = key_terms.shape[0] // (2 * REACH + 1)
    key_total = key_terms[REACH * row_count : (REACH + 1) * row_count]
    value_total = value_terms[REACH * row_count : (REACH + 1) * row_count]
    for position, offset in enumerate(range(-REACH, REACH + 1)):
        if offset != 0:
            piece_pair = (
                key_terms[position * row_count : (position + 1) * row_count],
                value_terms[position * row_count : (position + 1) * row_count],
            )
            received = shifted((piece_pair[0], piece_pair[1]), "wide", offset)
            key_total = key_total + received[0]
            value_total = value_total + received[1]
    return (key_total, value_total)


def project_qkv(layer_in, weights):
    layer_float = layer_in.astype(jnp.float32)
    normed_one = layer_norm(
        layer_float, weights[0].astype(jnp.float32), weights[1].astype(jnp.float32)
    ).astype(jnp.bfloat16)
    mixed = jnp.dot(normed_one, weights[2], preferred_element_type=jnp.float32)
    queries = (mixed[:, :D] + weights[3][0].astype(jnp.float32)).astype(jnp.bfloat16)
    key_own = mixed[:, D : 2 * D].astype(jnp.bfloat16)
    value_own = (mixed[:, 2 * D :] + weights[3][1].astype(jnp.float32)).astype(jnp.bfloat16)
    return (layer_float, normed_one, queries, key_own, value_own)


def attention_probs(queries, keys_near, same_image):
    score_scale = 1.0 / math.sqrt(HEAD_DIM)
    scores = (
        jnp.einsum(
            "qhd,khd->hqk",
            heads_of(queries),
            heads_of(keys_near),
            preferred_element_type=jnp.float32,
        )
        * score_scale
    )
    scores = jnp.where(same_image[None], scores, MASKED_SCORE)
    row_max = jnp.max(scores, axis=-1, keepdims=True)
    exponent = jnp.exp(scores - row_max)
    return exponent / jnp.sum(exponent, axis=-1, keepdims=True)


def finish_layer(layer_float, queries, keys_near, values_near, same_image, weights, hidden_bias):
    probs = attention_probs(queries, keys_near, same_image)
    probs_low = probs.astype(jnp.bfloat16)
    attended = jnp.einsum(
        "hqk,khd->qhd", probs_low, heads_of(values_near), preferred_element_type=jnp.float32
    )
    attended = attended.reshape(queries.shape[0], D).astype(jnp.bfloat16)
    residual = (
        layer_float
        + jnp.dot(attended, weights[4], preferred_element_type=jnp.float32)
        + weights[5].astype(jnp.float32)
    )
    normed_two = layer_norm(
        residual, weights[6].astype(jnp.float32), weights[7].astype(jnp.float32)
    ).astype(jnp.bfloat16)
    hidden_pre = jnp.dot(
        normed_two, weights[8], preferred_element_type=jnp.float32
    ) + hidden_bias.astype(jnp.float32)
    hidden = gelu_tanh(hidden_pre).astype(jnp.bfloat16)
    output = (
        residual
        + jnp.dot(hidden, weights[9], preferred_element_type=jnp.float32)
        + weights[10].astype(jnp.float32)
    )
    return (probs, probs_low, attended, residual, normed_two, hidden_pre, hidden, output)


def layer_backward(
    layer_float,
    normed_one,
    queries,
    keys_near,
    values_near,
    same_image,
    weights,
    hidden_bias,
    grad_out,
):
    score_scale = 1.0 / math.sqrt(HEAD_DIM)
    probs, probs_low, attended, residual, normed_two, hidden_pre, hidden, output = finish_layer(
        layer_float, queries, keys_near, values_near, same_image, weights, hidden_bias
    )
    feed_grad = grad_out.astype(jnp.bfloat16)
    grad_fc2_weight = jnp.einsum("tf,td->fd", hidden, feed_grad, preferred_element_type=jnp.float32)
    grad_fc2_bias = jnp.sum(feed_grad.astype(jnp.float32), axis=0)
    hidden_grad = jnp.einsum("td,fd->tf", feed_grad, weights[9], preferred_element_type=jnp.float32)
    primal_gelu, gelu_pull = jax.vjp(gelu_tanh, hidden_pre)
    pre_grad = gelu_pull(hidden_grad)[0].astype(jnp.bfloat16)
    grad_fc1_bias = jnp.sum(pre_grad.astype(jnp.float32), axis=0)
    grad_fc1_weight = jnp.einsum(
        "td,tf->df", normed_two, pre_grad, preferred_element_type=jnp.float32
    )
    normed_two_grad = jnp.einsum(
        "tf,df->td", pre_grad, weights[8], preferred_element_type=jnp.float32
    )
    primal_two, norm_two_pull = jax.vjp(
        layer_norm, residual, weights[6].astype(jnp.float32), weights[7].astype(jnp.float32)
    )
    residual_part, grad_ln2_gain, grad_ln2_bias = norm_two_pull(normed_two_grad)
    residual_grad = grad_out + residual_part
    branch_grad = residual_grad.astype(jnp.bfloat16)
    grad_out_bias = jnp.sum(branch_grad.astype(jnp.float32), axis=0)
    grad_out_weight = jnp.einsum(
        "tc,td->cd", attended, branch_grad, preferred_element_type=jnp.float32
    )
    attended_grad = jnp.einsum(
        "td,cd->tc", branch_grad, weights[4], preferred_element_type=jnp.float32
    ).astype(jnp.bfloat16)
    attended_heads = heads_of(attended_grad)
    probs_grad = jnp.einsum(
        "qhd,khd->hqk", attended_heads, heads_of(values_near), preferred_element_type=jnp.float32
    )
    value_terms = jnp.einsum(
        "hqk,qhd->khd", probs_low, attended_heads, preferred_element_type=jnp.float32
    )
    score_grad = (
        probs * (probs_grad - jnp.sum(probs * probs_grad, axis=-1, keepdims=True))
    ).astype(jnp.bfloat16)
    query_grad = (
        jnp.einsum(
            "hqk,khd->qhd", score_grad, heads_of(keys_near), preferred_element_type=jnp.float32
        )
        * score_scale
    )
    query_grad = query_grad.reshape(queries.shape[0], D).astype(jnp.bfloat16)
    key_terms = (
        jnp.einsum(
            "hqk,qhd->khd", score_grad, heads_of(queries), preferred_element_type=jnp.float32
        )
        * score_scale
    )
    key_total, value_total = return_key_grads(key_terms.reshape(-1, D), value_terms.reshape(-1, D))
    key_grad = key_total.astype(jnp.bfloat16)
    value_grad = value_total.astype(jnp.bfloat16)
    grad_qv_bias = jnp.stack(
        [
            jnp.sum(query_grad.astype(jnp.float32), axis=0),
            jnp.sum(value_grad.astype(jnp.float32), axis=0),
        ]
    )
    mixed_grad = jnp.concatenate([query_grad, key_grad, value_grad], axis=1)
    grad_qkv_weight = jnp.einsum(
        "tc,tk->ck", normed_one, mixed_grad, preferred_element_type=jnp.float32
    )
    normed_one_grad = jnp.einsum(
        "tk,ck->tc", mixed_grad, weights[2], preferred_element_type=jnp.float32
    )
    primal_one, norm_one_pull = jax.vjp(
        layer_norm, layer_float, weights[0].astype(jnp.float32), weights[1].astype(jnp.float32)
    )
    input_part, grad_ln1_gain, grad_ln1_bias = norm_one_pull(normed_one_grad)
    input_grad = residual_grad + input_part
    grad_terms = (
        grad_ln1_gain,
        grad_ln1_bias,
        grad_qkv_weight,
        grad_qv_bias,
        grad_out_weight,
        grad_out_bias,
        grad_ln2_gain,
        grad_ln2_bias,
        grad_fc1_weight,
        grad_fc2_weight,
        grad_fc2_bias,
    )
    return (input_grad, grad_terms, grad_fc1_bias)


def on_device_near(
    tokens,
    cotangent,
    image_of_block,
    ln1_gain,
    ln1_bias,
    qkv_weight,
    qv_bias,
    out_weight,
    out_bias,
    ln2_gain,
    ln2_bias,
    fc1_weight,
    fc1_bias,
    fc2_weight,
    fc2_bias,
):
    section_rank = lax.axis_index("section")
    wide_rank = lax.axis_index("wide")
    micro_count = tokens.shape[0]
    weights = (
        lax.all_gather(ln1_gain[0], "wide", axis=0, tiled=True),
        lax.all_gather(ln1_bias[0], "wide", axis=0, tiled=True),
        lax.all_gather(qkv_weight[0], "wide", axis=0, tiled=True),
        lax.all_gather(qv_bias[0], "wide", axis=1, tiled=True),
        lax.all_gather(out_weight[0], "wide", axis=0, tiled=True),
        lax.all_gather(out_bias[0], "wide", axis=0, tiled=True),
        lax.all_gather(ln2_gain[0], "wide", axis=0, tiled=True),
        lax.all_gather(ln2_bias[0], "wide", axis=0, tiled=True),
        lax.all_gather(fc1_weight[0], "wide", axis=0, tiled=True),
        lax.all_gather(fc2_weight[0], "wide", axis=1, tiled=True),
        lax.all_gather(fc2_bias[0], "wide", axis=0, tiled=True),
    )
    hidden_bias = fc1_bias[0]
    inputs_kept = jnp.zeros_like(tokens)
    outputs_kept = jnp.zeros_like(tokens)
    incoming = jnp.zeros_like(tokens[0])
    for tick_number in range(micro_count + 1):
        batch_index = tick_number - section_rank
        is_live = (batch_index >= 0) & (batch_index < micro_count)
        batch_slot = jnp.clip(batch_index, 0, micro_count - 1)
        own_tokens = tokens[min(tick_number, micro_count - 1)]
        layer_in = jnp.where(section_rank == 0, own_tokens, incoming)
        same_image = image_mask(image_of_block, batch_slot, wide_rank)
        layer_float, normed_one, queries, key_own, value_own = project_qkv(layer_in, weights)
        keys_near, values_near = near_keys(key_own, value_own, False)
        output = finish_layer(
            layer_float, queries, keys_near, values_near, same_image, weights, hidden_bias
        )[-1]
        output_low = output.astype(jnp.bfloat16)
        inputs_kept = keep_slot(inputs_kept, layer_in, batch_slot, is_live)
        outputs_kept = keep_slot(outputs_kept, output_low, batch_slot, is_live)
        if tick_number < micro_count:
            incoming = shifted(output_low, "section", 1)
    weights_back = (
        lax.all_gather(ln1_gain[0], "wide", axis=0, tiled=True),
        lax.all_gather(ln1_bias[0], "wide", axis=0, tiled=True),
        lax.all_gather(qkv_weight[0], "wide", axis=0, tiled=True),
        lax.all_gather(qv_bias[0], "wide", axis=1, tiled=True),
        lax.all_gather(out_weight[0], "wide", axis=0, tiled=True),
        lax.all_gather(out_bias[0], "wide", axis=0, tiled=True),
        lax.all_gather(ln2_gain[0], "wide", axis=0, tiled=True),
        lax.all_gather(ln2_bias[0], "wide", axis=0, tiled=True),
        lax.all_gather(fc1_weight[0], "wide", axis=0, tiled=True),
        lax.all_gather(fc2_weight[0], "wide", axis=1, tiled=True),
        lax.all_gather(fc2_bias[0], "wide", axis=0, tiled=True),
    )
    grad_totals = tuple((jnp.zeros(array.shape, jnp.float32) for array in weights_back))
    hidden_bias_total = jnp.zeros(hidden_bias.shape, jnp.float32)
    input_grads = jnp.zeros(tokens.shape, jnp.float32)
    incoming_grad = jnp.zeros(tokens.shape[1:], jnp.bfloat16)
    for tick_number in range(micro_count + 1):
        batch_index = tick_number - 1 + section_rank
        is_live = (batch_index >= 0) & (batch_index < micro_count)
        batch_slot = jnp.clip(batch_index, 0, micro_count - 1)
        from_cotangent = cotangent[min(tick_number, micro_count - 1)].astype(jnp.float32)
        grad_out = jnp.where(
            section_rank == 1, from_cotangent, incoming_grad.astype(jnp.float32)
        ) * is_live.astype(jnp.float32)
        layer_in = lax.dynamic_index_in_dim(inputs_kept, batch_slot, 0, keepdims=False)
        same_image = image_mask(image_of_block, batch_slot, wide_rank)
        layer_float, normed_one, queries, key_own, value_own = project_qkv(layer_in, weights_back)
        keys_near, values_near = near_keys(key_own, value_own, True)
        input_grad, grad_terms, hidden_bias_term = layer_backward(
            layer_float,
            normed_one,
            queries,
            keys_near,
            values_near,
            same_image,
            weights_back,
            hidden_bias,
            grad_out,
        )
        grad_totals = tuple(
            (old_total + new_term for old_total, new_term in zip(grad_totals, grad_terms))
        )
        hidden_bias_total = hidden_bias_total + hidden_bias_term
        input_grads = keep_slot(input_grads, input_grad, batch_slot, is_live)
        if tick_number < micro_count:
            incoming_grad = shifted(input_grad.astype(jnp.bfloat16), "section", -1)
    (
        grad_ln1_gain,
        grad_ln1_bias,
        grad_qkv_weight,
        grad_qv_bias,
        grad_out_weight,
        grad_out_bias,
        grad_ln2_gain,
        grad_ln2_bias,
        grad_fc1_weight,
        grad_fc2_weight,
        grad_fc2_bias,
    ) = grad_totals
    row_sums = (
        lax.psum_scatter(grad_ln1_gain, "wide", scatter_dimension=0, tiled=True),
        lax.psum_scatter(grad_ln1_bias, "wide", scatter_dimension=0, tiled=True),
        lax.psum_scatter(grad_qkv_weight, "wide", scatter_dimension=0, tiled=True),
        lax.psum_scatter(grad_out_weight, "wide", scatter_dimension=0, tiled=True),
        lax.psum_scatter(grad_out_bias, "wide", scatter_dimension=0, tiled=True),
        lax.psum_scatter(grad_ln2_gain, "wide", scatter_dimension=0, tiled=True),
        lax.psum_scatter(grad_ln2_bias, "wide", scatter_dimension=0, tiled=True),
        lax.psum_scatter(grad_fc1_weight, "wide", scatter_dimension=0, tiled=True),
        lax.psum_scatter(grad_fc2_bias, "wide", scatter_dimension=0, tiled=True),
    )
    column_sums = (
        lax.psum_scatter(grad_qv_bias, "wide", scatter_dimension=1, tiled=True),
        lax.psum_scatter(grad_fc2_weight, "wide", scatter_dimension=1, tiled=True),
    )
    hidden_bias_sum = lax.psum(hidden_bias_total, "wide")
    return (
        outputs_kept[None],
        input_grads[None],
        row_sums[0][None],
        row_sums[1][None],
        row_sums[2][None],
        column_sums[0][None],
        row_sums[3][None],
        row_sums[4][None],
        row_sums[5][None],
        row_sums[6][None],
        row_sums[7][None],
        hidden_bias_sum[None],
        column_sums[1][None],
        row_sums[8][None],
    )


def specs():
    ins = (
        P(None, "wide", None),
        P(None, "wide", None),
        P(),
        P("section", "wide"),
        P("section", "wide"),
        P("section", "wide", None),
        P("section", None, "wide"),
        P("section", "wide", None),
        P("section", "wide"),
        P("section", "wide"),
        P("section", "wide"),
        P("section", "wide", None),
        P("section", None),
        P("section", None, "wide"),
        P("section", "wide"),
    )
    outs = (
        P("section", None, "wide", None),
        P("section", None, "wide", None),
        P("section", "wide"),
        P("section", "wide"),
        P("section", "wide", None),
        P("section", None, "wide"),
        P("section", "wide", None),
        P("section", "wide"),
        P("section", "wide"),
        P("section", "wide"),
        P("section", "wide", None),
        P("section", None),
        P("section", None, "wide"),
        P("section", "wide"),
    )
    return ins, outs


def solution(mesh):
    ins, outs = specs()
    body = on_device if mesh.shape["wide"] == HEADS else on_device_near
    return jax.shard_map(body, mesh=mesh, in_specs=ins, out_specs=outs, check_vma=False)
```

```python
import functools
import math

import jax
import jax.numpy as jnp
from jax import lax
from jax.experimental import pallas as pl
from jax.experimental.pallas import tpu as pltpu
from jax.sharding import PartitionSpec as P

D = 1152
HEADS = 16
HEAD_DIM = 72
FF = 4304
FFP = -(-FF // 256) * 256
SPLIT = 9 * 256
BLOCK = 128
IMG_BLOCKS = 6
EPSILON = 1e-06
MASKED_SCORE = -1e30
SCALE = 1.0 / math.sqrt(HEAD_DIM)
MESH = pl.DeviceIdType.MESH
BF = jnp.bfloat16
F32 = jnp.float32


def place():
    return lax.axis_index("section"), lax.axis_index("wide")


class Gather:
    def __init__(self, pieces, ins, outs, sems, twice=()):
        self.pieces, self.ins, self.outs, self.count, self.twice = pieces, ins, outs, len(pieces), twice
        self.local_sem = sems[0]
        self.up, self.down, self.yy, self.cc = [(sems[1 + 2 * i], sems[2 + 2 * i]) for i in range(4)]
        self.sec, self.me = place()
        self.z, self.low = self.me // 4, self.me % 4
        self.other_y = self.me - self.low + flip(self.low, 2)
        self.other_c = self.me - self.low + flip(self.low, 1)

    @staticmethod
    def semaphores(pieces, arrays):
        dma = pltpu.SemaphoreType.DMA
        return [dma((arrays,))] + [dma((pieces, 8))] * 4 + [dma((pieces, 4))] * 2 + [dma((pieces, 8))] * 2

    def part(self, piece, origin=None):
        array, at, end = self.pieces[piece]
        return self.ins[array].at[:, at:end] if origin is None else self.outs[array].at[origin, :, at:end]

    def send(self, piece, origin, sems, slot, target, first=False):
        return pltpu.make_async_remote_copy(
            src_ref=self.part(piece) if first else self.part(piece, origin),
            dst_ref=self.part(piece, origin),
            send_sem=sems[0].at[piece, slot],
            recv_sem=sems[1].at[piece, slot],
            device_id=(self.sec, target),
            device_id_type=MESH,
        )

    def mine(self, array):
        return pltpu.make_async_copy(self.ins[array], self.outs[array].at[self.me], self.local_sem.at[array])

    def along(self, piece, origin, first, go_up, go_down, column=0):
        slot = origin // 4 + 4 * column
        if go_up:

            @pl.when(self.z < 3)
            def _():
                self.send(piece, origin, self.up, slot, self.me + 4, first).start()

        if go_down:

            @pl.when(self.z > 0)
            def _():
                self.send(piece, origin, self.down, slot, self.me - 4, first).start()

        if piece not in self.twice or first:
            self.send(piece, origin, self.yy, origin // 4, self.other_y, first).start()
        self.send(piece, origin, self.cc, slot, self.other_c, first).start()

    def columns(self, piece):
        return (0, 1) if piece in self.twice else (0,)

    def step(self, piece, step):
        if step == 1 and piece in self.twice:
            self.send(piece, self.other_y, self.yy, self.z, self.other_y).wait_recv()
            self.along(piece, self.other_y, False, True, True, 1)

        @pl.when(self.z - step >= 0)
        def _():
            for column in self.columns(piece):
                origin = (self.me, self.other_y)[column] - 4 * step
                self.send(piece, origin, self.up, self.z - step + 4 * column, self.me).wait_recv()
                self.along(piece, origin, False, True, False, column)

        @pl.when(self.z + step <= 3)
        def _():
            for column in self.columns(piece):
                origin = (self.me, self.other_y)[column] + 4 * step
                self.send(piece, origin, self.down, self.z + step + 4 * column, self.me).wait_recv()
                self.along(piece, origin, False, False, True, column)

    def slots(self, first, last):
        for k in range(first, last):
            if k == 0:
                for array in range(len(self.ins)):
                    self.mine(array).start()
            if k < self.count:
                self.along(k, self.me, True, True, True)
            for step in range(1, 4):
                if 0 <= k - step < self.count:
                    self.step(k - step, step)

    def across(self, pieces):
        far = self.other_y % 4
        for piece in pieces:
            for step in range(0 if piece in self.twice else 4):
                zo = (self.z + step) % 4
                origin = zo * 4 + far
                self.send(piece, origin, self.yy, zo, self.other_y).wait_recv()
                self.send(piece, origin, self.cc, 4 + zo, self.other_c).start()

    def arrived(self, pieces):
        for piece in pieces:
            for slot in range(8):
                self.send(piece, self.me, self.cc, slot, self.other_c).wait_recv()

    def finish(self):
        for zo in range(4):
            for piece in range(self.count):
                if piece not in self.twice:
                    self.send(piece, self.me, self.yy, zo, self.other_y).wait_send()
                elif zo == 0:
                    self.send(piece, self.me, self.yy, self.z, self.other_y).wait_send()
                for slot in (zo, 4 + zo):
                    self.send(piece, self.me, self.cc, slot, self.other_c).wait_send()

                @pl.when((zo <= self.z) & (self.z < 3))
                def _():
                    for column in self.columns(piece):
                        self.send(piece, self.me, self.up, zo + 4 * column, self.me).wait_send()

                @pl.when((zo >= self.z) & (self.z > 0))
                def _():
                    for column in self.columns(piece):
                        self.send(piece, self.me, self.down, zo + 4 * column, self.me).wait_send()


def flip(low, k):
    return [low, low + 1 - 2 * (low % 2), (low + 2) % 4, 3 - low][k]


def greet_all(count, sec, me):
    barrier = pltpu.get_barrier_semaphore()
    for d in range(1, count):
        pl.semaphore_signal(barrier, inc=1, device_id=(sec, (me + d) % count), device_id_type=MESH)
    pl.semaphore_wait(barrier, count - 1)


class Whole:
    def __init__(self, zero, one, cols=None):
        self.sources, self.cols = (zero, one), cols

    def shape(self):
        rows, cols = self.sources[0].shape
        return (4, rows, cols if self.cols is None else self.cols[1] - self.cols[0])

    def source(self, ref, low, k):
        return ref if self.cols is None else ref.at[:, self.cols[0] : self.cols[1]]

    forwarded = True


class Rows:
    def __init__(self, zero, one):
        self.sources = (zero, one)

    def shape(self):
        return self.sources[0].shape

    def source(self, ref, low, k):
        return ref.at[flip(low, k)]

    forwarded = False


class PlaneCopies:
    def __init__(self, item, zero_ref, one_ref, slot, local_sem, send_sem, recv_sem):
        self.item, self.refs, self.slot = item, (zero_ref, one_ref), slot
        self.local_sem, self.send_sem, self.recv_sem = local_sem, send_sem, recv_sem
        self.sec, self.me = place()
        self.low = self.me % 4

    def remote(self, src, k, to):
        return pltpu.make_async_remote_copy(
            src_ref=src,
            dst_ref=self.slot(k),
            send_sem=self.send_sem.at[k],
            recv_sem=self.recv_sem.at[k],
            device_id=(self.sec, self.me - self.low + flip(self.low, to)),
            device_id_type=MESH,
        )

    def local(self, ref):
        return pltpu.make_async_copy(self.item.source(ref, self.low, 0), self.slot(0), self.local_sem)

    def start(self):
        def go(ref):
            self.local(ref).start()
            for k in (2, 1) if self.item.forwarded else (2, 3, 1):
                self.remote(self.item.source(ref, self.low, k), k, k).start()

        @pl.when(self.sec == 0)
        def _():
            go(self.refs[0])

        @pl.when(self.sec == 1)
        def _():
            go(self.refs[1])

    def forward(self):
        if self.item.forwarded:
            self.remote(self.slot(2), 2, 2).wait_recv()
            self.remote(self.slot(2), 3, 1).start()

    def finish(self):
        self.local(self.refs[0]).wait()
        for k in (1, 2, 3):
            self.remote(self.slot(k), k, k).wait_send()
            if k != 2 or not self.item.forwarded:
                self.remote(self.slot(k), k, k).wait_recv()


def dot(a, b):
    return jnp.dot(a, b, preferred_element_type=F32)


def window(image_of_block):
    micro, blocks = image_of_block.shape
    own, other = image_of_block[:, :, None], image_of_block[:, None, :]
    begin = jnp.sum((other < own).astype(jnp.int32), axis=2)
    end = jnp.sum((other <= own).astype(jnp.int32), axis=2)
    first = jnp.minimum(begin, blocks - IMG_BLOCKS)
    shape = (micro, blocks, IMG_BLOCKS, BLOCK)
    at = first[:, :, None, None] + lax.broadcasted_iota(jnp.int32, shape, 2)
    same = (at >= begin[:, :, None, None]) & (at < end[:, :, None, None])
    return first, jnp.where(same, 0.0, MASKED_SCORE).astype(F32)


def near_rows(ref, start):
    return jnp.concatenate([ref[start + j] for j in range(IMG_BLOCKS)], axis=0)


def near_columns(ref, start):
    return jnp.concatenate([ref[start + j] for j in range(IMG_BLOCKS)], axis=1)


def fetch(pairs, buffers, sems, sec):
    for which in range(2):

        @pl.when(sec == which)
        def _():
            for i, buffer in enumerate(buffers):
                pltpu.make_async_copy(pairs[2 * i + which], buffer, sems.at[i]).start()


def fetched(pairs, buffers, sems):
    for i, buffer in enumerate(buffers):
        pltpu.make_async_copy(pairs[2 * i], buffer, sems.at[i]).wait()


class ToAll:
    def __init__(self, block, dst, send, recv, sec, me, count):
        self.block, self.dst, self.send, self.recv = block, dst, send, recv
        self.sec, self.me, self.count = sec, me, count

    def copy(self, d):
        return pltpu.make_async_remote_copy(
            src_ref=self.block(d),
            dst_ref=self.dst.at[self.me],
            send_sem=self.send.at[d],
            recv_sem=self.recv.at[d],
            device_id=(self.sec, (self.me + d) % self.count),
            device_id_type=MESH,
        )

    def start(self):
        for d in sorted(range(1, self.count), key=lambda d: abs(d - self.count // 2)):
            self.copy(d).start()

    def start_one(self, d):
        @pl.when(d > 0)
        def _():
            self.copy(d).start()

    def wait(self):
        for d in range(1, self.count):
            self.copy(d).wait()


class Forward:
    def __init__(self, tick, near, x_ref, outs, scratch):
        self.first_ref, self.bias_ref = near
        self.x_ref = x_ref
        self.qkv_ref, self.lse_ref, self.att_ref = outs
        self.k_all, self.vt_all, self.o_buf, self.local_sem, *sems = scratch
        self.count = x_ref.shape[0]
        sec, self.me = place()
        self.slot = jnp.minimum(jnp.maximum(tick - sec, 0), 1)
        rest = (sec, self.me, self.count)
        self.arrive = ToAll(lambda d: x_ref.at[(self.me + d) % self.count], self.qkv_ref, *sems[:2], *rest)
        self.leave = ToAll(lambda d: self.o_buf.at[d], self.att_ref, *sems[2:], *rest)

    @staticmethod
    def scratch(blocks):
        dma = pltpu.SemaphoreType.DMA
        return [
            pltpu.VMEM((blocks, BLOCK, HEAD_DIM), BF),
            pltpu.VMEM((blocks, HEAD_DIM, BLOCK), BF),
            pltpu.VMEM((blocks, HEAD_DIM, BLOCK), BF),
            dma,
        ] + [dma((blocks,))] * 4

    @staticmethod
    def shapes(blocks):
        return [
            jax.ShapeDtypeStruct((blocks, 3 * HEAD_DIM, BLOCK), BF),
            jax.ShapeDtypeStruct((blocks, 1, BLOCK), F32),
            jax.ShapeDtypeStruct((blocks, HEAD_DIM, BLOCK), BF),
        ]

    def own(self):
        return pltpu.make_async_copy(self.x_ref.at[self.me], self.qkv_ref.at[self.me], self.local_sem)

    def start(self):
        self.arrive.start()
        self.own().start()

    def wait_in(self):
        self.own().wait()
        self.arrive.wait()

    def compute(self):
        def arrange(j, carry):
            part = self.qkv_ref[j].astype(F32)
            self.k_all[j] = part[HEAD_DIM : 2 * HEAD_DIM].T.astype(BF)
            self.vt_all[j] = part[2 * HEAD_DIM :].astype(BF)
            return carry

        lax.fori_loop(0, self.count, arrange, 0)

        def one_block(d, carry):
            i = (self.me + d) % self.count
            start = self.first_ref[self.slot, i]
            qt = self.qkv_ref[i].astype(F32)[:HEAD_DIM].astype(BF)
            s = dot(near_rows(self.k_all, start), qt) * SCALE
            bias = self.bias_ref[self.slot, i]
            parts = [s[j * BLOCK : (j + 1) * BLOCK] + bias[j : j + 1] for j in range(IMG_BLOCKS)]
            top = parts[0]
            for part in parts[1:]:
                top = jnp.maximum(top, part)
            top = jnp.max(top, axis=0, keepdims=True)
            exps = [jnp.exp(part - top) for part in parts]
            total = exps[0]
            for part in exps[1:]:
                total = total + part
            total = jnp.sum(total, axis=0, keepdims=True)
            e = jnp.concatenate([part.astype(BF) for part in exps], axis=0)
            o = dot(near_columns(self.vt_all, start), e)
            self.o_buf[d] = (o / total).astype(BF)
            self.lse_ref[i] = top + jnp.log(total)
            self.leave.start_one(d)
            return carry

        lax.fori_loop(0, self.count, one_block, 0)
        self.att_ref[self.me] = self.o_buf[0]

    def wait_out(self):
        self.leave.wait()


class Backward:
    def __init__(self, tick, near, kept, x_ref, outs, scratch):
        self.first_ref, self.bias_ref = near
        self.kept, self.x_ref = kept, x_ref
        self.dq_ref, self.dkv_ref = outs
        self.qkv_ref, self.lse_ref, self.do_ref = scratch[:3]
        self.k_all, self.kt_all, self.v_all, self.q_all, self.do_all, self.p_all, self.s_all = scratch[3:10]
        self.dq_buf, self.dkv_buf, self.kept_sem, self.local_sem = scratch[10:14]
        sems = scratch[14:]
        self.count = x_ref.shape[0]
        self.sec, self.me = place()
        self.slot = jnp.minimum(jnp.maximum(tick - 1 + self.sec, 0), 1)
        rest = (self.sec, self.me, self.count)
        self.arrive = ToAll(lambda d: x_ref.at[(self.me + d) % self.count], self.do_ref, *sems[:2], *rest)
        self.leave_q = ToAll(lambda d: self.dq_buf.at[d], self.dq_ref, *sems[2:4], *rest)
        self.leave_kv = ToAll(lambda d: self.dkv_buf.at[d], self.dkv_ref, *sems[4:], *rest)

    @staticmethod
    def scratch(blocks):
        dma = pltpu.SemaphoreType.DMA
        return [
            pltpu.VMEM((blocks, 3 * HEAD_DIM, BLOCK), BF),
            pltpu.VMEM((blocks, 1, BLOCK), F32),
            pltpu.VMEM((blocks, HEAD_DIM, BLOCK), BF),
            pltpu.VMEM((blocks, BLOCK, HEAD_DIM), BF),
            pltpu.VMEM((blocks, HEAD_DIM, BLOCK), BF),
            pltpu.VMEM((blocks, BLOCK, HEAD_DIM), BF),
            pltpu.VMEM((blocks, BLOCK, HEAD_DIM), BF),
            pltpu.VMEM((blocks, BLOCK, HEAD_DIM), BF),
            pltpu.VMEM((blocks, IMG_BLOCKS, BLOCK, BLOCK), BF),
            pltpu.VMEM((blocks, IMG_BLOCKS, BLOCK, BLOCK), BF),
            pltpu.VMEM((blocks, HEAD_DIM, BLOCK), BF),
            pltpu.VMEM((blocks, 2 * HEAD_DIM, BLOCK), BF),
            dma((2,)),
            dma,
        ] + [dma((blocks,))] * 6

    def own(self):
        return pltpu.make_async_copy(self.x_ref.at[self.me], self.do_ref.at[self.me], self.local_sem)

    def start(self):
        self.arrive.start()
        self.own().start()
        fetch(self.kept, (self.qkv_ref, self.lse_ref), self.kept_sem, self.sec)

    def arrange(self):
        fetched(self.kept, (self.qkv_ref, self.lse_ref), self.kept_sem)

        def one(j, carry):
            part = self.qkv_ref[j].astype(F32)
            self.q_all[j] = part[:HEAD_DIM].T.astype(BF)
            self.k_all[j] = part[HEAD_DIM : 2 * HEAD_DIM].T.astype(BF)
            self.v_all[j] = part[2 * HEAD_DIM :].T.astype(BF)
            self.kt_all[j] = part[HEAD_DIM : 2 * HEAD_DIM].astype(BF)
            return carry

        lax.fori_loop(0, self.count, one, 0)

    def wait_in(self):
        self.own().wait()
        self.arrive.wait()

    def by_query(self):
        def turn(j, carry):
            self.do_all[j] = self.do_ref[j].astype(F32).T.astype(BF)
            return carry

        lax.fori_loop(0, self.count, turn, 0)

        def one(d, carry):
            i = (self.me + d) % self.count
            start = self.first_ref[self.slot, i]
            qt = self.qkv_ref[i].astype(F32)[:HEAD_DIM].astype(BF)
            s = dot(near_rows(self.k_all, start), qt) * SCALE
            shift = self.bias_ref[self.slot, i] - self.lse_ref[i]
            probs = [jnp.exp(s[j * BLOCK : (j + 1) * BLOCK] + shift[j : j + 1]) for j in range(IMG_BLOCKS)]
            dp = dot(near_rows(self.v_all, start), self.do_ref[i])
            total = probs[0] * dp[:BLOCK]
            for j in range(1, IMG_BLOCKS):
                total = total + probs[j] * dp[j * BLOCK : (j + 1) * BLOCK]
            total = jnp.sum(total, axis=0, keepdims=True)
            ds = jnp.concatenate(
                [(probs[j] * (dp[j * BLOCK : (j + 1) * BLOCK] - total)).astype(BF) for j in range(IMG_BLOCKS)], axis=0
            )
            for j in range(IMG_BLOCKS):
                self.p_all[i, j] = probs[j].astype(BF)
                self.s_all[i, j] = ds[j * BLOCK : (j + 1) * BLOCK]
            self.dq_buf[d] = (dot(near_columns(self.kt_all, start), ds) * SCALE).astype(BF)
            self.leave_q.start_one(d)
            return carry

        lax.fori_loop(0, self.count, one, 0)
        self.dq_ref[self.me] = self.dq_buf[0]

    def by_key(self):
        def one(d, carry):
            j = (self.me + d) % self.count
            start = self.first_ref[self.slot, j]
            place_in = jnp.clip(j - start, 0, IMG_BLOCKS - 1)
            same = (self.bias_ref[self.slot, j] == 0.0).astype(F32).astype(BF)
            p, ds = [], []
            for m in range(IMG_BLOCKS):
                p.append(self.p_all[start + m, place_in] * same[m : m + 1])
                ds.append(self.s_all[start + m, place_in] * same[m : m + 1])
            dv = dot(jnp.concatenate(p, axis=1), near_rows(self.do_all, start))
            dk = dot(jnp.concatenate(ds, axis=1), near_rows(self.q_all, start)) * SCALE
            self.dkv_buf[d] = jnp.concatenate([dk.T, dv.T], axis=0).astype(BF)
            self.leave_kv.start_one(d)
            return carry

        lax.fori_loop(0, self.count, one, 0)
        self.dkv_ref[self.me] = self.dkv_buf[0]

    def wait_out(self):
        self.leave_q.wait()
        self.leave_kv.wait()


def attention_kernel(ahead, behind, items, *refs):
    refs = list(refs)

    def take(n):
        part = refs[:n]
        del refs[:n]
        return part

    n = len(items)
    near = take(2)
    x_ref = take(1) if ahead is not None else None
    kept, g_ref = (take(4), take(1)) if behind is not None else (None, None)
    sources = take(2 * n)
    ahead_out = take(3) if ahead is not None else None
    behind_out = take(2) if behind is not None else None
    outs = take(n)
    f = b = None
    blocks = (x_ref or g_ref)[0].shape[0]
    sec, me = place()
    if ahead is not None:
        f = Forward(ahead, near, x_ref[0], ahead_out, take(len(Forward.scratch(blocks))))
    if behind is not None:
        b = Backward(behind, near, kept, g_ref[0], behind_out, take(len(Backward.scratch(blocks))))
    copies = []
    for i, item in enumerate(items):
        into = lambda k, i=i: outs[i].at[k]
        copies.append(PlaneCopies(item, sources[2 * i], sources[2 * i + 1], into, *take(3)))
    greet_all(blocks, sec, me)

    if b:
        b.start()
        b.arrange()
        b.wait_in()
    if f:
        f.start()
    if f and not b:
        f.wait_in()
    for copy in copies:
        copy.start()
    if b:
        b.by_query()
        b.by_key()
    if f and b:
        f.wait_in()
    if f:
        f.compute()
    for copy in copies:
        copy.forward()
    if f:
        f.wait_out()
    if b:
        b.wait_out()
    for copy in copies:
        copy.finish()


def attention(near, cid, ahead=None, behind=None, items=()):
    first_in = ahead[1] if ahead else behind[1]
    blocks = first_in.shape[0]
    n = len(items)
    sources = [source for item in items for source in item.sources]
    anywhere, vmem, smem = [pl.BlockSpec(memory_space=m) for m in (pl.ANY, pltpu.VMEM, pltpu.SMEM)]
    dma = pltpu.SemaphoreType.DMA
    args, scratch, shapes = [], [], []
    if ahead:
        args.append(ahead[1])
        scratch += Forward.scratch(blocks)
        shapes += Forward.shapes(blocks)
    if behind:
        args += [*behind[2], behind[1]]
        scratch += Backward.scratch(blocks)
        shapes += [
            jax.ShapeDtypeStruct((blocks, HEAD_DIM, BLOCK), BF),
            jax.ShapeDtypeStruct((blocks, 2 * HEAD_DIM, BLOCK), BF),
        ]
    args += sources
    scratch += [dma, dma((4,)), dma((4,))] * n
    in_vmem = len(shapes)
    shapes += [jax.ShapeDtypeStruct(item.shape(), BF) for item in items]
    out = pl.pallas_call(
        functools.partial(attention_kernel, ahead and ahead[0], behind and behind[0], list(items)),
        out_shape=shapes,
        in_specs=[smem, vmem] + [anywhere] * len(args),
        out_specs=[vmem] * in_vmem + [anywhere] * n,
        scratch_shapes=scratch,
        compiler_params=pltpu.CompilerParams(collective_id=cid, has_side_effects=True, vmem_limit_bytes=60 << 20),
    )(*near, *args)
    out = list(out)
    three, out = (out[:3], out[3:]) if ahead else (None, out)
    two, out = (out[:2], out[2:]) if behind else (None, out)
    return three, two, out


def slices(width, step=1024):
    return [(at, min(at + step, width)) for at in range(0, width, step)]


class Stream:
    def __init__(self, pairs, sems):
        self.copies = {}
        for i, (name, ref, buf, cols) in enumerate(pairs):
            src, dst = ref.at[:, cols[0] : cols[1]], buf.at[:, cols[0] : cols[1]]
            self.copies[name, cols[0]] = pltpu.make_async_copy(src, dst, sems.at[i])

    def start(self):
        for copy in self.copies.values():
            copy.start()

    def wait(self, name, at):
        self.copies[name, at].wait()


def normalised(x):
    mean = jnp.mean(x, axis=-1, keepdims=True)
    centred = x - mean
    rstd = lax.rsqrt(jnp.mean(centred * centred, axis=-1, keepdims=True) + EPSILON)
    return centred * rstd, rstd


def norm_backward(grad, xhat, rstd, gain):
    g = grad * gain
    part = g - jnp.mean(g, axis=-1, keepdims=True) - xhat * jnp.mean(g * xhat, axis=-1, keepdims=True)
    return part * rstd, jnp.sum(grad * xhat, axis=0, keepdims=True), jnp.sum(grad, axis=0, keepdims=True)


def greet_plane(sec, me):
    barrier = pltpu.get_barrier_semaphore()
    low = me % 4
    for k in range(1, 4):
        pl.semaphore_signal(barrier, inc=1, device_id=(sec, me - low + flip(low, k)), device_id_type=MESH)
    pl.semaphore_wait(barrier, 3)


class Load:
    def __init__(self, items):
        self.items = list(items)
        self.sources = [source for item in items for source in item.sources]
        self.shapes = [jax.ShapeDtypeStruct(item.shape(), BF) for item in items]
        dma = pltpu.SemaphoreType.DMA
        self.scratch = [dma, dma((4,)), dma((4,))] * len(self.items)

    def begin(self, sources, outs, sems):
        copies = []
        if self.items:
            greet_plane(*place())
        for i, item in enumerate(self.items):
            into = lambda k, i=i: outs[i].at[k]
            copies.append(PlaneCopies(item, sources[2 * i], sources[2 * i + 1], into, *sems[3 * i : 3 * i + 3]))
            copies[-1].start()
        return copies


def gelu_tanh(v):
    c = math.sqrt(2.0 / math.pi)
    return 0.5 * v * (1.0 + jnp.tanh(c * (v + 0.044715 * (v * v * v))))


def gelu_slope(v):
    c = math.sqrt(2.0 / math.pi)
    square = v * v
    t = jnp.tanh(c * (v + 0.044715 * (square * v)))
    return 0.5 * (1.0 + t) + 0.5 * v * (1.0 - t * t) * (c * (1.0 + 3 * 0.044715 * square))


def nt(a, b):
    return lax.dot_general(a, b, (((1,), (1,)), ((), ())), preferred_element_type=F32)


def put_owners(ref, x):
    turned = x.T
    for w in range(HEADS):
        ref[w % 4, w // 4] = turned[w * HEAD_DIM : (w + 1) * HEAD_DIM].astype(BF)


GAIN1, BIAS1, OUT_BIAS, GAIN2, BIAS2, FC2_BIAS = 0, 1, 4, 5, 6, 7


def row(vec_ref, i):
    return vec_ref[i : i + 1, :]


def pick(sec, zero_ref, one_ref):
    return jnp.where(sec == 0, zero_ref[...].astype(F32), one_ref[...].astype(F32))


def qkv_kernel(tok_ref, inc_ref, vec_ref, bias_ref, w_ref, qkv_ref, n1_ref, w_buf, t_buf, sems):
    sec, _ = place()
    stream = Stream([("w", w_ref, w_buf, cols) for cols in slices(3 * D, 384)], sems)
    stream.start()
    xhat, _ = normalised(pick(sec, tok_ref, inc_ref))
    n1 = xhat * row(vec_ref, GAIN1) + row(vec_ref, BIAS1)
    low = n1.astype(BF)
    for at, end in slices(3 * D, 384):
        stream.wait("w", at)
        t_buf[at:end, :] = (dot(low, w_buf[:, at:end]) + bias_ref[:, at:end]).T
    for h in range(HEADS):
        parts = [t_buf[p * D + h * HEAD_DIM : p * D + (h + 1) * HEAD_DIM, :] for p in range(3)]
        qkv_ref[h] = jnp.concatenate(parts, axis=0).astype(BF)
    put_owners(n1_ref, low.astype(F32))


def qkv_forward(tok, inc, vec, bias, w):
    tokens = tok.shape[0]
    anywhere, vmem = pl.BlockSpec(memory_space=pl.ANY), pl.BlockSpec(memory_space=pltpu.VMEM)
    return pl.pallas_call(
        qkv_kernel,
        out_shape=[
            jax.ShapeDtypeStruct((HEADS, 3 * HEAD_DIM, tokens), BF),
            jax.ShapeDtypeStruct((4, 4, HEAD_DIM, tokens), BF),
        ],
        in_specs=[vmem] * 4 + [anywhere],
        out_specs=[vmem] * 2,
        scratch_shapes=[
            pltpu.VMEM((D, 3 * D), BF),
            pltpu.VMEM((3 * D, tokens), F32),
            pltpu.SemaphoreType.DMA((len(slices(3 * D, 384)),)),
        ],
        compiler_params=pltpu.CompilerParams(vmem_limit_bytes=60 << 20),
    )(tok, inc, vec, bias, w)


def first_kernel(first_ref, bias_ref, tok_ref, *refs):
    refs = list(refs)

    def take(n):
        part = refs[:n]
        del refs[:n]
        return part

    shards = take(5)
    ahead_out = take(3)
    n1_ref, small_all, w_qkv = take(3)
    whole = take(3)
    w_buf, t_buf, x_buf, w_sem = take(4)
    f = Forward(0, (first_ref, bias_ref), x_buf, ahead_out, take(len(Forward.scratch(HEADS))))
    work = Gather(first_pieces(shards), shards, (w_buf, small_all, *whole), take(9), TWICE)
    soon, later = [list(range(SOON)), list(range(SOON, work.count))]
    sec, me = place()
    greet_all(HEADS, sec, me)
    work.slots(0, 1)
    xhat, _ = normalised(tok_ref[...].astype(F32))
    xhat = xhat.T
    work.slots(1, SOON + 3)
    for array in range(len(shards)):
        work.mine(array).wait()
    work.across(soon)
    work.arrived(soon)
    keep = pltpu.make_async_copy(w_buf, w_qkv, w_sem)
    keep.start()
    work.slots(SOON + 3, SOON + 4)
    small = jnp.concatenate([small_all[w].astype(F32) for w in range(HEADS)], axis=0)
    n1 = (xhat * small[:, 0:1] + small[:, 1:2]).astype(BF).astype(F32)
    for w in range(HEADS):
        n1_ref[w % 4, w // 4] = n1[w * HEAD_DIM : (w + 1) * HEAD_DIM].astype(BF)
    low = n1.T.astype(BF)

    def columns(i, carry):
        here = pl.ds(pl.multiple_of(i * 384, 384), 384)
        w = jnp.concatenate([w_buf[shard, :, here].astype(F32) for shard in range(HEADS)], axis=0)
        t_buf[here, :] = dot(low, w.astype(BF)).T
        return carry

    lax.fori_loop(0, 3 * D // 384, columns, 0)
    for h in range(HEADS):
        rows = slice(h * HEAD_DIM, (h + 1) * HEAD_DIM)
        parts = [t_buf[p * D + h * HEAD_DIM : p * D + (h + 1) * HEAD_DIM, :] for p in range(3)]
        parts = [parts[0] + small[rows, 2:3], parts[1], parts[2] + small[rows, 3:4]]
        x_buf[h] = jnp.concatenate(parts, axis=0).astype(BF)
    f.start()
    work.slots(SOON + 4, SOON + 5)
    f.wait_in()
    work.slots(SOON + 5, SOON + 7)
    f.compute()
    work.slots(SOON + 7, work.count + 3)
    f.wait_out()
    work.across(later)
    work.arrived(later)
    work.finish()
    keep.wait()


SOON = 4
TWICE = (4,)


def first_pieces(shards):
    pieces = [(1, 0, BLOCK)]
    for array in (0, 2, 3, 4):
        pieces += [(array, at, end) for at, end in slices(shards[array].shape[1], D)]
    return pieces


def first_tick(near, tok, shards, cid):
    tokens = tok.shape[0]
    anywhere, vmem, smem = [pl.BlockSpec(memory_space=m) for m in (pl.ANY, pltpu.VMEM, pltpu.SMEM)]
    whole = [jax.ShapeDtypeStruct((HEADS,) + shard.shape, BF) for shard in shards]
    return pl.pallas_call(
        first_kernel,
        out_shape=Forward.shapes(HEADS)
        + [jax.ShapeDtypeStruct((4, 4, HEAD_DIM, tokens), BF), whole[1], whole[0]]
        + whole[2:],
        in_specs=[smem, vmem, vmem] + [anywhere] * 5,
        out_specs=[vmem] * 5 + [anywhere] * 4,
        scratch_shapes=[
            pltpu.VMEM((HEADS,) + shards[0].shape, BF),
            pltpu.VMEM((3 * D, tokens), F32),
            pltpu.VMEM((HEADS, 3 * HEAD_DIM, tokens), BF),
            pltpu.SemaphoreType.DMA,
        ]
        + Forward.scratch(HEADS)
        + Gather.semaphores(len(first_pieces(shards)), len(shards)),
        compiler_params=pltpu.CompilerParams(collective_id=cid, has_side_effects=True, vmem_limit_bytes=60 << 20),
    )(*near, tok, *shards)


def greet_section(sec, me):
    barrier = pltpu.get_barrier_semaphore()
    pl.semaphore_signal(barrier, inc=1, device_id=(1 - sec, me), device_id_type=MESH)
    pl.semaphore_wait(barrier, 1)


def to_section(src, dst, send_sem, recv_sem, sec, me):
    return pltpu.make_async_remote_copy(
        src_ref=src, dst_ref=dst, send_sem=send_sem, recv_sem=recv_sem, device_id=(1 - sec, me), device_id_type=MESH
    )


def feed_kernel(shift, load, *refs):
    n = len(load.items)
    tok_ref, inc_ref, att_ref, vec_ref, bias_ref, out_w, fc1_w, fc2_w = refs[:8]
    sources, refs = refs[8 : 8 + 2 * n], refs[8 + 2 * n :]
    res_ref, pre_ref, hidden_ref, n2_ref, att_rows_ref, low_ref = refs[:6]
    refs = refs[6:]
    if shift:
        next_ref, refs = refs[0], refs[1:]
    outs, refs = refs[:n], refs[n:]
    refs, load_sems = refs[: len(refs) - 3 * n], refs[len(refs) - 3 * n :]
    out_buf, fc1_buf, fc2_buf, t_buf, sems = refs[:5]
    sec, me = place()
    pairs = [("out", out_w, out_buf, (0, D))]
    pairs += [("fc1", fc1_w, fc1_buf, cols) for cols in slices(FFP)]
    pairs += [("fc2", fc2_w, fc2_buf, cols) for cols in slices(FFP)]
    stream = Stream(pairs, sems)
    stream.start()
    if shift:
        greet_section(sec, me)
    taken = load.begin(sources, outs, load_sems)
    att = jnp.concatenate([att_ref[h].astype(F32) for h in range(HEADS)], axis=0).T.astype(BF)
    for w in range(HEADS):
        att_rows_ref[w % 4, w // 4] = att_ref[w]
    stream.wait("out", 0)
    residual = pick(sec, tok_ref, inc_ref) + dot(att, out_buf[...]) + row(vec_ref, OUT_BIAS)
    res_ref[...] = residual
    xhat, _ = normalised(residual)
    n2 = (xhat * row(vec_ref, GAIN2) + row(vec_ref, BIAS2)).astype(BF)
    total = None
    for at, end in slices(FFP):
        stream.wait("fc1", at)
        pre = dot(n2, fc1_buf[:, at:end]) + bias_ref[:, at:end]
        pre_ref[:, at:end] = pre
        hidden = gelu_tanh(pre)
        hidden_ref[:, at:end] = hidden.astype(BF)
        t_buf[at:end, :] = hidden.T.astype(BF)
    for at, end in slices(FFP):
        stream.wait("fc2", at)
    total = dot(fc2_buf[...], t_buf[...])
    low_ref[...] = (residual + total.T + row(vec_ref, FC2_BIAS)).astype(BF)
    if shift:
        copy = to_section(low_ref, next_ref, refs[5], refs[6], sec, me)
        copy.start()
    for one in taken:
        one.forward()
    put_owners(n2_ref, n2.astype(F32))
    if shift:
        copy.wait()
    for one in taken:
        one.finish()


def feed_forward(tok, inc, att, vec, bias, out_w, fc1_w, fc2_w, cid, shift, items=()):
    tokens = tok.shape[0]
    load = Load(items)
    anywhere, vmem = pl.BlockSpec(memory_space=pl.ANY), pl.BlockSpec(memory_space=pltpu.VMEM)
    dma = pltpu.SemaphoreType.DMA
    params = {} if cid is None else dict(collective_id=cid, has_side_effects=True)
    rows = jax.ShapeDtypeStruct((4, 4, HEAD_DIM, tokens), BF)
    low = jax.ShapeDtypeStruct((tokens, D), BF)
    return pl.pallas_call(
        functools.partial(feed_kernel, shift, load),
        out_shape=[
            jax.ShapeDtypeStruct((tokens, D), F32),
            jax.ShapeDtypeStruct((tokens, FFP), F32),
            jax.ShapeDtypeStruct((tokens, FFP), BF),
            rows,
            rows,
            low,
        ]
        + [low] * shift
        + load.shapes,
        in_specs=[vmem] * 5 + [anywhere] * (3 + len(load.sources)),
        out_specs=[vmem] * (6 + shift) + [anywhere] * len(load.shapes),
        scratch_shapes=[
            pltpu.VMEM((D, D), BF),
            pltpu.VMEM((D, FFP), BF),
            pltpu.VMEM((D, FFP), BF),
            pltpu.VMEM((FFP, tokens), BF),
            dma((1 + 2 * len(slices(FFP)),)),
        ]
        + [dma, dma] * shift
        + load.scratch,
        compiler_params=pltpu.CompilerParams(vmem_limit_bytes=60 << 20, **params),
    )(tok, inc, att, vec, bias, out_w, fc1_w, fc2_w, *load.sources)


def feed_back_kernel(load, cot_ref, inc_ref, vec_ref, *refs):
    n = len(load.items)
    kept, refs = refs[:4], refs[4:]
    out_w, fc1_w, fc2_w = refs[:3]
    sources, refs = refs[3 : 3 + 2 * n], refs[3 + 2 * n :]
    rg_ref, ag_ref, fc_ref, pg_ref, branch_ref, sum_ref, fsum_ref = refs[:7]
    outs, refs = refs[7 : 7 + n], refs[7 + n :]
    pre_buf, res_buf, out_buf, fc1_buf, fc2_buf, t_buf, kept_sem, sems = refs[:8]
    sec, _ = place()
    pairs = []
    pairs += [("fc2", fc2_w, fc2_buf, cols) for cols in slices(FFP)]
    pairs += [("fc1", fc1_w, fc1_buf, cols) for cols in slices(FFP)]
    pairs.append(("out", out_w, out_buf, (0, D)))
    stream = Stream(pairs, sems)
    fetch(kept, (pre_buf, res_buf), kept_sem, sec)
    stream.start()
    taken = load.begin(sources, outs, refs[8:])
    grad = jnp.where(sec == 0, inc_ref[...].astype(F32), cot_ref[...].astype(F32))
    fc_grad = grad.astype(BF)
    put_owners(fc_ref, grad)
    fetched(kept, (pre_buf, res_buf), kept_sem)
    total = None
    for at, end in slices(FFP):
        slope = gelu_slope(pre_buf[:, at:end])
        stream.wait("fc2", at)
        pre_wide = dot(fc_grad, fc2_buf[:, at:end]) * slope
        pre_grad = pre_wide.astype(BF)
        pg_ref[:, at:end] = pre_grad
        fsum_ref[:, at:end] = jnp.sum(pre_grad.astype(F32), axis=0, keepdims=True)
        t_buf[at:end, :] = pre_wide.T.astype(BF)
    for at, end in slices(FFP):
        stream.wait("fc1", at)
    total = dot(fc1_buf[...], t_buf[...])
    xhat, rstd = normalised(res_buf[...])
    part, gain_sum, bias_sum = norm_backward(total.T, xhat, rstd, row(vec_ref, GAIN2))
    residual_grad = grad + part
    rg_ref[...] = residual_grad
    branch = residual_grad.astype(BF)
    branch_ref[...] = branch
    for one in taken:
        one.forward()
    stream.wait("out", 0)
    att_grad = dot(out_buf[...], residual_grad.T.astype(BF))
    for h in range(HEADS):
        ag_ref[h] = att_grad[h * HEAD_DIM : (h + 1) * HEAD_DIM].astype(BF)
    sum_ref[0:1, :] = jnp.sum(branch.astype(F32), axis=0, keepdims=True)
    sum_ref[1:2, :] = gain_sum
    sum_ref[2:3, :] = bias_sum
    sum_ref[3:4, :] = jnp.sum(fc_grad.astype(F32), axis=0, keepdims=True)
    for one in taken:
        one.finish()


def feed_backward(cot, inc, vec, kept, out_w, fc1_w, fc2_w, cid, items=()):
    tokens = cot.shape[0]
    load = Load(items)
    params = {} if cid is None else dict(collective_id=cid, has_side_effects=True)
    anywhere, vmem = pl.BlockSpec(memory_space=pl.ANY), pl.BlockSpec(memory_space=pltpu.VMEM)
    dma = pltpu.SemaphoreType.DMA
    return pl.pallas_call(
        functools.partial(feed_back_kernel, load),
        out_shape=[
            jax.ShapeDtypeStruct((tokens, D), F32),
            jax.ShapeDtypeStruct((HEADS, HEAD_DIM, tokens), BF),
            jax.ShapeDtypeStruct((4, 4, HEAD_DIM, tokens), BF),
            jax.ShapeDtypeStruct((tokens, FFP), BF),
            jax.ShapeDtypeStruct((tokens, D), BF),
            jax.ShapeDtypeStruct((4, D), F32),
            jax.ShapeDtypeStruct((1, FFP), F32),
        ]
        + load.shapes,
        in_specs=[vmem] * 3 + [anywhere] * (7 + len(load.sources)),
        out_specs=[vmem] * 7 + [anywhere] * len(load.shapes),
        scratch_shapes=[
            pltpu.VMEM((tokens, FFP), F32),
            pltpu.VMEM((tokens, D), F32),
            pltpu.VMEM((D, D), BF),
            pltpu.VMEM((D, FFP), BF),
            pltpu.VMEM((D, FFP), BF),
            pltpu.VMEM((FFP, tokens), BF),
            dma((2,)),
            dma((1 + 2 * len(slices(FFP)),)),
        ]
        + load.scratch,
        compiler_params=pltpu.CompilerParams(vmem_limit_bytes=60 << 20, **params),
    )(cot, inc, vec, *kept, out_w, fc1_w, fc2_w, *load.sources)


def qkv_back_kernel(shift, load, *refs):
    n = len(load.items)
    tok_ref, inc_ref, vec_ref, rg_ref, dq_ref, dkv_ref, w_ref = refs[:7]
    sources, refs = refs[7 : 7 + 2 * n], refs[7 + 2 * n :]
    grad_ref, dqkv_ref, sum_ref, qsum_ref = refs[:4]
    refs = refs[4:]
    if shift:
        next_ref, refs = refs[0], refs[1:]
    outs, refs = refs[:n], refs[n:]
    refs, load_sems = refs[: len(refs) - 3 * n], refs[len(refs) - 3 * n :]
    w_buf, sems = refs[:2]
    sec, me = place()
    stream = Stream([("w", w_ref, w_buf, cols) for cols in slices(3 * D, 384)], sems)
    stream.start()
    if shift:
        greet_section(sec, me)
    taken = load.begin(sources, outs, load_sems)
    kv = [dkv_ref[h].astype(F32) for h in range(HEADS)]
    rows = [dq_ref[h].astype(F32) for h in range(HEADS)]
    rows += [part[:HEAD_DIM] for part in kv] + [part[HEAD_DIM:] for part in kv]
    dqkv = jnp.concatenate(rows, axis=0).astype(BF)
    dqkv_ref[...] = dqkv
    qsum_ref[...] = nt(jnp.ones((8, dqkv.shape[1]), BF), dqkv)
    total = None
    for at, end in slices(3 * D, 384):
        stream.wait("w", at)
        part = dot(w_buf[:, at:end], dqkv[at:end])
        total = part if total is None else total + part
    xhat, rstd = normalised(pick(sec, tok_ref, inc_ref))
    part, gain_sum, bias_sum = norm_backward(total.T, xhat, rstd, row(vec_ref, GAIN1))
    grad = rg_ref[...] + part
    grad_ref[...] = grad
    if shift:
        low_buf = refs[2]
        low_buf[...] = grad.astype(BF)
        copy = to_section(low_buf, next_ref, refs[3], refs[4], sec, me)
        copy.start()
    sum_ref[0:1, :] = gain_sum
    sum_ref[1:2, :] = bias_sum
    if shift:
        copy.wait()
    for one in taken:
        one.forward()
    for one in taken:
        one.finish()


def qkv_backward(tok, inc, vec, residual_grad, dq, dkv, w, cid, shift, items=()):
    tokens = tok.shape[0]
    load = Load(items)
    anywhere, vmem = pl.BlockSpec(memory_space=pl.ANY), pl.BlockSpec(memory_space=pltpu.VMEM)
    dma = pltpu.SemaphoreType.DMA
    params = {} if cid is None else dict(collective_id=cid, has_side_effects=True)
    return pl.pallas_call(
        functools.partial(qkv_back_kernel, shift, load),
        out_shape=[
            jax.ShapeDtypeStruct((tokens, D), F32),
            jax.ShapeDtypeStruct((3 * D, tokens), BF),
            jax.ShapeDtypeStruct((2, D), F32),
            jax.ShapeDtypeStruct((8, 3 * D), F32),
        ]
        + [jax.ShapeDtypeStruct((tokens, D), BF)] * shift
        + load.shapes,
        in_specs=[vmem] * 6 + [anywhere] * (1 + len(load.sources)),
        out_specs=[vmem] * (4 + shift) + [anywhere] * len(load.shapes),
        scratch_shapes=[pltpu.VMEM((D, 3 * D), BF), dma((len(slices(3 * D, 384)),))]
        + [pltpu.VMEM((tokens, D), BF), dma, dma] * shift
        + load.scratch,
        compiler_params=pltpu.CompilerParams(vmem_limit_bytes=60 << 20, **params),
    )(tok, inc, vec, residual_grad, dq, dkv, w, *load.sources)


def pad_ff(x):
    return jnp.pad(x, ((0, 0),) * (x.ndim - 1) + ((0, FFP - FF),))


TENSORS = ("fc2", "fc1", "out", "qkv")


def final_kernel(tiles, early, late, *refs):
    refs = list(refs)

    def take(n):
        part = refs[:n]
        del refs[:n]
        return part

    small_ref = take(1)[0]
    x_refs = {name: take(2) for name in TENSORS}
    early_refs = take(len(early))
    late_refs = take(2 * len(late))
    small_out = take(1)[0]
    out_refs = dict(zip(TENSORS, take(4)))
    y_bufs = dict(zip(TENSORS, take(4)))
    x_buf = take(1)[0]
    g_bufs, one_bufs, two_bufs = [dict(zip(TENSORS, take(4))) for _ in range(3)]
    small_got = take(1)[0]
    early_sem, small_send, small_recv = take(3)
    sems = {name: take(4) for name in TENSORS}
    late_sems = [take(3) for _ in late]

    sec, me = place()
    z, low = me // 4, me % 4
    pair = z + 1 - 2 * (z % 2)
    count = small_ref.shape[0]
    greet_all(count, sec, me)

    def begin(name):
        for other, one in behind:
            if other == name:
                one.start()

    loads = []
    for i, (name, batch, cols) in enumerate(early):
        dst = y_bufs[name].at[4 * batch : 4 * batch + 4]
        if cols is not None:
            dst = dst.at[:, :, cols[0] : cols[1]]
        loads.append((name, pltpu.make_async_copy(early_refs[i], dst, early_sem.at[i])))
        if name == "fc2":
            loads[-1][1].start()
    behind = []
    for i, (name, batch, item) in enumerate(late):

        def slot(k, name=name, batch=batch, item=item):
            ref = y_bufs[name].at[4 * batch + k]
            return ref if item.cols is None else ref.at[:, item.cols[0] : item.cols[1]]

        behind.append((name, PlaneCopies(item, late_refs[2 * i], late_refs[2 * i + 1], slot, *late_sems[i])))
    begin("fc1")
    smalls = []
    for d in range(1, count):
        target = (me + d) % count
        smalls.append(
            pltpu.make_async_remote_copy(
                src_ref=small_ref.at[target],
                dst_ref=small_got.at[d],
                send_sem=small_send.at[d],
                recv_sem=small_recv.at[d],
                device_id=(sec, target),
                device_id_type=MESH,
            )
        )
        smalls[-1].start()

    def first(name, i):
        send, recv = sems[name][0], sems[name][1]
        return pltpu.make_async_remote_copy(
            src_ref=g_bufs[name].at[i, 2:4],
            dst_ref=one_bufs[name].at[i],
            send_sem=send.at[i],
            recv_sem=recv.at[i],
            device_id=(sec, pair * 4 + low),
            device_id_type=MESH,
        )

    def second(name, i):
        send, recv = sems[name][2], sems[name][3]
        return pltpu.make_async_remote_copy(
            src_ref=g_bufs[name].at[i, 1],
            dst_ref=two_bufs[name].at[i],
            send_sem=send.at[i],
            recv_sem=recv.at[i],
            device_id=(sec, (3 - z) * 4 + low),
            device_id_type=MESH,
        )

    def ready(name):
        for other, one in behind:
            if other == name:
                one.forward()
        if name in ("fc1", "qkv"):
            begin({"fc1": "qkv", "qkv": "out"}[name])
        for other, load in loads:
            if other == name:
                load.wait()
            elif name == "fc2":
                load.start()
        for other, one in behind:
            if other == name:
                one.finish()
        rows = []
        for owner in (z, 3 - z, pair, 3 - pair):
            rows.append(
                jnp.concatenate(
                    [x_refs[name][batch][k, owner].astype(F32) for batch in range(2) for k in range(4)], axis=1
                )
            )
        x_buf[...] = jnp.concatenate(rows, axis=0).astype(BF)

    def columns(name, i):
        width = tiles[name][1]
        return pl.ds(pl.multiple_of(i * width, 128), width)

    def compute(name, i):
        width = tiles[name][1]
        buf = y_bufs[name]
        if name == "qkv":
            rows = pl.ds(pl.multiple_of(i * width, 128), width)
            y = jnp.concatenate([buf[part, rows, :] for part in range(8)], axis=1)
            total = lax.dot_general(x_buf[...], y, (((1,), (1,)), ((), ())), preferred_element_type=F32)
        else:
            y = jnp.concatenate([buf[part, :, columns(name, i)] for part in range(8)], axis=0)
            total = dot(x_buf[...], y)
        g_bufs[name][i] = total.reshape(4, HEAD_DIM, width).astype(BF)
        first(name, i).start()

    def middle(name, i):
        first(name, i).wait_recv()
        out_refs[name][:, columns(name, i)] = g_bufs[name][i, 0].astype(F32) + one_bufs[name][i, 0].astype(F32)
        g_bufs[name][i, 1] = (g_bufs[name][i, 1].astype(F32) + one_bufs[name][i, 1].astype(F32)).astype(BF)
        second(name, i).start()

    def finish(name, i):
        second(name, i).wait_recv()
        out_refs[name][:, columns(name, i)] += two_bufs[name][i].astype(F32)
        first(name, i).wait_send()
        second(name, i).wait_send()

    def loop(name, *steps):
        def body(i, carry):
            for step, which in steps:
                step(which, i)
            return carry

        lax.fori_loop(0, tiles[name][0], body, 0)

    ready("fc2")
    loop("fc2", (compute, "fc2"))
    ready("fc1")
    loop("fc1", (compute, "fc1"), (middle, "fc2"))
    loop("fc1", (middle, "fc1"), (finish, "fc2"))
    ready("qkv")
    loop("qkv", (compute, "qkv"))
    ready("out")
    loop("out", (compute, "out"))
    loop("fc1", (finish, "fc1"))
    loop("qkv", (middle, "qkv"))
    loop("out", (middle, "out"))
    for copy in smalls:
        copy.wait()
    total = small_ref[me]
    for d in range(1, count):
        total = total + small_got[d]
    small_out[...] = total
    loop("qkv", (finish, "qkv"))
    loop("out", (finish, "out"))


def final(small, xs, early, late, cid):
    count = small.shape[0]
    tokens = xs["qkv"][0].shape[-1]
    widths = {"fc2": FFP, "fc1": FFP, "out": D, "qkv": 3 * D}
    tiles = {name: (w // (256 if name[0] == "f" else 384), 256 if name[0] == "f" else 384) for name, w in widths.items()}
    anywhere, vmem = pl.BlockSpec(memory_space=pl.ANY), pl.BlockSpec(memory_space=pltpu.VMEM)
    args = [small] + [x for name in TENSORS for x in xs[name]]
    n_vmem = len(args)
    args += [e[3] for e in early] + [source for _, _, item in late for source in item.sources]
    dma = pltpu.SemaphoreType.DMA
    scratch = []
    for name in TENSORS:
        shape = (8, widths[name], tokens) if name == "qkv" else (8, tokens, widths[name])
        scratch.append(pltpu.VMEM(shape, BF))
    scratch.append(pltpu.VMEM((4 * HEAD_DIM, 8 * tokens), BF))
    for lead in ((4,), (2,), ()):
        for name in TENSORS:
            scratch.append(pltpu.VMEM((tiles[name][0],) + lead + (HEAD_DIM, tiles[name][1]), BF))
    scratch.append(pltpu.VMEM(small.shape, F32))
    scratch += [dma((len(early),)), dma((count,)), dma((count,))]
    for name in TENSORS:
        scratch += [dma((tiles[name][0],))] * 4
    scratch += [dma, dma((4,)), dma((4,))] * len(late)
    out = pl.pallas_call(
        functools.partial(final_kernel, tiles, [e[:3] for e in early], late),
        out_shape=[jax.ShapeDtypeStruct(small.shape[1:], F32)]
        + [jax.ShapeDtypeStruct((HEAD_DIM, widths[name]), F32) for name in TENSORS],
        in_specs=[vmem] * n_vmem + [anywhere] * (len(args) - n_vmem),
        out_specs=[vmem] * 5,
        scratch_shapes=scratch,
        compiler_params=pltpu.CompilerParams(
            collective_id=cid, has_side_effects=True, vmem_limit_bytes=60 << 20
        ),
    )(*args)
    return out[0], dict(zip(TENSORS, out[1:]))


def on_device(
    tokens,
    cotangent,
    image_of_block,
    ln1_gain,
    ln1_bias,
    qkv_weight,
    qv_bias,
    out_weight,
    out_bias,
    ln2_gain,
    ln2_bias,
    fc1_weight,
    fc1_bias,
    fc2_weight,
    fc2_bias,
):
    sec, me = place()
    small = jnp.stack(
        [ln1_gain[0], ln1_bias[0], qv_bias[0, 0], qv_bias[0, 1], out_bias[0], ln2_gain[0], ln2_bias[0], fc2_bias[0]],
        axis=1,
    )
    small = jnp.pad(small, ((0, 0), (0, BLOCK - 8)))
    near = window(image_of_block)
    shards = [qkv_weight[0], small, out_weight[0], pad_ff(fc1_weight[0]), pad_ff(fc2_weight[0].T)]
    *three, n1, small_all, w_qkv, w_out, w_fc1, w_fc2t = first_tick(near, tokens[0], shards, 2)
    w_qkv = w_qkv.reshape(D, 3 * D)
    w_out = w_out.reshape(D, D)
    w_fc1 = w_fc1.reshape(D, FFP)
    w_fc2t = w_fc2t.reshape(D, FFP)
    vec = small_all.reshape(D, BLOCK)[:, :8].T.astype(F32)
    b_qkv = jnp.concatenate([vec[2:3], jnp.zeros((1, D), F32), vec[3:4]], axis=1)
    b_fc1 = pad_ff(fc1_bias[0]).astype(F32).reshape(1, FFP)

    def choose(at_zero, at_one):
        return jnp.where(sec == 0, at_zero, at_one)

    saved, sent, back, done, input_grads = [], {}, [], [], []
    incoming = [tokens[0]]

    def token_inputs(tick):
        return tokens[min(tick, 1)], incoming[tick]

    def feed(tick, qkv, lse, att, n1, cid, shift, items=()):
        fed = feed_forward(*token_inputs(tick), att, vec, b_fc1, w_out, w_fc1, w_fc2t, cid, shift, items)
        saved.append(
            dict(qkv=qkv, lse=lse, n1=n1, residual=fed[0], pre=fed[1], hidden=fed[2], n2=fed[3], att=fed[4], low=fed[5])
        )
        return fed

    def kept(tick, *names):
        return [saved[at][name] for name in names for at in ((1, 1), (0, 2), (1, 1))[tick]]

    def feed_back(tick, incoming_grad, cid=None, items=()):
        residual_grad, att_grad, fc, pre, branch, four, fsum, *got = feed_backward(
            cotangent[min(tick, 1)], incoming_grad, vec, kept(tick, "pre", "residual"), w_out, w_fc1, w_fc2t, cid, items
        )
        back.append(dict(fc=fc, pre=pre, branch=branch))
        return residual_grad, att_grad, [*four, fsum], got

    def qkv_back(tick, residual_grad, dq, dkv, sums, cid, shift, items=()):
        inputs = (tokens[max(tick - 1, 0)], incoming[min(tick + 1, 2)])
        input_grad, dqkv, two, qsum, *rest = qkv_backward(
            *inputs, vec, residual_grad, dq, dkv, w_qkv, cid, shift, items
        )
        back[tick]["dqkv"] = dqkv
        input_grads.append(input_grad)
        done.append([two[0], two[1], qsum[0, :D], qsum[0, 2 * D :], *sums])
        return rest

    incoming.append(feed(0, *three, n1, 8, True)[6])

    qkv, n1 = qkv_forward(*token_inputs(1), vec, b_qkv, w_qkv)
    three, _, _ = attention(near, 3, ahead=(1, qkv))
    incoming.append(lax.ppermute(feed(1, *three, n1, None, False)[5], "section", [(0, 1)]))

    def first_batch(name, cols=None):
        return Whole(saved[0][name], saved[1][name], cols)

    def second_batch(name, cols=None):
        return Whole(saved[1][name], saved[2][name], cols)

    residual_grad, att_grad, sums, got = feed_back(0, tokens[0], 11, [first_batch("hidden", (SPLIT, FFP))])
    sent["h0b"] = got[0]
    qkv, n1 = qkv_forward(*token_inputs(2), vec, b_qkv, w_qkv)
    items = [Rows(saved[0][name], saved[1][name]) for name in ("n1", "att", "n2")]
    items.append(first_batch("hidden", (0, SPLIT)))
    three, two, got = attention(near, 4, ahead=(2, qkv), behind=(0, att_grad, kept(0, "qkv", "lse")), items=items)
    sent["n1_0"], sent["att_0"], sent["n2_0"], sent["h0a"] = got
    qkv_back(0, residual_grad, *two, sums, None, False)
    incoming_grad = lax.ppermute(input_grads[0].astype(BF), "section", [(1, 0)])
    feed(2, *three, n1, None, False)
    outputs = jnp.stack([choose(saved[m]["low"], saved[m + 1]["low"]) for m in range(2)])

    residual_grad, att_grad, sums, got = feed_back(1, incoming_grad, 12, [second_batch("hidden", (0, SPLIT))])
    sent["h1a"] = got[0]
    items = [Rows(saved[1][name], saved[2][name]) for name in ("n1", "att", "n2")]
    items.append(second_batch("hidden", (SPLIT, FFP)))
    _, two, got = attention(near, 5, behind=(1, att_grad, kept(1, "qkv", "lse")), items=items)
    sent["n1_1"], sent["att_1"], sent["n2_1"], sent["h1b"] = got
    incoming_grad = qkv_back(1, residual_grad, *two, sums, 9, True)[0]

    residual_grad, att_grad, sums, got = feed_back(
        2, incoming_grad, 13, [Whole(back[1]["pre"], back[0]["pre"], (0, SPLIT))]
    )
    sent["pre_0a"] = got[0]
    items = [Rows(back[1]["fc"], back[0]["fc"]), Rows(back[2]["fc"], back[1]["fc"])]
    items.append(Whole(back[1]["pre"], back[0]["pre"], (SPLIT, FFP)))
    _, two, got = attention(near, 6, behind=(2, att_grad, kept(2, "qkv", "lse")), items=items)
    sent["fc_0"], sent["fc_1"], sent["pre_0b"] = got
    qkv_back(2, residual_grad, *two, sums, None, False)
    input_grads = jnp.stack([choose(input_grads[m + 1], input_grads[m]) for m in range(2)])

    sums = [choose(done[1][i] + done[2][i], done[0][i] + done[1][i]) for i in range(9)]
    by_owner = jnp.stack(sums[:8]).reshape(8, HEADS, HEAD_DIM).transpose(1, 0, 2)
    by_owner = jnp.pad(by_owner, ((0, 0), (0, 0), (0, BLOCK - HEAD_DIM)))
    lines = FFP // BLOCK
    to_all = jnp.broadcast_to(sums[8].reshape(1, lines, BLOCK), (HEADS, lines, BLOCK))
    to_all = jnp.pad(to_all, ((0, 0), (0, 40 - lines), (0, 0)))
    xs = {
        "fc2": [sent["fc_0"], sent["fc_1"]],
        "fc1": [sent["n2_0"], sent["n2_1"]],
        "out": [sent["att_0"], sent["att_1"]],
        "qkv": [sent["n1_0"], sent["n1_1"]],
    }
    early = [
        ("fc2", 0, (0, SPLIT), sent["h0a"]),
        ("fc2", 0, (SPLIT, FFP), sent["h0b"]),
        ("fc2", 1, (0, SPLIT), sent["h1a"]),
        ("fc2", 1, (SPLIT, FFP), sent["h1b"]),
        ("fc1", 0, (0, SPLIT), sent["pre_0a"]),
        ("fc1", 0, (SPLIT, FFP), sent["pre_0b"]),
    ]
    late = [
        ("fc1", 1, Whole(back[2]["pre"], back[1]["pre"])),
        ("qkv", 0, Whole(back[1]["dqkv"], back[0]["dqkv"])),
        ("qkv", 1, Whole(back[2]["dqkv"], back[1]["dqkv"])),
        ("out", 0, Whole(back[1]["branch"], back[0]["branch"])),
        ("out", 1, Whole(back[2]["branch"], back[1]["branch"])),
    ]
    packed, grads = final(jnp.concatenate([by_owner, to_all], axis=1), xs, early, late, 10)
    g_small = packed[:8, :HEAD_DIM]
    g_fc1_bias = packed[8 : 8 + lines].reshape(FFP)[:FF]
    return (
        outputs[None],
        input_grads[None],
        g_small[0][None],
        g_small[1][None],
        grads["qkv"][None],
        g_small[2:4][None],
        grads["out"][None],
        g_small[4][None],
        g_small[5][None],
        g_small[6][None],
        grads["fc1"][:, :FF][None],
        g_fc1_bias[None],
        grads["fc2"].T[:FF][None],
        g_small[7][None],
    )


BLK_DEV = 1
REACH = 5


def shifted(value, axis, steps):
    count = lax.axis_size(axis)
    initial, last = (max(0, -steps), min(count, count - steps))
    return lax.ppermute(value, axis, [(source, source + steps) for source in range(initial, last)])


def layer_norm(values_in, scale_gain, shift_bias):
    row_mean = jnp.mean(values_in, axis=-1, keepdims=True)
    centred = values_in - row_mean
    row_var = jnp.mean(centred * centred, axis=-1, keepdims=True)
    return centred * lax.rsqrt(row_var + EPSILON) * scale_gain + shift_bias


def gelu_tanh(pre_value):
    return jax.nn.gelu(pre_value, approximate=True)


def heads_of(values_in):
    return values_in.reshape(values_in.shape[0], HEADS, HEAD_DIM)


def image_mask(image_of_block, batch_slot, wide_rank):
    padding = REACH * BLK_DEV
    padded = jnp.pad(image_of_block, ((0, 0), (padding, padding)), constant_values=-1)
    image_row = lax.dynamic_index_in_dim(padded, batch_slot, 0, keepdims=False)
    key_blocks = lax.dynamic_slice_in_dim(image_row, wide_rank * BLK_DEV, (2 * REACH + 1) * BLK_DEV)
    query_blocks = lax.dynamic_slice_in_dim(image_row, wide_rank * BLK_DEV + padding, BLK_DEV)
    return jnp.repeat(query_blocks, BLOCK)[:, None] == jnp.repeat(key_blocks, BLOCK)[None, :]


def keep_slot(buffer_all, new_value, batch_slot, is_live):
    previous = lax.dynamic_index_in_dim(buffer_all, batch_slot, 0, keepdims=False)
    chosen = jnp.where(is_live, new_value, previous)
    return lax.dynamic_update_index_in_dim(buffer_all, chosen, batch_slot, 0)


def near_keys(key_own, value_own, backward_pass):
    key_parts = []
    value_parts = []
    for offset in range(-REACH, REACH + 1):
        if offset == 0:
            received = (key_own, value_own)
        elif backward_pass:
            received = shifted((key_own, value_own), "wide", -offset)
        else:
            received = shifted((key_own, value_own), "wide", -offset)
        key_parts.append(received[0])
        value_parts.append(received[1])
    return (jnp.concatenate(key_parts, axis=0), jnp.concatenate(value_parts, axis=0))


def return_key_grads(key_terms, value_terms):
    row_count = key_terms.shape[0] // (2 * REACH + 1)
    key_total = key_terms[REACH * row_count : (REACH + 1) * row_count]
    value_total = value_terms[REACH * row_count : (REACH + 1) * row_count]
    for position, offset in enumerate(range(-REACH, REACH + 1)):
        if offset != 0:
            piece_pair = (
                key_terms[position * row_count : (position + 1) * row_count],
                value_terms[position * row_count : (position + 1) * row_count],
            )
            received = shifted((piece_pair[0], piece_pair[1]), "wide", offset)
            key_total = key_total + received[0]
            value_total = value_total + received[1]
    return (key_total, value_total)


def project_qkv(layer_in, weights):
    layer_float = layer_in.astype(jnp.float32)
    normed_one = layer_norm(
        layer_float, weights[0].astype(jnp.float32), weights[1].astype(jnp.float32)
    ).astype(jnp.bfloat16)
    mixed = jnp.dot(normed_one, weights[2], preferred_element_type=jnp.float32)
    queries = (mixed[:, :D] + weights[3][0].astype(jnp.float32)).astype(jnp.bfloat16)
    key_own = mixed[:, D : 2 * D].astype(jnp.bfloat16)
    value_own = (mixed[:, 2 * D :] + weights[3][1].astype(jnp.float32)).astype(jnp.bfloat16)
    return (layer_float, normed_one, queries, key_own, value_own)


def attention_probs(queries, keys_near, same_image):
    score_scale = 1.0 / math.sqrt(HEAD_DIM)
    scores = (
        jnp.einsum(
            "qhd,khd->hqk",
            heads_of(queries),
            heads_of(keys_near),
            preferred_element_type=jnp.float32,
        )
        * score_scale
    )
    scores = jnp.where(same_image[None], scores, MASKED_SCORE)
    row_max = jnp.max(scores, axis=-1, keepdims=True)
    exponent = jnp.exp(scores - row_max)
    return exponent / jnp.sum(exponent, axis=-1, keepdims=True)


def finish_layer(layer_float, queries, keys_near, values_near, same_image, weights, hidden_bias):
    probs = attention_probs(queries, keys_near, same_image)
    probs_low = probs.astype(jnp.bfloat16)
    attended = jnp.einsum(
        "hqk,khd->qhd", probs_low, heads_of(values_near), preferred_element_type=jnp.float32
    )
    attended = attended.reshape(queries.shape[0], D).astype(jnp.bfloat16)
    residual = (
        layer_float
        + jnp.dot(attended, weights[4], preferred_element_type=jnp.float32)
        + weights[5].astype(jnp.float32)
    )
    normed_two = layer_norm(
        residual, weights[6].astype(jnp.float32), weights[7].astype(jnp.float32)
    ).astype(jnp.bfloat16)
    hidden_pre = jnp.dot(
        normed_two, weights[8], preferred_element_type=jnp.float32
    ) + hidden_bias.astype(jnp.float32)
    hidden = gelu_tanh(hidden_pre).astype(jnp.bfloat16)
    output = (
        residual
        + jnp.dot(hidden, weights[9], preferred_element_type=jnp.float32)
        + weights[10].astype(jnp.float32)
    )
    return (probs, probs_low, attended, residual, normed_two, hidden_pre, hidden, output)


def layer_backward(
    layer_float,
    normed_one,
    queries,
    keys_near,
    values_near,
    same_image,
    weights,
    hidden_bias,
    grad_out,
):
    score_scale = 1.0 / math.sqrt(HEAD_DIM)
    probs, probs_low, attended, residual, normed_two, hidden_pre, hidden, output = finish_layer(
        layer_float, queries, keys_near, values_near, same_image, weights, hidden_bias
    )
    feed_grad = grad_out.astype(jnp.bfloat16)
    grad_fc2_weight = jnp.einsum("tf,td->fd", hidden, feed_grad, preferred_element_type=jnp.float32)
    grad_fc2_bias = jnp.sum(feed_grad.astype(jnp.float32), axis=0)
    hidden_grad = jnp.einsum("td,fd->tf", feed_grad, weights[9], preferred_element_type=jnp.float32)
    primal_gelu, gelu_pull = jax.vjp(gelu_tanh, hidden_pre)
    pre_grad = gelu_pull(hidden_grad)[0].astype(jnp.bfloat16)
    grad_fc1_bias = jnp.sum(pre_grad.astype(jnp.float32), axis=0)
    grad_fc1_weight = jnp.einsum(
        "td,tf->df", normed_two, pre_grad, preferred_element_type=jnp.float32
    )
    normed_two_grad = jnp.einsum(
        "tf,df->td", pre_grad, weights[8], preferred_element_type=jnp.float32
    )
    primal_two, norm_two_pull = jax.vjp(
        layer_norm, residual, weights[6].astype(jnp.float32), weights[7].astype(jnp.float32)
    )
    residual_part, grad_ln2_gain, grad_ln2_bias = norm_two_pull(normed_two_grad)
    residual_grad = grad_out + residual_part
    branch_grad = residual_grad.astype(jnp.bfloat16)
    grad_out_bias = jnp.sum(branch_grad.astype(jnp.float32), axis=0)
    grad_out_weight = jnp.einsum(
        "tc,td->cd", attended, branch_grad, preferred_element_type=jnp.float32
    )
    attended_grad = jnp.einsum(
        "td,cd->tc", branch_grad, weights[4], preferred_element_type=jnp.float32
    ).astype(jnp.bfloat16)
    attended_heads = heads_of(attended_grad)
    probs_grad = jnp.einsum(
        "qhd,khd->hqk", attended_heads, heads_of(values_near), preferred_element_type=jnp.float32
    )
    value_terms = jnp.einsum(
        "hqk,qhd->khd", probs_low, attended_heads, preferred_element_type=jnp.float32
    )
    score_grad = (
        probs * (probs_grad - jnp.sum(probs * probs_grad, axis=-1, keepdims=True))
    ).astype(jnp.bfloat16)
    query_grad = (
        jnp.einsum(
            "hqk,khd->qhd", score_grad, heads_of(keys_near), preferred_element_type=jnp.float32
        )
        * score_scale
    )
    query_grad = query_grad.reshape(queries.shape[0], D).astype(jnp.bfloat16)
    key_terms = (
        jnp.einsum(
            "hqk,qhd->khd", score_grad, heads_of(queries), preferred_element_type=jnp.float32
        )
        * score_scale
    )
    key_total, value_total = return_key_grads(key_terms.reshape(-1, D), value_terms.reshape(-1, D))
    key_grad = key_total.astype(jnp.bfloat16)
    value_grad = value_total.astype(jnp.bfloat16)
    grad_qv_bias = jnp.stack(
        [
            jnp.sum(query_grad.astype(jnp.float32), axis=0),
            jnp.sum(value_grad.astype(jnp.float32), axis=0),
        ]
    )
    mixed_grad = jnp.concatenate([query_grad, key_grad, value_grad], axis=1)
    grad_qkv_weight = jnp.einsum(
        "tc,tk->ck", normed_one, mixed_grad, preferred_element_type=jnp.float32
    )
    normed_one_grad = jnp.einsum(
        "tk,ck->tc", mixed_grad, weights[2], preferred_element_type=jnp.float32
    )
    primal_one, norm_one_pull = jax.vjp(
        layer_norm, layer_float, weights[0].astype(jnp.float32), weights[1].astype(jnp.float32)
    )
    input_part, grad_ln1_gain, grad_ln1_bias = norm_one_pull(normed_one_grad)
    input_grad = residual_grad + input_part
    grad_terms = (
        grad_ln1_gain,
        grad_ln1_bias,
        grad_qkv_weight,
        grad_qv_bias,
        grad_out_weight,
        grad_out_bias,
        grad_ln2_gain,
        grad_ln2_bias,
        grad_fc1_weight,
        grad_fc2_weight,
        grad_fc2_bias,
    )
    return (input_grad, grad_terms, grad_fc1_bias)


def on_device_near(
    tokens,
    cotangent,
    image_of_block,
    ln1_gain,
    ln1_bias,
    qkv_weight,
    qv_bias,
    out_weight,
    out_bias,
    ln2_gain,
    ln2_bias,
    fc1_weight,
    fc1_bias,
    fc2_weight,
    fc2_bias,
):
    section_rank = lax.axis_index("section")
    wide_rank = lax.axis_index("wide")
    micro_count = tokens.shape[0]
    weights = (
        lax.all_gather(ln1_gain[0], "wide", axis=0, tiled=True),
        lax.all_gather(ln1_bias[0], "wide", axis=0, tiled=True),
        lax.all_gather(qkv_weight[0], "wide", axis=0, tiled=True),
        lax.all_gather(qv_bias[0], "wide", axis=1, tiled=True),
        lax.all_gather(out_weight[0], "wide", axis=0, tiled=True),
        lax.all_gather(out_bias[0], "wide", axis=0, tiled=True),
        lax.all_gather(ln2_gain[0], "wide", axis=0, tiled=True),
        lax.all_gather(ln2_bias[0], "wide", axis=0, tiled=True),
        lax.all_gather(fc1_weight[0], "wide", axis=0, tiled=True),
        lax.all_gather(fc2_weight[0], "wide", axis=1, tiled=True),
        lax.all_gather(fc2_bias[0], "wide", axis=0, tiled=True),
    )
    hidden_bias = fc1_bias[0]
    inputs_kept = jnp.zeros_like(tokens)
    outputs_kept = jnp.zeros_like(tokens)
    incoming = jnp.zeros_like(tokens[0])
    for tick_number in range(micro_count + 1):
        batch_index = tick_number - section_rank
        is_live = (batch_index >= 0) & (batch_index < micro_count)
        batch_slot = jnp.clip(batch_index, 0, micro_count - 1)
        own_tokens = tokens[min(tick_number, micro_count - 1)]
        layer_in = jnp.where(section_rank == 0, own_tokens, incoming)
        same_image = image_mask(image_of_block, batch_slot, wide_rank)
        layer_float, normed_one, queries, key_own, value_own = project_qkv(layer_in, weights)
        keys_near, values_near = near_keys(key_own, value_own, False)
        output = finish_layer(
            layer_float, queries, keys_near, values_near, same_image, weights, hidden_bias
        )[-1]
        output_low = output.astype(jnp.bfloat16)
        inputs_kept = keep_slot(inputs_kept, layer_in, batch_slot, is_live)
        outputs_kept = keep_slot(outputs_kept, output_low, batch_slot, is_live)
        if tick_number < micro_count:
            incoming = shifted(output_low, "section", 1)
    weights_back = (
        lax.all_gather(ln1_gain[0], "wide", axis=0, tiled=True),
        lax.all_gather(ln1_bias[0], "wide", axis=0, tiled=True),
        lax.all_gather(qkv_weight[0], "wide", axis=0, tiled=True),
        lax.all_gather(qv_bias[0], "wide", axis=1, tiled=True),
        lax.all_gather(out_weight[0], "wide", axis=0, tiled=True),
        lax.all_gather(out_bias[0], "wide", axis=0, tiled=True),
        lax.all_gather(ln2_gain[0], "wide", axis=0, tiled=True),
        lax.all_gather(ln2_bias[0], "wide", axis=0, tiled=True),
        lax.all_gather(fc1_weight[0], "wide", axis=0, tiled=True),
        lax.all_gather(fc2_weight[0], "wide", axis=1, tiled=True),
        lax.all_gather(fc2_bias[0], "wide", axis=0, tiled=True),
    )
    grad_totals = tuple((jnp.zeros(array.shape, jnp.float32) for array in weights_back))
    hidden_bias_total = jnp.zeros(hidden_bias.shape, jnp.float32)
    input_grads = jnp.zeros(tokens.shape, jnp.float32)
    incoming_grad = jnp.zeros(tokens.shape[1:], jnp.bfloat16)
    for tick_number in range(micro_count + 1):
        batch_index = tick_number - 1 + section_rank
        is_live = (batch_index >= 0) & (batch_index < micro_count)
        batch_slot = jnp.clip(batch_index, 0, micro_count - 1)
        from_cotangent = cotangent[min(tick_number, micro_count - 1)].astype(jnp.float32)
        grad_out = jnp.where(
            section_rank == 1, from_cotangent, incoming_grad.astype(jnp.float32)
        ) * is_live.astype(jnp.float32)
        layer_in = lax.dynamic_index_in_dim(inputs_kept, batch_slot, 0, keepdims=False)
        same_image = image_mask(image_of_block, batch_slot, wide_rank)
        layer_float, normed_one, queries, key_own, value_own = project_qkv(layer_in, weights_back)
        keys_near, values_near = near_keys(key_own, value_own, True)
        input_grad, grad_terms, hidden_bias_term = layer_backward(
            layer_float,
            normed_one,
            queries,
            keys_near,
            values_near,
            same_image,
            weights_back,
            hidden_bias,
            grad_out,
        )
        grad_totals = tuple(
            (old_total + new_term for old_total, new_term in zip(grad_totals, grad_terms))
        )
        hidden_bias_total = hidden_bias_total + hidden_bias_term
        input_grads = keep_slot(input_grads, input_grad, batch_slot, is_live)
        if tick_number < micro_count:
            incoming_grad = shifted(input_grad.astype(jnp.bfloat16), "section", -1)
    (
        grad_ln1_gain,
        grad_ln1_bias,
        grad_qkv_weight,
        grad_qv_bias,
        grad_out_weight,
        grad_out_bias,
        grad_ln2_gain,
        grad_ln2_bias,
        grad_fc1_weight,
        grad_fc2_weight,
        grad_fc2_bias,
    ) = grad_totals
    row_sums = (
        lax.psum_scatter(grad_ln1_gain, "wide", scatter_dimension=0, tiled=True),
        lax.psum_scatter(grad_ln1_bias, "wide", scatter_dimension=0, tiled=True),
        lax.psum_scatter(grad_qkv_weight, "wide", scatter_dimension=0, tiled=True),
        lax.psum_scatter(grad_out_weight, "wide", scatter_dimension=0, tiled=True),
        lax.psum_scatter(grad_out_bias, "wide", scatter_dimension=0, tiled=True),
        lax.psum_scatter(grad_ln2_gain, "wide", scatter_dimension=0, tiled=True),
        lax.psum_scatter(grad_ln2_bias, "wide", scatter_dimension=0, tiled=True),
        lax.psum_scatter(grad_fc1_weight, "wide", scatter_dimension=0, tiled=True),
        lax.psum_scatter(grad_fc2_bias, "wide", scatter_dimension=0, tiled=True),
    )
    column_sums = (
        lax.psum_scatter(grad_qv_bias, "wide", scatter_dimension=1, tiled=True),
        lax.psum_scatter(grad_fc2_weight, "wide", scatter_dimension=1, tiled=True),
    )
    hidden_bias_sum = lax.psum(hidden_bias_total, "wide")
    return (
        outputs_kept[None],
        input_grads[None],
        row_sums[0][None],
        row_sums[1][None],
        row_sums[2][None],
        column_sums[0][None],
        row_sums[3][None],
        row_sums[4][None],
        row_sums[5][None],
        row_sums[6][None],
        row_sums[7][None],
        hidden_bias_sum[None],
        column_sums[1][None],
        row_sums[8][None],
    )


def specs():
    ins = (
        P(None, "wide", None),
        P(None, "wide", None),
        P(),
        P("section", "wide"),
        P("section", "wide"),
        P("section", "wide", None),
        P("section", None, "wide"),
        P("section", "wide", None),
        P("section", "wide"),
        P("section", "wide"),
        P("section", "wide"),
        P("section", "wide", None),
        P("section", None),
        P("section", None, "wide"),
        P("section", "wide"),
    )
    outs = (
        P("section", None, "wide", None),
        P("section", None, "wide", None),
        P("section", "wide"),
        P("section", "wide"),
        P("section", "wide", None),
        P("section", None, "wide"),
        P("section", "wide", None),
        P("section", "wide"),
        P("section", "wide"),
        P("section", "wide"),
        P("section", "wide", None),
        P("section", None),
        P("section", None, "wide"),
        P("section", "wide"),
    )
    return ins, outs


def solution(mesh):
    ins, outs = specs()
    body = on_device if mesh.shape["wide"] == HEADS else on_device_near
    return jax.shard_map(body, mesh=mesh, in_specs=ins, out_specs=outs, check_vma=False)
```

```python
import functools
import math

import jax
import jax.numpy as jnp
from jax import lax
from jax.experimental import pallas as pl
from jax.experimental.pallas import tpu as pltpu
from jax.sharding import PartitionSpec as P

D = 1152
HEADS = 16
HEAD_DIM = 72
FF = 4304
FFP = -(-FF // 256) * 256
SPLIT = 9 * 256
BLOCK = 128
IMG_BLOCKS = 6
EPSILON = 1e-06
MASKED_SCORE = -1e30
SCALE = 1.0 / math.sqrt(HEAD_DIM)
MESH = pl.DeviceIdType.MESH
BF = jnp.bfloat16
F32 = jnp.float32


def place():
    return lax.axis_index("section"), lax.axis_index("wide")


class Gather:
    def __init__(self, pieces, ins, outs, sems, twice=()):
        self.pieces, self.ins, self.outs, self.count, self.twice = pieces, ins, outs, len(pieces), twice
        self.local_sem = sems[0]
        self.up, self.down, self.yy, self.cc = [(sems[1 + 2 * i], sems[2 + 2 * i]) for i in range(4)]
        self.sec, self.me = place()
        self.z, self.low = self.me // 4, self.me % 4
        self.other_y = self.me - self.low + flip(self.low, 2)
        self.other_c = self.me - self.low + flip(self.low, 1)

    @staticmethod
    def semaphores(pieces, arrays):
        dma = pltpu.SemaphoreType.DMA
        return [dma((arrays,))] + [dma((pieces, 8))] * 4 + [dma((pieces, 4))] * 2 + [dma((pieces, 8))] * 2

    def part(self, piece, origin=None):
        array, at, end = self.pieces[piece]
        return self.ins[array].at[:, at:end] if origin is None else self.outs[array].at[origin, :, at:end]

    def send(self, piece, origin, sems, slot, target, first=False):
        return pltpu.make_async_remote_copy(
            src_ref=self.part(piece) if first else self.part(piece, origin),
            dst_ref=self.part(piece, origin),
            send_sem=sems[0].at[piece, slot],
            recv_sem=sems[1].at[piece, slot],
            device_id=(self.sec, target),
            device_id_type=MESH,
        )

    def mine(self, array):
        return pltpu.make_async_copy(self.ins[array], self.outs[array].at[self.me], self.local_sem.at[array])

    def along(self, piece, origin, first, go_up, go_down, column=0):
        slot = origin // 4 + 4 * column
        if go_up:

            @pl.when(self.z < 3)
            def _():
                self.send(piece, origin, self.up, slot, self.me + 4, first).start()

        if go_down:

            @pl.when(self.z > 0)
            def _():
                self.send(piece, origin, self.down, slot, self.me - 4, first).start()

        if piece not in self.twice or first:
            self.send(piece, origin, self.yy, origin // 4, self.other_y, first).start()
        self.send(piece, origin, self.cc, slot, self.other_c, first).start()

    def columns(self, piece):
        return (0, 1) if piece in self.twice else (0,)

    def step(self, piece, step):
        if step == 1 and piece in self.twice:
            self.send(piece, self.other_y, self.yy, self.z, self.other_y).wait_recv()
            self.along(piece, self.other_y, False, True, True, 1)

        @pl.when(self.z - step >= 0)
        def _():
            for column in self.columns(piece):
                origin = (self.me, self.other_y)[column] - 4 * step
                self.send(piece, origin, self.up, self.z - step + 4 * column, self.me).wait_recv()
                self.along(piece, origin, False, True, False, column)

        @pl.when(self.z + step <= 3)
        def _():
            for column in self.columns(piece):
                origin = (self.me, self.other_y)[column] + 4 * step
                self.send(piece, origin, self.down, self.z + step + 4 * column, self.me).wait_recv()
                self.along(piece, origin, False, False, True, column)

    def slots(self, first, last):
        for k in range(first, last):
            if k == 0:
                for array in range(len(self.ins)):
                    self.mine(array).start()
            if k < self.count:
                self.along(k, self.me, True, True, True)
            for step in range(1, 4):
                if 0 <= k - step < self.count:
                    self.step(k - step, step)

    def across(self, pieces):
        far = self.other_y % 4
        for piece in pieces:
            for step in range(0 if piece in self.twice else 4):
                zo = (self.z + step) % 4
                origin = zo * 4 + far
                self.send(piece, origin, self.yy, zo, self.other_y).wait_recv()
                self.send(piece, origin, self.cc, 4 + zo, self.other_c).start()

    def arrived(self, pieces):
        for piece in pieces:
            for slot in range(8):
                self.send(piece, self.me, self.cc, slot, self.other_c).wait_recv()

    def finish(self):
        for zo in range(4):
            for piece in range(self.count):
                if piece not in self.twice:
                    self.send(piece, self.me, self.yy, zo, self.other_y).wait_send()
                elif zo == 0:
                    self.send(piece, self.me, self.yy, self.z, self.other_y).wait_send()
                for slot in (zo, 4 + zo):
                    self.send(piece, self.me, self.cc, slot, self.other_c).wait_send()

                @pl.when((zo <= self.z) & (self.z < 3))
                def _():
                    for column in self.columns(piece):
                        self.send(piece, self.me, self.up, zo + 4 * column, self.me).wait_send()

                @pl.when((zo >= self.z) & (self.z > 0))
                def _():
                    for column in self.columns(piece):
                        self.send(piece, self.me, self.down, zo + 4 * column, self.me).wait_send()


def flip(low, k):
    return [low, low + 1 - 2 * (low % 2), (low + 2) % 4, 3 - low][k]


def greet_all(count, sec, me, meanwhile=lambda: None):
    barrier = pltpu.get_barrier_semaphore()
    for d in range(1, count):
        pl.semaphore_signal(barrier, inc=1, device_id=(sec, (me + d) % count), device_id_type=MESH)
    meanwhile()
    pl.semaphore_wait(barrier, count - 1)


class Whole:
    def __init__(self, zero, one, cols=None):
        self.sources, self.cols = (zero, one), cols

    def shape(self):
        rows, cols = self.sources[0].shape
        return (4, rows, cols if self.cols is None else self.cols[1] - self.cols[0])

    def source(self, ref, low, k):
        return ref if self.cols is None else ref.at[:, self.cols[0] : self.cols[1]]

    forwarded = True


class Rows:
    def __init__(self, zero, one):
        self.sources = (zero, one)

    def shape(self):
        return self.sources[0].shape

    def source(self, ref, low, k):
        return ref.at[flip(low, k)]

    forwarded = False


class PlaneCopies:
    def __init__(self, item, zero_ref, one_ref, slot, local_sem, send_sem, recv_sem):
        self.item, self.refs, self.slot = item, (zero_ref, one_ref), slot
        self.local_sem, self.send_sem, self.recv_sem = local_sem, send_sem, recv_sem
        self.sec, self.me = place()
        self.low = self.me % 4

    def remote(self, src, k, to):
        return pltpu.make_async_remote_copy(
            src_ref=src,
            dst_ref=self.slot(k),
            send_sem=self.send_sem.at[k],
            recv_sem=self.recv_sem.at[k],
            device_id=(self.sec, self.me - self.low + flip(self.low, to)),
            device_id_type=MESH,
        )

    def local(self, ref):
        return pltpu.make_async_copy(self.item.source(ref, self.low, 0), self.slot(0), self.local_sem)

    def start(self):
        def go(ref):
            self.local(ref).start()
            for k in (2, 1) if self.item.forwarded else (2, 3, 1):
                self.remote(self.item.source(ref, self.low, k), k, k).start()

        @pl.when(self.sec == 0)
        def _():
            go(self.refs[0])

        @pl.when(self.sec == 1)
        def _():
            go(self.refs[1])

    def forward(self):
        if self.item.forwarded:
            self.remote(self.slot(2), 2, 2).wait_recv()
            self.remote(self.slot(2), 3, 1).start()

    def finish(self):
        self.local(self.refs[0]).wait()
        for k in (1, 2, 3):
            self.remote(self.slot(k), k, k).wait_send()
            if k != 2 or not self.item.forwarded:
                self.remote(self.slot(k), k, k).wait_recv()


def dot(a, b):
    return jnp.dot(a, b, preferred_element_type=F32)


def window(image_of_block):
    micro, blocks = image_of_block.shape
    own, other = image_of_block[:, :, None], image_of_block[:, None, :]
    begin = jnp.sum((other < own).astype(jnp.int32), axis=2)
    end = jnp.sum((other <= own).astype(jnp.int32), axis=2)
    first = jnp.minimum(begin, blocks - IMG_BLOCKS)
    shape = (micro, blocks, IMG_BLOCKS, BLOCK)
    at = first[:, :, None, None] + lax.broadcasted_iota(jnp.int32, shape, 2)
    same = (at >= begin[:, :, None, None]) & (at < end[:, :, None, None])
    return first, jnp.where(same, 0.0, MASKED_SCORE).astype(F32)


def near_rows(ref, start):
    return jnp.concatenate([ref[start + j] for j in range(IMG_BLOCKS)], axis=0)


def near_columns(ref, start):
    return jnp.concatenate([ref[start + j] for j in range(IMG_BLOCKS)], axis=1)


def fetch(pairs, buffers, sems, sec):
    for which in range(2):

        @pl.when(sec == which)
        def _():
            for i, buffer in enumerate(buffers):
                pltpu.make_async_copy(pairs[2 * i + which], buffer, sems.at[i]).start()


def fetched(pairs, buffers, sems):
    for i, buffer in enumerate(buffers):
        pltpu.make_async_copy(pairs[2 * i], buffer, sems.at[i]).wait()


class ToAll:
    def __init__(self, block, dst, send, recv, sec, me, count):
        self.block, self.dst, self.send, self.recv = block, dst, send, recv
        self.sec, self.me, self.count = sec, me, count

    def copy(self, d):
        return pltpu.make_async_remote_copy(
            src_ref=self.block(d),
            dst_ref=self.dst.at[self.me],
            send_sem=self.send.at[d],
            recv_sem=self.recv.at[d],
            device_id=(self.sec, (self.me + d) % self.count),
            device_id_type=MESH,
        )

    def start(self):
        for d in sorted(range(1, self.count), key=lambda d: abs(d - self.count // 2)):
            self.copy(d).start()

    def start_one(self, d):
        @pl.when(d > 0)
        def _():
            self.copy(d).start()

    def wait(self):
        for d in range(1, self.count):
            self.copy(d).wait()


class Forward:
    def __init__(self, tick, near, x_ref, outs, scratch):
        self.first_ref, self.bias_ref = near
        self.x_ref = x_ref
        self.qkv_ref, self.lse_ref, self.att_ref = outs
        self.k_all, self.vt_all, self.o_buf, self.local_sem, *sems = scratch
        self.count = x_ref.shape[0]
        sec, self.me = place()
        self.slot = jnp.minimum(jnp.maximum(tick - sec, 0), 1)
        rest = (sec, self.me, self.count)
        self.arrive = ToAll(lambda d: x_ref.at[(self.me + d) % self.count], self.qkv_ref, *sems[:2], *rest)
        self.leave = ToAll(lambda d: self.o_buf.at[d], self.att_ref, *sems[2:], *rest)

    @staticmethod
    def scratch(blocks):
        dma = pltpu.SemaphoreType.DMA
        return [
            pltpu.VMEM((blocks, BLOCK, HEAD_DIM), BF),
            pltpu.VMEM((blocks, HEAD_DIM, BLOCK), BF),
            pltpu.VMEM((blocks, HEAD_DIM, BLOCK), BF),
            dma,
        ] + [dma((blocks,))] * 4

    @staticmethod
    def shapes(blocks):
        return [
            jax.ShapeDtypeStruct((blocks, 3 * HEAD_DIM, BLOCK), BF),
            jax.ShapeDtypeStruct((blocks, 1, BLOCK), F32),
            jax.ShapeDtypeStruct((blocks, HEAD_DIM, BLOCK), BF),
        ]

    def own(self):
        return pltpu.make_async_copy(self.x_ref.at[self.me], self.qkv_ref.at[self.me], self.local_sem)

    def start(self):
        self.arrive.start()
        self.own().start()

    def wait_in(self):
        self.own().wait()
        self.arrive.wait()

    def compute(self):
        def arrange(j, carry):
            part = self.qkv_ref[j].astype(F32)
            self.k_all[j] = part[HEAD_DIM : 2 * HEAD_DIM].T.astype(BF)
            self.vt_all[j] = part[2 * HEAD_DIM :].astype(BF)
            return carry

        lax.fori_loop(0, self.count, arrange, 0)

        def one_block(d, carry):
            i = (self.me + d) % self.count
            start = self.first_ref[self.slot, i]
            qt = self.qkv_ref[i].astype(F32)[:HEAD_DIM].astype(BF)
            s = dot(near_rows(self.k_all, start), qt) * SCALE
            bias = self.bias_ref[self.slot, i]
            parts = [s[j * BLOCK : (j + 1) * BLOCK] + bias[j : j + 1] for j in range(IMG_BLOCKS)]
            top = parts[0]
            for part in parts[1:]:
                top = jnp.maximum(top, part)
            top = jnp.max(top, axis=0, keepdims=True)
            exps = [jnp.exp(part - top) for part in parts]
            total = exps[0]
            for part in exps[1:]:
                total = total + part
            total = jnp.sum(total, axis=0, keepdims=True)
            e = jnp.concatenate([part.astype(BF) for part in exps], axis=0)
            o = dot(near_columns(self.vt_all, start), e)
            self.o_buf[d] = (o / total).astype(BF)
            self.lse_ref[i] = top + jnp.log(total)
            self.leave.start_one(d)
            return carry

        lax.fori_loop(0, self.count, one_block, 0)
        self.att_ref[self.me] = self.o_buf[0]

    def wait_out(self):
        self.leave.wait()


class Backward:
    def __init__(self, tick, near, kept, x_ref, outs, scratch):
        self.first_ref, self.bias_ref = near
        self.kept, self.x_ref = kept, x_ref
        self.dq_ref, self.dkv_ref = outs
        self.qkv_ref, self.lse_ref, self.do_ref = scratch[:3]
        self.k_all, self.kt_all, self.v_all, self.q_all, self.do_all, self.p_all, self.s_all = scratch[3:10]
        self.dq_buf, self.dkv_buf, self.kept_sem, self.local_sem = scratch[10:14]
        sems = scratch[14:]
        self.count = x_ref.shape[0]
        self.sec, self.me = place()
        self.slot = jnp.minimum(jnp.maximum(tick - 1 + self.sec, 0), 1)
        rest = (self.sec, self.me, self.count)
        self.arrive = ToAll(lambda d: x_ref.at[(self.me + d) % self.count], self.do_ref, *sems[:2], *rest)
        self.leave_q = ToAll(lambda d: self.dq_buf.at[d], self.dq_ref, *sems[2:4], *rest)
        self.leave_kv = ToAll(lambda d: self.dkv_buf.at[d], self.dkv_ref, *sems[4:], *rest)

    @staticmethod
    def scratch(blocks):
        dma = pltpu.SemaphoreType.DMA
        return [
            pltpu.VMEM((blocks, 3 * HEAD_DIM, BLOCK), BF),
            pltpu.VMEM((blocks, 1, BLOCK), F32),
            pltpu.VMEM((blocks, HEAD_DIM, BLOCK), BF),
            pltpu.VMEM((blocks, BLOCK, HEAD_DIM), BF),
            pltpu.VMEM((blocks, HEAD_DIM, BLOCK), BF),
            pltpu.VMEM((blocks, BLOCK, HEAD_DIM), BF),
            pltpu.VMEM((blocks, BLOCK, HEAD_DIM), BF),
            pltpu.VMEM((blocks, BLOCK, HEAD_DIM), BF),
            pltpu.VMEM((blocks, IMG_BLOCKS, BLOCK, BLOCK), BF),
            pltpu.VMEM((blocks, IMG_BLOCKS, BLOCK, BLOCK), BF),
            pltpu.VMEM((blocks, HEAD_DIM, BLOCK), BF),
            pltpu.VMEM((blocks, 2 * HEAD_DIM, BLOCK), BF),
            dma((2,)),
            dma,
        ] + [dma((blocks,))] * 6

    def own(self):
        return pltpu.make_async_copy(self.x_ref.at[self.me], self.do_ref.at[self.me], self.local_sem)

    def start(self):
        self.arrive.start()
        self.own().start()
        fetch(self.kept, (self.qkv_ref, self.lse_ref), self.kept_sem, self.sec)

    def arrange(self):
        fetched(self.kept, (self.qkv_ref, self.lse_ref), self.kept_sem)

        def one(j, carry):
            part = self.qkv_ref[j].astype(F32)
            self.q_all[j] = part[:HEAD_DIM].T.astype(BF)
            self.k_all[j] = part[HEAD_DIM : 2 * HEAD_DIM].T.astype(BF)
            self.v_all[j] = part[2 * HEAD_DIM :].T.astype(BF)
            self.kt_all[j] = part[HEAD_DIM : 2 * HEAD_DIM].astype(BF)
            return carry

        lax.fori_loop(0, self.count, one, 0)

    def wait_in(self):
        self.own().wait()
        self.arrive.wait()

    def by_query(self):
        def turn(j, carry):
            self.do_all[j] = self.do_ref[j].astype(F32).T.astype(BF)
            return carry

        lax.fori_loop(0, self.count, turn, 0)

        def one(d, carry):
            i = (self.me + d) % self.count
            start = self.first_ref[self.slot, i]
            qt = self.qkv_ref[i].astype(F32)[:HEAD_DIM].astype(BF)
            s = dot(near_rows(self.k_all, start), qt) * SCALE
            shift = self.bias_ref[self.slot, i] - self.lse_ref[i]
            probs = [jnp.exp(s[j * BLOCK : (j + 1) * BLOCK] + shift[j : j + 1]) for j in range(IMG_BLOCKS)]
            dp = dot(near_rows(self.v_all, start), self.do_ref[i])
            total = probs[0] * dp[:BLOCK]
            for j in range(1, IMG_BLOCKS):
                total = total + probs[j] * dp[j * BLOCK : (j + 1) * BLOCK]
            total = jnp.sum(total, axis=0, keepdims=True)
            ds = jnp.concatenate(
                [(probs[j] * (dp[j * BLOCK : (j + 1) * BLOCK] - total)).astype(BF) for j in range(IMG_BLOCKS)], axis=0
            )
            for j in range(IMG_BLOCKS):
                self.p_all[i, j] = probs[j].astype(BF)
                self.s_all[i, j] = ds[j * BLOCK : (j + 1) * BLOCK]
            self.dq_buf[d] = (dot(near_columns(self.kt_all, start), ds) * SCALE).astype(BF)
            self.leave_q.start_one(d)
            return carry

        lax.fori_loop(0, self.count, one, 0)
        self.dq_ref[self.me] = self.dq_buf[0]

    def by_key(self):
        def one(d, carry):
            j = (self.me + d) % self.count
            start = self.first_ref[self.slot, j]
            place_in = jnp.clip(j - start, 0, IMG_BLOCKS - 1)
            same = (self.bias_ref[self.slot, j] == 0.0).astype(F32).astype(BF)
            p, ds = [], []
            for m in range(IMG_BLOCKS):
                p.append(self.p_all[start + m, place_in] * same[m : m + 1])
                ds.append(self.s_all[start + m, place_in] * same[m : m + 1])
            dv = dot(jnp.concatenate(p, axis=1), near_rows(self.do_all, start))
            dk = dot(jnp.concatenate(ds, axis=1), near_rows(self.q_all, start)) * SCALE
            self.dkv_buf[d] = jnp.concatenate([dk.T, dv.T], axis=0).astype(BF)
            self.leave_kv.start_one(d)
            return carry

        lax.fori_loop(0, self.count, one, 0)
        self.dkv_ref[self.me] = self.dkv_buf[0]

    def wait_out(self):
        self.leave_q.wait()
        self.leave_kv.wait()


def attention_kernel(ahead, behind, items, *refs):
    refs = list(refs)

    def take(n):
        part = refs[:n]
        del refs[:n]
        return part

    n = len(items)
    near = take(2)
    x_ref = take(1) if ahead is not None else None
    kept, g_ref = (take(4), take(1)) if behind is not None else (None, None)
    sources = take(2 * n)
    ahead_out = take(3) if ahead is not None else None
    behind_out = take(2) if behind is not None else None
    outs = take(n)
    f = b = None
    blocks = (x_ref or g_ref)[0].shape[0]
    sec, me = place()
    if ahead is not None:
        f = Forward(ahead, near, x_ref[0], ahead_out, take(len(Forward.scratch(blocks))))
    if behind is not None:
        b = Backward(behind, near, kept, g_ref[0], behind_out, take(len(Backward.scratch(blocks))))
    copies = []
    for i, item in enumerate(items):
        into = lambda k, i=i: outs[i].at[k]
        copies.append(PlaneCopies(item, sources[2 * i], sources[2 * i + 1], into, *take(3)))
    greet_all(blocks, sec, me)

    if b:
        b.start()
        b.arrange()
        b.wait_in()
    if f:
        f.start()
    if f and not b:
        f.wait_in()
    for copy in copies:
        copy.start()
    if b:
        b.by_query()
        b.by_key()
    if f and b:
        f.wait_in()
    if f:
        f.compute()
    for copy in copies:
        copy.forward()
    if f:
        f.wait_out()
    if b:
        b.wait_out()
    for copy in copies:
        copy.finish()


def attention(near, cid, ahead=None, behind=None, items=()):
    first_in = ahead[1] if ahead else behind[1]
    blocks = first_in.shape[0]
    n = len(items)
    sources = [source for item in items for source in item.sources]
    anywhere, vmem, smem = [pl.BlockSpec(memory_space=m) for m in (pl.ANY, pltpu.VMEM, pltpu.SMEM)]
    dma = pltpu.SemaphoreType.DMA
    args, scratch, shapes = [], [], []
    if ahead:
        args.append(ahead[1])
        scratch += Forward.scratch(blocks)
        shapes += Forward.shapes(blocks)
    if behind:
        args += [*behind[2], behind[1]]
        scratch += Backward.scratch(blocks)
        shapes += [
            jax.ShapeDtypeStruct((blocks, HEAD_DIM, BLOCK), BF),
            jax.ShapeDtypeStruct((blocks, 2 * HEAD_DIM, BLOCK), BF),
        ]
    args += sources
    scratch += [dma, dma((4,)), dma((4,))] * n
    in_vmem = len(shapes)
    shapes += [jax.ShapeDtypeStruct(item.shape(), BF) for item in items]
    out = pl.pallas_call(
        functools.partial(attention_kernel, ahead and ahead[0], behind and behind[0], list(items)),
        out_shape=shapes,
        in_specs=[smem, vmem] + [anywhere] * len(args),
        out_specs=[vmem] * in_vmem + [anywhere] * n,
        scratch_shapes=scratch,
        compiler_params=pltpu.CompilerParams(collective_id=cid, has_side_effects=True, vmem_limit_bytes=60 << 20),
    )(*near, *args)
    out = list(out)
    three, out = (out[:3], out[3:]) if ahead else (None, out)
    two, out = (out[:2], out[2:]) if behind else (None, out)
    return three, two, out


def slices(width, step=1024):
    return [(at, min(at + step, width)) for at in range(0, width, step)]


class Stream:
    def __init__(self, pairs, sems):
        self.copies = {}
        for i, (name, ref, buf, cols) in enumerate(pairs):
            src, dst = ref.at[:, cols[0] : cols[1]], buf.at[:, cols[0] : cols[1]]
            self.copies[name, cols[0]] = pltpu.make_async_copy(src, dst, sems.at[i])

    def start(self):
        for copy in self.copies.values():
            copy.start()

    def wait(self, name, at):
        self.copies[name, at].wait()


def normalised(x):
    mean = jnp.mean(x, axis=-1, keepdims=True)
    centred = x - mean
    rstd = lax.rsqrt(jnp.mean(centred * centred, axis=-1, keepdims=True) + EPSILON)
    return centred * rstd, rstd


def norm_backward(grad, xhat, rstd, gain):
    g = grad * gain
    part = g - jnp.mean(g, axis=-1, keepdims=True) - xhat * jnp.mean(g * xhat, axis=-1, keepdims=True)
    return part * rstd, jnp.sum(grad * xhat, axis=0, keepdims=True), jnp.sum(grad, axis=0, keepdims=True)


def greet_plane(sec, me):
    barrier = pltpu.get_barrier_semaphore()
    low = me % 4
    for k in range(1, 4):
        pl.semaphore_signal(barrier, inc=1, device_id=(sec, me - low + flip(low, k)), device_id_type=MESH)
    pl.semaphore_wait(barrier, 3)


class Load:
    def __init__(self, items):
        self.items = list(items)
        self.sources = [source for item in items for source in item.sources]
        self.shapes = [jax.ShapeDtypeStruct(item.shape(), BF) for item in items]
        dma = pltpu.SemaphoreType.DMA
        self.scratch = [dma, dma((4,)), dma((4,))] * len(self.items)

    def begin(self, sources, outs, sems):
        copies = []
        if self.items:
            greet_plane(*place())
        for i, item in enumerate(self.items):
            into = lambda k, i=i: outs[i].at[k]
            copies.append(PlaneCopies(item, sources[2 * i], sources[2 * i + 1], into, *sems[3 * i : 3 * i + 3]))
            copies[-1].start()
        return copies


def gelu_tanh(v):
    c = math.sqrt(2.0 / math.pi)
    return 0.5 * v * (1.0 + jnp.tanh(c * (v + 0.044715 * (v * v * v))))


def gelu_slope(v):
    c = math.sqrt(2.0 / math.pi)
    square = v * v
    t = jnp.tanh(c * (v + 0.044715 * (square * v)))
    return 0.5 * (1.0 + t) + 0.5 * v * (1.0 - t * t) * (c * (1.0 + 3 * 0.044715 * square))


def nt(a, b):
    return lax.dot_general(a, b, (((1,), (1,)), ((), ())), preferred_element_type=F32)


def put_owners(ref, x):
    turned = x.T
    for w in range(HEADS):
        ref[w % 4, w // 4] = turned[w * HEAD_DIM : (w + 1) * HEAD_DIM].astype(BF)


GAIN1, BIAS1, OUT_BIAS, GAIN2, BIAS2, FC2_BIAS = 0, 1, 4, 5, 6, 7


def row(vec_ref, i):
    return vec_ref[i : i + 1, :]


def pick(sec, zero_ref, one_ref):
    return jnp.where(sec == 0, zero_ref[...].astype(F32), one_ref[...].astype(F32))


def qkv_kernel(tok_ref, inc_ref, vec_ref, bias_ref, w_ref, qkv_ref, n1_ref, w_buf, t_buf, sems):
    sec, _ = place()
    stream = Stream([("w", w_ref, w_buf, cols) for cols in slices(3 * D, 384)], sems)
    stream.start()
    xhat, _ = normalised(pick(sec, tok_ref, inc_ref))
    n1 = xhat * row(vec_ref, GAIN1) + row(vec_ref, BIAS1)
    low = n1.astype(BF)
    for at, end in slices(3 * D, 384):
        stream.wait("w", at)
        t_buf[at:end, :] = (dot(low, w_buf[:, at:end]) + bias_ref[:, at:end]).T
    for h in range(HEADS):
        parts = [t_buf[p * D + h * HEAD_DIM : p * D + (h + 1) * HEAD_DIM, :] for p in range(3)]
        qkv_ref[h] = jnp.concatenate(parts, axis=0).astype(BF)
    put_owners(n1_ref, low.astype(F32))


def qkv_forward(tok, inc, vec, bias, w):
    tokens = tok.shape[0]
    anywhere, vmem = pl.BlockSpec(memory_space=pl.ANY), pl.BlockSpec(memory_space=pltpu.VMEM)
    return pl.pallas_call(
        qkv_kernel,
        out_shape=[
            jax.ShapeDtypeStruct((HEADS, 3 * HEAD_DIM, tokens), BF),
            jax.ShapeDtypeStruct((4, 4, HEAD_DIM, tokens), BF),
        ],
        in_specs=[vmem] * 4 + [anywhere],
        out_specs=[vmem] * 2,
        scratch_shapes=[
            pltpu.VMEM((D, 3 * D), BF),
            pltpu.VMEM((3 * D, tokens), F32),
            pltpu.SemaphoreType.DMA((len(slices(3 * D, 384)),)),
        ],
        compiler_params=pltpu.CompilerParams(vmem_limit_bytes=60 << 20),
    )(tok, inc, vec, bias, w)


def first_kernel(first_ref, bias_ref, tok_ref, *refs):
    refs = list(refs)

    def take(n):
        part = refs[:n]
        del refs[:n]
        return part

    shards = take(5)
    ahead_out = take(3)
    n1_ref, small_all, w_qkv = take(3)
    whole = take(3)
    w_buf, t_buf, x_buf, w_sem = take(4)
    f = Forward(0, (first_ref, bias_ref), x_buf, ahead_out, take(len(Forward.scratch(HEADS))))
    work = Gather(first_pieces(shards), shards, (w_buf, small_all, *whole), take(9), TWICE)
    soon, later = [list(range(SOON)), list(range(SOON, work.count))]
    sec, me = place()
    greet_all(HEADS, sec, me)
    work.slots(0, 1)
    xhat, _ = normalised(tok_ref[...].astype(F32))
    xhat = xhat.T
    work.slots(1, SOON + 3)
    for array in range(len(shards)):
        work.mine(array).wait()
    work.across(soon)
    work.arrived(soon)
    keep = pltpu.make_async_copy(w_buf, w_qkv, w_sem)
    keep.start()
    work.slots(SOON + 3, SOON + 4)
    small = jnp.concatenate([small_all[w].astype(F32) for w in range(HEADS)], axis=0)
    n1 = (xhat * small[:, 0:1] + small[:, 1:2]).astype(BF).astype(F32)
    for w in range(HEADS):
        n1_ref[w % 4, w // 4] = n1[w * HEAD_DIM : (w + 1) * HEAD_DIM].astype(BF)
    low = n1.T.astype(BF)

    def columns(i, carry):
        here = pl.ds(pl.multiple_of(i * 384, 384), 384)
        w = jnp.concatenate([w_buf[shard, :, here].astype(F32) for shard in range(HEADS)], axis=0)
        t_buf[here, :] = dot(low, w.astype(BF)).T
        return carry

    lax.fori_loop(0, 3 * D // 384, columns, 0)
    for h in range(HEADS):
        rows = slice(h * HEAD_DIM, (h + 1) * HEAD_DIM)
        parts = [t_buf[p * D + h * HEAD_DIM : p * D + (h + 1) * HEAD_DIM, :] for p in range(3)]
        parts = [parts[0] + small[rows, 2:3], parts[1], parts[2] + small[rows, 3:4]]
        x_buf[h] = jnp.concatenate(parts, axis=0).astype(BF)
    f.start()
    work.slots(SOON + 4, SOON + 5)
    f.wait_in()
    work.slots(SOON + 5, SOON + 7)
    f.compute()
    work.slots(SOON + 7, work.count + 3)
    f.wait_out()
    work.across(later)
    work.arrived(later)
    work.finish()
    keep.wait()


SOON = 4
TWICE = (4,)


def first_pieces(shards):
    pieces = [(1, 0, BLOCK)]
    for array in (0, 2, 3, 4):
        pieces += [(array, at, end) for at, end in slices(shards[array].shape[1], D)]
    return pieces


def first_tick(near, tok, shards, cid):
    tokens = tok.shape[0]
    anywhere, vmem, smem = [pl.BlockSpec(memory_space=m) for m in (pl.ANY, pltpu.VMEM, pltpu.SMEM)]
    whole = [jax.ShapeDtypeStruct((HEADS,) + shard.shape, BF) for shard in shards]
    return pl.pallas_call(
        first_kernel,
        out_shape=Forward.shapes(HEADS)
        + [jax.ShapeDtypeStruct((4, 4, HEAD_DIM, tokens), BF), whole[1], whole[0]]
        + whole[2:],
        in_specs=[smem, vmem, vmem] + [anywhere] * 5,
        out_specs=[vmem] * 5 + [anywhere] * 4,
        scratch_shapes=[
            pltpu.VMEM((HEADS,) + shards[0].shape, BF),
            pltpu.VMEM((3 * D, tokens), F32),
            pltpu.VMEM((HEADS, 3 * HEAD_DIM, tokens), BF),
            pltpu.SemaphoreType.DMA,
        ]
        + Forward.scratch(HEADS)
        + Gather.semaphores(len(first_pieces(shards)), len(shards)),
        compiler_params=pltpu.CompilerParams(collective_id=cid, has_side_effects=True, vmem_limit_bytes=60 << 20),
    )(*near, tok, *shards)


def greet_section(sec, me):
    barrier = pltpu.get_barrier_semaphore()
    pl.semaphore_signal(barrier, inc=1, device_id=(1 - sec, me), device_id_type=MESH)
    pl.semaphore_wait(barrier, 1)


def to_section(src, dst, send_sem, recv_sem, sec, me):
    return pltpu.make_async_remote_copy(
        src_ref=src, dst_ref=dst, send_sem=send_sem, recv_sem=recv_sem, device_id=(1 - sec, me), device_id_type=MESH
    )


def feed_kernel(shift, load, *refs):
    n = len(load.items)
    tok_ref, inc_ref, att_ref, vec_ref, bias_ref, out_w, fc1_w, fc2_w = refs[:8]
    sources, refs = refs[8 : 8 + 2 * n], refs[8 + 2 * n :]
    res_ref, pre_ref, hidden_ref, n2_ref, att_rows_ref, low_ref = refs[:6]
    refs = refs[6:]
    if shift:
        next_ref, refs = refs[0], refs[1:]
    outs, refs = refs[:n], refs[n:]
    refs, load_sems = refs[: len(refs) - 3 * n], refs[len(refs) - 3 * n :]
    out_buf, fc1_buf, fc2_buf, t_buf, sems = refs[:5]
    sec, me = place()
    pairs = [("out", out_w, out_buf, (0, D))]
    pairs += [("fc1", fc1_w, fc1_buf, cols) for cols in slices(FFP)]
    pairs += [("fc2", fc2_w, fc2_buf, cols) for cols in slices(FFP)]
    stream = Stream(pairs, sems)
    stream.start()
    if shift:
        greet_section(sec, me)
    taken = load.begin(sources, outs, load_sems)
    att = jnp.concatenate([att_ref[h].astype(F32) for h in range(HEADS)], axis=0).T.astype(BF)
    for w in range(HEADS):
        att_rows_ref[w % 4, w // 4] = att_ref[w]
    stream.wait("out", 0)
    residual = pick(sec, tok_ref, inc_ref) + dot(att, out_buf[...]) + row(vec_ref, OUT_BIAS)
    res_ref[...] = residual
    xhat, _ = normalised(residual)
    n2 = (xhat * row(vec_ref, GAIN2) + row(vec_ref, BIAS2)).astype(BF)
    total = None
    for at, end in slices(FFP):
        stream.wait("fc1", at)
        pre = dot(n2, fc1_buf[:, at:end]) + bias_ref[:, at:end]
        pre_ref[:, at:end] = pre
        hidden = gelu_tanh(pre)
        hidden_ref[:, at:end] = hidden.astype(BF)
        t_buf[at:end, :] = hidden.T.astype(BF)
    for at, end in slices(FFP):
        stream.wait("fc2", at)
    total = dot(fc2_buf[...], t_buf[...])
    low_ref[...] = (residual + total.T + row(vec_ref, FC2_BIAS)).astype(BF)
    if shift:
        copy = to_section(low_ref, next_ref, refs[5], refs[6], sec, me)
        copy.start()
    for one in taken:
        one.forward()
    put_owners(n2_ref, n2.astype(F32))
    if shift:
        copy.wait()
    for one in taken:
        one.finish()


def feed_forward(tok, inc, att, vec, bias, out_w, fc1_w, fc2_w, cid, shift, items=()):
    tokens = tok.shape[0]
    load = Load(items)
    anywhere, vmem = pl.BlockSpec(memory_space=pl.ANY), pl.BlockSpec(memory_space=pltpu.VMEM)
    dma = pltpu.SemaphoreType.DMA
    params = {} if cid is None else dict(collective_id=cid, has_side_effects=True)
    rows = jax.ShapeDtypeStruct((4, 4, HEAD_DIM, tokens), BF)
    low = jax.ShapeDtypeStruct((tokens, D), BF)
    return pl.pallas_call(
        functools.partial(feed_kernel, shift, load),
        out_shape=[
            jax.ShapeDtypeStruct((tokens, D), F32),
            jax.ShapeDtypeStruct((tokens, FFP), F32),
            jax.ShapeDtypeStruct((tokens, FFP), BF),
            rows,
            rows,
            low,
        ]
        + [low] * shift
        + load.shapes,
        in_specs=[vmem] * 5 + [anywhere] * (3 + len(load.sources)),
        out_specs=[vmem] * (6 + shift) + [anywhere] * len(load.shapes),
        scratch_shapes=[
            pltpu.VMEM((D, D), BF),
            pltpu.VMEM((D, FFP), BF),
            pltpu.VMEM((D, FFP), BF),
            pltpu.VMEM((FFP, tokens), BF),
            dma((1 + 2 * len(slices(FFP)),)),
        ]
        + [dma, dma] * shift
        + load.scratch,
        compiler_params=pltpu.CompilerParams(vmem_limit_bytes=60 << 20, **params),
    )(tok, inc, att, vec, bias, out_w, fc1_w, fc2_w, *load.sources)


def feed_back_kernel(load, cot_ref, inc_ref, vec_ref, *refs):
    n = len(load.items)
    kept, refs = refs[:4], refs[4:]
    out_w, fc1_w, fc2_w = refs[:3]
    sources, refs = refs[3 : 3 + 2 * n], refs[3 + 2 * n :]
    rg_ref, ag_ref, fc_ref, pg_ref, branch_ref, sum_ref = refs[:6]
    outs, refs = refs[6 : 6 + n], refs[6 + n :]
    pre_buf, res_buf, out_buf, fc1_buf, fc2_buf, t_buf, kept_sem, sems = refs[:8]
    sec, _ = place()
    pairs = []
    pairs += [("fc2", fc2_w, fc2_buf, cols) for cols in slices(FFP)]
    pairs += [("fc1", fc1_w, fc1_buf, cols) for cols in slices(FFP)]
    pairs.append(("out", out_w, out_buf, (0, D)))
    stream = Stream(pairs, sems)
    fetch(kept, (pre_buf, res_buf), kept_sem, sec)
    stream.start()
    taken = load.begin(sources, outs, refs[8:])
    grad = jnp.where(sec == 0, inc_ref[...].astype(F32), cot_ref[...].astype(F32))
    fc_grad = grad.astype(BF)
    put_owners(fc_ref, grad)
    fetched(kept, (pre_buf, res_buf), kept_sem)
    total = None
    for at, end in slices(FFP):
        slope = gelu_slope(pre_buf[:, at:end])
        stream.wait("fc2", at)
        pre_wide = dot(fc_grad, fc2_buf[:, at:end]) * slope
        pre_grad = pre_wide.astype(BF)
        pg_ref[:, at:end] = pre_grad
        t_buf[at:end, :] = pre_wide.T.astype(BF)
    for at, end in slices(FFP):
        stream.wait("fc1", at)
    total = dot(fc1_buf[...], t_buf[...])
    xhat, rstd = normalised(res_buf[...])
    part, gain_sum, bias_sum = norm_backward(total.T, xhat, rstd, row(vec_ref, GAIN2))
    residual_grad = grad + part
    rg_ref[...] = residual_grad
    branch = residual_grad.astype(BF)
    branch_ref[...] = branch
    for one in taken:
        one.forward()
    stream.wait("out", 0)
    att_grad = dot(out_buf[...], residual_grad.T.astype(BF))
    for h in range(HEADS):
        ag_ref[h] = att_grad[h * HEAD_DIM : (h + 1) * HEAD_DIM].astype(BF)
    sum_ref[0:1, :] = jnp.sum(branch.astype(F32), axis=0, keepdims=True)
    sum_ref[1:2, :] = gain_sum
    sum_ref[2:3, :] = bias_sum
    sum_ref[3:4, :] = jnp.sum(fc_grad.astype(F32), axis=0, keepdims=True)
    for one in taken:
        one.finish()


def feed_backward(cot, inc, vec, kept, out_w, fc1_w, fc2_w, cid, items=()):
    tokens = cot.shape[0]
    load = Load(items)
    params = {} if cid is None else dict(collective_id=cid, has_side_effects=True)
    anywhere, vmem = pl.BlockSpec(memory_space=pl.ANY), pl.BlockSpec(memory_space=pltpu.VMEM)
    dma = pltpu.SemaphoreType.DMA
    return pl.pallas_call(
        functools.partial(feed_back_kernel, load),
        out_shape=[
            jax.ShapeDtypeStruct((tokens, D), F32),
            jax.ShapeDtypeStruct((HEADS, HEAD_DIM, tokens), BF),
            jax.ShapeDtypeStruct((4, 4, HEAD_DIM, tokens), BF),
            jax.ShapeDtypeStruct((tokens, FFP), BF),
            jax.ShapeDtypeStruct((tokens, D), BF),
            jax.ShapeDtypeStruct((4, D), F32),
        ]
        + load.shapes,
        in_specs=[vmem] * 3 + [anywhere] * (7 + len(load.sources)),
        out_specs=[vmem] * 6 + [anywhere] * len(load.shapes),
        scratch_shapes=[
            pltpu.VMEM((tokens, FFP), F32),
            pltpu.VMEM((tokens, D), F32),
            pltpu.VMEM((D, D), BF),
            pltpu.VMEM((D, FFP), BF),
            pltpu.VMEM((D, FFP), BF),
            pltpu.VMEM((FFP, tokens), BF),
            dma((2,)),
            dma((1 + 2 * len(slices(FFP)),)),
        ]
        + load.scratch,
        compiler_params=pltpu.CompilerParams(vmem_limit_bytes=60 << 20, **params),
    )(cot, inc, vec, *kept, out_w, fc1_w, fc2_w, *load.sources)


def qkv_back_kernel(shift, load, *refs):
    n = len(load.items)
    tok_ref, inc_ref, vec_ref, rg_ref, dq_ref, dkv_ref, w_ref = refs[:7]
    sources, refs = refs[7 : 7 + 2 * n], refs[7 + 2 * n :]
    grad_ref, dqkv_ref, sum_ref, qsum_ref = refs[:4]
    refs = refs[4:]
    if shift:
        next_ref, refs = refs[0], refs[1:]
    outs, refs = refs[:n], refs[n:]
    refs, load_sems = refs[: len(refs) - 3 * n], refs[len(refs) - 3 * n :]
    w_buf, sems = refs[:2]
    sec, me = place()
    stream = Stream([("w", w_ref, w_buf, cols) for cols in slices(3 * D, 384)], sems)
    stream.start()
    if shift:
        greet_section(sec, me)
    taken = load.begin(sources, outs, load_sems)
    kv = [dkv_ref[h].astype(F32) for h in range(HEADS)]
    rows = [dq_ref[h].astype(F32) for h in range(HEADS)]
    rows += [part[:HEAD_DIM] for part in kv] + [part[HEAD_DIM:] for part in kv]
    dqkv = jnp.concatenate(rows, axis=0).astype(BF)
    dqkv_ref[...] = dqkv
    qsum_ref[...] = nt(jnp.ones((8, dqkv.shape[1]), BF), dqkv)
    total = None
    for at, end in slices(3 * D, 384):
        stream.wait("w", at)
        part = dot(w_buf[:, at:end], dqkv[at:end])
        total = part if total is None else total + part
    xhat, rstd = normalised(pick(sec, tok_ref, inc_ref))
    part, gain_sum, bias_sum = norm_backward(total.T, xhat, rstd, row(vec_ref, GAIN1))
    grad = rg_ref[...] + part
    grad_ref[...] = grad
    if shift:
        low_buf = refs[2]
        low_buf[...] = grad.astype(BF)
        copy = to_section(low_buf, next_ref, refs[3], refs[4], sec, me)
        copy.start()
    sum_ref[0:1, :] = gain_sum
    sum_ref[1:2, :] = bias_sum
    if shift:
        copy.wait()
    for one in taken:
        one.forward()
    for one in taken:
        one.finish()


def qkv_backward(tok, inc, vec, residual_grad, dq, dkv, w, cid, shift, items=()):
    tokens = tok.shape[0]
    load = Load(items)
    anywhere, vmem = pl.BlockSpec(memory_space=pl.ANY), pl.BlockSpec(memory_space=pltpu.VMEM)
    dma = pltpu.SemaphoreType.DMA
    params = {} if cid is None else dict(collective_id=cid, has_side_effects=True)
    return pl.pallas_call(
        functools.partial(qkv_back_kernel, shift, load),
        out_shape=[
            jax.ShapeDtypeStruct((tokens, D), F32),
            jax.ShapeDtypeStruct((3 * D, tokens), BF),
            jax.ShapeDtypeStruct((2, D), F32),
            jax.ShapeDtypeStruct((8, 3 * D), F32),
        ]
        + [jax.ShapeDtypeStruct((tokens, D), BF)] * shift
        + load.shapes,
        in_specs=[vmem] * 6 + [anywhere] * (1 + len(load.sources)),
        out_specs=[vmem] * (4 + shift) + [anywhere] * len(load.shapes),
        scratch_shapes=[pltpu.VMEM((D, 3 * D), BF), dma((len(slices(3 * D, 384)),))]
        + [pltpu.VMEM((tokens, D), BF), dma, dma] * shift
        + load.scratch,
        compiler_params=pltpu.CompilerParams(vmem_limit_bytes=60 << 20, **params),
    )(tok, inc, vec, residual_grad, dq, dkv, w, *load.sources)


def pad_ff(x):
    return jnp.pad(x, ((0, 0),) * (x.ndim - 1) + ((0, FFP - FF),))


TENSORS = ("fc2", "fc1", "out", "qkv")


def final_kernel(tiles, early, late, *refs):
    refs = list(refs)

    def take(n):
        part = refs[:n]
        del refs[:n]
        return part

    small_ref = take(1)[0]
    x_refs = {name: take(2) for name in TENSORS}
    early_refs = take(len(early))
    late_refs = take(2 * len(late))
    small_out, bias_out = take(2)
    out_refs = dict(zip(TENSORS, take(4)))
    y_bufs = dict(zip(TENSORS, take(4)))
    x_buf = take(1)[0]
    g_bufs, one_bufs, two_bufs = [dict(zip(TENSORS, take(4))) for _ in range(3)]
    small_got, bias_buf, bias_got = take(3)
    early_sem, small_send, small_recv, bias_send, bias_recv = take(5)
    sems = {name: take(4) for name in TENSORS}
    late_sems = [take(3) for _ in late]

    sec, me = place()
    z, low = me // 4, me % 4
    pair = z + 1 - 2 * (z % 2)
    count = small_ref.shape[0]

    def begin(name):
        for other, one in behind:
            if other == name:
                one.start()

    loads = []
    for i, (name, batch, cols) in enumerate(early):
        dst = y_bufs[name].at[4 * batch : 4 * batch + 4]
        if cols is not None:
            dst = dst.at[:, :, cols[0] : cols[1]]
        loads.append((name, cols, pltpu.make_async_copy(early_refs[i], dst, early_sem.at[i])))

    def place_rows(name):
        rows = []
        for owner in (z, 3 - z, pair, 3 - pair):
            rows.append(
                jnp.concatenate(
                    [x_refs[name][batch][k, owner].astype(F32) for batch in range(2) for k in range(4)], axis=1
                )
            )
        x_buf[...] = jnp.concatenate(rows, axis=0).astype(BF)

    def meanwhile():
        for cols in ((0, SPLIT), (SPLIT, FFP)):
            for name, part, load in loads:
                if name == "fc2" and part == cols:
                    load.start()
        place_rows("fc2")

    greet_all(count, sec, me, meanwhile)
    behind = []
    for i, (name, batch, item) in enumerate(late):

        def slot(k, name=name, batch=batch, item=item):
            ref = y_bufs[name].at[4 * batch + k]
            return ref if item.cols is None else ref.at[:, item.cols[0] : item.cols[1]]

        behind.append((name, PlaneCopies(item, late_refs[2 * i], late_refs[2 * i + 1], slot, *late_sems[i])))
    begin("fc1")
    smalls = []
    for d in range(1, count):
        target = (me + d) % count
        smalls.append(
            pltpu.make_async_remote_copy(
                src_ref=small_ref.at[target],
                dst_ref=small_got.at[d],
                send_sem=small_send.at[d],
                recv_sem=small_recv.at[d],
                device_id=(sec, target),
                device_id_type=MESH,
            )
        )
        smalls[-1].start()

    def first(name, i):
        send, recv = sems[name][0], sems[name][1]
        return pltpu.make_async_remote_copy(
            src_ref=g_bufs[name].at[i, 2:4],
            dst_ref=one_bufs[name].at[i],
            send_sem=send.at[i],
            recv_sem=recv.at[i],
            device_id=(sec, pair * 4 + low),
            device_id_type=MESH,
        )

    def second(name, i):
        send, recv = sems[name][2], sems[name][3]
        return pltpu.make_async_remote_copy(
            src_ref=g_bufs[name].at[i, 1],
            dst_ref=two_bufs[name].at[i],
            send_sem=send.at[i],
            recv_sem=recv.at[i],
            device_id=(sec, (3 - z) * 4 + low),
            device_id_type=MESH,
        )

    def ready(name):
        for other, one in behind:
            if other == name:
                one.forward()
        if name in ("fc1", "qkv"):
            begin({"fc1": "qkv", "qkv": "out"}[name])
        for other, _, load in loads:
            if other == name:
                load.wait()
        for other, one in behind:
            if other == name:
                one.finish()
        place_rows(name)

    def compute_first():
        for cols in ((0, SPLIT), (SPLIT, FFP)):
            for name, part, load in loads:
                if name == "fc2" and part == cols:
                    load.wait()
                elif name != "fc2" and cols[0]:
                    load.start()
            width = tiles["fc2"][1]
            lax.fori_loop(cols[0] // width, cols[1] // width, lambda i, carry: (compute("fc2", i), carry)[1], 0)

    def columns(name, i):
        width = tiles[name][1]
        return pl.ds(pl.multiple_of(i * width, 128), width)

    def compute(name, i):
        width = tiles[name][1]
        buf = y_bufs[name]
        if name == "qkv":
            rows = pl.ds(pl.multiple_of(i * width, 128), width)
            y = jnp.concatenate([buf[part, rows, :] for part in range(8)], axis=1)
            total = lax.dot_general(x_buf[...], y, (((1,), (1,)), ((), ())), preferred_element_type=F32)
        else:
            y = jnp.concatenate([buf[part, :, columns(name, i)] for part in range(8)], axis=0)
            total = dot(x_buf[...], y)
        if name == "fc1":
            bias_buf[i] = dot(jnp.ones((8, y.shape[0]), BF), y)[0:1]
        g_bufs[name][i] = total.reshape(4, HEAD_DIM, width).astype(BF)
        first(name, i).start()

    def bias_copy(k):
        target = (me + 4 * k) % count
        return pltpu.make_async_remote_copy(
            src_ref=bias_buf,
            dst_ref=bias_got.at[k - 1],
            send_sem=bias_send.at[k - 1],
            recv_sem=bias_recv.at[k - 1],
            device_id=(sec, target),
            device_id_type=MESH,
        )

    def middle(name, i):
        first(name, i).wait_recv()
        out_refs[name][:, columns(name, i)] = g_bufs[name][i, 0].astype(F32) + one_bufs[name][i, 0].astype(F32)
        g_bufs[name][i, 1] = (g_bufs[name][i, 1].astype(F32) + one_bufs[name][i, 1].astype(F32)).astype(BF)
        second(name, i).start()

    def finish(name, i):
        second(name, i).wait_recv()
        out_refs[name][:, columns(name, i)] += two_bufs[name][i].astype(F32)
        first(name, i).wait_send()
        second(name, i).wait_send()

    def loop(name, *steps):
        def body(i, carry):
            for step, which in steps:
                step(which, i)
            return carry

        lax.fori_loop(0, tiles[name][0], body, 0)

    compute_first()
    loop("fc2", (middle, "fc2"))
    ready("fc1")
    loop("fc1", (compute, "fc1"))
    for k in range(1, 4):
        bias_copy(k).start()
    loop("fc1", (middle, "fc1"), (finish, "fc2"))
    ready("qkv")
    loop("qkv", (compute, "qkv"))
    ready("out")
    loop("out", (compute, "out"))
    loop("fc1", (finish, "fc1"))
    loop("qkv", (middle, "qkv"))
    loop("out", (middle, "out"))
    for copy in smalls:
        copy.wait()
    total = small_ref[me]
    for d in range(1, count):
        total = total + small_got[d]
    small_out[...] = total
    for k in range(1, 4):
        bias_copy(k).wait()
    bias_out[...] = bias_buf[...] + bias_got[0] + bias_got[1] + bias_got[2]
    loop("qkv", (finish, "qkv"))
    loop("out", (finish, "out"))


def final(small, xs, early, late, cid):
    count = small.shape[0]
    tokens = xs["qkv"][0].shape[-1]
    widths = {"fc2": FFP, "fc1": FFP, "out": D, "qkv": 3 * D}
    tiles = {name: (w // (256 if name[0] == "f" else 384), 256 if name[0] == "f" else 384) for name, w in widths.items()}
    anywhere, vmem = pl.BlockSpec(memory_space=pl.ANY), pl.BlockSpec(memory_space=pltpu.VMEM)
    args = [small] + [x for name in TENSORS for x in xs[name]]
    n_vmem = len(args)
    args += [e[3] for e in early] + [source for _, _, item in late for source in item.sources]
    dma = pltpu.SemaphoreType.DMA
    scratch = []
    for name in TENSORS:
        shape = (8, widths[name], tokens) if name == "qkv" else (8, tokens, widths[name])
        scratch.append(pltpu.VMEM(shape, BF))
    scratch.append(pltpu.VMEM((4 * HEAD_DIM, 8 * tokens), BF))
    for lead in ((4,), (2,), ()):
        for name in TENSORS:
            scratch.append(pltpu.VMEM((tiles[name][0],) + lead + (HEAD_DIM, tiles[name][1]), BF))
    bias = (tiles["fc1"][0], 1, tiles["fc1"][1])
    scratch += [pltpu.VMEM(small.shape, F32), pltpu.VMEM(bias, F32), pltpu.VMEM((3,) + bias, F32)]
    scratch += [dma((len(early),)), dma((count,)), dma((count,)), dma((3,)), dma((3,))]
    for name in TENSORS:
        scratch += [dma((tiles[name][0],))] * 4
    scratch += [dma, dma((4,)), dma((4,))] * len(late)
    out = pl.pallas_call(
        functools.partial(final_kernel, tiles, [e[:3] for e in early], late),
        out_shape=[jax.ShapeDtypeStruct(small.shape[1:], F32), jax.ShapeDtypeStruct(bias, F32)]
        + [jax.ShapeDtypeStruct((HEAD_DIM, widths[name]), F32) for name in TENSORS],
        in_specs=[vmem] * n_vmem + [anywhere] * (len(args) - n_vmem),
        out_specs=[vmem] * 6,
        scratch_shapes=scratch,
        compiler_params=pltpu.CompilerParams(
            collective_id=cid, has_side_effects=True, vmem_limit_bytes=60 << 20
        ),
    )(*args)
    return out[0], out[1].reshape(FFP), dict(zip(TENSORS, out[2:]))


def on_device(
    tokens,
    cotangent,
    image_of_block,
    ln1_gain,
    ln1_bias,
    qkv_weight,
    qv_bias,
    out_weight,
    out_bias,
    ln2_gain,
    ln2_bias,
    fc1_weight,
    fc1_bias,
    fc2_weight,
    fc2_bias,
):
    sec, me = place()
    small = jnp.stack(
        [ln1_gain[0], ln1_bias[0], qv_bias[0, 0], qv_bias[0, 1], out_bias[0], ln2_gain[0], ln2_bias[0], fc2_bias[0]],
        axis=1,
    )
    small = jnp.pad(small, ((0, 0), (0, BLOCK - 8)))
    near = window(image_of_block)
    shards = [qkv_weight[0], small, out_weight[0], pad_ff(fc1_weight[0]), pad_ff(fc2_weight[0].T)]
    *three, n1, small_all, w_qkv, w_out, w_fc1, w_fc2t = first_tick(near, tokens[0], shards, 2)
    w_qkv = w_qkv.reshape(D, 3 * D)
    w_out = w_out.reshape(D, D)
    w_fc1 = w_fc1.reshape(D, FFP)
    w_fc2t = w_fc2t.reshape(D, FFP)
    vec = small_all.reshape(D, BLOCK)[:, :8].T.astype(F32)
    b_qkv = jnp.concatenate([vec[2:3], jnp.zeros((1, D), F32), vec[3:4]], axis=1)
    b_fc1 = pad_ff(fc1_bias[0]).astype(F32).reshape(1, FFP)

    def choose(at_zero, at_one):
        return jnp.where(sec == 0, at_zero, at_one)

    saved, sent, back, done, input_grads = [], {}, [], [], []
    incoming = [tokens[0]]

    def token_inputs(tick):
        return tokens[min(tick, 1)], incoming[tick]

    def feed(tick, qkv, lse, att, n1, cid, shift, items=()):
        fed = feed_forward(*token_inputs(tick), att, vec, b_fc1, w_out, w_fc1, w_fc2t, cid, shift, items)
        saved.append(
            dict(qkv=qkv, lse=lse, n1=n1, residual=fed[0], pre=fed[1], hidden=fed[2], n2=fed[3], att=fed[4], low=fed[5])
        )
        return fed

    def kept(tick, *names):
        return [saved[at][name] for name in names for at in ((1, 1), (0, 2), (1, 1))[tick]]

    def feed_back(tick, incoming_grad, cid=None, items=()):
        residual_grad, att_grad, fc, pre, branch, four, *got = feed_backward(
            cotangent[min(tick, 1)], incoming_grad, vec, kept(tick, "pre", "residual"), w_out, w_fc1, w_fc2t, cid, items
        )
        back.append(dict(fc=fc, pre=pre, branch=branch))
        return residual_grad, att_grad, list(four), got

    def qkv_back(tick, residual_grad, dq, dkv, sums, cid, shift, items=()):
        inputs = (tokens[max(tick - 1, 0)], incoming[min(tick + 1, 2)])
        input_grad, dqkv, two, qsum, *rest = qkv_backward(
            *inputs, vec, residual_grad, dq, dkv, w_qkv, cid, shift, items
        )
        back[tick]["dqkv"] = dqkv
        input_grads.append(input_grad)
        done.append([two[0], two[1], qsum[0, :D], qsum[0, 2 * D :], *sums])
        return rest

    incoming.append(feed(0, *three, n1, 8, True)[6])

    qkv, n1 = qkv_forward(*token_inputs(1), vec, b_qkv, w_qkv)
    three, _, _ = attention(near, 3, ahead=(1, qkv))
    incoming.append(lax.ppermute(feed(1, *three, n1, None, False)[5], "section", [(0, 1)]))

    def first_batch(name, cols=None):
        return Whole(saved[0][name], saved[1][name], cols)

    def second_batch(name, cols=None):
        return Whole(saved[1][name], saved[2][name], cols)

    residual_grad, att_grad, sums, got = feed_back(0, tokens[0], 11, [first_batch("hidden", (SPLIT, FFP))])
    sent["h0b"] = got[0]
    qkv, n1 = qkv_forward(*token_inputs(2), vec, b_qkv, w_qkv)
    items = [Rows(saved[0][name], saved[1][name]) for name in ("n1", "att", "n2")]
    items.append(first_batch("hidden", (0, SPLIT)))
    three, two, got = attention(near, 4, ahead=(2, qkv), behind=(0, att_grad, kept(0, "qkv", "lse")), items=items)
    sent["n1_0"], sent["att_0"], sent["n2_0"], sent["h0a"] = got
    qkv_back(0, residual_grad, *two, sums, None, False)
    incoming_grad = lax.ppermute(input_grads[0].astype(BF), "section", [(1, 0)])
    feed(2, *three, n1, None, False)
    outputs = jnp.stack([choose(saved[m]["low"], saved[m + 1]["low"]) for m in range(2)])

    residual_grad, att_grad, sums, got = feed_back(1, incoming_grad, 12, [second_batch("hidden", (0, SPLIT))])
    sent["h1a"] = got[0]
    items = [Rows(saved[1][name], saved[2][name]) for name in ("n1", "att", "n2")]
    items.append(second_batch("hidden", (SPLIT, FFP)))
    _, two, got = attention(near, 5, behind=(1, att_grad, kept(1, "qkv", "lse")), items=items)
    sent["n1_1"], sent["att_1"], sent["n2_1"], sent["h1b"] = got
    incoming_grad = qkv_back(1, residual_grad, *two, sums, 9, True)[0]

    residual_grad, att_grad, sums, _ = feed_back(2, incoming_grad)
    items = [Rows(back[1]["fc"], back[0]["fc"]), Rows(back[2]["fc"], back[1]["fc"])]
    items.append(Whole(back[1]["pre"], back[0]["pre"], (SPLIT, FFP)))
    _, two, got = attention(near, 6, behind=(2, att_grad, kept(2, "qkv", "lse")), items=items)
    sent["fc_0"], sent["fc_1"], sent["pre_0b"] = got
    qkv_back(2, residual_grad, *two, sums, None, False)
    input_grads = jnp.stack([choose(input_grads[m + 1], input_grads[m]) for m in range(2)])

    sums = [choose(done[1][i] + done[2][i], done[0][i] + done[1][i]) for i in range(8)]
    by_owner = jnp.stack(sums).reshape(8, HEADS, HEAD_DIM).transpose(1, 0, 2)
    by_owner = jnp.pad(by_owner, ((0, 0), (0, 0), (0, BLOCK - HEAD_DIM)))
    xs = {
        "fc2": [sent["fc_0"], sent["fc_1"]],
        "fc1": [sent["n2_0"], sent["n2_1"]],
        "out": [sent["att_0"], sent["att_1"]],
        "qkv": [sent["n1_0"], sent["n1_1"]],
    }
    early = [
        ("fc2", 0, (0, SPLIT), sent["h0a"]),
        ("fc2", 0, (SPLIT, FFP), sent["h0b"]),
        ("fc2", 1, (0, SPLIT), sent["h1a"]),
        ("fc2", 1, (SPLIT, FFP), sent["h1b"]),
        ("fc1", 0, (SPLIT, FFP), sent["pre_0b"]),
    ]
    late = [
        ("fc1", 0, Whole(back[1]["pre"], back[0]["pre"], (0, SPLIT))),
        ("fc1", 1, Whole(back[2]["pre"], back[1]["pre"])),
        ("qkv", 0, Whole(back[1]["dqkv"], back[0]["dqkv"])),
        ("qkv", 1, Whole(back[2]["dqkv"], back[1]["dqkv"])),
        ("out", 0, Whole(back[1]["branch"], back[0]["branch"])),
        ("out", 1, Whole(back[2]["branch"], back[1]["branch"])),
    ]
    packed, bias, grads = final(by_owner, xs, early, late, 10)
    g_small = packed[:, :HEAD_DIM]
    g_fc1_bias = bias[:FF]
    return (
        outputs[None],
        input_grads[None],
        g_small[0][None],
        g_small[1][None],
        grads["qkv"][None],
        g_small[2:4][None],
        grads["out"][None],
        g_small[4][None],
        g_small[5][None],
        g_small[6][None],
        grads["fc1"][:, :FF][None],
        g_fc1_bias[None],
        grads["fc2"].T[:FF][None],
        g_small[7][None],
    )


BLK_DEV = 1
REACH = 5


def shifted(value, axis, steps):
    count = lax.axis_size(axis)
    initial, last = (max(0, -steps), min(count, count - steps))
    return lax.ppermute(value, axis, [(source, source + steps) for source in range(initial, last)])


def layer_norm(values_in, scale_gain, shift_bias):
    row_mean = jnp.mean(values_in, axis=-1, keepdims=True)
    centred = values_in - row_mean
    row_var = jnp.mean(centred * centred, axis=-1, keepdims=True)
    return centred * lax.rsqrt(row_var + EPSILON) * scale_gain + shift_bias


def gelu_tanh(pre_value):
    return jax.nn.gelu(pre_value, approximate=True)


def heads_of(values_in):
    return values_in.reshape(values_in.shape[0], HEADS, HEAD_DIM)


def image_mask(image_of_block, batch_slot, wide_rank):
    padding = REACH * BLK_DEV
    padded = jnp.pad(image_of_block, ((0, 0), (padding, padding)), constant_values=-1)
    image_row = lax.dynamic_index_in_dim(padded, batch_slot, 0, keepdims=False)
    key_blocks = lax.dynamic_slice_in_dim(image_row, wide_rank * BLK_DEV, (2 * REACH + 1) * BLK_DEV)
    query_blocks = lax.dynamic_slice_in_dim(image_row, wide_rank * BLK_DEV + padding, BLK_DEV)
    return jnp.repeat(query_blocks, BLOCK)[:, None] == jnp.repeat(key_blocks, BLOCK)[None, :]


def keep_slot(buffer_all, new_value, batch_slot, is_live):
    previous = lax.dynamic_index_in_dim(buffer_all, batch_slot, 0, keepdims=False)
    chosen = jnp.where(is_live, new_value, previous)
    return lax.dynamic_update_index_in_dim(buffer_all, chosen, batch_slot, 0)


def near_keys(key_own, value_own, backward_pass):
    key_parts = []
    value_parts = []
    for offset in range(-REACH, REACH + 1):
        if offset == 0:
            received = (key_own, value_own)
        elif backward_pass:
            received = shifted((key_own, value_own), "wide", -offset)
        else:
            received = shifted((key_own, value_own), "wide", -offset)
        key_parts.append(received[0])
        value_parts.append(received[1])
    return (jnp.concatenate(key_parts, axis=0), jnp.concatenate(value_parts, axis=0))


def return_key_grads(key_terms, value_terms):
    row_count = key_terms.shape[0] // (2 * REACH + 1)
    key_total = key_terms[REACH * row_count : (REACH + 1) * row_count]
    value_total = value_terms[REACH * row_count : (REACH + 1) * row_count]
    for position, offset in enumerate(range(-REACH, REACH + 1)):
        if offset != 0:
            piece_pair = (
                key_terms[position * row_count : (position + 1) * row_count],
                value_terms[position * row_count : (position + 1) * row_count],
            )
            received = shifted((piece_pair[0], piece_pair[1]), "wide", offset)
            key_total = key_total + received[0]
            value_total = value_total + received[1]
    return (key_total, value_total)


def project_qkv(layer_in, weights):
    layer_float = layer_in.astype(jnp.float32)
    normed_one = layer_norm(
        layer_float, weights[0].astype(jnp.float32), weights[1].astype(jnp.float32)
    ).astype(jnp.bfloat16)
    mixed = jnp.dot(normed_one, weights[2], preferred_element_type=jnp.float32)
    queries = (mixed[:, :D] + weights[3][0].astype(jnp.float32)).astype(jnp.bfloat16)
    key_own = mixed[:, D : 2 * D].astype(jnp.bfloat16)
    value_own = (mixed[:, 2 * D :] + weights[3][1].astype(jnp.float32)).astype(jnp.bfloat16)
    return (layer_float, normed_one, queries, key_own, value_own)


def attention_probs(queries, keys_near, same_image):
    score_scale = 1.0 / math.sqrt(HEAD_DIM)
    scores = (
        jnp.einsum(
            "qhd,khd->hqk",
            heads_of(queries),
            heads_of(keys_near),
            preferred_element_type=jnp.float32,
        )
        * score_scale
    )
    scores = jnp.where(same_image[None], scores, MASKED_SCORE)
    row_max = jnp.max(scores, axis=-1, keepdims=True)
    exponent = jnp.exp(scores - row_max)
    return exponent / jnp.sum(exponent, axis=-1, keepdims=True)


def finish_layer(layer_float, queries, keys_near, values_near, same_image, weights, hidden_bias):
    probs = attention_probs(queries, keys_near, same_image)
    probs_low = probs.astype(jnp.bfloat16)
    attended = jnp.einsum(
        "hqk,khd->qhd", probs_low, heads_of(values_near), preferred_element_type=jnp.float32
    )
    attended = attended.reshape(queries.shape[0], D).astype(jnp.bfloat16)
    residual = (
        layer_float
        + jnp.dot(attended, weights[4], preferred_element_type=jnp.float32)
        + weights[5].astype(jnp.float32)
    )
    normed_two = layer_norm(
        residual, weights[6].astype(jnp.float32), weights[7].astype(jnp.float32)
    ).astype(jnp.bfloat16)
    hidden_pre = jnp.dot(
        normed_two, weights[8], preferred_element_type=jnp.float32
    ) + hidden_bias.astype(jnp.float32)
    hidden = gelu_tanh(hidden_pre).astype(jnp.bfloat16)
    output = (
        residual
        + jnp.dot(hidden, weights[9], preferred_element_type=jnp.float32)
        + weights[10].astype(jnp.float32)
    )
    return (probs, probs_low, attended, residual, normed_two, hidden_pre, hidden, output)


def layer_backward(
    layer_float,
    normed_one,
    queries,
    keys_near,
    values_near,
    same_image,
    weights,
    hidden_bias,
    grad_out,
):
    score_scale = 1.0 / math.sqrt(HEAD_DIM)
    probs, probs_low, attended, residual, normed_two, hidden_pre, hidden, output = finish_layer(
        layer_float, queries, keys_near, values_near, same_image, weights, hidden_bias
    )
    feed_grad = grad_out.astype(jnp.bfloat16)
    grad_fc2_weight = jnp.einsum("tf,td->fd", hidden, feed_grad, preferred_element_type=jnp.float32)
    grad_fc2_bias = jnp.sum(feed_grad.astype(jnp.float32), axis=0)
    hidden_grad = jnp.einsum("td,fd->tf", feed_grad, weights[9], preferred_element_type=jnp.float32)
    primal_gelu, gelu_pull = jax.vjp(gelu_tanh, hidden_pre)
    pre_grad = gelu_pull(hidden_grad)[0].astype(jnp.bfloat16)
    grad_fc1_bias = jnp.sum(pre_grad.astype(jnp.float32), axis=0)
    grad_fc1_weight = jnp.einsum(
        "td,tf->df", normed_two, pre_grad, preferred_element_type=jnp.float32
    )
    normed_two_grad = jnp.einsum(
        "tf,df->td", pre_grad, weights[8], preferred_element_type=jnp.float32
    )
    primal_two, norm_two_pull = jax.vjp(
        layer_norm, residual, weights[6].astype(jnp.float32), weights[7].astype(jnp.float32)
    )
    residual_part, grad_ln2_gain, grad_ln2_bias = norm_two_pull(normed_two_grad)
    residual_grad = grad_out + residual_part
    branch_grad = residual_grad.astype(jnp.bfloat16)
    grad_out_bias = jnp.sum(branch_grad.astype(jnp.float32), axis=0)
    grad_out_weight = jnp.einsum(
        "tc,td->cd", attended, branch_grad, preferred_element_type=jnp.float32
    )
    attended_grad = jnp.einsum(
        "td,cd->tc", branch_grad, weights[4], preferred_element_type=jnp.float32
    ).astype(jnp.bfloat16)
    attended_heads = heads_of(attended_grad)
    probs_grad = jnp.einsum(
        "qhd,khd->hqk", attended_heads, heads_of(values_near), preferred_element_type=jnp.float32
    )
    value_terms = jnp.einsum(
        "hqk,qhd->khd", probs_low, attended_heads, preferred_element_type=jnp.float32
    )
    score_grad = (
        probs * (probs_grad - jnp.sum(probs * probs_grad, axis=-1, keepdims=True))
    ).astype(jnp.bfloat16)
    query_grad = (
        jnp.einsum(
            "hqk,khd->qhd", score_grad, heads_of(keys_near), preferred_element_type=jnp.float32
        )
        * score_scale
    )
    query_grad = query_grad.reshape(queries.shape[0], D).astype(jnp.bfloat16)
    key_terms = (
        jnp.einsum(
            "hqk,qhd->khd", score_grad, heads_of(queries), preferred_element_type=jnp.float32
        )
        * score_scale
    )
    key_total, value_total = return_key_grads(key_terms.reshape(-1, D), value_terms.reshape(-1, D))
    key_grad = key_total.astype(jnp.bfloat16)
    value_grad = value_total.astype(jnp.bfloat16)
    grad_qv_bias = jnp.stack(
        [
            jnp.sum(query_grad.astype(jnp.float32), axis=0),
            jnp.sum(value_grad.astype(jnp.float32), axis=0),
        ]
    )
    mixed_grad = jnp.concatenate([query_grad, key_grad, value_grad], axis=1)
    grad_qkv_weight = jnp.einsum(
        "tc,tk->ck", normed_one, mixed_grad, preferred_element_type=jnp.float32
    )
    normed_one_grad = jnp.einsum(
        "tk,ck->tc", mixed_grad, weights[2], preferred_element_type=jnp.float32
    )
    primal_one, norm_one_pull = jax.vjp(
        layer_norm, layer_float, weights[0].astype(jnp.float32), weights[1].astype(jnp.float32)
    )
    input_part, grad_ln1_gain, grad_ln1_bias = norm_one_pull(normed_one_grad)
    input_grad = residual_grad + input_part
    grad_terms = (
        grad_ln1_gain,
        grad_ln1_bias,
        grad_qkv_weight,
        grad_qv_bias,
        grad_out_weight,
        grad_out_bias,
        grad_ln2_gain,
        grad_ln2_bias,
        grad_fc1_weight,
        grad_fc2_weight,
        grad_fc2_bias,
    )
    return (input_grad, grad_terms, grad_fc1_bias)


def on_device_near(
    tokens,
    cotangent,
    image_of_block,
    ln1_gain,
    ln1_bias,
    qkv_weight,
    qv_bias,
    out_weight,
    out_bias,
    ln2_gain,
    ln2_bias,
    fc1_weight,
    fc1_bias,
    fc2_weight,
    fc2_bias,
):
    section_rank = lax.axis_index("section")
    wide_rank = lax.axis_index("wide")
    micro_count = tokens.shape[0]
    weights = (
        lax.all_gather(ln1_gain[0], "wide", axis=0, tiled=True),
        lax.all_gather(ln1_bias[0], "wide", axis=0, tiled=True),
        lax.all_gather(qkv_weight[0], "wide", axis=0, tiled=True),
        lax.all_gather(qv_bias[0], "wide", axis=1, tiled=True),
        lax.all_gather(out_weight[0], "wide", axis=0, tiled=True),
        lax.all_gather(out_bias[0], "wide", axis=0, tiled=True),
        lax.all_gather(ln2_gain[0], "wide", axis=0, tiled=True),
        lax.all_gather(ln2_bias[0], "wide", axis=0, tiled=True),
        lax.all_gather(fc1_weight[0], "wide", axis=0, tiled=True),
        lax.all_gather(fc2_weight[0], "wide", axis=1, tiled=True),
        lax.all_gather(fc2_bias[0], "wide", axis=0, tiled=True),
    )
    hidden_bias = fc1_bias[0]
    inputs_kept = jnp.zeros_like(tokens)
    outputs_kept = jnp.zeros_like(tokens)
    incoming = jnp.zeros_like(tokens[0])
    for tick_number in range(micro_count + 1):
        batch_index = tick_number - section_rank
        is_live = (batch_index >= 0) & (batch_index < micro_count)
        batch_slot = jnp.clip(batch_index, 0, micro_count - 1)
        own_tokens = tokens[min(tick_number, micro_count - 1)]
        layer_in = jnp.where(section_rank == 0, own_tokens, incoming)
        same_image = image_mask(image_of_block, batch_slot, wide_rank)
        layer_float, normed_one, queries, key_own, value_own = project_qkv(layer_in, weights)
        keys_near, values_near = near_keys(key_own, value_own, False)
        output = finish_layer(
            layer_float, queries, keys_near, values_near, same_image, weights, hidden_bias
        )[-1]
        output_low = output.astype(jnp.bfloat16)
        inputs_kept = keep_slot(inputs_kept, layer_in, batch_slot, is_live)
        outputs_kept = keep_slot(outputs_kept, output_low, batch_slot, is_live)
        if tick_number < micro_count:
            incoming = shifted(output_low, "section", 1)
    weights_back = (
        lax.all_gather(ln1_gain[0], "wide", axis=0, tiled=True),
        lax.all_gather(ln1_bias[0], "wide", axis=0, tiled=True),
        lax.all_gather(qkv_weight[0], "wide", axis=0, tiled=True),
        lax.all_gather(qv_bias[0], "wide", axis=1, tiled=True),
        lax.all_gather(out_weight[0], "wide", axis=0, tiled=True),
        lax.all_gather(out_bias[0], "wide", axis=0, tiled=True),
        lax.all_gather(ln2_gain[0], "wide", axis=0, tiled=True),
        lax.all_gather(ln2_bias[0], "wide", axis=0, tiled=True),
        lax.all_gather(fc1_weight[0], "wide", axis=0, tiled=True),
        lax.all_gather(fc2_weight[0], "wide", axis=1, tiled=True),
        lax.all_gather(fc2_bias[0], "wide", axis=0, tiled=True),
    )
    grad_totals = tuple((jnp.zeros(array.shape, jnp.float32) for array in weights_back))
    hidden_bias_total = jnp.zeros(hidden_bias.shape, jnp.float32)
    input_grads = jnp.zeros(tokens.shape, jnp.float32)
    incoming_grad = jnp.zeros(tokens.shape[1:], jnp.bfloat16)
    for tick_number in range(micro_count + 1):
        batch_index = tick_number - 1 + section_rank
        is_live = (batch_index >= 0) & (batch_index < micro_count)
        batch_slot = jnp.clip(batch_index, 0, micro_count - 1)
        from_cotangent = cotangent[min(tick_number, micro_count - 1)].astype(jnp.float32)
        grad_out = jnp.where(
            section_rank == 1, from_cotangent, incoming_grad.astype(jnp.float32)
        ) * is_live.astype(jnp.float32)
        layer_in = lax.dynamic_index_in_dim(inputs_kept, batch_slot, 0, keepdims=False)
        same_image = image_mask(image_of_block, batch_slot, wide_rank)
        layer_float, normed_one, queries, key_own, value_own = project_qkv(layer_in, weights_back)
        keys_near, values_near = near_keys(key_own, value_own, True)
        input_grad, grad_terms, hidden_bias_term = layer_backward(
            layer_float,
            normed_one,
            queries,
            keys_near,
            values_near,
            same_image,
            weights_back,
            hidden_bias,
            grad_out,
        )
        grad_totals = tuple(
            (old_total + new_term for old_total, new_term in zip(grad_totals, grad_terms))
        )
        hidden_bias_total = hidden_bias_total + hidden_bias_term
        input_grads = keep_slot(input_grads, input_grad, batch_slot, is_live)
        if tick_number < micro_count:
            incoming_grad = shifted(input_grad.astype(jnp.bfloat16), "section", -1)
    (
        grad_ln1_gain,
        grad_ln1_bias,
        grad_qkv_weight,
        grad_qv_bias,
        grad_out_weight,
        grad_out_bias,
        grad_ln2_gain,
        grad_ln2_bias,
        grad_fc1_weight,
        grad_fc2_weight,
        grad_fc2_bias,
    ) = grad_totals
    row_sums = (
        lax.psum_scatter(grad_ln1_gain, "wide", scatter_dimension=0, tiled=True),
        lax.psum_scatter(grad_ln1_bias, "wide", scatter_dimension=0, tiled=True),
        lax.psum_scatter(grad_qkv_weight, "wide", scatter_dimension=0, tiled=True),
        lax.psum_scatter(grad_out_weight, "wide", scatter_dimension=0, tiled=True),
        lax.psum_scatter(grad_out_bias, "wide", scatter_dimension=0, tiled=True),
        lax.psum_scatter(grad_ln2_gain, "wide", scatter_dimension=0, tiled=True),
        lax.psum_scatter(grad_ln2_bias, "wide", scatter_dimension=0, tiled=True),
        lax.psum_scatter(grad_fc1_weight, "wide", scatter_dimension=0, tiled=True),
        lax.psum_scatter(grad_fc2_bias, "wide", scatter_dimension=0, tiled=True),
    )
    column_sums = (
        lax.psum_scatter(grad_qv_bias, "wide", scatter_dimension=1, tiled=True),
        lax.psum_scatter(grad_fc2_weight, "wide", scatter_dimension=1, tiled=True),
    )
    hidden_bias_sum = lax.psum(hidden_bias_total, "wide")
    return (
        outputs_kept[None],
        input_grads[None],
        row_sums[0][None],
        row_sums[1][None],
        row_sums[2][None],
        column_sums[0][None],
        row_sums[3][None],
        row_sums[4][None],
        row_sums[5][None],
        row_sums[6][None],
        row_sums[7][None],
        hidden_bias_sum[None],
        column_sums[1][None],
        row_sums[8][None],
    )


def specs():
    ins = (
        P(None, "wide", None),
        P(None, "wide", None),
        P(),
        P("section", "wide"),
        P("section", "wide"),
        P("section", "wide", None),
        P("section", None, "wide"),
        P("section", "wide", None),
        P("section", "wide"),
        P("section", "wide"),
        P("section", "wide"),
        P("section", "wide", None),
        P("section", None),
        P("section", None, "wide"),
        P("section", "wide"),
    )
    outs = (
        P("section", None, "wide", None),
        P("section", None, "wide", None),
        P("section", "wide"),
        P("section", "wide"),
        P("section", "wide", None),
        P("section", None, "wide"),
        P("section", "wide", None),
        P("section", "wide"),
        P("section", "wide"),
        P("section", "wide"),
        P("section", "wide", None),
        P("section", None),
        P("section", None, "wide"),
        P("section", "wide"),
    )
    return ins, outs


def solution(mesh):
    ins, outs = specs()
    body = on_device if mesh.shape["wide"] == HEADS else on_device_near
    return jax.shard_map(body, mesh=mesh, in_specs=ins, out_specs=outs, check_vma=False)
```

```python
import functools
import math

import jax
import jax.numpy as jnp
from jax import lax
from jax.experimental import pallas as pl
from jax.experimental.pallas import tpu as pltpu
from jax.sharding import PartitionSpec as P

D = 1152
HEADS = 16
HEAD_DIM = 72
FF = 4304
FFP = -(-FF // 256) * 256
SPLIT = 9 * 256
BLOCK = 128
IMG_BLOCKS = 6
EPSILON = 1e-06
MASKED_SCORE = -1e30
SCALE = 1.0 / math.sqrt(HEAD_DIM)
MESH = pl.DeviceIdType.MESH
BF = jnp.bfloat16
F32 = jnp.float32


def place():
    return lax.axis_index("section"), lax.axis_index("wide")


class Gather:
    def __init__(self, pieces, ins, outs, sems, twice=()):
        self.pieces, self.ins, self.outs, self.count, self.twice = pieces, ins, outs, len(pieces), twice
        self.local_sem = sems[0]
        self.up, self.down, self.yy, self.cc = [(sems[1 + 2 * i], sems[2 + 2 * i]) for i in range(4)]
        self.sec, self.me = place()
        self.z, self.low = self.me // 4, self.me % 4
        self.other_y = self.me - self.low + flip(self.low, 2)
        self.other_c = self.me - self.low + flip(self.low, 1)

    @staticmethod
    def semaphores(pieces, arrays):
        dma = pltpu.SemaphoreType.DMA
        return [dma((arrays,))] + [dma((pieces, 8))] * 4 + [dma((pieces, 4))] * 2 + [dma((pieces, 8))] * 2

    def part(self, piece, origin=None):
        array, at, end = self.pieces[piece]
        return self.ins[array].at[:, at:end] if origin is None else self.outs[array].at[origin, :, at:end]

    def send(self, piece, origin, sems, slot, target, first=False):
        return pltpu.make_async_remote_copy(
            src_ref=self.part(piece) if first else self.part(piece, origin),
            dst_ref=self.part(piece, origin),
            send_sem=sems[0].at[piece, slot],
            recv_sem=sems[1].at[piece, slot],
            device_id=(self.sec, target),
            device_id_type=MESH,
        )

    def mine(self, array):
        return pltpu.make_async_copy(self.ins[array], self.outs[array].at[self.me], self.local_sem.at[array])

    def along(self, piece, origin, first, go_up, go_down, column=0):
        slot = origin // 4 + 4 * column
        if go_up:

            @pl.when(self.z < 3)
            def _():
                self.send(piece, origin, self.up, slot, self.me + 4, first).start()

        if go_down:

            @pl.when(self.z > 0)
            def _():
                self.send(piece, origin, self.down, slot, self.me - 4, first).start()

        if piece not in self.twice or first:
            self.send(piece, origin, self.yy, origin // 4, self.other_y, first).start()
        self.send(piece, origin, self.cc, slot, self.other_c, first).start()

    def columns(self, piece):
        return (0, 1) if piece in self.twice else (0,)

    def step(self, piece, step):
        if step == 1 and piece in self.twice:
            self.send(piece, self.other_y, self.yy, self.z, self.other_y).wait_recv()
            self.along(piece, self.other_y, False, True, True, 1)

        @pl.when(self.z - step >= 0)
        def _():
            for column in self.columns(piece):
                origin = (self.me, self.other_y)[column] - 4 * step
                self.send(piece, origin, self.up, self.z - step + 4 * column, self.me).wait_recv()
                self.along(piece, origin, False, True, False, column)

        @pl.when(self.z + step <= 3)
        def _():
            for column in self.columns(piece):
                origin = (self.me, self.other_y)[column] + 4 * step
                self.send(piece, origin, self.down, self.z + step + 4 * column, self.me).wait_recv()
                self.along(piece, origin, False, False, True, column)

    def slots(self, first, last):
        for k in range(first, last):
            if k == 0:
                for array in range(len(self.ins)):
                    self.mine(array).start()
            if k < self.count:
                self.along(k, self.me, True, True, True)
            for step in range(1, 4):
                if 0 <= k - step < self.count:
                    self.step(k - step, step)

    def across(self, pieces):
        far = self.other_y % 4
        for piece in pieces:
            for step in range(0 if piece in self.twice else 4):
                zo = (self.z + step) % 4
                origin = zo * 4 + far
                self.send(piece, origin, self.yy, zo, self.other_y).wait_recv()
                self.send(piece, origin, self.cc, 4 + zo, self.other_c).start()

    def arrived(self, pieces):
        for piece in pieces:
            for slot in range(8):
                self.send(piece, self.me, self.cc, slot, self.other_c).wait_recv()

    def finish(self):
        for zo in range(4):
            for piece in range(self.count):
                if piece not in self.twice:
                    self.send(piece, self.me, self.yy, zo, self.other_y).wait_send()
                elif zo == 0:
                    self.send(piece, self.me, self.yy, self.z, self.other_y).wait_send()
                for slot in (zo, 4 + zo):
                    self.send(piece, self.me, self.cc, slot, self.other_c).wait_send()

                @pl.when((zo <= self.z) & (self.z < 3))
                def _():
                    for column in self.columns(piece):
                        self.send(piece, self.me, self.up, zo + 4 * column, self.me).wait_send()

                @pl.when((zo >= self.z) & (self.z > 0))
                def _():
                    for column in self.columns(piece):
                        self.send(piece, self.me, self.down, zo + 4 * column, self.me).wait_send()


def flip(low, k):
    return [low, low + 1 - 2 * (low % 2), (low + 2) % 4, 3 - low][k]


def greet_all(count, sec, me, meanwhile=lambda: None):
    barrier = pltpu.get_barrier_semaphore()
    for d in range(1, count):
        pl.semaphore_signal(barrier, inc=1, device_id=(sec, (me + d) % count), device_id_type=MESH)
    meanwhile()
    pl.semaphore_wait(barrier, count - 1)


class Whole:
    def __init__(self, zero, one, cols=None):
        self.sources, self.cols = (zero, one), cols

    def shape(self):
        rows, cols = self.sources[0].shape
        return (4, rows, cols if self.cols is None else self.cols[1] - self.cols[0])

    def source(self, ref, low, k):
        return ref if self.cols is None else ref.at[:, self.cols[0] : self.cols[1]]

    forwarded = True


class Rows:
    def __init__(self, zero, one):
        self.sources = (zero, one)

    def shape(self):
        return self.sources[0].shape

    def source(self, ref, low, k):
        return ref.at[flip(low, k)]

    forwarded = False


class PlaneCopies:
    def __init__(self, item, zero_ref, one_ref, slot, local_sem, send_sem, recv_sem):
        self.item, self.refs, self.slot = item, (zero_ref, one_ref), slot
        self.local_sem, self.send_sem, self.recv_sem = local_sem, send_sem, recv_sem
        self.sec, self.me = place()
        self.low = self.me % 4

    def remote(self, src, k, to):
        return pltpu.make_async_remote_copy(
            src_ref=src,
            dst_ref=self.slot(k),
            send_sem=self.send_sem.at[k],
            recv_sem=self.recv_sem.at[k],
            device_id=(self.sec, self.me - self.low + flip(self.low, to)),
            device_id_type=MESH,
        )

    def local(self, ref):
        return pltpu.make_async_copy(self.item.source(ref, self.low, 0), self.slot(0), self.local_sem)

    def start(self):
        def go(ref):
            self.local(ref).start()
            for k in (2, 1) if self.item.forwarded else (2, 3, 1):
                self.remote(self.item.source(ref, self.low, k), k, k).start()

        @pl.when(self.sec == 0)
        def _():
            go(self.refs[0])

        @pl.when(self.sec == 1)
        def _():
            go(self.refs[1])

    def forward(self):
        if self.item.forwarded:
            self.remote(self.slot(2), 2, 2).wait_recv()
            self.remote(self.slot(2), 3, 1).start()

    def finish(self):
        self.local(self.refs[0]).wait()
        for k in (1, 2, 3):
            self.remote(self.slot(k), k, k).wait_send()
            if k != 2 or not self.item.forwarded:
                self.remote(self.slot(k), k, k).wait_recv()


def dot(a, b):
    return jnp.dot(a, b, preferred_element_type=F32)


def window(image_of_block):
    micro, blocks = image_of_block.shape
    own, other = image_of_block[:, :, None], image_of_block[:, None, :]
    begin = jnp.sum((other < own).astype(jnp.int32), axis=2)
    end = jnp.sum((other <= own).astype(jnp.int32), axis=2)
    first = jnp.minimum(begin, blocks - IMG_BLOCKS)
    shape = (micro, blocks, IMG_BLOCKS, BLOCK)
    at = first[:, :, None, None] + lax.broadcasted_iota(jnp.int32, shape, 2)
    same = (at >= begin[:, :, None, None]) & (at < end[:, :, None, None])
    return first, jnp.where(same, 0.0, MASKED_SCORE).astype(F32)


def near_rows(ref, start):
    return jnp.concatenate([ref[start + j] for j in range(IMG_BLOCKS)], axis=0)


def near_columns(ref, start):
    return jnp.concatenate([ref[start + j] for j in range(IMG_BLOCKS)], axis=1)


def fetch(pairs, buffers, sems, sec):
    for which in range(2):

        @pl.when(sec == which)
        def _():
            for i, buffer in enumerate(buffers):
                pltpu.make_async_copy(pairs[2 * i + which], buffer, sems.at[i]).start()


def fetched(pairs, buffers, sems):
    for i, buffer in enumerate(buffers):
        pltpu.make_async_copy(pairs[2 * i], buffer, sems.at[i]).wait()


class ToAll:
    def __init__(self, block, dst, send, recv, sec, me, count):
        self.block, self.dst, self.send, self.recv = block, dst, send, recv
        self.sec, self.me, self.count = sec, me, count

    def copy(self, d):
        return pltpu.make_async_remote_copy(
            src_ref=self.block(d),
            dst_ref=self.dst.at[self.me],
            send_sem=self.send.at[d],
            recv_sem=self.recv.at[d],
            device_id=(self.sec, (self.me + d) % self.count),
            device_id_type=MESH,
        )

    def start(self):
        for d in sorted(range(1, self.count), key=lambda d: abs(d - self.count // 2)):
            self.copy(d).start()

    def start_one(self, d):
        @pl.when(d > 0)
        def _():
            self.copy(d).start()

    def wait(self):
        for d in range(1, self.count):
            self.copy(d).wait()


class Forward:
    def __init__(self, tick, near, x_ref, outs, scratch):
        self.first_ref, self.bias_ref = near
        self.x_ref = x_ref
        self.qkv_ref, self.lse_ref, self.att_ref = outs
        self.k_all, self.vt_all, self.o_buf, self.local_sem, *sems = scratch
        self.count = x_ref.shape[0]
        sec, self.me = place()
        self.slot = jnp.minimum(jnp.maximum(tick - sec, 0), 1)
        rest = (sec, self.me, self.count)
        self.arrive = ToAll(lambda d: x_ref.at[(self.me + d) % self.count], self.qkv_ref, *sems[:2], *rest)
        self.leave = ToAll(lambda d: self.o_buf.at[d], self.att_ref, *sems[2:], *rest)

    @staticmethod
    def scratch(blocks):
        dma = pltpu.SemaphoreType.DMA
        return [
            pltpu.VMEM((blocks, BLOCK, HEAD_DIM), BF),
            pltpu.VMEM((blocks, HEAD_DIM, BLOCK), BF),
            pltpu.VMEM((blocks, HEAD_DIM, BLOCK), BF),
            dma,
        ] + [dma((blocks,))] * 4

    @staticmethod
    def shapes(blocks):
        return [
            jax.ShapeDtypeStruct((blocks, 3 * HEAD_DIM, BLOCK), BF),
            jax.ShapeDtypeStruct((blocks, 1, BLOCK), F32),
            jax.ShapeDtypeStruct((blocks, HEAD_DIM, BLOCK), BF),
        ]

    def own(self):
        return pltpu.make_async_copy(self.x_ref.at[self.me], self.qkv_ref.at[self.me], self.local_sem)

    def start(self):
        self.arrive.start()
        self.own().start()

    def wait_in(self):
        self.own().wait()
        self.arrive.wait()

    def compute(self):
        def arrange(j, carry):
            part = self.qkv_ref[j].astype(F32)
            self.k_all[j] = part[HEAD_DIM : 2 * HEAD_DIM].T.astype(BF)
            self.vt_all[j] = part[2 * HEAD_DIM :].astype(BF)
            return carry

        lax.fori_loop(0, self.count, arrange, 0)

        def one_block(d, carry):
            i = (self.me + d) % self.count
            start = self.first_ref[self.slot, i]
            qt = self.qkv_ref[i].astype(F32)[:HEAD_DIM].astype(BF)
            s = dot(near_rows(self.k_all, start), qt) * SCALE
            bias = self.bias_ref[self.slot, i]
            parts = [s[j * BLOCK : (j + 1) * BLOCK] + bias[j : j + 1] for j in range(IMG_BLOCKS)]
            top = parts[0]
            for part in parts[1:]:
                top = jnp.maximum(top, part)
            top = jnp.max(top, axis=0, keepdims=True)
            exps = [jnp.exp(part - top) for part in parts]
            total = exps[0]
            for part in exps[1:]:
                total = total + part
            total = jnp.sum(total, axis=0, keepdims=True)
            e = jnp.concatenate([part.astype(BF) for part in exps], axis=0)
            o = dot(near_columns(self.vt_all, start), e)
            self.o_buf[d] = (o / total).astype(BF)
            self.lse_ref[i] = top + jnp.log(total)
            self.leave.start_one(d)
            return carry

        lax.fori_loop(0, self.count, one_block, 0)
        self.att_ref[self.me] = self.o_buf[0]

    def wait_out(self):
        self.leave.wait()


class Backward:
    def __init__(self, tick, near, kept, x_ref, outs, scratch):
        self.first_ref, self.bias_ref = near
        self.kept, self.x_ref = kept, x_ref
        self.dq_ref, self.dkv_ref = outs
        self.qkv_ref, self.lse_ref, self.do_ref = scratch[:3]
        self.k_all, self.kt_all, self.v_all, self.q_all, self.do_all, self.p_all, self.s_all = scratch[3:10]
        self.dq_buf, self.dkv_buf, self.kept_sem, self.local_sem = scratch[10:14]
        sems = scratch[14:]
        self.count = x_ref.shape[0]
        self.sec, self.me = place()
        self.slot = jnp.minimum(jnp.maximum(tick - 1 + self.sec, 0), 1)
        rest = (self.sec, self.me, self.count)
        self.arrive = ToAll(lambda d: x_ref.at[(self.me + d) % self.count], self.do_ref, *sems[:2], *rest)
        self.leave_q = ToAll(lambda d: self.dq_buf.at[d], self.dq_ref, *sems[2:4], *rest)
        self.leave_kv = ToAll(lambda d: self.dkv_buf.at[d], self.dkv_ref, *sems[4:], *rest)

    @staticmethod
    def scratch(blocks):
        dma = pltpu.SemaphoreType.DMA
        return [
            pltpu.VMEM((blocks, 3 * HEAD_DIM, BLOCK), BF),
            pltpu.VMEM((blocks, 1, BLOCK), F32),
            pltpu.VMEM((blocks, HEAD_DIM, BLOCK), BF),
            pltpu.VMEM((blocks, BLOCK, HEAD_DIM), BF),
            pltpu.VMEM((blocks, HEAD_DIM, BLOCK), BF),
            pltpu.VMEM((blocks, BLOCK, HEAD_DIM), BF),
            pltpu.VMEM((blocks, BLOCK, HEAD_DIM), BF),
            pltpu.VMEM((blocks, BLOCK, HEAD_DIM), BF),
            pltpu.VMEM((blocks, IMG_BLOCKS, BLOCK, BLOCK), BF),
            pltpu.VMEM((blocks, IMG_BLOCKS, BLOCK, BLOCK), BF),
            pltpu.VMEM((blocks, HEAD_DIM, BLOCK), BF),
            pltpu.VMEM((blocks, 2 * HEAD_DIM, BLOCK), BF),
            dma((2,)),
            dma,
        ] + [dma((blocks,))] * 6

    def own(self):
        return pltpu.make_async_copy(self.x_ref.at[self.me], self.do_ref.at[self.me], self.local_sem)

    def start(self):
        self.arrive.start()
        self.own().start()
        fetch(self.kept, (self.qkv_ref, self.lse_ref), self.kept_sem, self.sec)

    def arrange(self):
        fetched(self.kept, (self.qkv_ref, self.lse_ref), self.kept_sem)

        def one(j, carry):
            part = self.qkv_ref[j].astype(F32)
            self.q_all[j] = part[:HEAD_DIM].T.astype(BF)
            self.k_all[j] = part[HEAD_DIM : 2 * HEAD_DIM].T.astype(BF)
            self.v_all[j] = part[2 * HEAD_DIM :].T.astype(BF)
            self.kt_all[j] = part[HEAD_DIM : 2 * HEAD_DIM].astype(BF)
            return carry

        lax.fori_loop(0, self.count, one, 0)

    def wait_in(self):
        self.own().wait()
        self.arrive.wait()

    def by_query(self):
        def turn(j, carry):
            self.do_all[j] = self.do_ref[j].astype(F32).T.astype(BF)
            return carry

        lax.fori_loop(0, self.count, turn, 0)

        def one(d, carry):
            i = (self.me + d) % self.count
            start = self.first_ref[self.slot, i]
            qt = self.qkv_ref[i].astype(F32)[:HEAD_DIM].astype(BF)
            s = dot(near_rows(self.k_all, start), qt) * SCALE
            shift = self.bias_ref[self.slot, i] - self.lse_ref[i]
            probs = [jnp.exp(s[j * BLOCK : (j + 1) * BLOCK] + shift[j : j + 1]) for j in range(IMG_BLOCKS)]
            dp = dot(near_rows(self.v_all, start), self.do_ref[i])
            total = probs[0] * dp[:BLOCK]
            for j in range(1, IMG_BLOCKS):
                total = total + probs[j] * dp[j * BLOCK : (j + 1) * BLOCK]
            total = jnp.sum(total, axis=0, keepdims=True)
            ds = jnp.concatenate(
                [(probs[j] * (dp[j * BLOCK : (j + 1) * BLOCK] - total)).astype(BF) for j in range(IMG_BLOCKS)], axis=0
            )
            for j in range(IMG_BLOCKS):
                self.p_all[i, j] = probs[j].astype(BF)
                self.s_all[i, j] = ds[j * BLOCK : (j + 1) * BLOCK]
            self.dq_buf[d] = (dot(near_columns(self.kt_all, start), ds) * SCALE).astype(BF)
            self.leave_q.start_one(d)
            return carry

        lax.fori_loop(0, self.count, one, 0)
        self.dq_ref[self.me] = self.dq_buf[0]

    def by_key(self):
        def one(d, carry):
            j = (self.me + d) % self.count
            start = self.first_ref[self.slot, j]
            place_in = jnp.clip(j - start, 0, IMG_BLOCKS - 1)
            same = (self.bias_ref[self.slot, j] == 0.0).astype(F32).astype(BF)
            p, ds = [], []
            for m in range(IMG_BLOCKS):
                p.append(self.p_all[start + m, place_in] * same[m : m + 1])
                ds.append(self.s_all[start + m, place_in] * same[m : m + 1])
            dv = dot(jnp.concatenate(p, axis=1), near_rows(self.do_all, start))
            dk = dot(jnp.concatenate(ds, axis=1), near_rows(self.q_all, start)) * SCALE
            self.dkv_buf[d] = jnp.concatenate([dk.T, dv.T], axis=0).astype(BF)
            self.leave_kv.start_one(d)
            return carry

        lax.fori_loop(0, self.count, one, 0)
        self.dkv_ref[self.me] = self.dkv_buf[0]

    def wait_out(self):
        self.leave_q.wait()
        self.leave_kv.wait()


def attention_kernel(ahead, behind, items, *refs):
    refs = list(refs)

    def take(n):
        part = refs[:n]
        del refs[:n]
        return part

    n = len(items)
    near = take(2)
    x_ref = take(1) if ahead is not None else None
    kept, g_ref = (take(4), take(1)) if behind is not None else (None, None)
    sources = take(2 * n)
    ahead_out = take(3) if ahead is not None else None
    behind_out = take(2) if behind is not None else None
    outs = take(n)
    f = b = None
    blocks = (x_ref or g_ref)[0].shape[0]
    sec, me = place()
    if ahead is not None:
        f = Forward(ahead, near, x_ref[0], ahead_out, take(len(Forward.scratch(blocks))))
    if behind is not None:
        b = Backward(behind, near, kept, g_ref[0], behind_out, take(len(Backward.scratch(blocks))))
    copies = []
    for i, item in enumerate(items):
        into = lambda k, i=i: outs[i].at[k]
        copies.append(PlaneCopies(item, sources[2 * i], sources[2 * i + 1], into, *take(3)))
    greet_all(blocks, sec, me)

    if b:
        b.start()
        b.arrange()
        b.wait_in()
    if f:
        f.start()
    if f and not b:
        f.wait_in()
    for copy in reversed(copies):
        copy.start()
    if b:
        b.by_query()
        b.by_key()
    if f and b:
        f.wait_in()
    if f:
        f.compute()
    for copy in copies:
        copy.forward()
    if f:
        f.wait_out()
    if b:
        b.wait_out()
    for copy in copies:
        copy.finish()


def attention(near, cid, ahead=None, behind=None, items=()):
    first_in = ahead[1] if ahead else behind[1]
    blocks = first_in.shape[0]
    n = len(items)
    sources = [source for item in items for source in item.sources]
    anywhere, vmem, smem = [pl.BlockSpec(memory_space=m) for m in (pl.ANY, pltpu.VMEM, pltpu.SMEM)]
    dma = pltpu.SemaphoreType.DMA
    args, scratch, shapes = [], [], []
    if ahead:
        args.append(ahead[1])
        scratch += Forward.scratch(blocks)
        shapes += Forward.shapes(blocks)
    if behind:
        args += [*behind[2], behind[1]]
        scratch += Backward.scratch(blocks)
        shapes += [
            jax.ShapeDtypeStruct((blocks, HEAD_DIM, BLOCK), BF),
            jax.ShapeDtypeStruct((blocks, 2 * HEAD_DIM, BLOCK), BF),
        ]
    args += sources
    scratch += [dma, dma((4,)), dma((4,))] * n
    in_vmem = len(shapes)
    shapes += [jax.ShapeDtypeStruct(item.shape(), BF) for item in items]
    out = pl.pallas_call(
        functools.partial(attention_kernel, ahead and ahead[0], behind and behind[0], list(items)),
        out_shape=shapes,
        in_specs=[smem, vmem] + [anywhere] * len(args),
        out_specs=[vmem] * in_vmem + [anywhere] * n,
        scratch_shapes=scratch,
        compiler_params=pltpu.CompilerParams(collective_id=cid, has_side_effects=True, vmem_limit_bytes=60 << 20),
    )(*near, *args)
    out = list(out)
    three, out = (out[:3], out[3:]) if ahead else (None, out)
    two, out = (out[:2], out[2:]) if behind else (None, out)
    return three, two, out


def slices(width, step=1024):
    return [(at, min(at + step, width)) for at in range(0, width, step)]


class Stream:
    def __init__(self, pairs, sems):
        self.copies = {}
        for i, (name, ref, buf, cols) in enumerate(pairs):
            src, dst = ref.at[:, cols[0] : cols[1]], buf.at[:, cols[0] : cols[1]]
            self.copies[name, cols[0]] = pltpu.make_async_copy(src, dst, sems.at[i])

    def start(self):
        for copy in self.copies.values():
            copy.start()

    def wait(self, name, at):
        self.copies[name, at].wait()


def normalised(x):
    mean = jnp.mean(x, axis=-1, keepdims=True)
    centred = x - mean
    rstd = lax.rsqrt(jnp.mean(centred * centred, axis=-1, keepdims=True) + EPSILON)
    return centred * rstd, rstd


def norm_backward(grad, xhat, rstd, gain):
    g = grad * gain
    part = g - jnp.mean(g, axis=-1, keepdims=True) - xhat * jnp.mean(g * xhat, axis=-1, keepdims=True)
    return part * rstd, jnp.sum(grad * xhat, axis=0, keepdims=True), jnp.sum(grad, axis=0, keepdims=True)


def greet_plane(sec, me):
    barrier = pltpu.get_barrier_semaphore()
    low = me % 4
    for k in range(1, 4):
        pl.semaphore_signal(barrier, inc=1, device_id=(sec, me - low + flip(low, k)), device_id_type=MESH)
    pl.semaphore_wait(barrier, 3)


class Load:
    def __init__(self, items):
        self.items = list(items)
        self.sources = [source for item in items for source in item.sources]
        self.shapes = [jax.ShapeDtypeStruct(item.shape(), BF) for item in items]
        dma = pltpu.SemaphoreType.DMA
        self.scratch = [dma, dma((4,)), dma((4,))] * len(self.items)

    def begin(self, sources, outs, sems):
        copies = []
        if self.items:
            greet_plane(*place())
        for i, item in enumerate(self.items):
            into = lambda k, i=i: outs[i].at[k]
            copies.append(PlaneCopies(item, sources[2 * i], sources[2 * i + 1], into, *sems[3 * i : 3 * i + 3]))
            copies[-1].start()
        return copies


def gelu_tanh(v):
    c = math.sqrt(2.0 / math.pi)
    return 0.5 * v * (1.0 + jnp.tanh(c * (v + 0.044715 * (v * v * v))))


def gelu_slope(v):
    c = math.sqrt(2.0 / math.pi)
    square = v * v
    t = jnp.tanh(c * (v + 0.044715 * (square * v)))
    return 0.5 * (1.0 + t) + 0.5 * v * (1.0 - t * t) * (c * (1.0 + 3 * 0.044715 * square))


def nt(a, b):
    return lax.dot_general(a, b, (((1,), (1,)), ((), ())), preferred_element_type=F32)


def put_owners(ref, x):
    turned = x.T
    for w in range(HEADS):
        ref[w % 4, w // 4] = turned[w * HEAD_DIM : (w + 1) * HEAD_DIM].astype(BF)


GAIN1, BIAS1, OUT_BIAS, GAIN2, BIAS2, FC2_BIAS = 0, 1, 4, 5, 6, 7


def row(vec_ref, i):
    return vec_ref[i : i + 1, :]


def pick(sec, zero_ref, one_ref):
    return jnp.where(sec == 0, zero_ref[...].astype(F32), one_ref[...].astype(F32))


def qkv_kernel(tok_ref, inc_ref, vec_ref, bias_ref, w_ref, qkv_ref, n1_ref, w_buf, t_buf, sems):
    sec, _ = place()
    stream = Stream([("w", w_ref, w_buf, cols) for cols in slices(3 * D, 384)], sems)
    stream.start()
    xhat, _ = normalised(pick(sec, tok_ref, inc_ref))
    n1 = xhat * row(vec_ref, GAIN1) + row(vec_ref, BIAS1)
    low = n1.astype(BF)
    for at, end in slices(3 * D, 384):
        stream.wait("w", at)
        t_buf[at:end, :] = (dot(low, w_buf[:, at:end]) + bias_ref[:, at:end]).T
    for h in range(HEADS):
        parts = [t_buf[p * D + h * HEAD_DIM : p * D + (h + 1) * HEAD_DIM, :] for p in range(3)]
        qkv_ref[h] = jnp.concatenate(parts, axis=0).astype(BF)
    put_owners(n1_ref, low.astype(F32))


def qkv_forward(tok, inc, vec, bias, w):
    tokens = tok.shape[0]
    anywhere, vmem = pl.BlockSpec(memory_space=pl.ANY), pl.BlockSpec(memory_space=pltpu.VMEM)
    return pl.pallas_call(
        qkv_kernel,
        out_shape=[
            jax.ShapeDtypeStruct((HEADS, 3 * HEAD_DIM, tokens), BF),
            jax.ShapeDtypeStruct((4, 4, HEAD_DIM, tokens), BF),
        ],
        in_specs=[vmem] * 4 + [anywhere],
        out_specs=[vmem] * 2,
        scratch_shapes=[
            pltpu.VMEM((D, 3 * D), BF),
            pltpu.VMEM((3 * D, tokens), F32),
            pltpu.SemaphoreType.DMA((len(slices(3 * D, 384)),)),
        ],
        compiler_params=pltpu.CompilerParams(vmem_limit_bytes=60 << 20),
    )(tok, inc, vec, bias, w)


def first_kernel(first_ref, bias_ref, tok_ref, *refs):
    refs = list(refs)

    def take(n):
        part = refs[:n]
        del refs[:n]
        return part

    shards = take(5)
    ahead_out = take(3)
    n1_ref, small_all, w_qkv = take(3)
    whole = take(3)
    w_buf, t_buf, x_buf, w_sem = take(4)
    f = Forward(0, (first_ref, bias_ref), x_buf, ahead_out, take(len(Forward.scratch(HEADS))))
    work = Gather(first_pieces(shards), shards, (w_buf, small_all, *whole), take(9), TWICE)
    soon, later = [list(range(SOON)), list(range(SOON, work.count))]
    sec, me = place()
    greet_all(HEADS, sec, me)
    work.slots(0, 1)
    xhat, _ = normalised(tok_ref[...].astype(F32))
    xhat = xhat.T
    work.slots(1, SOON + 3)
    for array in range(len(shards)):
        work.mine(array).wait()
    work.across(soon)
    work.arrived(soon)
    keep = pltpu.make_async_copy(w_buf, w_qkv, w_sem)
    keep.start()
    work.slots(SOON + 3, SOON + 4)
    small = jnp.concatenate([small_all[w].astype(F32) for w in range(HEADS)], axis=0)
    n1 = (xhat * small[:, 0:1] + small[:, 1:2]).astype(BF).astype(F32)
    for w in range(HEADS):
        n1_ref[w % 4, w // 4] = n1[w * HEAD_DIM : (w + 1) * HEAD_DIM].astype(BF)
    low = n1.T.astype(BF)

    def columns(i, carry):
        here = pl.ds(pl.multiple_of(i * 384, 384), 384)
        w = jnp.concatenate([w_buf[shard, :, here].astype(F32) for shard in range(HEADS)], axis=0)
        t_buf[here, :] = dot(low, w.astype(BF)).T
        return carry

    lax.fori_loop(0, 3 * D // 384, columns, 0)
    for h in range(HEADS):
        rows = slice(h * HEAD_DIM, (h + 1) * HEAD_DIM)
        parts = [t_buf[p * D + h * HEAD_DIM : p * D + (h + 1) * HEAD_DIM, :] for p in range(3)]
        parts = [parts[0] + small[rows, 2:3], parts[1], parts[2] + small[rows, 3:4]]
        x_buf[h] = jnp.concatenate(parts, axis=0).astype(BF)
    f.start()
    work.slots(SOON + 4, SOON + 5)
    f.wait_in()
    work.slots(SOON + 5, SOON + 7)
    f.compute()
    work.slots(SOON + 7, work.count + 3)
    f.wait_out()
    work.across(later)
    work.arrived(later)
    work.finish()
    keep.wait()


SOON = 4
TWICE = (4,)


def first_pieces(shards):
    pieces = [(1, 0, BLOCK)]
    for array in (0, 2, 3, 4):
        pieces += [(array, at, end) for at, end in slices(shards[array].shape[1], D)]
    return pieces


def first_tick(near, tok, shards, cid):
    tokens = tok.shape[0]
    anywhere, vmem, smem = [pl.BlockSpec(memory_space=m) for m in (pl.ANY, pltpu.VMEM, pltpu.SMEM)]
    whole = [jax.ShapeDtypeStruct((HEADS,) + shard.shape, BF) for shard in shards]
    return pl.pallas_call(
        first_kernel,
        out_shape=Forward.shapes(HEADS)
        + [jax.ShapeDtypeStruct((4, 4, HEAD_DIM, tokens), BF), whole[1], whole[0]]
        + whole[2:],
        in_specs=[smem, vmem, vmem] + [anywhere] * 5,
        out_specs=[vmem] * 5 + [anywhere] * 4,
        scratch_shapes=[
            pltpu.VMEM((HEADS,) + shards[0].shape, BF),
            pltpu.VMEM((3 * D, tokens), F32),
            pltpu.VMEM((HEADS, 3 * HEAD_DIM, tokens), BF),
            pltpu.SemaphoreType.DMA,
        ]
        + Forward.scratch(HEADS)
        + Gather.semaphores(len(first_pieces(shards)), len(shards)),
        compiler_params=pltpu.CompilerParams(collective_id=cid, has_side_effects=True, vmem_limit_bytes=60 << 20),
    )(*near, tok, *shards)


def greet_section(sec, me):
    barrier = pltpu.get_barrier_semaphore()
    pl.semaphore_signal(barrier, inc=1, device_id=(1 - sec, me), device_id_type=MESH)
    pl.semaphore_wait(barrier, 1)


def to_section(src, dst, send_sem, recv_sem, sec, me):
    return pltpu.make_async_remote_copy(
        src_ref=src, dst_ref=dst, send_sem=send_sem, recv_sem=recv_sem, device_id=(1 - sec, me), device_id_type=MESH
    )


def feed_kernel(shift, load, *refs):
    n = len(load.items)
    tok_ref, inc_ref, att_ref, vec_ref, bias_ref, out_w, fc1_w, fc2_w = refs[:8]
    sources, refs = refs[8 : 8 + 2 * n], refs[8 + 2 * n :]
    res_ref, pre_ref, hidden_ref, n2_ref, att_rows_ref, low_ref = refs[:6]
    refs = refs[6:]
    if shift:
        next_ref, refs = refs[0], refs[1:]
    outs, refs = refs[:n], refs[n:]
    refs, load_sems = refs[: len(refs) - 3 * n], refs[len(refs) - 3 * n :]
    out_buf, fc1_buf, fc2_buf, t_buf, sems = refs[:5]
    sec, me = place()
    pairs = [("out", out_w, out_buf, (0, D))]
    pairs += [("fc1", fc1_w, fc1_buf, cols) for cols in slices(FFP)]
    pairs += [("fc2", fc2_w, fc2_buf, cols) for cols in slices(FFP)]
    stream = Stream(pairs, sems)
    stream.start()
    if shift:
        greet_section(sec, me)
    taken = load.begin(sources, outs, load_sems)
    att = jnp.concatenate([att_ref[h].astype(F32) for h in range(HEADS)], axis=0).T.astype(BF)
    for w in range(HEADS):
        att_rows_ref[w % 4, w // 4] = att_ref[w]
    stream.wait("out", 0)
    residual = pick(sec, tok_ref, inc_ref) + dot(att, out_buf[...]) + row(vec_ref, OUT_BIAS)
    res_ref[...] = residual
    xhat, _ = normalised(residual)
    n2 = (xhat * row(vec_ref, GAIN2) + row(vec_ref, BIAS2)).astype(BF)
    total = None
    for at, end in slices(FFP):
        stream.wait("fc1", at)
        pre = dot(n2, fc1_buf[:, at:end]) + bias_ref[:, at:end]
        pre_ref[:, at:end] = pre
        hidden = gelu_tanh(pre)
        hidden_ref[:, at:end] = hidden.astype(BF)
        t_buf[at:end, :] = hidden.T.astype(BF)
    for at, end in slices(FFP):
        stream.wait("fc2", at)
    total = dot(fc2_buf[...], t_buf[...])
    low_ref[...] = (residual + total.T + row(vec_ref, FC2_BIAS)).astype(BF)
    if shift:
        copy = to_section(low_ref, next_ref, refs[5], refs[6], sec, me)
        copy.start()
    for one in taken:
        one.forward()
    put_owners(n2_ref, n2.astype(F32))
    if shift:
        copy.wait()
    for one in taken:
        one.finish()


def feed_forward(tok, inc, att, vec, bias, out_w, fc1_w, fc2_w, cid, shift, items=()):
    tokens = tok.shape[0]
    load = Load(items)
    anywhere, vmem = pl.BlockSpec(memory_space=pl.ANY), pl.BlockSpec(memory_space=pltpu.VMEM)
    dma = pltpu.SemaphoreType.DMA
    params = {} if cid is None else dict(collective_id=cid, has_side_effects=True)
    rows = jax.ShapeDtypeStruct((4, 4, HEAD_DIM, tokens), BF)
    low = jax.ShapeDtypeStruct((tokens, D), BF)
    return pl.pallas_call(
        functools.partial(feed_kernel, shift, load),
        out_shape=[
            jax.ShapeDtypeStruct((tokens, D), F32),
            jax.ShapeDtypeStruct((tokens, FFP), F32),
            jax.ShapeDtypeStruct((tokens, FFP), BF),
            rows,
            rows,
            low,
        ]
        + [low] * shift
        + load.shapes,
        in_specs=[vmem] * 5 + [anywhere] * (3 + len(load.sources)),
        out_specs=[vmem] * (6 + shift) + [anywhere] * len(load.shapes),
        scratch_shapes=[
            pltpu.VMEM((D, D), BF),
            pltpu.VMEM((D, FFP), BF),
            pltpu.VMEM((D, FFP), BF),
            pltpu.VMEM((FFP, tokens), BF),
            dma((1 + 2 * len(slices(FFP)),)),
        ]
        + [dma, dma] * shift
        + load.scratch,
        compiler_params=pltpu.CompilerParams(vmem_limit_bytes=60 << 20, **params),
    )(tok, inc, att, vec, bias, out_w, fc1_w, fc2_w, *load.sources)


def feed_back_kernel(load, cot_ref, inc_ref, vec_ref, *refs):
    n = len(load.items)
    kept, refs = refs[:4], refs[4:]
    out_w, fc1_w, fc2_w = refs[:3]
    sources, refs = refs[3 : 3 + 2 * n], refs[3 + 2 * n :]
    rg_ref, ag_ref, fc_ref, pg_ref, branch_ref, sum_ref = refs[:6]
    outs, refs = refs[6 : 6 + n], refs[6 + n :]
    pre_buf, res_buf, out_buf, fc1_buf, fc2_buf, t_buf, kept_sem, sems = refs[:8]
    sec, _ = place()
    pairs = []
    pairs += [("fc2", fc2_w, fc2_buf, cols) for cols in slices(FFP)]
    pairs += [("fc1", fc1_w, fc1_buf, cols) for cols in slices(FFP)]
    pairs.append(("out", out_w, out_buf, (0, D)))
    stream = Stream(pairs, sems)
    fetch(kept, (pre_buf, res_buf), kept_sem, sec)
    stream.start()
    taken = load.begin(sources, outs, refs[8:])
    grad = jnp.where(sec == 0, inc_ref[...].astype(F32), cot_ref[...].astype(F32))
    fc_grad = grad.astype(BF)
    put_owners(fc_ref, grad)
    fetched(kept, (pre_buf, res_buf), kept_sem)
    total = None
    for at, end in slices(FFP):
        slope = gelu_slope(pre_buf[:, at:end])
        stream.wait("fc2", at)
        pre_wide = dot(fc_grad, fc2_buf[:, at:end]) * slope
        pre_grad = pre_wide.astype(BF)
        pg_ref[:, at:end] = pre_grad
        t_buf[at:end, :] = pre_wide.T.astype(BF)
    for at, end in slices(FFP):
        stream.wait("fc1", at)
    total = dot(fc1_buf[...], t_buf[...])
    xhat, rstd = normalised(res_buf[...])
    part, gain_sum, bias_sum = norm_backward(total.T, xhat, rstd, row(vec_ref, GAIN2))
    residual_grad = grad + part
    rg_ref[...] = residual_grad
    branch = residual_grad.astype(BF)
    branch_ref[...] = branch
    for one in taken:
        one.forward()
    stream.wait("out", 0)
    att_grad = dot(out_buf[...], residual_grad.T.astype(BF))
    for h in range(HEADS):
        ag_ref[h] = att_grad[h * HEAD_DIM : (h + 1) * HEAD_DIM].astype(BF)
    sum_ref[0:1, :] = jnp.sum(branch.astype(F32), axis=0, keepdims=True)
    sum_ref[1:2, :] = gain_sum
    sum_ref[2:3, :] = bias_sum
    sum_ref[3:4, :] = jnp.sum(fc_grad.astype(F32), axis=0, keepdims=True)
    for one in taken:
        one.finish()


def feed_backward(cot, inc, vec, kept, out_w, fc1_w, fc2_w, cid, items=()):
    tokens = cot.shape[0]
    load = Load(items)
    params = {} if cid is None else dict(collective_id=cid, has_side_effects=True)
    anywhere, vmem = pl.BlockSpec(memory_space=pl.ANY), pl.BlockSpec(memory_space=pltpu.VMEM)
    dma = pltpu.SemaphoreType.DMA
    return pl.pallas_call(
        functools.partial(feed_back_kernel, load),
        out_shape=[
            jax.ShapeDtypeStruct((tokens, D), F32),
            jax.ShapeDtypeStruct((HEADS, HEAD_DIM, tokens), BF),
            jax.ShapeDtypeStruct((4, 4, HEAD_DIM, tokens), BF),
            jax.ShapeDtypeStruct((tokens, FFP), BF),
            jax.ShapeDtypeStruct((tokens, D), BF),
            jax.ShapeDtypeStruct((4, D), F32),
        ]
        + load.shapes,
        in_specs=[vmem] * 3 + [anywhere] * (7 + len(load.sources)),
        out_specs=[vmem] * 6 + [anywhere] * len(load.shapes),
        scratch_shapes=[
            pltpu.VMEM((tokens, FFP), F32),
            pltpu.VMEM((tokens, D), F32),
            pltpu.VMEM((D, D), BF),
            pltpu.VMEM((D, FFP), BF),
            pltpu.VMEM((D, FFP), BF),
            pltpu.VMEM((FFP, tokens), BF),
            dma((2,)),
            dma((1 + 2 * len(slices(FFP)),)),
        ]
        + load.scratch,
        compiler_params=pltpu.CompilerParams(vmem_limit_bytes=60 << 20, **params),
    )(cot, inc, vec, *kept, out_w, fc1_w, fc2_w, *load.sources)


def qkv_back_kernel(shift, load, *refs):
    n = len(load.items)
    tok_ref, inc_ref, vec_ref, rg_ref, dq_ref, dkv_ref, w_ref = refs[:7]
    sources, refs = refs[7 : 7 + 2 * n], refs[7 + 2 * n :]
    grad_ref, dqkv_ref, sum_ref, qsum_ref = refs[:4]
    refs = refs[4:]
    if shift:
        next_ref, refs = refs[0], refs[1:]
    outs, refs = refs[:n], refs[n:]
    refs, load_sems = refs[: len(refs) - 3 * n], refs[len(refs) - 3 * n :]
    w_buf, sems = refs[:2]
    sec, me = place()
    stream = Stream([("w", w_ref, w_buf, cols) for cols in slices(3 * D, 384)], sems)
    stream.start()
    if shift:
        greet_section(sec, me)
    taken = load.begin(sources, outs, load_sems)
    kv = [dkv_ref[h].astype(F32) for h in range(HEADS)]
    rows = [dq_ref[h].astype(F32) for h in range(HEADS)]
    rows += [part[:HEAD_DIM] for part in kv] + [part[HEAD_DIM:] for part in kv]
    dqkv = jnp.concatenate(rows, axis=0).astype(BF)
    dqkv_ref[...] = dqkv
    qsum_ref[...] = nt(jnp.ones((8, dqkv.shape[1]), BF), dqkv)
    total = None
    for at, end in slices(3 * D, 384):
        stream.wait("w", at)
        part = dot(w_buf[:, at:end], dqkv[at:end])
        total = part if total is None else total + part
    xhat, rstd = normalised(pick(sec, tok_ref, inc_ref))
    part, gain_sum, bias_sum = norm_backward(total.T, xhat, rstd, row(vec_ref, GAIN1))
    grad = rg_ref[...] + part
    grad_ref[...] = grad
    if shift:
        low_buf = refs[2]
        low_buf[...] = grad.astype(BF)
        copy = to_section(low_buf, next_ref, refs[3], refs[4], sec, me)
        copy.start()
    sum_ref[0:1, :] = gain_sum
    sum_ref[1:2, :] = bias_sum
    if shift:
        copy.wait()
    for one in taken:
        one.forward()
    for one in taken:
        one.finish()


def qkv_backward(tok, inc, vec, residual_grad, dq, dkv, w, cid, shift, items=()):
    tokens = tok.shape[0]
    load = Load(items)
    anywhere, vmem = pl.BlockSpec(memory_space=pl.ANY), pl.BlockSpec(memory_space=pltpu.VMEM)
    dma = pltpu.SemaphoreType.DMA
    params = {} if cid is None else dict(collective_id=cid, has_side_effects=True)
    return pl.pallas_call(
        functools.partial(qkv_back_kernel, shift, load),
        out_shape=[
            jax.ShapeDtypeStruct((tokens, D), F32),
            jax.ShapeDtypeStruct((3 * D, tokens), BF),
            jax.ShapeDtypeStruct((2, D), F32),
            jax.ShapeDtypeStruct((8, 3 * D), F32),
        ]
        + [jax.ShapeDtypeStruct((tokens, D), BF)] * shift
        + load.shapes,
        in_specs=[vmem] * 6 + [anywhere] * (1 + len(load.sources)),
        out_specs=[vmem] * (4 + shift) + [anywhere] * len(load.shapes),
        scratch_shapes=[pltpu.VMEM((D, 3 * D), BF), dma((len(slices(3 * D, 384)),))]
        + [pltpu.VMEM((tokens, D), BF), dma, dma] * shift
        + load.scratch,
        compiler_params=pltpu.CompilerParams(vmem_limit_bytes=60 << 20, **params),
    )(tok, inc, vec, residual_grad, dq, dkv, w, *load.sources)


def pad_ff(x):
    return jnp.pad(x, ((0, 0),) * (x.ndim - 1) + ((0, FFP - FF),))


TENSORS = ("fc2", "fc1", "out", "qkv")


def final_kernel(tiles, early, late, *refs):
    refs = list(refs)

    def take(n):
        part = refs[:n]
        del refs[:n]
        return part

    small_ref = take(1)[0]
    x_refs = {name: take(2) for name in TENSORS}
    early_refs = take(len(early))
    late_refs = take(2 * len(late))
    small_out, bias_out = take(2)
    out_refs = dict(zip(TENSORS, take(4)))
    y_bufs = dict(zip(TENSORS, take(4)))
    x_buf = take(1)[0]
    g_bufs, one_bufs, two_bufs = [dict(zip(TENSORS, take(4))) for _ in range(3)]
    small_got, bias_buf, bias_got = take(3)
    early_sem, small_send, small_recv, bias_send, bias_recv = take(5)
    sems = {name: take(4) for name in TENSORS}
    late_sems = [take(3) for _ in late]

    sec, me = place()
    z, low = me // 4, me % 4
    pair = z + 1 - 2 * (z % 2)
    count = small_ref.shape[0]

    def begin(name):
        for other, one in behind:
            if other == name:
                one.start()

    loads = []
    for i, (name, batch, cols) in enumerate(early):
        dst = y_bufs[name].at[4 * batch : 4 * batch + 4]
        if cols is not None:
            dst = dst.at[:, :, cols[0] : cols[1]]
        loads.append((name, cols, pltpu.make_async_copy(early_refs[i], dst, early_sem.at[i])))

    def place_rows(name):
        rows = []
        for owner in (z, 3 - z, pair, 3 - pair):
            rows.append(
                jnp.concatenate(
                    [x_refs[name][batch][k, owner].astype(F32) for batch in range(2) for k in range(4)], axis=1
                )
            )
        x_buf[...] = jnp.concatenate(rows, axis=0).astype(BF)

    def meanwhile():
        for cols in ((0, SPLIT), (SPLIT, FFP)):
            for name, part, load in loads:
                if name == "fc2" and part == cols:
                    load.start()
        place_rows("fc2")

    greet_all(count, sec, me, meanwhile)
    behind = []
    for i, (name, batch, item) in enumerate(late):

        def slot(k, name=name, batch=batch, item=item):
            ref = y_bufs[name].at[4 * batch + k]
            return ref if item.cols is None else ref.at[:, item.cols[0] : item.cols[1]]

        behind.append((name, PlaneCopies(item, late_refs[2 * i], late_refs[2 * i + 1], slot, *late_sems[i])))
    begin("fc1")
    smalls = []
    for d in range(1, count):
        target = (me + d) % count
        smalls.append(
            pltpu.make_async_remote_copy(
                src_ref=small_ref.at[target],
                dst_ref=small_got.at[d],
                send_sem=small_send.at[d],
                recv_sem=small_recv.at[d],
                device_id=(sec, target),
                device_id_type=MESH,
            )
        )
        smalls[-1].start()

    def first(name, i):
        send, recv = sems[name][0], sems[name][1]
        return pltpu.make_async_remote_copy(
            src_ref=g_bufs[name].at[i, 2:4],
            dst_ref=one_bufs[name].at[i],
            send_sem=send.at[i],
            recv_sem=recv.at[i],
            device_id=(sec, pair * 4 + low),
            device_id_type=MESH,
        )

    def second(name, i):
        send, recv = sems[name][2], sems[name][3]
        return pltpu.make_async_remote_copy(
            src_ref=g_bufs[name].at[i, 1],
            dst_ref=two_bufs[name].at[i],
            send_sem=send.at[i],
            recv_sem=recv.at[i],
            device_id=(sec, (3 - z) * 4 + low),
            device_id_type=MESH,
        )

    def ready(name):
        for other, one in behind:
            if other == name:
                one.forward()
        if name in ("fc1", "qkv"):
            begin({"fc1": "qkv", "qkv": "out"}[name])
        for other, _, load in loads:
            if other == name:
                load.wait()
        for other, one in behind:
            if other == name:
                one.finish()
        place_rows(name)

    def compute_first():
        for cols in ((0, SPLIT), (SPLIT, FFP)):
            for name, part, load in loads:
                if name == "fc2" and part == cols:
                    load.wait()
                elif name != "fc2" and cols[0]:
                    load.start()
            width = tiles["fc2"][1]
            lax.fori_loop(cols[0] // width, cols[1] // width, lambda i, carry: (compute("fc2", i), carry)[1], 0)

    def columns(name, i):
        width = tiles[name][1]
        return pl.ds(pl.multiple_of(i * width, 128), width)

    def compute(name, i):
        width = tiles[name][1]
        buf = y_bufs[name]
        if name == "qkv":
            rows = pl.ds(pl.multiple_of(i * width, 128), width)
            y = jnp.concatenate([buf[part, rows, :] for part in range(8)], axis=1)
            total = lax.dot_general(x_buf[...], y, (((1,), (1,)), ((), ())), preferred_element_type=F32)
        else:
            y = jnp.concatenate([buf[part, :, columns(name, i)] for part in range(8)], axis=0)
            total = dot(x_buf[...], y)
        if name == "fc1":
            bias_buf[i] = dot(jnp.ones((8, y.shape[0]), BF), y)[0:1]
        g_bufs[name][i] = total.reshape(4, HEAD_DIM, width).astype(BF)
        first(name, i).start()

    def bias_copy(k):
        target = (me + 4 * k) % count
        return pltpu.make_async_remote_copy(
            src_ref=bias_buf,
            dst_ref=bias_got.at[k - 1],
            send_sem=bias_send.at[k - 1],
            recv_sem=bias_recv.at[k - 1],
            device_id=(sec, target),
            device_id_type=MESH,
        )

    def middle(name, i):
        first(name, i).wait_recv()
        out_refs[name][:, columns(name, i)] = g_bufs[name][i, 0].astype(F32) + one_bufs[name][i, 0].astype(F32)
        g_bufs[name][i, 1] = (g_bufs[name][i, 1].astype(F32) + one_bufs[name][i, 1].astype(F32)).astype(BF)
        second(name, i).start()

    def finish(name, i):
        second(name, i).wait_recv()
        out_refs[name][:, columns(name, i)] += two_bufs[name][i].astype(F32)
        first(name, i).wait_send()
        second(name, i).wait_send()

    def loop(name, *steps):
        def body(i, carry):
            for step, which in steps:
                step(which, i)
            return carry

        lax.fori_loop(0, tiles[name][0], body, 0)

    compute_first()
    loop("fc2", (middle, "fc2"))
    ready("fc1")
    loop("fc1", (compute, "fc1"))
    for k in range(1, 4):
        bias_copy(k).start()
    loop("fc1", (middle, "fc1"), (finish, "fc2"))
    ready("qkv")
    loop("qkv", (compute, "qkv"))
    ready("out")
    loop("out", (compute, "out"))
    loop("fc1", (finish, "fc1"))
    loop("qkv", (middle, "qkv"))
    loop("out", (middle, "out"))
    for copy in smalls:
        copy.wait()
    total = small_ref[me]
    for d in range(1, count):
        total = total + small_got[d]
    small_out[...] = total
    for k in range(1, 4):
        bias_copy(k).wait()
    bias_out[...] = bias_buf[...] + bias_got[0] + bias_got[1] + bias_got[2]
    loop("qkv", (finish, "qkv"))
    loop("out", (finish, "out"))


def final(small, xs, early, late, cid):
    count = small.shape[0]
    tokens = xs["qkv"][0].shape[-1]
    widths = {"fc2": FFP, "fc1": FFP, "out": D, "qkv": 3 * D}
    tiles = {name: (w // (256 if name[0] == "f" else 384), 256 if name[0] == "f" else 384) for name, w in widths.items()}
    anywhere, vmem = pl.BlockSpec(memory_space=pl.ANY), pl.BlockSpec(memory_space=pltpu.VMEM)
    args = [small] + [x for name in TENSORS for x in xs[name]]
    n_vmem = len(args)
    args += [e[3] for e in early] + [source for _, _, item in late for source in item.sources]
    dma = pltpu.SemaphoreType.DMA
    scratch = []
    for name in TENSORS:
        shape = (8, widths[name], tokens) if name == "qkv" else (8, tokens, widths[name])
        scratch.append(pltpu.VMEM(shape, BF))
    scratch.append(pltpu.VMEM((4 * HEAD_DIM, 8 * tokens), BF))
    for lead in ((4,), (2,), ()):
        for name in TENSORS:
            scratch.append(pltpu.VMEM((tiles[name][0],) + lead + (HEAD_DIM, tiles[name][1]), BF))
    bias = (tiles["fc1"][0], 1, tiles["fc1"][1])
    scratch += [pltpu.VMEM(small.shape, F32), pltpu.VMEM(bias, F32), pltpu.VMEM((3,) + bias, F32)]
    scratch += [dma((len(early),)), dma((count,)), dma((count,)), dma((3,)), dma((3,))]
    for name in TENSORS:
        scratch += [dma((tiles[name][0],))] * 4
    scratch += [dma, dma((4,)), dma((4,))] * len(late)
    out = pl.pallas_call(
        functools.partial(final_kernel, tiles, [e[:3] for e in early], late),
        out_shape=[jax.ShapeDtypeStruct(small.shape[1:], F32), jax.ShapeDtypeStruct(bias, F32)]
        + [jax.ShapeDtypeStruct((HEAD_DIM, widths[name]), F32) for name in TENSORS],
        in_specs=[vmem] * n_vmem + [anywhere] * (len(args) - n_vmem),
        out_specs=[vmem] * 6,
        scratch_shapes=scratch,
        compiler_params=pltpu.CompilerParams(
            collective_id=cid, has_side_effects=True, vmem_limit_bytes=60 << 20
        ),
    )(*args)
    return out[0], out[1].reshape(FFP), dict(zip(TENSORS, out[2:]))


def on_device(
    tokens,
    cotangent,
    image_of_block,
    ln1_gain,
    ln1_bias,
    qkv_weight,
    qv_bias,
    out_weight,
    out_bias,
    ln2_gain,
    ln2_bias,
    fc1_weight,
    fc1_bias,
    fc2_weight,
    fc2_bias,
):
    sec, me = place()
    small = jnp.stack(
        [ln1_gain[0], ln1_bias[0], qv_bias[0, 0], qv_bias[0, 1], out_bias[0], ln2_gain[0], ln2_bias[0], fc2_bias[0]],
        axis=1,
    )
    small = jnp.pad(small, ((0, 0), (0, BLOCK - 8)))
    near = window(image_of_block)
    shards = [qkv_weight[0], small, out_weight[0], pad_ff(fc1_weight[0]), pad_ff(fc2_weight[0].T)]
    *three, n1, small_all, w_qkv, w_out, w_fc1, w_fc2t = first_tick(near, tokens[0], shards, 2)
    w_qkv = w_qkv.reshape(D, 3 * D)
    w_out = w_out.reshape(D, D)
    w_fc1 = w_fc1.reshape(D, FFP)
    w_fc2t = w_fc2t.reshape(D, FFP)
    vec = small_all.reshape(D, BLOCK)[:, :8].T.astype(F32)
    b_qkv = jnp.concatenate([vec[2:3], jnp.zeros((1, D), F32), vec[3:4]], axis=1)
    b_fc1 = pad_ff(fc1_bias[0]).astype(F32).reshape(1, FFP)

    def choose(at_zero, at_one):
        return jnp.where(sec == 0, at_zero, at_one)

    saved, sent, back, done, input_grads = [], {}, [], [], []
    incoming = [tokens[0]]

    def token_inputs(tick):
        return tokens[min(tick, 1)], incoming[tick]

    def feed(tick, qkv, lse, att, n1, cid, shift, items=()):
        fed = feed_forward(*token_inputs(tick), att, vec, b_fc1, w_out, w_fc1, w_fc2t, cid, shift, items)
        saved.append(
            dict(qkv=qkv, lse=lse, n1=n1, residual=fed[0], pre=fed[1], hidden=fed[2], n2=fed[3], att=fed[4], low=fed[5])
        )
        return fed

    def kept(tick, *names):
        return [saved[at][name] for name in names for at in ((1, 1), (0, 2), (1, 1))[tick]]

    def feed_back(tick, incoming_grad, cid=None, items=()):
        residual_grad, att_grad, fc, pre, branch, four, *got = feed_backward(
            cotangent[min(tick, 1)], incoming_grad, vec, kept(tick, "pre", "residual"), w_out, w_fc1, w_fc2t, cid, items
        )
        back.append(dict(fc=fc, pre=pre, branch=branch))
        return residual_grad, att_grad, list(four), got

    def qkv_back(tick, residual_grad, dq, dkv, sums, cid, shift, items=()):
        inputs = (tokens[max(tick - 1, 0)], incoming[min(tick + 1, 2)])
        input_grad, dqkv, two, qsum, *rest = qkv_backward(
            *inputs, vec, residual_grad, dq, dkv, w_qkv, cid, shift, items
        )
        back[tick]["dqkv"] = dqkv
        input_grads.append(input_grad)
        done.append([two[0], two[1], qsum[0, :D], qsum[0, 2 * D :], *sums])
        return rest

    incoming.append(feed(0, *three, n1, 8, True)[6])

    qkv, n1 = qkv_forward(*token_inputs(1), vec, b_qkv, w_qkv)
    three, _, _ = attention(near, 3, ahead=(1, qkv))
    incoming.append(lax.ppermute(feed(1, *three, n1, None, False)[5], "section", [(0, 1)]))

    def first_batch(name, cols=None):
        return Whole(saved[0][name], saved[1][name], cols)

    def second_batch(name, cols=None):
        return Whole(saved[1][name], saved[2][name], cols)

    residual_grad, att_grad, sums, got = feed_back(0, tokens[0], 11, [first_batch("hidden", (SPLIT, FFP))])
    sent["h0b"] = got[0]
    qkv, n1 = qkv_forward(*token_inputs(2), vec, b_qkv, w_qkv)
    items = [Rows(saved[0][name], saved[1][name]) for name in ("n1", "att", "n2")]
    items.append(first_batch("hidden", (0, SPLIT)))
    three, two, got = attention(near, 4, ahead=(2, qkv), behind=(0, att_grad, kept(0, "qkv", "lse")), items=items)
    sent["n1_0"], sent["att_0"], sent["n2_0"], sent["h0a"] = got
    qkv_back(0, residual_grad, *two, sums, None, False)
    incoming_grad = lax.ppermute(input_grads[0].astype(BF), "section", [(1, 0)])
    feed(2, *three, n1, None, False)
    outputs = jnp.stack([choose(saved[m]["low"], saved[m + 1]["low"]) for m in range(2)])

    residual_grad, att_grad, sums, got = feed_back(1, incoming_grad, 12, [second_batch("hidden", (0, SPLIT))])
    sent["h1a"] = got[0]
    items = [Rows(saved[1][name], saved[2][name]) for name in ("n1", "att", "n2")]
    items.append(second_batch("hidden", (SPLIT, FFP)))
    _, two, got = attention(near, 5, behind=(1, att_grad, kept(1, "qkv", "lse")), items=items)
    sent["n1_1"], sent["att_1"], sent["n2_1"], sent["h1b"] = got
    incoming_grad = qkv_back(1, residual_grad, *two, sums, 9, True)[0]

    residual_grad, att_grad, sums, _ = feed_back(2, incoming_grad)
    items = [Rows(back[1]["fc"], back[0]["fc"]), Rows(back[2]["fc"], back[1]["fc"])]
    items.append(Whole(back[1]["pre"], back[0]["pre"], (SPLIT, FFP)))
    _, two, got = attention(near, 6, behind=(2, att_grad, kept(2, "qkv", "lse")), items=items)
    sent["fc_0"], sent["fc_1"], sent["pre_0b"] = got
    qkv_back(2, residual_grad, *two, sums, None, False)
    input_grads = jnp.stack([choose(input_grads[m + 1], input_grads[m]) for m in range(2)])

    sums = [choose(done[1][i] + done[2][i], done[0][i] + done[1][i]) for i in range(8)]
    by_owner = jnp.stack(sums).reshape(8, HEADS, HEAD_DIM).transpose(1, 0, 2)
    by_owner = jnp.pad(by_owner, ((0, 0), (0, 0), (0, BLOCK - HEAD_DIM)))
    xs = {
        "fc2": [sent["fc_0"], sent["fc_1"]],
        "fc1": [sent["n2_0"], sent["n2_1"]],
        "out": [sent["att_0"], sent["att_1"]],
        "qkv": [sent["n1_0"], sent["n1_1"]],
    }
    early = [
        ("fc2", 0, (0, SPLIT), sent["h0a"]),
        ("fc2", 0, (SPLIT, FFP), sent["h0b"]),
        ("fc2", 1, (0, SPLIT), sent["h1a"]),
        ("fc2", 1, (SPLIT, FFP), sent["h1b"]),
        ("fc1", 0, (SPLIT, FFP), sent["pre_0b"]),
    ]
    late = [
        ("fc1", 0, Whole(back[1]["pre"], back[0]["pre"], (0, SPLIT))),
        ("fc1", 1, Whole(back[2]["pre"], back[1]["pre"])),
        ("qkv", 0, Whole(back[1]["dqkv"], back[0]["dqkv"])),
        ("qkv", 1, Whole(back[2]["dqkv"], back[1]["dqkv"])),
        ("out", 0, Whole(back[1]["branch"], back[0]["branch"])),
        ("out", 1, Whole(back[2]["branch"], back[1]["branch"])),
    ]
    packed, bias, grads = final(by_owner, xs, early, late, 10)
    g_small = packed[:, :HEAD_DIM]
    g_fc1_bias = bias[:FF]
    return (
        outputs[None],
        input_grads[None],
        g_small[0][None],
        g_small[1][None],
        grads["qkv"][None],
        g_small[2:4][None],
        grads["out"][None],
        g_small[4][None],
        g_small[5][None],
        g_small[6][None],
        grads["fc1"][:, :FF][None],
        g_fc1_bias[None],
        grads["fc2"].T[:FF][None],
        g_small[7][None],
    )


BLK_DEV = 1
REACH = 5


def shifted(value, axis, steps):
    count = lax.axis_size(axis)
    initial, last = (max(0, -steps), min(count, count - steps))
    return lax.ppermute(value, axis, [(source, source + steps) for source in range(initial, last)])


def layer_norm(values_in, scale_gain, shift_bias):
    row_mean = jnp.mean(values_in, axis=-1, keepdims=True)
    centred = values_in - row_mean
    row_var = jnp.mean(centred * centred, axis=-1, keepdims=True)
    return centred * lax.rsqrt(row_var + EPSILON) * scale_gain + shift_bias


def gelu_tanh(pre_value):
    return jax.nn.gelu(pre_value, approximate=True)


def heads_of(values_in):
    return values_in.reshape(values_in.shape[0], HEADS, HEAD_DIM)


def image_mask(image_of_block, batch_slot, wide_rank):
    padding = REACH * BLK_DEV
    padded = jnp.pad(image_of_block, ((0, 0), (padding, padding)), constant_values=-1)
    image_row = lax.dynamic_index_in_dim(padded, batch_slot, 0, keepdims=False)
    key_blocks = lax.dynamic_slice_in_dim(image_row, wide_rank * BLK_DEV, (2 * REACH + 1) * BLK_DEV)
    query_blocks = lax.dynamic_slice_in_dim(image_row, wide_rank * BLK_DEV + padding, BLK_DEV)
    return jnp.repeat(query_blocks, BLOCK)[:, None] == jnp.repeat(key_blocks, BLOCK)[None, :]


def keep_slot(buffer_all, new_value, batch_slot, is_live):
    previous = lax.dynamic_index_in_dim(buffer_all, batch_slot, 0, keepdims=False)
    chosen = jnp.where(is_live, new_value, previous)
    return lax.dynamic_update_index_in_dim(buffer_all, chosen, batch_slot, 0)


def near_keys(key_own, value_own, backward_pass):
    key_parts = []
    value_parts = []
    for offset in range(-REACH, REACH + 1):
        if offset == 0:
            received = (key_own, value_own)
        elif backward_pass:
            received = shifted((key_own, value_own), "wide", -offset)
        else:
            received = shifted((key_own, value_own), "wide", -offset)
        key_parts.append(received[0])
        value_parts.append(received[1])
    return (jnp.concatenate(key_parts, axis=0), jnp.concatenate(value_parts, axis=0))


def return_key_grads(key_terms, value_terms):
    row_count = key_terms.shape[0] // (2 * REACH + 1)
    key_total = key_terms[REACH * row_count : (REACH + 1) * row_count]
    value_total = value_terms[REACH * row_count : (REACH + 1) * row_count]
    for position, offset in enumerate(range(-REACH, REACH + 1)):
        if offset != 0:
            piece_pair = (
                key_terms[position * row_count : (position + 1) * row_count],
                value_terms[position * row_count : (position + 1) * row_count],
            )
            received = shifted((piece_pair[0], piece_pair[1]), "wide", offset)
            key_total = key_total + received[0]
            value_total = value_total + received[1]
    return (key_total, value_total)


def project_qkv(layer_in, weights):
    layer_float = layer_in.astype(jnp.float32)
    normed_one = layer_norm(
        layer_float, weights[0].astype(jnp.float32), weights[1].astype(jnp.float32)
    ).astype(jnp.bfloat16)
    mixed = jnp.dot(normed_one, weights[2], preferred_element_type=jnp.float32)
    queries = (mixed[:, :D] + weights[3][0].astype(jnp.float32)).astype(jnp.bfloat16)
    key_own = mixed[:, D : 2 * D].astype(jnp.bfloat16)
    value_own = (mixed[:, 2 * D :] + weights[3][1].astype(jnp.float32)).astype(jnp.bfloat16)
    return (layer_float, normed_one, queries, key_own, value_own)


def attention_probs(queries, keys_near, same_image):
    score_scale = 1.0 / math.sqrt(HEAD_DIM)
    scores = (
        jnp.einsum(
            "qhd,khd->hqk",
            heads_of(queries),
            heads_of(keys_near),
            preferred_element_type=jnp.float32,
        )
        * score_scale
    )
    scores = jnp.where(same_image[None], scores, MASKED_SCORE)
    row_max = jnp.max(scores, axis=-1, keepdims=True)
    exponent = jnp.exp(scores - row_max)
    return exponent / jnp.sum(exponent, axis=-1, keepdims=True)


def finish_layer(layer_float, queries, keys_near, values_near, same_image, weights, hidden_bias):
    probs = attention_probs(queries, keys_near, same_image)
    probs_low = probs.astype(jnp.bfloat16)
    attended = jnp.einsum(
        "hqk,khd->qhd", probs_low, heads_of(values_near), preferred_element_type=jnp.float32
    )
    attended = attended.reshape(queries.shape[0], D).astype(jnp.bfloat16)
    residual = (
        layer_float
        + jnp.dot(attended, weights[4], preferred_element_type=jnp.float32)
        + weights[5].astype(jnp.float32)
    )
    normed_two = layer_norm(
        residual, weights[6].astype(jnp.float32), weights[7].astype(jnp.float32)
    ).astype(jnp.bfloat16)
    hidden_pre = jnp.dot(
        normed_two, weights[8], preferred_element_type=jnp.float32
    ) + hidden_bias.astype(jnp.float32)
    hidden = gelu_tanh(hidden_pre).astype(jnp.bfloat16)
    output = (
        residual
        + jnp.dot(hidden, weights[9], preferred_element_type=jnp.float32)
        + weights[10].astype(jnp.float32)
    )
    return (probs, probs_low, attended, residual, normed_two, hidden_pre, hidden, output)


def layer_backward(
    layer_float,
    normed_one,
    queries,
    keys_near,
    values_near,
    same_image,
    weights,
    hidden_bias,
    grad_out,
):
    score_scale = 1.0 / math.sqrt(HEAD_DIM)
    probs, probs_low, attended, residual, normed_two, hidden_pre, hidden, output = finish_layer(
        layer_float, queries, keys_near, values_near, same_image, weights, hidden_bias
    )
    feed_grad = grad_out.astype(jnp.bfloat16)
    grad_fc2_weight = jnp.einsum("tf,td->fd", hidden, feed_grad, preferred_element_type=jnp.float32)
    grad_fc2_bias = jnp.sum(feed_grad.astype(jnp.float32), axis=0)
    hidden_grad = jnp.einsum("td,fd->tf", feed_grad, weights[9], preferred_element_type=jnp.float32)
    primal_gelu, gelu_pull = jax.vjp(gelu_tanh, hidden_pre)
    pre_grad = gelu_pull(hidden_grad)[0].astype(jnp.bfloat16)
    grad_fc1_bias = jnp.sum(pre_grad.astype(jnp.float32), axis=0)
    grad_fc1_weight = jnp.einsum(
        "td,tf->df", normed_two, pre_grad, preferred_element_type=jnp.float32
    )
    normed_two_grad = jnp.einsum(
        "tf,df->td", pre_grad, weights[8], preferred_element_type=jnp.float32
    )
    primal_two, norm_two_pull = jax.vjp(
        layer_norm, residual, weights[6].astype(jnp.float32), weights[7].astype(jnp.float32)
    )
    residual_part, grad_ln2_gain, grad_ln2_bias = norm_two_pull(normed_two_grad)
    residual_grad = grad_out + residual_part
    branch_grad = residual_grad.astype(jnp.bfloat16)
    grad_out_bias = jnp.sum(branch_grad.astype(jnp.float32), axis=0)
    grad_out_weight = jnp.einsum(
        "tc,td->cd", attended, branch_grad, preferred_element_type=jnp.float32
    )
    attended_grad = jnp.einsum(
        "td,cd->tc", branch_grad, weights[4], preferred_element_type=jnp.float32
    ).astype(jnp.bfloat16)
    attended_heads = heads_of(attended_grad)
    probs_grad = jnp.einsum(
        "qhd,khd->hqk", attended_heads, heads_of(values_near), preferred_element_type=jnp.float32
    )
    value_terms = jnp.einsum(
        "hqk,qhd->khd", probs_low, attended_heads, preferred_element_type=jnp.float32
    )
    score_grad = (
        probs * (probs_grad - jnp.sum(probs * probs_grad, axis=-1, keepdims=True))
    ).astype(jnp.bfloat16)
    query_grad = (
        jnp.einsum(
            "hqk,khd->qhd", score_grad, heads_of(keys_near), preferred_element_type=jnp.float32
        )
        * score_scale
    )
    query_grad = query_grad.reshape(queries.shape[0], D).astype(jnp.bfloat16)
    key_terms = (
        jnp.einsum(
            "hqk,qhd->khd", score_grad, heads_of(queries), preferred_element_type=jnp.float32
        )
        * score_scale
    )
    key_total, value_total = return_key_grads(key_terms.reshape(-1, D), value_terms.reshape(-1, D))
    key_grad = key_total.astype(jnp.bfloat16)
    value_grad = value_total.astype(jnp.bfloat16)
    grad_qv_bias = jnp.stack(
        [
            jnp.sum(query_grad.astype(jnp.float32), axis=0),
            jnp.sum(value_grad.astype(jnp.float32), axis=0),
        ]
    )
    mixed_grad = jnp.concatenate([query_grad, key_grad, value_grad], axis=1)
    grad_qkv_weight = jnp.einsum(
        "tc,tk->ck", normed_one, mixed_grad, preferred_element_type=jnp.float32
    )
    normed_one_grad = jnp.einsum(
        "tk,ck->tc", mixed_grad, weights[2], preferred_element_type=jnp.float32
    )
    primal_one, norm_one_pull = jax.vjp(
        layer_norm, layer_float, weights[0].astype(jnp.float32), weights[1].astype(jnp.float32)
    )
    input_part, grad_ln1_gain, grad_ln1_bias = norm_one_pull(normed_one_grad)
    input_grad = residual_grad + input_part
    grad_terms = (
        grad_ln1_gain,
        grad_ln1_bias,
        grad_qkv_weight,
        grad_qv_bias,
        grad_out_weight,
        grad_out_bias,
        grad_ln2_gain,
        grad_ln2_bias,
        grad_fc1_weight,
        grad_fc2_weight,
        grad_fc2_bias,
    )
    return (input_grad, grad_terms, grad_fc1_bias)


def on_device_near(
    tokens,
    cotangent,
    image_of_block,
    ln1_gain,
    ln1_bias,
    qkv_weight,
    qv_bias,
    out_weight,
    out_bias,
    ln2_gain,
    ln2_bias,
    fc1_weight,
    fc1_bias,
    fc2_weight,
    fc2_bias,
):
    section_rank = lax.axis_index("section")
    wide_rank = lax.axis_index("wide")
    micro_count = tokens.shape[0]
    weights = (
        lax.all_gather(ln1_gain[0], "wide", axis=0, tiled=True),
        lax.all_gather(ln1_bias[0], "wide", axis=0, tiled=True),
        lax.all_gather(qkv_weight[0], "wide", axis=0, tiled=True),
        lax.all_gather(qv_bias[0], "wide", axis=1, tiled=True),
        lax.all_gather(out_weight[0], "wide", axis=0, tiled=True),
        lax.all_gather(out_bias[0], "wide", axis=0, tiled=True),
        lax.all_gather(ln2_gain[0], "wide", axis=0, tiled=True),
        lax.all_gather(ln2_bias[0], "wide", axis=0, tiled=True),
        lax.all_gather(fc1_weight[0], "wide", axis=0, tiled=True),
        lax.all_gather(fc2_weight[0], "wide", axis=1, tiled=True),
        lax.all_gather(fc2_bias[0], "wide", axis=0, tiled=True),
    )
    hidden_bias = fc1_bias[0]
    inputs_kept = jnp.zeros_like(tokens)
    outputs_kept = jnp.zeros_like(tokens)
    incoming = jnp.zeros_like(tokens[0])
    for tick_number in range(micro_count + 1):
        batch_index = tick_number - section_rank
        is_live = (batch_index >= 0) & (batch_index < micro_count)
        batch_slot = jnp.clip(batch_index, 0, micro_count - 1)
        own_tokens = tokens[min(tick_number, micro_count - 1)]
        layer_in = jnp.where(section_rank == 0, own_tokens, incoming)
        same_image = image_mask(image_of_block, batch_slot, wide_rank)
        layer_float, normed_one, queries, key_own, value_own = project_qkv(layer_in, weights)
        keys_near, values_near = near_keys(key_own, value_own, False)
        output = finish_layer(
            layer_float, queries, keys_near, values_near, same_image, weights, hidden_bias
        )[-1]
        output_low = output.astype(jnp.bfloat16)
        inputs_kept = keep_slot(inputs_kept, layer_in, batch_slot, is_live)
        outputs_kept = keep_slot(outputs_kept, output_low, batch_slot, is_live)
        if tick_number < micro_count:
            incoming = shifted(output_low, "section", 1)
    weights_back = (
        lax.all_gather(ln1_gain[0], "wide", axis=0, tiled=True),
        lax.all_gather(ln1_bias[0], "wide", axis=0, tiled=True),
        lax.all_gather(qkv_weight[0], "wide", axis=0, tiled=True),
        lax.all_gather(qv_bias[0], "wide", axis=1, tiled=True),
        lax.all_gather(out_weight[0], "wide", axis=0, tiled=True),
        lax.all_gather(out_bias[0], "wide", axis=0, tiled=True),
        lax.all_gather(ln2_gain[0], "wide", axis=0, tiled=True),
        lax.all_gather(ln2_bias[0], "wide", axis=0, tiled=True),
        lax.all_gather(fc1_weight[0], "wide", axis=0, tiled=True),
        lax.all_gather(fc2_weight[0], "wide", axis=1, tiled=True),
        lax.all_gather(fc2_bias[0], "wide", axis=0, tiled=True),
    )
    grad_totals = tuple((jnp.zeros(array.shape, jnp.float32) for array in weights_back))
    hidden_bias_total = jnp.zeros(hidden_bias.shape, jnp.float32)
    input_grads = jnp.zeros(tokens.shape, jnp.float32)
    incoming_grad = jnp.zeros(tokens.shape[1:], jnp.bfloat16)
    for tick_number in range(micro_count + 1):
        batch_index = tick_number - 1 + section_rank
        is_live = (batch_index >= 0) & (batch_index < micro_count)
        batch_slot = jnp.clip(batch_index, 0, micro_count - 1)
        from_cotangent = cotangent[min(tick_number, micro_count - 1)].astype(jnp.float32)
        grad_out = jnp.where(
            section_rank == 1, from_cotangent, incoming_grad.astype(jnp.float32)
        ) * is_live.astype(jnp.float32)
        layer_in = lax.dynamic_index_in_dim(inputs_kept, batch_slot, 0, keepdims=False)
        same_image = image_mask(image_of_block, batch_slot, wide_rank)
        layer_float, normed_one, queries, key_own, value_own = project_qkv(layer_in, weights_back)
        keys_near, values_near = near_keys(key_own, value_own, True)
        input_grad, grad_terms, hidden_bias_term = layer_backward(
            layer_float,
            normed_one,
            queries,
            keys_near,
            values_near,
            same_image,
            weights_back,
            hidden_bias,
            grad_out,
        )
        grad_totals = tuple(
            (old_total + new_term for old_total, new_term in zip(grad_totals, grad_terms))
        )
        hidden_bias_total = hidden_bias_total + hidden_bias_term
        input_grads = keep_slot(input_grads, input_grad, batch_slot, is_live)
        if tick_number < micro_count:
            incoming_grad = shifted(input_grad.astype(jnp.bfloat16), "section", -1)
    (
        grad_ln1_gain,
        grad_ln1_bias,
        grad_qkv_weight,
        grad_qv_bias,
        grad_out_weight,
        grad_out_bias,
        grad_ln2_gain,
        grad_ln2_bias,
        grad_fc1_weight,
        grad_fc2_weight,
        grad_fc2_bias,
    ) = grad_totals
    row_sums = (
        lax.psum_scatter(grad_ln1_gain, "wide", scatter_dimension=0, tiled=True),
        lax.psum_scatter(grad_ln1_bias, "wide", scatter_dimension=0, tiled=True),
        lax.psum_scatter(grad_qkv_weight, "wide", scatter_dimension=0, tiled=True),
        lax.psum_scatter(grad_out_weight, "wide", scatter_dimension=0, tiled=True),
        lax.psum_scatter(grad_out_bias, "wide", scatter_dimension=0, tiled=True),
        lax.psum_scatter(grad_ln2_gain, "wide", scatter_dimension=0, tiled=True),
        lax.psum_scatter(grad_ln2_bias, "wide", scatter_dimension=0, tiled=True),
        lax.psum_scatter(grad_fc1_weight, "wide", scatter_dimension=0, tiled=True),
        lax.psum_scatter(grad_fc2_bias, "wide", scatter_dimension=0, tiled=True),
    )
    column_sums = (
        lax.psum_scatter(grad_qv_bias, "wide", scatter_dimension=1, tiled=True),
        lax.psum_scatter(grad_fc2_weight, "wide", scatter_dimension=1, tiled=True),
    )
    hidden_bias_sum = lax.psum(hidden_bias_total, "wide")
    return (
        outputs_kept[None],
        input_grads[None],
        row_sums[0][None],
        row_sums[1][None],
        row_sums[2][None],
        column_sums[0][None],
        row_sums[3][None],
        row_sums[4][None],
        row_sums[5][None],
        row_sums[6][None],
        row_sums[7][None],
        hidden_bias_sum[None],
        column_sums[1][None],
        row_sums[8][None],
    )


def specs():
    ins = (
        P(None, "wide", None),
        P(None, "wide", None),
        P(),
        P("section", "wide"),
        P("section", "wide"),
        P("section", "wide", None),
        P("section", None, "wide"),
        P("section", "wide", None),
        P("section", "wide"),
        P("section", "wide"),
        P("section", "wide"),
        P("section", "wide", None),
        P("section", None),
        P("section", None, "wide"),
        P("section", "wide"),
    )
    outs = (
        P("section", None, "wide", None),
        P("section", None, "wide", None),
        P("section", "wide"),
        P("section", "wide"),
        P("section", "wide", None),
        P("section", None, "wide"),
        P("section", "wide", None),
        P("section", "wide"),
        P("section", "wide"),
        P("section", "wide"),
        P("section", "wide", None),
        P("section", None),
        P("section", None, "wide"),
        P("section", "wide"),
    )
    return ins, outs


def solution(mesh):
    ins, outs = specs()
    body = on_device if mesh.shape["wide"] == HEADS else on_device_near
    return jax.shard_map(body, mesh=mesh, in_specs=ins, out_specs=outs, check_vma=False)
```
